32 devices in a mesh: ens: 4 (over y, x), horiz: 8 (over z, core).
Axes of the slice: x: 2, y: 2, z: 4, core: 2. Of those that a mesh axis runs over, the one named last changes fastest.
Arguments:
- prognostic: float32 [4, 128, 32, 128], P('ens', None, 'horiz'), may hold values from -6 to 6
- diffusivity: float32 [4, 32, 32, 128], P('ens', None, 'horiz'), may hold values from 0.1 to 10
- mixing: float32 [2, 32, 128], P(None, 'horiz'), may hold values from 0.03 to 0.24
- cotangent: float32 [4, 128, 32, 128], P('ens', None, 'horiz'), may hold values from -6 to 6
- tile_cols: int32 [4, 8, 3, 128], P('ens', 'horiz'), may hold values from 0 to 511, as said below
- pad_mask: int32 [4, 8, 3, 128], P('ens', 'horiz'), may hold values 0 or 1
- tile_count: int32 [4, 8], P('ens', 'horiz'), may hold values from 1 to 3, as said below
- w_in: bfloat16 [1024, 128], replicated, may hold values from -0.5 to 0.5
- w_mid: bfloat16 [1024, 1024], replicated, may hold values from -0.1875 to 0.1875
- w_out: bfloat16 [128, 1024], replicated, may hold values from -0.1875 to 0.1875
Outputs:
- state_next: float32 [4, 128, 32, 128], P('ens', None, 'horiz')
- state_grad: float32 [4, 128, 32, 128], P('ens', None, 'horiz')
- grad_in: float32 [1024, 128], replicated
- grad_mid: float32 [1024, 1024], replicated
- grad_out: float32 [128, 1024], replicated
The draws below stay inside these ranges and needn't reach their ends.
Inputs may be any that keep to these rules, and one draw needn't show every extreme that they name: `tile_cols`: within one member and block all 3 x 128 entries name different columns. Tiles 0 to tile_count - 1 of a block are in use; in every member some block uses all 3.
All inputs are finite; a program needn't handle non-finite values. No bound on the sum of `pad_mask` on one device may be relied on, other than what follows from the above.
Results may differ from the reference program's by a relative error of at most 0.0071.
Values may be sent and summed in bfloat16 or wider, within the bound.
No kernel may reach another device: no remote copies, remote signals or barrier semaphores. Data moves between devices by JAX's collectives and lax.ppermute only.
A program may use at most 64 MiB of HBM per device.

```python
import math
import jax
import jax.numpy as jnp
from jax import lax

LEVELS = 32
UNITS = 1024
LATITUDES = 128
TILE_COLS = 128
DYN_STEPS = 2
FIELDS = 128
CELLS = 512
TILES_DEV = 3
MEMBERS = 4
BLOCKS = 8
LONGITUDES = 32
COLUMNS = 16384


def draw_tile_cols(key, part):
    block_keys = jax.random.split(key, MEMBERS * BLOCKS)

    def one_block(block_key):
        return jax.random.permutation(block_key, CELLS)[:TILES_DEV * TILE_COLS]
    picked = jax.vmap(one_block)(block_keys)
    return picked.reshape(MEMBERS, BLOCKS, TILES_DEV, TILE_COLS).astype(jnp.int32)


def draw_tile_count(key, part):
    draw_key, pick_key = jax.random.split(key)
    spread_draw = jax.random.randint(draw_key, (MEMBERS, BLOCKS), 0, TILES_DEV)
    counts = 1 + spread_draw * spread_draw // TILES_DEV
    busiest = jax.random.randint(pick_key, (MEMBERS, 1), 0, BLOCKS)
    block_index = jnp.arange(BLOCKS)[None, :]
    return jnp.where(block_index == busiest, TILES_DEV, counts).astype(jnp.int32)


def set_ends(entries, own_key, least, largest):
    place = [jax.random.randint(jax.random.fold_in(own_key, axis), (), 0, length) for axis, length in enumerate(entries.shape)]
    longest = entries.shape.index(max(entries.shape))
    next_to = place[:longest] + [(place[longest] + 1) % entries.shape[longest]] + place[longest + 1:]
    return entries.at[tuple(place)].set(least).at[tuple(next_to)].set(largest)


def steps_of(stream_key, dims, shards, least, high):
    gain, own = 1.0, jax.random.fold_in(stream_key, 6)
    for axis_at, parts in shards:
        draws = jnp.exp(jax.random.uniform(jax.random.fold_in(own, axis_at), (parts,), jnp.float32, least / len(shards), high / len(shards)))
        gain = gain * jnp.repeat(draws, dims[axis_at] // parts).reshape([-1 if axis == axis_at else 1 for axis in range(len(dims))])
    return gain


def bell_draw(rng, extent, deviation, most, pieces=(), held_as=jnp.bfloat16):
    values = jax.random.normal(rng, extent, jnp.float32) * deviation
    if len(pieces) > 0:
        values = steps_of(rng, extent, pieces, -0.22, 0.18) * values
    return jnp.clip(values, min=-most, max=most).astype(held_as)


def setup_inputs(seed: int = 0) -> dict:
    key_of = jax.random.split(jax.random.key(seed), 11)
    prognostic = bell_draw(key_of[0], (MEMBERS, FIELDS, LONGITUDES, LATITUDES), 1.0, 6.0, ((0, 4), (2, 8)), jnp.float32)
    diffusivity = jnp.clip(jnp.exp(math.log(10.0) - 4.6051702 * jax.random.uniform(key_of[1], (MEMBERS, LEVELS, LONGITUDES, LATITUDES), jnp.float32) ** steps_of(key_of[1], (MEMBERS, LEVELS, LONGITUDES, LATITUDES), ((0, 4), (2, 8)), -0.2, 0.2)), 0.1, 10.0)
    mixing = jnp.clip(jnp.exp(math.log(0.24) - 2.0794415 * jax.random.uniform(key_of[2], (2, LONGITUDES, LATITUDES), jnp.float32) ** steps_of(key_of[2], (2, LONGITUDES, LATITUDES), ((1, 8),), -0.2, 0.2)), 0.03, 0.24)
    cotangent = bell_draw(key_of[3], (MEMBERS, FIELDS, LONGITUDES, LATITUDES), 1.0, 6.0, ((0, 4), (2, 8)), jnp.float32)
    tile_cols = draw_tile_cols(jax.random.fold_in(key_of[10], 71), 0)
    pad_mask = set_ends((jax.random.randint(key_of[5], (MEMBERS, BLOCKS, TILES_DEV, TILE_COLS), 0, 4) < 3).astype(jnp.int32), jax.random.fold_in(key_of[5], 1), 0, 1)
    tile_count = draw_tile_count(jax.random.fold_in(key_of[10], 71), 0)
    w_in = bell_draw(key_of[7], (UNITS, FIELDS), FIELDS ** -0.5, 0.5)
    w_mid = bell_draw(key_of[8], (UNITS, UNITS), UNITS ** -0.5, 0.1875)
    w_out = bell_draw(key_of[9], (FIELDS, UNITS), UNITS ** -0.5, 0.1875)
    return dict(prognostic=prognostic, diffusivity=diffusivity, mixing=mixing, cotangent=cotangent, tile_cols=tile_cols, pad_mask=pad_mask, tile_count=tile_count, w_in=w_in, w_mid=w_mid, w_out=w_out)


def stencil_step(field_now, coef_lon, coef_lat):
    east_flux = coef_lon * (jnp.roll(field_now, -1, axis=-2) - field_now)
    west_flux = jnp.roll(east_flux, 1, axis=-2)
    rising = jnp.concatenate([field_now[..., 1:] - field_now[..., :-1], jnp.zeros_like(field_now[..., :1])], axis=-1)
    north_flux = coef_lat * rising
    south_flux = jnp.concatenate([jnp.zeros_like(north_flux[..., :1]), north_flux[..., :-1]], axis=-1)
    return field_now + east_flux - west_flux + (north_flux - south_flux)

def evolve(field_now, mixing):
    for repeat in range(DYN_STEPS):
        field_now = stencil_step(field_now, mixing[0], mixing[1])
    return field_now

def silu_slope(pre_act):
    sigma_val = jax.nn.sigmoid(pre_act)
    return sigma_val * (1.0 + pre_act * (1.0 - sigma_val))

def vertical_solve(coefficient, right_side):
    coef_below = jnp.concatenate([jnp.zeros_like(coefficient[:1]), coefficient[:-1]], axis=0)
    coef_above = jnp.concatenate([coefficient[:-1], jnp.zeros_like(coefficient[:1])], axis=0)
    diag_term = 1.0 + coef_below + coefficient
    by_level = jnp.transpose(right_side, (1, 0, 2))

    def sweep_down(carried, inputs):
        prev_ratio, prev_value = carried
        below_now, above_now, diag_now, right_now = inputs
        divisor = diag_now + below_now * prev_ratio
        ratio_now = -above_now / divisor
        value_now = (right_now + below_now * prev_value) / divisor
        return ((ratio_now, value_now), (ratio_now, value_now))
    start_state = (jnp.zeros_like(coefficient[0]), jnp.zeros_like(by_level[0]))
    _, (ratios, values) = lax.scan(sweep_down, start_state, (coef_below, coef_above, diag_term, by_level))

    def sweep_up(carried, inputs):
        ratio_now, value_now = inputs
        result = value_now - ratio_now * carried
        return (result, result)
    _, solved = lax.scan(sweep_up, jnp.zeros_like(by_level[0]), (ratios, values), reverse=True)
    return jnp.transpose(solved, (1, 0, 2))

def column_physics(x_tile, coef_tile, cot_tile, w_in, w_mid, w_out):
    fields = x_tile.shape[0]
    levels = coef_tile.shape[0]
    var_count = fields // levels
    contract_cols = (((1,), (1,)), ((), ()))
    contract_rows = (((0,), (0,)), ((), ()))
    pre_one = jnp.dot(w_in, x_tile, preferred_element_type=jnp.float32)
    act_one = jax.nn.silu(pre_one).astype(jnp.bfloat16)
    pre_two = jnp.dot(w_mid, act_one, preferred_element_type=jnp.float32)
    act_two = jax.nn.silu(pre_two).astype(jnp.bfloat16)
    tendency = jnp.dot(w_out, act_two, preferred_element_type=jnp.float32)
    coefficient = coef_tile.astype(jnp.float32)
    forced = (x_tile.astype(jnp.float32) + tendency).reshape(var_count, levels, -1)
    new_tile = vertical_solve(coefficient, forced).reshape(fields, -1)
    adjoint = vertical_solve(coefficient, cot_tile.astype(jnp.float32).reshape(var_count, levels, -1)).reshape(fields, -1)
    adjoint_half = adjoint.astype(jnp.bfloat16)
    grad_out = lax.dot_general(adjoint_half, act_two, contract_cols, preferred_element_type=jnp.float32)
    back_two = lax.dot_general(w_out, adjoint_half, contract_rows, preferred_element_type=jnp.float32)
    delta_two = (back_two * silu_slope(pre_two)).astype(jnp.bfloat16)
    grad_mid = lax.dot_general(delta_two, act_one, contract_cols, preferred_element_type=jnp.float32)
    back_one = lax.dot_general(w_mid, delta_two, contract_rows, preferred_element_type=jnp.float32)
    delta_one = (back_one * silu_slope(pre_one)).astype(jnp.bfloat16)
    grad_in = lax.dot_general(delta_one, x_tile, contract_cols, preferred_element_type=jnp.float32)
    grad_x = adjoint + lax.dot_general(w_in, delta_one, contract_rows, preferred_element_type=jnp.float32)
    return (new_tile.astype(jnp.bfloat16), grad_x.astype(jnp.bfloat16), grad_in, grad_mid, grad_out)

def to_blocks(field_now):
    members, row_count, longitudes, latitudes = field_now.shape
    split_view = field_now.reshape(members, row_count, BLOCKS, longitudes // BLOCKS * latitudes)
    return jnp.transpose(split_view, (0, 2, 1, 3))

def from_blocks(blocks, full_shape):
    return jnp.transpose(blocks, (0, 2, 1, 3)).reshape(full_shape)

def gather_tiles(blocks, tile_cols):

    def one_block(block_vals, columns):
        return block_vals[:, columns.reshape(-1)]
    picked = jax.vmap(jax.vmap(one_block))(blocks, tile_cols)
    members, block_total, row_count, _ = picked.shape
    return jnp.transpose(picked.reshape(members, block_total, row_count, TILES_DEV, TILE_COLS), (0, 1, 3, 2, 4))

def place_tiles(blocks, tile_cols, tile_vals, live_mask):

    def one_block(block_vals, columns, vals_here, live_here):
        flat_cols = columns.reshape(-1)
        row_count = block_vals.shape[0]
        fresh_vals = jnp.transpose(vals_here, (1, 0, 2)).reshape(row_count, -1).astype(jnp.float32)
        kept_vals = block_vals[:, flat_cols]
        return block_vals.at[:, flat_cols].set(jnp.where(live_here.reshape(-1)[None, :] > 0, fresh_vals, kept_vals))
    return jax.vmap(jax.vmap(one_block))(blocks, tile_cols, tile_vals, live_mask)

def flatten_tiles(tiles_arr):
    return tiles_arr.reshape((-1,) + tiles_arr.shape[3:])

def reference(prognostic, diffusivity, mixing, cotangent, tile_cols, pad_mask, tile_count, w_in, w_mid, w_out):
    moved = evolve(prognostic, mixing)
    tile_index = jnp.arange(TILES_DEV, dtype=jnp.int32)
    active = tile_index[None, None, :] < tile_count[:, :, None]
    live_mask = pad_mask * active[..., None].astype(jnp.int32)
    x_tiles = gather_tiles(to_blocks(moved), tile_cols).astype(jnp.bfloat16)
    coef_tiles = gather_tiles(to_blocks(diffusivity), tile_cols).astype(jnp.bfloat16)
    cot_tiles = (gather_tiles(to_blocks(cotangent), tile_cols) * live_mask[:, :, :, None, :].astype(jnp.float32)).astype(jnp.bfloat16)

    def visit(carried, inputs):
        sum_in, sum_mid, sum_out = carried
        x_tile, coef_tile, cot_tile, live_flag = inputs

        def compute(operands):
            return column_physics(operands[0], operands[1], operands[2], w_in, w_mid, w_out)

        def skip_tile(operands):
            return (jnp.zeros((FIELDS, TILE_COLS), jnp.bfloat16), jnp.zeros((FIELDS, TILE_COLS), jnp.bfloat16), jnp.zeros((UNITS, FIELDS), jnp.float32), jnp.zeros((UNITS, UNITS), jnp.float32), jnp.zeros((FIELDS, UNITS), jnp.float32))
        results = lax.cond(live_flag, compute, skip_tile, (x_tile, coef_tile, cot_tile))
        return ((sum_in + results[2], sum_mid + results[3], sum_out + results[4]), (results[0], results[1]))
    start_sums = (jnp.zeros((UNITS, FIELDS), jnp.float32), jnp.zeros((UNITS, UNITS), jnp.float32), jnp.zeros((FIELDS, UNITS), jnp.float32))
    sums, (new_tiles, grad_tiles) = lax.scan(visit, start_sums, (flatten_tiles(x_tiles), flatten_tiles(coef_tiles), flatten_tiles(cot_tiles), active.reshape(-1)))
    new_tiles = new_tiles.reshape(MEMBERS, BLOCKS, TILES_DEV, FIELDS, TILE_COLS)
    grad_tiles = grad_tiles.reshape(MEMBERS, BLOCKS, TILES_DEV, FIELDS, TILE_COLS)
    state_next = from_blocks(place_tiles(to_blocks(moved), tile_cols, new_tiles, live_mask), moved.shape)
    grad_field = from_blocks(place_tiles(to_blocks(cotangent), tile_cols, grad_tiles, live_mask), cotangent.shape)
    state_grad = evolve(grad_field, mixing)
    factor = 1.0 / math.sqrt(COLUMNS)
    return (state_next, state_grad, sums[0] * factor, sums[1] * factor, sums[2] * factor)
```

```python
import functools
import math

import jax
import jax.numpy as jnp
from jax import lax
from jax.experimental import pallas as pl
from jax.experimental.pallas import tpu as pltpu
from jax.sharding import PartitionSpec as P

DYN_STEPS = 2
BLOCK = 256
VMEM_LIMIT = 40 * 1024 * 1024
F32 = jnp.float32
BF16 = jnp.bfloat16
CONTRACT_LAST = (((1,), (1,)), ((), ()))
CONTRACT_FIRST = (((0,), (0,)), ((), ()))


def call(kernel, outs, scratch=(), smem=(), flops=0, moved=0, **names):
    def run(*operands):
        specs = [
            pl.BlockSpec(memory_space=pltpu.SMEM if place in smem else pltpu.VMEM)
            for place in range(len(operands))
        ]
        return pl.pallas_call(
            functools.partial(kernel, **names),
            out_shape=[jax.ShapeDtypeStruct(shape, dtype) for shape, dtype in outs],
            in_specs=specs,
            out_specs=[pl.BlockSpec(memory_space=pltpu.VMEM)] * len(outs),
            scratch_shapes=list(scratch),
            compiler_params=pltpu.CompilerParams(vmem_limit_bytes=VMEM_LIMIT),
            cost_estimate=pl.CostEstimate(flops=flops, bytes_accessed=moved, transcendentals=0),
        )(*operands)

    return run


def lat_term(field_now, coef_masked):
    lats = field_now.shape[1]
    north_flux = coef_masked * (pltpu.roll(field_now, lats - 1, 1) - field_now)
    return north_flux - pltpu.roll(north_flux, 1, 1)


def two_steps(rows, lon_coef, lat_coef):
    for repeat in range(DYN_STEPS):
        count = len(rows)
        fluxes = [
            lon_coef[place + repeat] * (rows[place + 1] - rows[place]) for place in range(count - 1)
        ]
        rows = [
            rows[place]
            + fluxes[place]
            - fluxes[place - 1]
            + lat_term(rows[place], lat_coef[place + repeat])
            for place in range(1, count - 1)
        ]
    return rows


def coefficients(mix_ref, low_mix, high_mix, lons):
    lats = mix_ref.shape[1]
    lane = lax.broadcasted_iota(jnp.int32, (1, lats), 1)
    inside = lane < lats - 1
    own_lon = [mix_ref[lon : lon + 1, :] for lon in range(lons)]
    own_lat = [mix_ref[lons + lon : lons + lon + 1, :] for lon in range(lons)]
    lon_coef = [low_mix[0:1, :], low_mix[1:2, :]] + own_lon + [high_mix[0:1, :], high_mix[1:2, :]]
    lat_coef = [low_mix[2:3, :], low_mix[3:4, :]] + own_lat + [high_mix[2:3, :], high_mix[3:4, :]]
    return lon_coef, [jnp.where(inside, coef, 0.0) for coef in lat_coef]


def pack_kernel(prog_ref, mix_ref, up_ref, down_ref, *, lons):
    fields = prog_ref.shape[0] // lons
    for out_ref, first in ((up_ref, lons - 2), (down_ref, 0)):
        for side in range(2):
            out_ref[side * fields : (side + 1) * fields, :] = prog_ref[
                pl.ds(first + side, fields, stride=lons), :
            ]
        out_ref[2 * fields : 2 * fields + 2, :] = mix_ref[first : first + 2, :]
        out_ref[2 * fields + 2 : 2 * fields + 4, :] = mix_ref[lons + first : lons + first + 2, :]
        out_ref[2 * fields + 4 :, :] = jnp.zeros_like(out_ref[2 * fields + 4 :, :])


def one_hot(cols_ref, cells):
    parts = []
    for tile in range(cols_ref.shape[0]):
        place = lax.broadcasted_iota(jnp.int32, (cells, cols_ref.shape[1]), 0)
        parts.append(jnp.where(place == cols_ref[tile : tile + 1, :], 1.0, 0.0))
    return jnp.concatenate(parts, axis=1).astype(BF16)


def live_row(count_ref, mask_ref):
    parts = []
    for tile in range(mask_ref.shape[0]):
        used = jnp.where(tile < count_ref[0, 0], 1, 0)
        parts.append((mask_ref[tile : tile + 1, :] * used).astype(F32))
    return jnp.concatenate(parts, axis=1)


def level_rows(levels, level, variables):
    return pl.ds(level, variables, stride=levels)


def solve(levels, variables, coef_ref, ratio_ref, inverse_ref, right_ref, out_ref):
    tiles, _, width = right_ref.shape
    spans = [slice(tile * width, (tile + 1) * width) for tile in range(tiles)]
    values = []
    for level in range(levels):
        inverse_now = inverse_ref[level : level + 1, :]
        if level > 0:
            carry_now = coef_ref[level - 1 : level, :] * inverse_now
        step = []
        for tile, span in enumerate(spans):
            right_now = right_ref[tile, level_rows(levels, level, variables), :]
            value_now = right_now * inverse_now[:, span]
            if level > 0:
                value_now = value_now + carry_now[:, span] * values[-1][tile]
            step.append(value_now)
        values.append(step)
    results = values[-1]
    for level in range(levels - 1, -1, -1):
        if level < levels - 1:
            ratio_now = ratio_ref[level : level + 1, :]
            results = [
                values[level][tile] - ratio_now[:, span] * results[tile]
                for tile, span in enumerate(spans)
            ]
        for tile in range(tiles):
            out_ref[tile, level_rows(levels, level, variables), :] = results[tile]


def split_tiles(ref, value):
    width = ref.shape[2]
    for tile in range(ref.shape[0]):
        ref[tile] = value[:, tile * width : (tile + 1) * width]


def join_tiles(ref):
    return jnp.concatenate([ref[tile] for tile in range(ref.shape[0])], axis=1)


def factorise(levels, coef_ref, ratio_ref, inverse_ref):
    ratio_prev = None
    for level in range(levels):
        coef_now = coef_ref[level : level + 1, :]
        divisor = 1.0 + coef_now
        if level > 0:
            below_now = coef_ref[level - 1 : level, :]
            divisor = divisor + below_now + below_now * ratio_prev
        inverse_now = 1.0 / divisor
        ratio_prev = -coef_now * inverse_now
        inverse_ref[level : level + 1, :] = inverse_now
        ratio_ref[level : level + 1, :] = ratio_prev


def by_cell(ref, rows, lons):
    return jnp.concatenate(
        [ref[pl.ds(lon, rows, stride=lons), :] for lon in range(lons)], axis=1
    )


def adjoint_kernel(
    count_ref,
    diff_ref,
    cot_ref,
    cols_ref,
    mask_ref,
    adj_ref,
    coef_ref,
    ratio_ref,
    inverse_ref,
    right_ref,
    *,
    lons,
):
    levels = diff_ref.shape[0] // lons
    fields = cot_ref.shape[0] // lons
    cells = lons * cot_ref.shape[1]
    spread = one_hot(cols_ref, cells)
    sources = jnp.concatenate(
        [by_cell(cot_ref, fields, lons), by_cell(diff_ref, levels, lons)], axis=0
    ).astype(BF16)
    picked = jnp.dot(sources, spread, preferred_element_type=F32)
    split_tiles(right_ref, picked[:fields] * live_row(count_ref, mask_ref))
    coef_ref[...] = picked[fields:]
    factorise(levels, coef_ref, ratio_ref, inverse_ref)
    solve(levels, fields // levels, coef_ref, ratio_ref, inverse_ref, right_ref, adj_ref)


def sigmoid(pre_act):
    return 0.5 * jnp.tanh(0.5 * pre_act) + 0.5


def forward_kernel(
    prog_ref,
    low_ref,
    high_ref,
    mix_ref,
    cols_ref,
    adj_ref,
    w_in_ref,
    w_mid_ref,
    w_out_ref,
    moved_ref,
    x_ref,
    act_two_ref,
    delta_two_ref,
    grad_ref,
    act_one_ref,
    *,
    lons,
):
    fields = prog_ref.shape[0] // lons
    units = w_mid_ref.shape[0]
    cells = lons * prog_ref.shape[1]
    lon_coef, lat_coef = coefficients(
        mix_ref,
        low_ref[2 * fields : 2 * fields + 4, :],
        high_ref[2 * fields : 2 * fields + 4, :],
        lons,
    )
    rows = [low_ref[side * fields : (side + 1) * fields, :] for side in range(2)]
    rows += [prog_ref[pl.ds(lon, fields, stride=lons), :] for lon in range(lons)]
    rows += [high_ref[side * fields : (side + 1) * fields, :] for side in range(2)]
    rows = two_steps(rows, lon_coef, lat_coef)
    for lon in range(lons):
        moved_ref[lon] = rows[lon]
    spread = one_hot(cols_ref, cells)
    sources = jnp.concatenate(rows, axis=1).astype(BF16)
    x_now = jnp.dot(sources, spread, preferred_element_type=F32).astype(BF16)
    x_ref[...] = x_now
    for start in range(0, units, BLOCK):
        pre_one = jnp.dot(w_in_ref[start : start + BLOCK, :], x_now, preferred_element_type=F32)
        act_one_ref[start : start + BLOCK, :] = (pre_one * sigmoid(pre_one)).astype(BF16)
    adj_half = join_tiles(adj_ref).astype(BF16)
    for start in range(0, units, BLOCK):
        pre_two = jnp.dot(
            w_mid_ref[start : start + BLOCK, :], act_one_ref[...], preferred_element_type=F32
        )
        sigma_val = sigmoid(pre_two)
        act_two_ref[start : start + BLOCK, :] = (pre_two * sigma_val).astype(BF16)
        back_two = lax.dot_general(
            w_out_ref[:, start : start + BLOCK],
            adj_half,
            CONTRACT_FIRST,
            preferred_element_type=F32,
        )
        slope = sigma_val * (1.0 + pre_two * (1.0 - sigma_val))
        delta_two_ref[start : start + BLOCK, :] = (back_two * slope).astype(BF16)
    for start in range(0, units, BLOCK):
        grad_ref[start : start + BLOCK, :] = lax.dot_general(
            delta_two_ref[start : start + BLOCK, :],
            act_one_ref[...],
            CONTRACT_LAST,
            preferred_element_type=F32,
        ).astype(BF16)


def backward_kernel(
    count_ref,
    moved_ref,
    cot_ref,
    cols_ref,
    mask_ref,
    x_ref,
    act_two_ref,
    delta_two_ref,
    adj_ref,
    coef_ref,
    ratio_ref,
    inverse_ref,
    w_in_ref,
    w_mid_ref,
    w_out_ref,
    small_ref,
    state_ref,
    field_ref,
    up_ref,
    down_ref,
    delta_one_ref,
    forced_ref,
    solved_ref,
    *,
    lons,
):
    fields = x_ref.shape[0]
    units = w_mid_ref.shape[0]
    levels = coef_ref.shape[0]
    lats = moved_ref.shape[2]
    x_now = x_ref[...]
    adj_now = join_tiles(adj_ref)
    for start in range(0, units, BLOCK):
        back_one = lax.dot_general(
            w_mid_ref[:, start : start + BLOCK],
            delta_two_ref[...],
            CONTRACT_FIRST,
            preferred_element_type=F32,
        )
        pre_one = jnp.dot(w_in_ref[start : start + BLOCK, :], x_now, preferred_element_type=F32)
        sigma_val = sigmoid(pre_one)
        slope = sigma_val * (1.0 + pre_one * (1.0 - sigma_val))
        delta_one_ref[start : start + BLOCK, :] = (back_one * slope).astype(BF16)
    adj_half = adj_now.astype(BF16)
    small_ref[:, :fields] = lax.dot_general(
        delta_one_ref[...], x_now, CONTRACT_LAST, preferred_element_type=F32
    ).astype(BF16)
    small_ref[:, fields:] = lax.dot_general(
        act_two_ref[...], adj_half, CONTRACT_LAST, preferred_element_type=F32
    ).astype(BF16)
    grad_x = adj_now + lax.dot_general(
        w_in_ref[...], delta_one_ref[...], CONTRACT_FIRST, preferred_element_type=F32
    )
    tendency = jnp.dot(w_out_ref[...], act_two_ref[...], preferred_element_type=F32)
    split_tiles(forced_ref, x_now.astype(F32) + tendency)
    solve(levels, fields // levels, coef_ref, ratio_ref, inverse_ref, forced_ref, solved_ref)
    live = live_row(count_ref, mask_ref)
    fresh = jnp.concatenate(
        [
            join_tiles(solved_ref) * live,
            grad_x * live,
            jnp.broadcast_to(live, (16, live.shape[1])),
        ],
        axis=0,
    ).astype(BF16)
    spread = one_hot(cols_ref, lons * lats)
    placed = lax.dot_general(fresh, spread, CONTRACT_LAST, preferred_element_type=F32)
    for lon in range(lons):
        here = slice(lon * lats, (lon + 1) * lats)
        taken = placed[2 * fields : 2 * fields + 1, here] > 0.5
        state_ref[pl.ds(lon, fields, stride=lons), :] = jnp.where(
            taken, placed[:fields, here], moved_ref[lon]
        )
        field_now = jnp.where(
            taken, placed[fields : 2 * fields, here], cot_ref[pl.ds(lon, fields, stride=lons), :]
        )
        field_ref[lon] = field_now
        if lon < 2:
            down_ref[lon] = field_now
        if lon >= lons - 2:
            up_ref[lon - (lons - 2)] = field_now


def last_kernel(field_ref, low_ref, high_ref, low_mix_ref, high_mix_ref, mix_ref, out_ref, *, lons):
    fields = field_ref.shape[1]
    lon_coef, lat_coef = coefficients(
        mix_ref,
        low_mix_ref[2 * fields : 2 * fields + 4, :],
        high_mix_ref[2 * fields : 2 * fields + 4, :],
        lons,
    )
    rows = [low_ref[0], low_ref[1]]
    rows += [field_ref[lon] for lon in range(lons)]
    rows += [high_ref[0], high_ref[1]]
    rows = two_steps(rows, lon_coef, lat_coef)
    for lon in range(lons):
        out_ref[pl.ds(lon, fields, stride=lons), :] = rows[lon]


def to_neighbours(upward, downward, axis):
    count = lax.axis_size(axis)
    forward = [(i, (i + 1) % count) for i in range(count)]
    backward = [(target, source) for source, target in forward]
    return lax.ppermute(upward, axis, forward), lax.ppermute(downward, axis, backward)


def per_device(
    prognostic, diffusivity, mixing, cotangent, tile_cols, pad_mask, tile_count, w_in, w_mid, w_out
):
    fields, lons, lats = prognostic.shape[1:]
    levels = diffusivity.shape[1]
    units = w_mid.shape[0]
    tiles, width = tile_cols.shape[2:]
    slots = tiles * width
    prog_rows = prognostic.reshape(fields * lons, lats)
    cot_rows = cotangent.reshape(fields * lons, lats)
    diff_rows = diffusivity.reshape(levels * lons, lats)
    mix_rows = mixing.reshape(2 * lons, lats)
    cols, mask = tile_cols[0, 0], pad_mask[0, 0]

    packed = ((2 * fields + 8, lats), F32)
    up_pack, down_pack = call(pack_kernel, [packed, packed], lons=lons)(prog_rows, mix_rows)
    low_pack, high_pack = to_neighbours(up_pack, down_pack, "horiz")

    adjoint, coef, ratio, inverse = call(
        adjoint_kernel,
        [((tiles, fields, width), F32)] + [((levels, slots), F32)] * 3,
        scratch=[pltpu.VMEM((tiles, fields, width), F32)],
        smem=(0,),
        flops=10**9,
        moved=10**6,
        lons=lons,
    )(tile_count, diff_rows, cot_rows, cols, mask)

    moved, x_now, act_two, delta_two, grad_mid = call(
        forward_kernel,
        [
            ((lons, fields, lats), F32),
            ((fields, slots), BF16),
            ((units, slots), BF16),
            ((units, slots), BF16),
            ((units, units), BF16),
        ],
        scratch=[pltpu.VMEM((units, slots), BF16)],
        flops=2 * 10**9,
        moved=6 * 10**6,
        lons=lons,
    )(prog_rows, low_pack, high_pack, mix_rows, cols, adjoint, w_in, w_mid, w_out)

    small, state_rows, grad_field, up_rows, down_rows = call(
        backward_kernel,
        [
            ((units, 2 * fields), BF16),
            ((fields * lons, lats), F32),
            ((lons, fields, lats), F32),
            ((2, fields, lats), F32),
            ((2, fields, lats), F32),
        ],
        scratch=[
            pltpu.VMEM((units, slots), BF16),
            pltpu.VMEM((tiles, fields, width), F32),
            pltpu.VMEM((tiles, fields, width), F32),
        ],
        smem=(0,),
        flops=2 * 10**9,
        moved=6 * 10**6,
        lons=lons,
    )(
        tile_count,
        moved,
        cot_rows,
        cols,
        mask,
        x_now,
        act_two,
        delta_two,
        adjoint,
        coef,
        ratio,
        inverse,
        w_in,
        w_mid,
        w_out,
    )
    low_rows, high_rows = to_neighbours(up_rows, down_rows, "horiz")
    (grad_rows,) = call(last_kernel, [((fields * lons, lats), F32)], lons=lons)(
        grad_field, low_rows, high_rows, low_pack, high_pack, mix_rows
    )

    sum_mid, sum_small = lax.psum((grad_mid, small), ("ens", "horiz"))
    column_total = lax.axis_size("ens") * lax.axis_size("horiz") * lons * lats
    factor = 1.0 / math.sqrt(column_total)
    return (
        state_rows.reshape(prognostic.shape),
        grad_rows.reshape(prognostic.shape),
        sum_small[:, :fields].astype(F32) * factor,
        sum_mid.astype(F32) * factor,
        sum_small[:, fields:].astype(F32).T * factor,
    )


def solution(mesh):
    placed = (
        P("ens", None, "horiz", None),
        P("ens", None, "horiz", None),
        P(None, "horiz", None),
        P("ens", None, "horiz", None),
        P("ens", "horiz", None, None),
        P("ens", "horiz", None, None),
        P("ens", "horiz"),
        P(),
        P(),
        P(),
    )
    return jax.shard_map(
        per_device,
        mesh=mesh,
        in_specs=placed,
        out_specs=(P("ens", None, "horiz", None), P("ens", None, "horiz", None), P(), P(), P()),
        check_vma=False,
    )
```

```python
import functools
import math

import jax
import jax.numpy as jnp
from jax import lax
from jax.experimental import pallas as pl
from jax.experimental.pallas import tpu as pltpu
from jax.sharding import PartitionSpec as P

DYN_STEPS = 2
BLOCK = 256
VMEM_LIMIT = 40 * 1024 * 1024
F32 = jnp.float32
BF16 = jnp.bfloat16
CONTRACT_LAST = (((1,), (1,)), ((), ()))
CONTRACT_FIRST = (((0,), (0,)), ((), ()))


def call(kernel, outs, scratch=(), smem=(), flops=0, moved=0, **names):
    def run(*operands):
        specs = [
            pl.BlockSpec(memory_space=pltpu.SMEM if place in smem else pltpu.VMEM)
            for place in range(len(operands))
        ]
        return pl.pallas_call(
            functools.partial(kernel, **names),
            out_shape=[jax.ShapeDtypeStruct(shape, dtype) for shape, dtype in outs],
            in_specs=specs,
            out_specs=[pl.BlockSpec(memory_space=pltpu.VMEM)] * len(outs),
            scratch_shapes=list(scratch),
            compiler_params=pltpu.CompilerParams(vmem_limit_bytes=VMEM_LIMIT),
            cost_estimate=pl.CostEstimate(flops=flops, bytes_accessed=moved, transcendentals=0),
        )(*operands)

    return run


def lat_term(field_now, coef_masked):
    lats = field_now.shape[1]
    north_flux = coef_masked * (pltpu.roll(field_now, lats - 1, 1) - field_now)
    return north_flux - pltpu.roll(north_flux, 1, 1)


def two_steps(rows, lon_coef, lat_coef):
    for repeat in range(DYN_STEPS):
        count = len(rows)
        fluxes = [
            lon_coef[place + repeat] * (rows[place + 1] - rows[place]) for place in range(count - 1)
        ]
        rows = [
            rows[place]
            + fluxes[place]
            - fluxes[place - 1]
            + lat_term(rows[place], lat_coef[place + repeat])
            for place in range(1, count - 1)
        ]
    return rows


def coefficients(mix_ref, low_mix, high_mix, lons):
    lats = mix_ref.shape[1]
    lane = lax.broadcasted_iota(jnp.int32, (1, lats), 1)
    inside = lane < lats - 1
    own_lon = [mix_ref[lon : lon + 1, :] for lon in range(lons)]
    own_lat = [mix_ref[lons + lon : lons + lon + 1, :] for lon in range(lons)]
    lon_coef = [low_mix[0:1, :], low_mix[1:2, :]] + own_lon + [high_mix[0:1, :], high_mix[1:2, :]]
    lat_coef = [low_mix[2:3, :], low_mix[3:4, :]] + own_lat + [high_mix[2:3, :], high_mix[3:4, :]]
    return lon_coef, [jnp.where(inside, coef, 0.0) for coef in lat_coef]


def pack_kernel(prog_ref, mix_ref, up_ref, down_ref, *, lons):
    fields = prog_ref.shape[0] // lons
    for out_ref, first in ((up_ref, lons - 2), (down_ref, 0)):
        for side in range(2):
            out_ref[side * fields : (side + 1) * fields, :] = prog_ref[
                pl.ds(first + side, fields, stride=lons), :
            ]
        out_ref[2 * fields : 2 * fields + 2, :] = mix_ref[first : first + 2, :]
        out_ref[2 * fields + 2 : 2 * fields + 4, :] = mix_ref[lons + first : lons + first + 2, :]
        out_ref[2 * fields + 4 :, :] = jnp.zeros_like(out_ref[2 * fields + 4 :, :])


def one_hot(cols_ref, cells):
    parts = []
    for tile in range(cols_ref.shape[0]):
        place = lax.broadcasted_iota(jnp.int32, (cells, cols_ref.shape[1]), 0)
        parts.append(jnp.where(place == cols_ref[tile : tile + 1, :], 1.0, 0.0))
    return jnp.concatenate(parts, axis=1).astype(BF16)


def live_row(count_ref, mask_ref):
    parts = []
    for tile in range(mask_ref.shape[0]):
        used = jnp.where(tile < count_ref[0, 0], 1, 0)
        parts.append((mask_ref[tile : tile + 1, :] * used).astype(F32))
    return jnp.concatenate(parts, axis=1)


def level_rows(levels, level, variables):
    return pl.ds(level, variables, stride=levels)


def solve(levels, variables, coef_ref, ratio_ref, inverse_ref, right_ref, out_ref):
    tiles, _, width = right_ref.shape
    spans = [slice(tile * width, (tile + 1) * width) for tile in range(tiles)]
    values = []
    for level in range(levels):
        inverse_now = inverse_ref[level : level + 1, :]
        if level > 0:
            carry_now = coef_ref[level - 1 : level, :] * inverse_now
        step = []
        for tile, span in enumerate(spans):
            right_now = right_ref[tile, level_rows(levels, level, variables), :]
            value_now = right_now * inverse_now[:, span]
            if level > 0:
                value_now = value_now + carry_now[:, span] * values[-1][tile]
            step.append(value_now)
        values.append(step)
    results = values[-1]
    for level in range(levels - 1, -1, -1):
        if level < levels - 1:
            ratio_now = ratio_ref[level : level + 1, :]
            results = [
                values[level][tile] - ratio_now[:, span] * results[tile]
                for tile, span in enumerate(spans)
            ]
        for tile in range(tiles):
            out_ref[tile, level_rows(levels, level, variables), :] = results[tile]


def split_tiles(ref, value):
    width = ref.shape[2]
    for tile in range(ref.shape[0]):
        ref[tile] = value[:, tile * width : (tile + 1) * width]


def join_tiles(ref):
    return jnp.concatenate([ref[tile] for tile in range(ref.shape[0])], axis=1)


def factorise(levels, coef_ref, ratio_ref, inverse_ref):
    ratio_prev = None
    for level in range(levels):
        coef_now = coef_ref[level : level + 1, :]
        divisor = 1.0 + coef_now
        if level > 0:
            below_now = coef_ref[level - 1 : level, :]
            divisor = divisor + below_now + below_now * ratio_prev
        inverse_now = 1.0 / divisor
        ratio_prev = -coef_now * inverse_now
        inverse_ref[level : level + 1, :] = inverse_now
        ratio_ref[level : level + 1, :] = ratio_prev


def by_cell(ref, rows, lons):
    return jnp.concatenate(
        [ref[pl.ds(lon, rows, stride=lons), :] for lon in range(lons)], axis=1
    )


def adjoint_kernel(
    count_ref,
    diff_ref,
    cot_ref,
    cols_ref,
    mask_ref,
    adj_ref,
    coef_ref,
    ratio_ref,
    inverse_ref,
    right_ref,
    *,
    lons,
):
    levels = diff_ref.shape[0] // lons
    fields = cot_ref.shape[0] // lons
    cells = lons * cot_ref.shape[1]
    spread = one_hot(cols_ref, cells)
    sources = jnp.concatenate(
        [by_cell(cot_ref, fields, lons), by_cell(diff_ref, levels, lons)], axis=0
    ).astype(BF16)
    picked = jnp.dot(sources, spread, preferred_element_type=F32)
    split_tiles(right_ref, picked[:fields] * live_row(count_ref, mask_ref))
    coef_ref[...] = picked[fields:]
    factorise(levels, coef_ref, ratio_ref, inverse_ref)
    solve(levels, fields // levels, coef_ref, ratio_ref, inverse_ref, right_ref, adj_ref)


def sigmoid(pre_act):
    return 0.5 * jnp.tanh(0.5 * pre_act) + 0.5


def forward_kernel(
    prog_ref,
    low_ref,
    high_ref,
    mix_ref,
    cols_ref,
    adj_ref,
    w_in_ref,
    w_mid_ref,
    w_out_ref,
    place_ref,
    moved_ref,
    x_ref,
    act_two_ref,
    delta_two_ref,
    keep_ref,
    send_ref,
    act_one_ref,
    *,
    lons,
):
    fields = prog_ref.shape[0] // lons
    units = w_mid_ref.shape[0]
    cells = lons * prog_ref.shape[1]
    lon_coef, lat_coef = coefficients(
        mix_ref,
        low_ref[2 * fields : 2 * fields + 4, :],
        high_ref[2 * fields : 2 * fields + 4, :],
        lons,
    )
    rows = [low_ref[side * fields : (side + 1) * fields, :] for side in range(2)]
    rows += [prog_ref[pl.ds(lon, fields, stride=lons), :] for lon in range(lons)]
    rows += [high_ref[side * fields : (side + 1) * fields, :] for side in range(2)]
    rows = two_steps(rows, lon_coef, lat_coef)
    for lon in range(lons):
        moved_ref[lon] = rows[lon]
    spread = one_hot(cols_ref, cells)
    sources = jnp.concatenate(rows, axis=1).astype(BF16)
    x_now = jnp.dot(sources, spread, preferred_element_type=F32).astype(BF16)
    x_ref[...] = x_now
    for start in range(0, units, BLOCK):
        pre_one = jnp.dot(w_in_ref[start : start + BLOCK, :], x_now, preferred_element_type=F32)
        act_one_ref[start : start + BLOCK, :] = (pre_one * sigmoid(pre_one)).astype(BF16)
    adj_half = join_tiles(adj_ref).astype(BF16)
    for start in range(0, units, BLOCK):
        pre_two = jnp.dot(
            w_mid_ref[start : start + BLOCK, :], act_one_ref[...], preferred_element_type=F32
        )
        sigma_val = sigmoid(pre_two)
        act_two_ref[start : start + BLOCK, :] = (pre_two * sigma_val).astype(BF16)
        back_two = lax.dot_general(
            w_out_ref[:, start : start + BLOCK],
            adj_half,
            CONTRACT_FIRST,
            preferred_element_type=F32,
        )
        slope = sigma_val * (1.0 + pre_two * (1.0 - sigma_val))
        delta_two_ref[start : start + BLOCK, :] = (back_two * slope).astype(BF16)
    for out_ref, half in ((send_ref, 1 - place_ref[0, 0]), (keep_ref, place_ref[0, 0])):
        for start in range(0, units // 2, BLOCK):
            out_ref[start : start + BLOCK, :] = lax.dot_general(
                delta_two_ref[pl.ds(half * (units // 2) + start, BLOCK), :],
                act_one_ref[...],
                CONTRACT_LAST,
                preferred_element_type=F32,
            ).astype(BF16)


def backward_kernel(
    count_ref,
    moved_ref,
    cot_ref,
    cols_ref,
    mask_ref,
    x_ref,
    act_two_ref,
    delta_two_ref,
    adj_ref,
    coef_ref,
    ratio_ref,
    inverse_ref,
    w_in_ref,
    w_mid_ref,
    w_out_ref,
    place_ref,
    keep_ref,
    send_ref,
    state_ref,
    field_ref,
    up_ref,
    down_ref,
    delta_one_ref,
    forced_ref,
    solved_ref,
    *,
    lons,
):
    fields = x_ref.shape[0]
    units = w_mid_ref.shape[0]
    levels = coef_ref.shape[0]
    lats = moved_ref.shape[2]
    x_now = x_ref[...]
    adj_now = join_tiles(adj_ref)
    for start in range(0, units, BLOCK):
        back_one = lax.dot_general(
            w_mid_ref[:, start : start + BLOCK],
            delta_two_ref[...],
            CONTRACT_FIRST,
            preferred_element_type=F32,
        )
        pre_one = jnp.dot(w_in_ref[start : start + BLOCK, :], x_now, preferred_element_type=F32)
        sigma_val = sigmoid(pre_one)
        slope = sigma_val * (1.0 + pre_one * (1.0 - sigma_val))
        delta_one_ref[start : start + BLOCK, :] = (back_one * slope).astype(BF16)
    adj_half = adj_now.astype(BF16)
    for out_ref, half in ((send_ref, 1 - place_ref[0, 0]), (keep_ref, place_ref[0, 0])):
        here = pl.ds(half * (units // 2), units // 2)
        out_ref[:, :fields] = lax.dot_general(
            delta_one_ref[here, :], x_now, CONTRACT_LAST, preferred_element_type=F32
        ).astype(BF16)
        out_ref[:, fields:] = lax.dot_general(
            act_two_ref[here, :], adj_half, CONTRACT_LAST, preferred_element_type=F32
        ).astype(BF16)
    grad_x = adj_now + lax.dot_general(
        w_in_ref[...], delta_one_ref[...], CONTRACT_FIRST, preferred_element_type=F32
    )
    tendency = jnp.dot(w_out_ref[...], act_two_ref[...], preferred_element_type=F32)
    split_tiles(forced_ref, x_now.astype(F32) + tendency)
    solve(levels, fields // levels, coef_ref, ratio_ref, inverse_ref, forced_ref, solved_ref)
    live = live_row(count_ref, mask_ref)
    fresh = jnp.concatenate(
        [
            join_tiles(solved_ref) * live,
            grad_x * live,
            jnp.broadcast_to(live, (16, live.shape[1])),
        ],
        axis=0,
    ).astype(BF16)
    spread = one_hot(cols_ref, lons * lats)
    placed = lax.dot_general(fresh, spread, CONTRACT_LAST, preferred_element_type=F32)
    for lon in range(lons):
        here = slice(lon * lats, (lon + 1) * lats)
        taken = placed[2 * fields : 2 * fields + 1, here] > 0.5
        state_ref[pl.ds(lon, fields, stride=lons), :] = jnp.where(
            taken, placed[:fields, here], moved_ref[lon]
        )
        field_now = jnp.where(
            taken, placed[fields : 2 * fields, here], cot_ref[pl.ds(lon, fields, stride=lons), :]
        )
        field_ref[lon] = field_now
        if lon < 2:
            down_ref[lon] = field_now
        if lon >= lons - 2:
            up_ref[lon - (lons - 2)] = field_now


def last_kernel(field_ref, low_ref, high_ref, low_mix_ref, high_mix_ref, mix_ref, out_ref, *, lons):
    fields = field_ref.shape[1]
    lon_coef, lat_coef = coefficients(
        mix_ref,
        low_mix_ref[2 * fields : 2 * fields + 4, :],
        high_mix_ref[2 * fields : 2 * fields + 4, :],
        lons,
    )
    rows = [low_ref[0], low_ref[1]]
    rows += [field_ref[lon] for lon in range(lons)]
    rows += [high_ref[0], high_ref[1]]
    rows = two_steps(rows, lon_coef, lat_coef)
    for lon in range(lons):
        out_ref[pl.ds(lon, fields, stride=lons), :] = rows[lon]


def core_sum_kernel(place_ref, *refs, parts):
    keeps, gots, outs = refs[: len(refs[:-parts]) // 2], refs[len(refs[:-parts]) // 2 : -parts], refs[-parts:]
    rows = outs[0].shape[0]
    for k in range(parts):
        start = pl.multiple_of((place_ref[0, 1] ^ k) * rows, rows)
        first = 0
        for keep_ref, got_ref in zip(keeps, gots):
            here = pl.ds(start, rows)
            columns = keep_ref.shape[1]
            outs[k][:, first : first + columns] = (
                keep_ref[here, :].astype(F32) + got_ref[here, :].astype(F32)
            ).astype(BF16)
            first += columns


def chip_sum_kernel(place_ref, *refs, terms, parts, which, factor):
    ins, outs = refs[:terms], refs[terms:]
    rows = outs[0].shape[0]
    for k in range(parts):
        start = pl.multiple_of((place_ref[0, which] ^ k) * rows, rows) if parts > 1 else 0
        total = None
        for ref in ins:
            term = ref[pl.ds(start, rows), :].astype(F32)
            total = term if total is None else total + term
        outs[k][...] = (total * factor).astype(BF16)


def join_kernel(place_ref, *refs, which):
    ins, out_ref = refs[:-1], refs[-1]
    rows = ins[0].shape[0]
    for k, ref in enumerate(ins):
        out_ref[pl.ds(pl.multiple_of((place_ref[0, which] ^ k) * rows, rows), rows), :] = ref[...]


def final_kernel(place_ref, own_ref, got_ref, mid_ref, in_ref, out_ref, *, factor):
    rows = own_ref.shape[0]
    mids, fields = mid_ref.shape[1], in_ref.shape[1]
    for ref, half in ((own_ref, place_ref[0, 0]), (got_ref, 1 - place_ref[0, 0])):
        start = pl.multiple_of(half * rows, rows)
        mid_ref[pl.ds(start, rows), :] = ref[:, :mids].astype(F32) * factor
        in_ref[pl.ds(start, rows), :] = ref[:, mids : mids + fields].astype(F32) * factor
        out_ref[:, pl.ds(start, rows)] = ref[:, mids + fields :].astype(F32).T * factor


def exchange(arrays, axis, stride):
    count = lax.axis_size(axis)
    return [
        lax.ppermute(array, axis, [(i, i ^ (k * stride)) for i in range(count)])
        for k, array in enumerate(arrays, 1)
    ]


def sum_over_all(place, keeps, sends, factor):
    members = lax.axis_size("ens")
    chips = lax.axis_size("horiz") // 2
    half = keeps[0].shape[0]
    columns = sum(keep.shape[1] for keep in keeps)
    quarter = half // members
    eighth = quarter // chips
    size = quarter * columns
    gots = [exchange([send], "horiz", 1)[0] for send in sends]
    parts = call(
        core_sum_kernel,
        [((quarter, columns), BF16)] * members,
        smem=(0,),
        flops=size * members,
        moved=size * members * 6,
        parts=members,
    )(place, *keeps, *gots)
    terms = [parts[0]] + exchange(parts[1:], "ens", 1)
    if eighth % 16 == 0 and chips <= 8:
        parts = call(
            chip_sum_kernel,
            [((eighth, columns), BF16)] * chips,
            smem=(0,),
            flops=size * members,
            moved=size * members * 2,
            terms=members,
            parts=chips,
            which=2,
            factor=1.0,
        )(place, *terms)
        terms = [parts[0]] + exchange(parts[1:], "horiz", 2)
        (own,) = call(
            chip_sum_kernel,
            [((eighth, columns), BF16)],
            smem=(0,),
            flops=size,
            moved=size * 2,
            terms=chips,
            parts=1,
            which=2,
            factor=factor,
        )(place, *terms)
        (own,) = call(
            join_kernel, [((quarter, columns), BF16)], smem=(0,), moved=size * 4, which=2
        )(place, own, *exchange([own] * (chips - 1), "horiz", 2))
    else:
        (own,) = call(
            chip_sum_kernel,
            [((quarter, columns), BF16)],
            smem=(0,),
            terms=members,
            parts=1,
            which=2,
            factor=1.0,
        )(place, *terms)
        core = place[0, 0]
        both = jnp.stack([jnp.where(core == side, own, 0.0).astype(F32) for side in range(2)])
        own = (lax.psum(both, "horiz")[core] * factor).astype(BF16)
    (own,) = call(
        join_kernel, [((half, columns), BF16)], smem=(0,), moved=size * 16, which=1
    )(place, own, *exchange([own] * (members - 1), "ens", 1))
    return own, exchange([own], "horiz", 1)[0]


def to_neighbours(upward, downward, axis):
    count = lax.axis_size(axis)
    forward = [(i, (i + 1) % count) for i in range(count)]
    backward = [(target, source) for source, target in forward]
    return lax.ppermute(upward, axis, forward), lax.ppermute(downward, axis, backward)


def per_device(
    prognostic, diffusivity, mixing, cotangent, tile_cols, pad_mask, tile_count, w_in, w_mid, w_out
):
    fields, lons, lats = prognostic.shape[1:]
    levels = diffusivity.shape[1]
    units = w_mid.shape[0]
    tiles, width = tile_cols.shape[2:]
    slots = tiles * width
    prog_rows = prognostic.reshape(fields * lons, lats)
    cot_rows = cotangent.reshape(fields * lons, lats)
    diff_rows = diffusivity.reshape(levels * lons, lats)
    mix_rows = mixing.reshape(2 * lons, lats)
    cols, mask = tile_cols[0, 0], pad_mask[0, 0]
    horiz = lax.axis_index("horiz")
    place = jnp.stack([horiz % 2, lax.axis_index("ens"), horiz // 2]).reshape(1, 3)

    packed = ((2 * fields + 8, lats), F32)
    up_pack, down_pack = call(pack_kernel, [packed, packed], lons=lons)(prog_rows, mix_rows)
    low_pack, high_pack = to_neighbours(up_pack, down_pack, "horiz")

    adjoint, coef, ratio, inverse = call(
        adjoint_kernel,
        [((tiles, fields, width), F32)] + [((levels, slots), F32)] * 3,
        scratch=[pltpu.VMEM((tiles, fields, width), F32)],
        smem=(0,),
        flops=10**9,
        moved=10**6,
        lons=lons,
    )(tile_count, diff_rows, cot_rows, cols, mask)

    moved, x_now, act_two, delta_two, keep_mid, send_mid = call(
        forward_kernel,
        [
            ((lons, fields, lats), F32),
            ((fields, slots), BF16),
            ((units, slots), BF16),
            ((units, slots), BF16),
            ((units // 2, units), BF16),
            ((units // 2, units), BF16),
        ],
        scratch=[pltpu.VMEM((units, slots), BF16)],
        flops=2 * 10**9,
        moved=6 * 10**6,
        smem=(9,),
        lons=lons,
    )(prog_rows, low_pack, high_pack, mix_rows, cols, adjoint, w_in, w_mid, w_out, place)

    keep_small, send_small, state_rows, grad_field, up_rows, down_rows = call(
        backward_kernel,
        [
            ((units // 2, 2 * fields), BF16),
            ((units // 2, 2 * fields), BF16),
            ((fields * lons, lats), F32),
            ((lons, fields, lats), F32),
            ((2, fields, lats), F32),
            ((2, fields, lats), F32),
        ],
        scratch=[
            pltpu.VMEM((units, slots), BF16),
            pltpu.VMEM((tiles, fields, width), F32),
            pltpu.VMEM((tiles, fields, width), F32),
        ],
        smem=(0, 15),
        flops=2 * 10**9,
        moved=6 * 10**6,
        lons=lons,
    )(
        tile_count,
        moved,
        cot_rows,
        cols,
        mask,
        x_now,
        act_two,
        delta_two,
        adjoint,
        coef,
        ratio,
        inverse,
        w_in,
        w_mid,
        w_out,
        place,
    )
    low_rows, high_rows = to_neighbours(up_rows, down_rows, "horiz")
    (grad_rows,) = call(last_kernel, [((fields * lons, lats), F32)], lons=lons)(
        grad_field, low_rows, high_rows, low_pack, high_pack, mix_rows
    )

    column_total = lax.axis_size("ens") * lax.axis_size("horiz") * lons * lats
    factor = 1.0 / math.sqrt(column_total)
    own, got = sum_over_all(place, [keep_mid, keep_small], [send_mid, send_small], factor)
    grad_mid, grad_in, grad_out = call(
        final_kernel,
        [((units, units), F32), ((units, fields), F32), ((fields, units), F32)],
        smem=(0,),
        factor=1.0,
    )(place, own, got)
    return (
        state_rows.reshape(prognostic.shape),
        grad_rows.reshape(prognostic.shape),
        grad_in,
        grad_mid,
        grad_out,
    )


def solution(mesh):
    placed = (
        P("ens", None, "horiz", None),
        P("ens", None, "horiz", None),
        P(None, "horiz", None),
        P("ens", None, "horiz", None),
        P("ens", "horiz", None, None),
        P("ens", "horiz", None, None),
        P("ens", "horiz"),
        P(),
        P(),
        P(),
    )
    return jax.shard_map(
        per_device,
        mesh=mesh,
        in_specs=placed,
        out_specs=(P("ens", None, "horiz", None), P("ens", None, "horiz", None), P(), P(), P()),
        check_vma=False,
    )
```

```python
import functools
import math

import jax
import jax.numpy as jnp
from jax import lax
from jax.experimental import pallas as pl
from jax.experimental.pallas import tpu as pltpu
from jax.sharding import PartitionSpec as P

DYN_STEPS = 2
BLOCK = 256
VMEM_LIMIT = 40 * 1024 * 1024
F32 = jnp.float32
BF16 = jnp.bfloat16
CONTRACT_LAST = (((1,), (1,)), ((), ()))
CONTRACT_FIRST = (((0,), (0,)), ((), ()))


def call(kernel, outs, scratch=(), smem=(), flops=0, moved=0, **names):
    def run(*operands):
        specs = [
            pl.BlockSpec(memory_space=pltpu.SMEM if place in smem else pltpu.VMEM)
            for place in range(len(operands))
        ]
        return pl.pallas_call(
            functools.partial(kernel, **names),
            out_shape=[jax.ShapeDtypeStruct(shape, dtype) for shape, dtype in outs],
            in_specs=specs,
            out_specs=[pl.BlockSpec(memory_space=pltpu.VMEM)] * len(outs),
            scratch_shapes=list(scratch),
            compiler_params=pltpu.CompilerParams(vmem_limit_bytes=VMEM_LIMIT),
            cost_estimate=pl.CostEstimate(flops=flops, bytes_accessed=moved, transcendentals=0),
        )(*operands)

    return run


def lat_term(field_now, coef_masked):
    lats = field_now.shape[1]
    north_flux = coef_masked * (pltpu.roll(field_now, lats - 1, 1) - field_now)
    return north_flux - pltpu.roll(north_flux, 1, 1)


def two_steps(rows, lon_coef, lat_coef):
    for repeat in range(DYN_STEPS):
        count = len(rows)
        fluxes = [
            lon_coef[place + repeat] * (rows[place + 1] - rows[place]) for place in range(count - 1)
        ]
        rows = [
            rows[place]
            + fluxes[place]
            - fluxes[place - 1]
            + lat_term(rows[place], lat_coef[place + repeat])
            for place in range(1, count - 1)
        ]
    return rows


def coefficients(mix_ref, low_mix, high_mix, lons):
    lats = mix_ref.shape[1]
    lane = lax.broadcasted_iota(jnp.int32, (1, lats), 1)
    inside = lane < lats - 1
    own_lon = [mix_ref[lon : lon + 1, :] for lon in range(lons)]
    own_lat = [mix_ref[lons + lon : lons + lon + 1, :] for lon in range(lons)]
    lon_coef = [low_mix[0:1, :], low_mix[1:2, :]] + own_lon + [high_mix[0:1, :], high_mix[1:2, :]]
    lat_coef = [low_mix[2:3, :], low_mix[3:4, :]] + own_lat + [high_mix[2:3, :], high_mix[3:4, :]]
    return lon_coef, [jnp.where(inside, coef, 0.0) for coef in lat_coef]


def pack_kernel(prog_ref, mix_ref, up_ref, down_ref, *, lons):
    fields = prog_ref.shape[0] // lons
    for out_ref, first in ((up_ref, lons - 2), (down_ref, 0)):
        for side in range(2):
            out_ref[side * fields : (side + 1) * fields, :] = prog_ref[
                pl.ds(first + side, fields, stride=lons), :
            ]
        out_ref[2 * fields : 2 * fields + 2, :] = mix_ref[first : first + 2, :]
        out_ref[2 * fields + 2 : 2 * fields + 4, :] = mix_ref[lons + first : lons + first + 2, :]
        out_ref[2 * fields + 4 :, :] = jnp.zeros_like(out_ref[2 * fields + 4 :, :])


def one_hot(cols_ref, cells):
    parts = []
    for tile in range(cols_ref.shape[0]):
        place = lax.broadcasted_iota(jnp.int32, (cells, cols_ref.shape[1]), 0)
        parts.append(jnp.where(place == cols_ref[tile : tile + 1, :], 1.0, 0.0))
    return jnp.concatenate(parts, axis=1).astype(BF16)


def live_row(count_ref, mask_ref):
    parts = []
    for tile in range(mask_ref.shape[0]):
        used = jnp.where(tile < count_ref[0, 0], 1, 0)
        parts.append((mask_ref[tile : tile + 1, :] * used).astype(F32))
    return jnp.concatenate(parts, axis=1)


def level_rows(levels, level, variables):
    return pl.ds(level, variables, stride=levels)


def solve(levels, variables, coef_ref, ratio_ref, inverse_ref, right_ref, out_ref):
    tiles, _, width = right_ref.shape
    spans = [slice(tile * width, (tile + 1) * width) for tile in range(tiles)]
    values = []
    for level in range(levels):
        inverse_now = inverse_ref[level : level + 1, :]
        if level > 0:
            carry_now = coef_ref[level - 1 : level, :] * inverse_now
        step = []
        for tile, span in enumerate(spans):
            right_now = right_ref[tile, level_rows(levels, level, variables), :]
            value_now = right_now * inverse_now[:, span]
            if level > 0:
                value_now = value_now + carry_now[:, span] * values[-1][tile]
            step.append(value_now)
        values.append(step)
    results = values[-1]
    for level in range(levels - 1, -1, -1):
        if level < levels - 1:
            ratio_now = ratio_ref[level : level + 1, :]
            results = [
                values[level][tile] - ratio_now[:, span] * results[tile]
                for tile, span in enumerate(spans)
            ]
        for tile in range(tiles):
            out_ref[tile, level_rows(levels, level, variables), :] = results[tile]


def split_tiles(ref, value):
    width = ref.shape[2]
    for tile in range(ref.shape[0]):
        ref[tile] = value[:, tile * width : (tile + 1) * width]


def join_tiles(ref):
    return jnp.concatenate([ref[tile] for tile in range(ref.shape[0])], axis=1)


def factorise(levels, coef_ref, ratio_ref, inverse_ref):
    ratio_prev = None
    for level in range(levels):
        coef_now = coef_ref[level : level + 1, :]
        divisor = 1.0 + coef_now
        if level > 0:
            below_now = coef_ref[level - 1 : level, :]
            divisor = divisor + below_now + below_now * ratio_prev
        inverse_now = 1.0 / divisor
        ratio_prev = -coef_now * inverse_now
        inverse_ref[level : level + 1, :] = inverse_now
        ratio_ref[level : level + 1, :] = ratio_prev


def by_cell(ref, rows, lons):
    return jnp.concatenate(
        [ref[pl.ds(lon, rows, stride=lons), :] for lon in range(lons)], axis=1
    )


def adjoint_kernel(
    count_ref,
    diff_ref,
    cot_ref,
    cols_ref,
    mask_ref,
    adj_ref,
    coef_ref,
    ratio_ref,
    inverse_ref,
    right_ref,
    *,
    lons,
):
    levels = diff_ref.shape[0] // lons
    fields = cot_ref.shape[0] // lons
    cells = lons * cot_ref.shape[1]
    spread = one_hot(cols_ref, cells)
    sources = jnp.concatenate(
        [by_cell(cot_ref, fields, lons), by_cell(diff_ref, levels, lons)], axis=0
    ).astype(BF16)
    picked = jnp.dot(sources, spread, preferred_element_type=F32)
    split_tiles(right_ref, picked[:fields] * live_row(count_ref, mask_ref))
    coef_ref[...] = picked[fields:]
    factorise(levels, coef_ref, ratio_ref, inverse_ref)
    solve(levels, fields // levels, coef_ref, ratio_ref, inverse_ref, right_ref, adj_ref)


def sigmoid(pre_act):
    return 0.5 * jnp.tanh(0.5 * pre_act) + 0.5


def forward_kernel(
    prog_ref,
    low_ref,
    high_ref,
    mix_ref,
    cols_ref,
    adj_ref,
    w_in_ref,
    w_mid_ref,
    w_out_ref,
    place_ref,
    moved_ref,
    x_ref,
    act_two_ref,
    delta_two_ref,
    keep_ref,
    send_ref,
    act_one_ref,
    *,
    lons,
):
    fields = prog_ref.shape[0] // lons
    units = w_mid_ref.shape[0]
    cells = lons * prog_ref.shape[1]
    lon_coef, lat_coef = coefficients(
        mix_ref,
        low_ref[2 * fields : 2 * fields + 4, :],
        high_ref[2 * fields : 2 * fields + 4, :],
        lons,
    )
    rows = [low_ref[side * fields : (side + 1) * fields, :] for side in range(2)]
    rows += [prog_ref[pl.ds(lon, fields, stride=lons), :] for lon in range(lons)]
    rows += [high_ref[side * fields : (side + 1) * fields, :] for side in range(2)]
    rows = two_steps(rows, lon_coef, lat_coef)
    for lon in range(lons):
        moved_ref[lon] = rows[lon]
    spread = one_hot(cols_ref, cells)
    sources = jnp.concatenate(rows, axis=1).astype(BF16)
    x_now = jnp.dot(sources, spread, preferred_element_type=F32).astype(BF16)
    x_ref[...] = x_now
    for start in range(0, units, BLOCK):
        pre_one = jnp.dot(w_in_ref[start : start + BLOCK, :], x_now, preferred_element_type=F32)
        act_one_ref[start : start + BLOCK, :] = (pre_one * sigmoid(pre_one)).astype(BF16)
    adj_half = join_tiles(adj_ref).astype(BF16)
    for start in range(0, units, BLOCK):
        pre_two = jnp.dot(
            w_mid_ref[start : start + BLOCK, :], act_one_ref[...], preferred_element_type=F32
        )
        sigma_val = sigmoid(pre_two)
        act_two_ref[start : start + BLOCK, :] = (pre_two * sigma_val).astype(BF16)
        back_two = lax.dot_general(
            w_out_ref[:, start : start + BLOCK],
            adj_half,
            CONTRACT_FIRST,
            preferred_element_type=F32,
        )
        slope = sigma_val * (1.0 + pre_two * (1.0 - sigma_val))
        delta_two_ref[start : start + BLOCK, :] = (back_two * slope).astype(BF16)
    for out_ref, half in ((send_ref, 1 - place_ref[0, 0]), (keep_ref, place_ref[0, 0])):
        for start in range(0, units // 2, BLOCK):
            out_ref[start : start + BLOCK, :] = lax.dot_general(
                delta_two_ref[pl.ds(half * (units // 2) + start, BLOCK), :],
                act_one_ref[...],
                CONTRACT_LAST,
                preferred_element_type=F32,
            ).astype(BF16)


def backward_kernel(
    count_ref,
    moved_ref,
    cot_ref,
    cols_ref,
    mask_ref,
    x_ref,
    act_two_ref,
    delta_two_ref,
    adj_ref,
    coef_ref,
    ratio_ref,
    inverse_ref,
    w_in_ref,
    w_mid_ref,
    w_out_ref,
    place_ref,
    keep_ref,
    send_ref,
    state_ref,
    field_ref,
    up_ref,
    down_ref,
    delta_one_ref,
    forced_ref,
    solved_ref,
    *,
    lons,
):
    fields = x_ref.shape[0]
    units = w_mid_ref.shape[0]
    levels = coef_ref.shape[0]
    lats = moved_ref.shape[2]
    x_now = x_ref[...]
    adj_now = join_tiles(adj_ref)
    for start in range(0, units, BLOCK):
        back_one = lax.dot_general(
            w_mid_ref[:, start : start + BLOCK],
            delta_two_ref[...],
            CONTRACT_FIRST,
            preferred_element_type=F32,
        )
        pre_one = jnp.dot(w_in_ref[start : start + BLOCK, :], x_now, preferred_element_type=F32)
        sigma_val = sigmoid(pre_one)
        slope = sigma_val * (1.0 + pre_one * (1.0 - sigma_val))
        delta_one_ref[start : start + BLOCK, :] = (back_one * slope).astype(BF16)
    adj_half = adj_now.astype(BF16)
    for out_ref, half in ((send_ref, 1 - place_ref[0, 0]), (keep_ref, place_ref[0, 0])):
        here = pl.ds(half * (units // 2), units // 2)
        out_ref[:, :fields] = lax.dot_general(
            delta_one_ref[here, :], x_now, CONTRACT_LAST, preferred_element_type=F32
        ).astype(BF16)
        out_ref[:, fields:] = lax.dot_general(
            act_two_ref[here, :], adj_half, CONTRACT_LAST, preferred_element_type=F32
        ).astype(BF16)
    grad_x = adj_now + lax.dot_general(
        w_in_ref[...], delta_one_ref[...], CONTRACT_FIRST, preferred_element_type=F32
    )
    tendency = jnp.dot(w_out_ref[...], act_two_ref[...], preferred_element_type=F32)
    split_tiles(forced_ref, x_now.astype(F32) + tendency)
    solve(levels, fields // levels, coef_ref, ratio_ref, inverse_ref, forced_ref, solved_ref)
    live = live_row(count_ref, mask_ref)
    fresh = jnp.concatenate(
        [
            join_tiles(solved_ref) * live,
            grad_x * live,
            jnp.broadcast_to(live, (16, live.shape[1])),
        ],
        axis=0,
    ).astype(BF16)
    spread = one_hot(cols_ref, lons * lats)
    placed = lax.dot_general(fresh, spread, CONTRACT_LAST, preferred_element_type=F32)
    for lon in range(lons):
        here = slice(lon * lats, (lon + 1) * lats)
        taken = placed[2 * fields : 2 * fields + 1, here] > 0.5
        state_ref[pl.ds(lon, fields, stride=lons), :] = jnp.where(
            taken, placed[:fields, here], moved_ref[lon]
        )
        field_now = jnp.where(
            taken, placed[fields : 2 * fields, here], cot_ref[pl.ds(lon, fields, stride=lons), :]
        )
        field_ref[lon] = field_now
        if lon < 2:
            down_ref[lon] = field_now
        if lon >= lons - 2:
            up_ref[lon - (lons - 2)] = field_now


def last_kernel(field_ref, low_ref, high_ref, low_mix_ref, high_mix_ref, mix_ref, out_ref, *, lons):
    fields = field_ref.shape[1]
    lon_coef, lat_coef = coefficients(
        mix_ref,
        low_mix_ref[2 * fields : 2 * fields + 4, :],
        high_mix_ref[2 * fields : 2 * fields + 4, :],
        lons,
    )
    rows = [low_ref[0], low_ref[1]]
    rows += [field_ref[lon] for lon in range(lons)]
    rows += [high_ref[0], high_ref[1]]
    rows = two_steps(rows, lon_coef, lat_coef)
    for lon in range(lons):
        out_ref[pl.ds(lon, fields, stride=lons), :] = rows[lon]


def core_sum_kernel(*refs):
    keeps, gots, out_ref = refs[: len(refs) // 2], refs[len(refs) // 2 : -1], refs[-1]
    first = 0
    for keep_ref, got_ref in zip(keeps, gots):
        columns = keep_ref.shape[1]
        out_ref[:, first : first + columns] = (
            keep_ref[...].astype(F32) + got_ref[...].astype(F32)
        ).astype(BF16)
        first += columns


def sum_kernel(terms_ref, *outs, factor):
    total = terms_ref[0].astype(F32)
    for place in range(1, terms_ref.shape[0]):
        total = total + terms_ref[place].astype(F32)
    for out_ref in outs:
        result = (total * factor).astype(BF16)
        if len(out_ref.shape) == 2:
            out_ref[...] = result
        else:
            for place in range(out_ref.shape[0]):
                out_ref[place] = result


def repeat_kernel(value_ref, out_ref):
    for place in range(out_ref.shape[0]):
        out_ref[place] = value_ref[...]


def final_kernel(place_ref, own_ref, got_ref, mid_ref, in_ref, out_ref, *, factor):
    rows = own_ref.shape[0]
    mids, fields = mid_ref.shape[1], in_ref.shape[1]
    for ref, half in ((own_ref, place_ref[0, 0]), (got_ref, 1 - place_ref[0, 0])):
        start = pl.multiple_of(half * rows, rows)
        mid_ref[pl.ds(start, rows), :] = ref[:, :mids].astype(F32) * factor
        in_ref[pl.ds(start, rows), :] = ref[:, mids : mids + fields].astype(F32) * factor
        out_ref[:, pl.ds(start, rows)] = ref[:, mids + fields :].astype(F32).T * factor


def other_core(array):
    count = lax.axis_size("horiz")
    return lax.ppermute(array, "horiz", [(i, i ^ 1) for i in range(count)])


def over_chips(array):
    count = lax.axis_size("horiz")
    groups = [list(range(core, count, 2)) for core in range(2)]
    return lax.all_to_all(array, "horiz", 0, 0, axis_index_groups=groups)


def over_members(array):
    return lax.all_to_all(array, "ens", 0, 0)


def sum_over_all(core, keeps, sends, factor, beside):
    members = lax.axis_size("ens")
    chips = lax.axis_size("horiz") // 2
    half = keeps[0].shape[0]
    columns = sum(keep.shape[1] for keep in keeps)
    quarter = half // members
    eighth = quarter // chips
    size = half * columns
    gots = [other_core(send) for send in sends]
    (summed,) = call(
        core_sum_kernel, [((half, columns), BF16)], flops=size, moved=size * 6
    )(*keeps, *gots)
    terms = over_members(summed.reshape(members, quarter, columns))
    terms, beside = lax.optimization_barrier((terms, beside))
    if eighth % 16 == 0 and chips <= 8:
        (summed,) = call(
            sum_kernel, [((quarter, columns), BF16)], flops=size, moved=size * 2, factor=1.0
        )(terms)
        terms = over_chips(summed.reshape(chips, eighth, columns))
        (repeated,) = call(
            sum_kernel, [((chips, eighth, columns), BF16)], flops=size, moved=size, factor=factor
        )(terms)
        own = over_chips(repeated).reshape(quarter, columns)
    else:
        (summed,) = call(sum_kernel, [((quarter, columns), BF16)], factor=1.0)(terms)
        both = jnp.stack([jnp.where(core == side, summed, 0.0).astype(F32) for side in range(2)])
        own = (lax.psum(both, "horiz")[core] * factor).astype(BF16)
    (repeated,) = call(
        repeat_kernel, [((members, quarter, columns), BF16)], flops=size, moved=size * 2
    )(own)
    own = over_members(repeated).reshape(half, columns)
    return own, other_core(own), beside


def to_neighbours(upward, downward, axis):
    count = lax.axis_size(axis)
    forward = [(i, (i + 1) % count) for i in range(count)]
    backward = [(target, source) for source, target in forward]
    return lax.ppermute(upward, axis, forward), lax.ppermute(downward, axis, backward)


def per_device(
    prognostic, diffusivity, mixing, cotangent, tile_cols, pad_mask, tile_count, w_in, w_mid, w_out
):
    fields, lons, lats = prognostic.shape[1:]
    levels = diffusivity.shape[1]
    units = w_mid.shape[0]
    tiles, width = tile_cols.shape[2:]
    slots = tiles * width
    prog_rows = prognostic.reshape(fields * lons, lats)
    cot_rows = cotangent.reshape(fields * lons, lats)
    diff_rows = diffusivity.reshape(levels * lons, lats)
    mix_rows = mixing.reshape(2 * lons, lats)
    cols, mask = tile_cols[0, 0], pad_mask[0, 0]
    horiz = lax.axis_index("horiz")
    place = (horiz % 2).reshape(1, 1)

    packed = ((2 * fields + 8, lats), F32)
    up_pack, down_pack = call(pack_kernel, [packed, packed], lons=lons)(prog_rows, mix_rows)
    low_pack, high_pack = to_neighbours(up_pack, down_pack, "horiz")

    adjoint, coef, ratio, inverse = call(
        adjoint_kernel,
        [((tiles, fields, width), F32)] + [((levels, slots), F32)] * 3,
        scratch=[pltpu.VMEM((tiles, fields, width), F32)],
        smem=(0,),
        flops=10**9,
        moved=10**6,
        lons=lons,
    )(tile_count, diff_rows, cot_rows, cols, mask)

    moved, x_now, act_two, delta_two, keep_mid, send_mid = call(
        forward_kernel,
        [
            ((lons, fields, lats), F32),
            ((fields, slots), BF16),
            ((units, slots), BF16),
            ((units, slots), BF16),
            ((units // 2, units), BF16),
            ((units // 2, units), BF16),
        ],
        scratch=[pltpu.VMEM((units, slots), BF16)],
        flops=2 * 10**9,
        moved=6 * 10**6,
        smem=(9,),
        lons=lons,
    )(prog_rows, low_pack, high_pack, mix_rows, cols, adjoint, w_in, w_mid, w_out, place)

    keep_small, send_small, state_rows, grad_field, up_rows, down_rows = call(
        backward_kernel,
        [
            ((units // 2, 2 * fields), BF16),
            ((units // 2, 2 * fields), BF16),
            ((fields * lons, lats), F32),
            ((lons, fields, lats), F32),
            ((2, fields, lats), F32),
            ((2, fields, lats), F32),
        ],
        scratch=[
            pltpu.VMEM((units, slots), BF16),
            pltpu.VMEM((tiles, fields, width), F32),
            pltpu.VMEM((tiles, fields, width), F32),
        ],
        smem=(0, 15),
        flops=2 * 10**9,
        moved=6 * 10**6,
        lons=lons,
    )(
        tile_count,
        moved,
        cot_rows,
        cols,
        mask,
        x_now,
        act_two,
        delta_two,
        adjoint,
        coef,
        ratio,
        inverse,
        w_in,
        w_mid,
        w_out,
        place,
    )
    low_rows, high_rows = to_neighbours(up_rows, down_rows, "horiz")
    (grad_rows,) = call(last_kernel, [((fields * lons, lats), F32)], lons=lons)(
        grad_field, low_rows, high_rows, low_pack, high_pack, mix_rows
    )

    column_total = lax.axis_size("ens") * lax.axis_size("horiz") * lons * lats
    factor = 1.0 / math.sqrt(column_total)
    own, got, grad_rows = sum_over_all(
        place[0, 0], [keep_mid, keep_small], [send_mid, send_small], factor, grad_rows
    )
    grad_mid, grad_in, grad_out = call(
        final_kernel,
        [((units, units), F32), ((units, fields), F32), ((fields, units), F32)],
        smem=(0,),
        factor=1.0,
    )(place, own, got)
    return (
        state_rows.reshape(prognostic.shape),
        grad_rows.reshape(prognostic.shape),
        grad_in,
        grad_mid,
        grad_out,
    )


def solution(mesh):
    placed = (
        P("ens", None, "horiz", None),
        P("ens", None, "horiz", None),
        P(None, "horiz", None),
        P("ens", None, "horiz", None),
        P("ens", "horiz", None, None),
        P("ens", "horiz", None, None),
        P("ens", "horiz"),
        P(),
        P(),
        P(),
    )
    return jax.shard_map(
        per_device,
        mesh=mesh,
        in_specs=placed,
        out_specs=(P("ens", None, "horiz", None), P("ens", None, "horiz", None), P(), P(), P()),
        check_vma=False,
    )
```

```python
import functools
import math

import jax
import jax.numpy as jnp
from jax import lax
from jax.experimental import pallas as pl
from jax.experimental.pallas import tpu as pltpu
from jax.sharding import PartitionSpec as P

DYN_STEPS = 2
BLOCK = 256
PACK_ROWS = 16
VMEM_LIMIT = 32 * 1024 * 1024
F32 = jnp.float32
BF16 = jnp.bfloat16
CONTRACT_LAST = (((1,), (1,)), ((), ()))
CONTRACT_FIRST = (((0,), (0,)), ((), ()))


def call(kernel, outs, scratch=(), smem=(), flops=0, moved=0, **names):
    def run(*operands):
        specs = [
            pl.BlockSpec(memory_space=pltpu.SMEM if place in smem else pltpu.VMEM)
            for place in range(len(operands))
        ]
        return pl.pallas_call(
            functools.partial(kernel, **names),
            out_shape=[jax.ShapeDtypeStruct(shape, dtype) for shape, dtype in outs],
            in_specs=specs,
            out_specs=[pl.BlockSpec(memory_space=pltpu.VMEM)] * len(outs),
            scratch_shapes=list(scratch),
            compiler_params=pltpu.CompilerParams(vmem_limit_bytes=VMEM_LIMIT),
            cost_estimate=pl.CostEstimate(flops=flops, bytes_accessed=moved, transcendentals=0),
        )(*operands)

    return run


def lat_term(field_now, coef_masked):
    lats = field_now.shape[1]
    north_flux = coef_masked * (pltpu.roll(field_now, lats - 1, 1) - field_now)
    return north_flux - pltpu.roll(north_flux, 1, 1)


def two_steps(rows, lon_coef, lat_coef):
    for repeat in range(DYN_STEPS):
        count = len(rows)
        fluxes = [
            lon_coef[place + repeat] * (rows[place + 1] - rows[place]) for place in range(count - 1)
        ]
        rows = [
            rows[place]
            + fluxes[place]
            - fluxes[place - 1]
            + lat_term(rows[place], lat_coef[place + repeat])
            for place in range(1, count - 1)
        ]
    return rows


def coefficients(mix_ref, low_mix, high_mix, lons):
    lats = mix_ref.shape[1]
    lane = lax.broadcasted_iota(jnp.int32, (1, lats), 1)
    inside = lane < lats - 1
    own_lon = [mix_ref[lon : lon + 1, :] for lon in range(lons)]
    own_lat = [mix_ref[lons + lon : lons + lon + 1, :] for lon in range(lons)]
    lon_coef = [low_mix[0:1, :], low_mix[1:2, :]] + own_lon + [high_mix[0:1, :], high_mix[1:2, :]]
    lat_coef = [low_mix[2:3, :], low_mix[3:4, :]] + own_lat + [high_mix[2:3, :], high_mix[3:4, :]]
    return lon_coef, [jnp.where(inside, coef, 0.0) for coef in lat_coef]


def pack_kernel(prog_ref, mix_ref, up_ref, down_ref, *, lons):
    fields = prog_ref.shape[0] // lons
    for out_ref, first in ((up_ref, lons - 2), (down_ref, 0)):
        for side in range(2):
            out_ref[side * fields : (side + 1) * fields, :] = prog_ref[
                pl.ds(first + side, fields, stride=lons), :
            ].astype(BF16)
        mix_rows = [mix_ref[first : first + 2, :], mix_ref[lons + first : lons + first + 2, :]]
        mix_rows.append(jnp.zeros((PACK_ROWS - 4, mix_ref.shape[1]), F32))
        out_ref[2 * fields :, :] = jnp.concatenate(mix_rows, axis=0).astype(BF16)


def halo_rows(pack_ref, fields):
    return [pack_ref[side * fields : (side + 1) * fields, :].astype(F32) for side in range(2)]


def halo_mixing(pack_ref, fields):
    return pack_ref[2 * fields :, :].astype(F32)


def one_hot(cols_ref, cells):
    parts = []
    for tile in range(cols_ref.shape[0]):
        place = lax.broadcasted_iota(jnp.int32, (cells, cols_ref.shape[1]), 0)
        parts.append(jnp.where(place == cols_ref[tile : tile + 1, :], 1.0, 0.0))
    return jnp.concatenate(parts, axis=1).astype(BF16)


def live_row(count_ref, mask_ref):
    parts = []
    for tile in range(mask_ref.shape[0]):
        used = jnp.where(tile < count_ref[0, 0], 1, 0)
        parts.append((mask_ref[tile : tile + 1, :] * used).astype(F32))
    return jnp.concatenate(parts, axis=1)


def level_rows(levels, level, variables):
    return pl.ds(level, variables, stride=levels)


def solve(levels, variables, coef_ref, ratio_ref, inverse_ref, right_ref, out_ref):
    tiles, _, width = right_ref.shape
    spans = [slice(tile * width, (tile + 1) * width) for tile in range(tiles)]
    values = []
    for level in range(levels):
        inverse_now = inverse_ref[level : level + 1, :]
        if level > 0:
            carry_now = coef_ref[level - 1 : level, :] * inverse_now
        step = []
        for tile, span in enumerate(spans):
            right_now = right_ref[tile, level_rows(levels, level, variables), :]
            value_now = right_now * inverse_now[:, span]
            if level > 0:
                value_now = value_now + carry_now[:, span] * values[-1][tile]
            step.append(value_now)
        values.append(step)
    results = values[-1]
    for level in range(levels - 1, -1, -1):
        if level < levels - 1:
            ratio_now = ratio_ref[level : level + 1, :]
            results = [
                values[level][tile] - ratio_now[:, span] * results[tile]
                for tile, span in enumerate(spans)
            ]
        for tile in range(tiles):
            out_ref[tile, level_rows(levels, level, variables), :] = results[tile]


def split_tiles(ref, value):
    width = ref.shape[2]
    for tile in range(ref.shape[0]):
        ref[tile] = value[:, tile * width : (tile + 1) * width]


def join_tiles(ref):
    return jnp.concatenate([ref[tile] for tile in range(ref.shape[0])], axis=1)


def factorise(levels, coef_ref, ratio_ref, inverse_ref):
    ratio_prev = None
    for level in range(levels):
        coef_now = coef_ref[level : level + 1, :]
        divisor = 1.0 + coef_now
        if level > 0:
            below_now = coef_ref[level - 1 : level, :]
            divisor = divisor + below_now + below_now * ratio_prev
        inverse_now = 1.0 / divisor
        ratio_prev = -coef_now * inverse_now
        inverse_ref[level : level + 1, :] = inverse_now
        ratio_ref[level : level + 1, :] = ratio_prev


def by_cell(ref, rows, lons):
    return jnp.concatenate(
        [ref[pl.ds(lon, rows, stride=lons), :] for lon in range(lons)], axis=1
    )


def adjoint_kernel(
    count_ref,
    diff_ref,
    cot_ref,
    cols_ref,
    mask_ref,
    adj_ref,
    coef_ref,
    ratio_ref,
    inverse_ref,
    right_ref,
    *,
    lons,
):
    levels = diff_ref.shape[0] // lons
    fields = cot_ref.shape[0] // lons
    cells = lons * cot_ref.shape[1]
    spread = one_hot(cols_ref, cells)
    sources = jnp.concatenate(
        [by_cell(cot_ref, fields, lons), by_cell(diff_ref, levels, lons)], axis=0
    ).astype(BF16)
    picked = jnp.dot(sources, spread, preferred_element_type=F32)
    split_tiles(right_ref, picked[:fields] * live_row(count_ref, mask_ref))
    coef_ref[...] = picked[fields:]
    factorise(levels, coef_ref, ratio_ref, inverse_ref)
    solve(levels, fields // levels, coef_ref, ratio_ref, inverse_ref, right_ref, adj_ref)


def sigmoid(pre_act):
    return 0.5 * jnp.tanh(0.5 * pre_act) + 0.5


def weight_product(left_ref, right, place_ref, keep_ref, send_ref, first, transposed=CONTRACT_LAST):
    half = left_ref.shape[0] // 2
    block = min(BLOCK, half)
    for out_ref, side in ((send_ref, 1 - place_ref[0, 0]), (keep_ref, place_ref[0, 0])):
        for start in range(0, half, block):
            out_ref[start : start + block, first : first + right.shape[0]] = lax.dot_general(
                left_ref[pl.ds(pl.multiple_of(side * half + start, block), block), :],
                right,
                transposed,
                preferred_element_type=F32,
            ).astype(BF16)


def forward_kernel(
    place_ref,
    prog_ref,
    low_ref,
    high_ref,
    mix_ref,
    cols_ref,
    adj_ref,
    w_in_ref,
    w_mid_ref,
    w_out_ref,
    moved_ref,
    x_ref,
    act_one_ref,
    act_two_ref,
    delta_two_ref,
    keep_ref,
    send_ref,
    *,
    lons,
):
    fields = prog_ref.shape[0] // lons
    units = w_mid_ref.shape[0]
    cells = lons * prog_ref.shape[1]
    low_rows, high_rows = halo_rows(low_ref, fields), halo_rows(high_ref, fields)
    lon_coef, lat_coef = coefficients(
        mix_ref, halo_mixing(low_ref, fields), halo_mixing(high_ref, fields), lons
    )
    rows = [prog_ref[pl.ds(lon, fields, stride=lons), :] for lon in range(lons)]
    rows = two_steps(low_rows + rows + high_rows, lon_coef, lat_coef)
    for lon in range(lons):
        moved_ref[lon] = rows[lon]
    spread = one_hot(cols_ref, cells)
    sources = jnp.concatenate(rows, axis=1).astype(BF16)
    x_now = jnp.dot(sources, spread, preferred_element_type=F32).astype(BF16)
    x_ref[...] = x_now
    for start in range(0, units, BLOCK):
        pre_one = jnp.dot(w_in_ref[start : start + BLOCK, :], x_now, preferred_element_type=F32)
        act_one_ref[start : start + BLOCK, :] = (pre_one * sigmoid(pre_one)).astype(BF16)
    adj_half = join_tiles(adj_ref).astype(BF16)
    for start in range(0, units, BLOCK):
        pre_two = jnp.dot(
            w_mid_ref[start : start + BLOCK, :], act_one_ref[...], preferred_element_type=F32
        )
        sigma_val = sigmoid(pre_two)
        act_two_ref[start : start + BLOCK, :] = (pre_two * sigma_val).astype(BF16)
        back_two = lax.dot_general(
            w_out_ref[:, start : start + BLOCK],
            adj_half,
            CONTRACT_FIRST,
            preferred_element_type=F32,
        )
        slope = sigma_val * (1.0 + pre_two * (1.0 - sigma_val))
        delta_two_ref[start : start + BLOCK, :] = (back_two * slope).astype(BF16)
    weight_product(
        delta_two_ref, act_one_ref[: keep_ref.shape[1], :], place_ref, keep_ref, send_ref, 0
    )


def backward_kernel(
    place_ref,
    x_ref,
    act_one_ref,
    act_two_ref,
    delta_two_ref,
    adj_ref,
    w_in_ref,
    w_mid_ref,
    delta_one_ref,
    keep_ref,
    send_ref,
):
    fields = x_ref.shape[0]
    units = w_mid_ref.shape[0]
    done = units + 2 * fields - keep_ref.shape[1]
    x_now = x_ref[...]
    for start in range(0, units, BLOCK):
        back_one = lax.dot_general(
            w_mid_ref[:, start : start + BLOCK],
            delta_two_ref[...],
            CONTRACT_FIRST,
            preferred_element_type=F32,
        )
        pre_one = jnp.dot(w_in_ref[start : start + BLOCK, :], x_now, preferred_element_type=F32)
        sigma_val = sigmoid(pre_one)
        slope = sigma_val * (1.0 + pre_one * (1.0 - sigma_val))
        delta_one_ref[start : start + BLOCK, :] = (back_one * slope).astype(BF16)
    weight_product(delta_two_ref, act_one_ref[done:, :], place_ref, keep_ref, send_ref, 0)
    weight_product(delta_one_ref, x_now, place_ref, keep_ref, send_ref, units - done)
    adj_half = join_tiles(adj_ref).astype(BF16)
    weight_product(act_two_ref, adj_half, place_ref, keep_ref, send_ref, units - done + fields)


def place_kernel(
    count_ref,
    moved_ref,
    cot_ref,
    cols_ref,
    mask_ref,
    x_ref,
    act_two_ref,
    delta_one_ref,
    adj_ref,
    coef_ref,
    ratio_ref,
    inverse_ref,
    w_in_ref,
    w_out_ref,
    state_ref,
    field_ref,
    up_ref,
    down_ref,
    forced_ref,
    solved_ref,
    *,
    lons,
):
    fields = x_ref.shape[0]
    levels = coef_ref.shape[0]
    lats = moved_ref.shape[2]
    tendency = jnp.dot(w_out_ref[...], act_two_ref[...], preferred_element_type=F32)
    split_tiles(forced_ref, x_ref[...].astype(F32) + tendency)
    solve(levels, fields // levels, coef_ref, ratio_ref, inverse_ref, forced_ref, solved_ref)
    grad_x = join_tiles(adj_ref) + lax.dot_general(
        w_in_ref[...], delta_one_ref[...], CONTRACT_FIRST, preferred_element_type=F32
    )
    live = live_row(count_ref, mask_ref)
    fresh = jnp.concatenate(
        [
            join_tiles(solved_ref) * live,
            grad_x * live,
            jnp.broadcast_to(live, (16, live.shape[1])),
        ],
        axis=0,
    ).astype(BF16)
    spread = one_hot(cols_ref, lons * lats)
    placed = lax.dot_general(fresh, spread, CONTRACT_LAST, preferred_element_type=F32)
    for lon in range(lons):
        here = slice(lon * lats, (lon + 1) * lats)
        taken = placed[2 * fields : 2 * fields + 1, here] > 0.5
        state_ref[pl.ds(lon, fields, stride=lons), :] = jnp.where(
            taken, placed[:fields, here], moved_ref[lon]
        )
        field_now = jnp.where(
            taken, placed[fields : 2 * fields, here], cot_ref[pl.ds(lon, fields, stride=lons), :]
        )
        field_ref[lon] = field_now
        if lon < 2:
            down_ref[lon * fields : (lon + 1) * fields, :] = field_now.astype(BF16)
        if lon >= lons - 2:
            side = lon - (lons - 2)
            up_ref[side * fields : (side + 1) * fields, :] = field_now.astype(BF16)


def last_kernel(field_ref, low_ref, high_ref, low_mix_ref, high_mix_ref, mix_ref, out_ref, *, lons):
    fields = field_ref.shape[1]
    low_rows, high_rows = halo_rows(low_ref, fields), halo_rows(high_ref, fields)
    lon_coef, lat_coef = coefficients(
        mix_ref, halo_mixing(low_mix_ref, fields), halo_mixing(high_mix_ref, fields), lons
    )
    rows = [field_ref[lon] for lon in range(lons)]
    rows = two_steps(low_rows + rows + high_rows, lon_coef, lat_coef)
    for lon in range(lons):
        out_ref[pl.ds(lon, fields, stride=lons), :] = rows[lon]


def core_sum_kernel(place_ref, keep_ref, got_ref, *outs):
    rows = outs[0].shape[0]
    for k, out_ref in enumerate(outs):
        here = pl.ds(pl.multiple_of((place_ref[0, 1] ^ k) * rows, rows), rows)
        out_ref[...] = (keep_ref[here, :].astype(F32) + got_ref[here, :].astype(F32)).astype(BF16)


def sum_kernel(place_ref, *refs, terms, which, factor):
    ins, outs = refs[:terms], refs[terms:]
    rows = outs[0].shape[0]
    for k, out_ref in enumerate(outs):
        start = pl.multiple_of((place_ref[0, which] ^ k) * rows, rows) if len(outs) > 1 else 0
        total = ins[0][pl.ds(start, rows), :].astype(F32)
        for ref in ins[1:]:
            total = total + ref[pl.ds(start, rows), :].astype(F32)
        out_ref[...] = (total * factor).astype(BF16)


def join_kernel(place_ref, *refs, which):
    ins, out_ref = refs[:-1], refs[-1]
    rows = ins[0].shape[0]
    for k, ref in enumerate(ins):
        out_ref[pl.ds(pl.multiple_of((place_ref[0, which] ^ k) * rows, rows), rows), :] = ref[...]


def final_kernel(place_ref, own_one, got_one, own_two, got_two, mid_ref, in_ref, out_ref):
    rows, first = own_one.shape
    fields = in_ref.shape[1]
    rest = mid_ref.shape[1] - first
    for one_ref, two_ref, half in (
        (own_one, own_two, place_ref[0, 0]),
        (got_one, got_two, 1 - place_ref[0, 0]),
    ):
        here = pl.ds(pl.multiple_of(half * rows, rows), rows)
        mid_ref[here, :first] = one_ref[...].astype(F32)
        mid_ref[here, first:] = two_ref[:, :rest].astype(F32)
        in_ref[here, :] = two_ref[:, rest : rest + fields].astype(F32)
        out_ref[:, here] = two_ref[:, rest + fields :].astype(F32).T


def exchange(arrays, axis, stride):
    count = lax.axis_size(axis)
    return [
        lax.ppermute(array, axis, [(i, i ^ (k * stride)) for i in range(count)])
        for k, array in enumerate(arrays, 1)
    ]


def sum_over_all(place, keep, send, factor, beside=None):
    members = lax.axis_size("ens")
    chips = lax.axis_size("horiz") // 2
    half, columns = keep.shape
    quarter = half // members
    eighth = quarter // chips
    size = half * columns
    (got,) = exchange([send], "horiz", 1)
    parts = call(
        core_sum_kernel,
        [((quarter, columns), BF16)] * members,
        smem=(0,),
        flops=size,
        moved=size * 6,
    )(place, keep, got)
    terms = [parts[0]] + exchange(parts[1:], "ens", 1)
    if beside is not None:
        terms, beside = lax.optimization_barrier((terms, beside))
    if eighth % 16 == 0 and chips <= 8:
        parts = call(
            sum_kernel,
            [((eighth, columns), BF16)] * chips,
            smem=(0,),
            flops=size,
            moved=size * 2,
            terms=members,
            which=2,
            factor=1.0,
        )(place, *terms)
        terms = [parts[0]] + exchange(parts[1:], "horiz", 2)
        (own,) = call(
            sum_kernel,
            [((eighth, columns), BF16)],
            smem=(0,),
            flops=size,
            moved=size,
            terms=chips,
            which=2,
            factor=factor,
        )(place, *terms)
        (own,) = call(
            join_kernel, [((quarter, columns), BF16)], smem=(0,), moved=size, which=2
        )(place, own, *exchange([own] * (chips - 1), "horiz", 2))
    else:
        (own,) = call(
            sum_kernel,
            [((quarter, columns), BF16)],
            smem=(0,),
            terms=members,
            which=2,
            factor=1.0,
        )(place, *terms)
        core = place[0, 0]
        both = jnp.stack([jnp.where(core == side, own, 0.0).astype(F32) for side in range(2)])
        own = (lax.psum(both, "horiz")[core] * factor).astype(BF16)
    (own,) = call(
        join_kernel, [((half, columns), BF16)], smem=(0,), moved=size * 4, which=1
    )(place, own, *exchange([own] * (members - 1), "ens", 1))
    return own, exchange([own], "horiz", 1)[0], beside


def to_neighbours(upward, downward, axis):
    count = lax.axis_size(axis)
    forward = [(i, (i + 1) % count) for i in range(count)]
    backward = [(target, source) for source, target in forward]
    return lax.ppermute(upward, axis, forward), lax.ppermute(downward, axis, backward)


def per_device(
    prognostic, diffusivity, mixing, cotangent, tile_cols, pad_mask, tile_count, w_in, w_mid, w_out
):
    fields, lons, lats = prognostic.shape[1:]
    levels = diffusivity.shape[1]
    units = w_mid.shape[0]
    tiles, width = tile_cols.shape[2:]
    slots = tiles * width
    prog_rows = prognostic.reshape(fields * lons, lats)
    cot_rows = cotangent.reshape(fields * lons, lats)
    diff_rows = diffusivity.reshape(levels * lons, lats)
    mix_rows = mixing.reshape(2 * lons, lats)
    cols, mask = tile_cols[0, 0], pad_mask[0, 0]
    horiz = lax.axis_index("horiz")
    place = jnp.stack([horiz % 2, lax.axis_index("ens"), horiz // 2]).reshape(1, 3)

    packed = ((2 * fields + PACK_ROWS, lats), BF16)
    up_pack, down_pack = call(pack_kernel, [packed, packed], lons=lons)(prog_rows, mix_rows)
    low_pack, high_pack = to_neighbours(up_pack, down_pack, "horiz")

    adjoint, coef, ratio, inverse = call(
        adjoint_kernel,
        [((tiles, fields, width), F32)] + [((levels, slots), F32)] * 3,
        scratch=[pltpu.VMEM((tiles, fields, width), F32)],
        smem=(0,),
        flops=10**9,
        moved=10**6,
        lons=lons,
    )(tile_count, diff_rows, cot_rows, cols, mask)

    hidden = ((units, slots), BF16)
    first = (units + 2 * fields) // 2
    chunk = ((units // 2, first), BF16)
    moved, x_now, act_one, act_two, delta_two, keep, send = call(
        forward_kernel,
        [((lons, fields, lats), F32), ((fields, slots), BF16), hidden, hidden, hidden, chunk, chunk],
        smem=(0,),
        flops=2 * 10**9,
        moved=6 * 10**6,
        lons=lons,
    )(place, prog_rows, low_pack, high_pack, mix_rows, cols, adjoint, w_in, w_mid, w_out)
    column_total = lax.axis_size("ens") * lax.axis_size("horiz") * lons * lats
    factor = 1.0 / math.sqrt(column_total)
    chunk_one = (keep, send)

    chunk = ((units // 2, units + 2 * fields - first), BF16)
    delta_one, keep, send = call(
        backward_kernel,
        [hidden, chunk, chunk],
        smem=(0,),
        flops=2 * 10**9,
        moved=6 * 10**6,
    )(place, x_now, act_one, act_two, delta_two, adjoint, w_in, w_mid)
    chunk_two = (keep, send)

    state_rows, grad_field, up_rows, down_rows = call(
        place_kernel,
        [
            ((fields * lons, lats), F32),
            ((lons, fields, lats), F32),
            ((2 * fields, lats), BF16),
            ((2 * fields, lats), BF16),
        ],
        scratch=[pltpu.VMEM((tiles, fields, width), F32)] * 2,
        smem=(0,),
        flops=10**9,
        moved=3 * 10**6,
        lons=lons,
    )(
        tile_count,
        moved,
        cot_rows,
        cols,
        mask,
        x_now,
        act_two,
        delta_one,
        adjoint,
        coef,
        ratio,
        inverse,
        w_in,
        w_out,
    )
    low_rows, high_rows = to_neighbours(up_rows, down_rows, "horiz")
    (grad_rows,) = call(
        last_kernel, [((fields * lons, lats), F32)], flops=10**6, moved=10**6, lons=lons
    )(grad_field, low_rows, high_rows, low_pack, high_pack, mix_rows)

    own_one, got_one, grad_rows = sum_over_all(place, *chunk_one, factor, grad_rows)
    own_two, got_two, _ = sum_over_all(place, *chunk_two, factor)
    grad_mid, grad_in, grad_out = call(
        final_kernel,
        [((units, units), F32), ((units, fields), F32), ((fields, units), F32)],
        smem=(0,),
        moved=8 * 10**6,
    )(place, own_one, got_one, own_two, got_two)
    return (
        state_rows.reshape(prognostic.shape),
        grad_rows.reshape(prognostic.shape),
        grad_in,
        grad_mid,
        grad_out,
    )


def solution(mesh):
    placed = (
        P("ens", None, "horiz", None),
        P("ens", None, "horiz", None),
        P(None, "horiz", None),
        P("ens", None, "horiz", None),
        P("ens", "horiz", None, None),
        P("ens", "horiz", None, None),
        P("ens", "horiz"),
        P(),
        P(),
        P(),
    )
    return jax.shard_map(
        per_device,
        mesh=mesh,
        in_specs=placed,
        out_specs=(P("ens", None, "horiz", None), P("ens", None, "horiz", None), P(), P(), P()),
        check_vma=False,
    )
```

```python
import functools
import math

import jax
import jax.numpy as jnp
from jax import lax
from jax.experimental import pallas as pl
from jax.experimental.pallas import tpu as pltpu
from jax.sharding import PartitionSpec as P

DYN_STEPS = 2
BLOCK = 256
PACK_ROWS = 16
VMEM_LIMIT = 32 * 1024 * 1024
F32 = jnp.float32
BF16 = jnp.bfloat16
CONTRACT_LAST = (((1,), (1,)), ((), ()))
CONTRACT_FIRST = (((0,), (0,)), ((), ()))


def call(kernel, outs, scratch=(), smem=(), flops=0, moved=0, **names):
    def run(*operands):
        specs = [
            pl.BlockSpec(memory_space=pltpu.SMEM if place in smem else pltpu.VMEM)
            for place in range(len(operands))
        ]
        return pl.pallas_call(
            functools.partial(kernel, **names),
            out_shape=[jax.ShapeDtypeStruct(shape, dtype) for shape, dtype in outs],
            in_specs=specs,
            out_specs=[pl.BlockSpec(memory_space=pltpu.VMEM)] * len(outs),
            scratch_shapes=list(scratch),
            compiler_params=pltpu.CompilerParams(vmem_limit_bytes=VMEM_LIMIT),
            cost_estimate=pl.CostEstimate(flops=flops, bytes_accessed=moved, transcendentals=0),
        )(*operands)

    return run


def lat_term(field_now, coef_masked):
    lats = field_now.shape[1]
    north_flux = coef_masked * (pltpu.roll(field_now, lats - 1, 1) - field_now)
    return north_flux - pltpu.roll(north_flux, 1, 1)


def two_steps(rows, lon_coef, lat_coef):
    for repeat in range(DYN_STEPS):
        count = len(rows)
        fluxes = [
            lon_coef[place + repeat] * (rows[place + 1] - rows[place]) for place in range(count - 1)
        ]
        rows = [
            rows[place]
            + fluxes[place]
            - fluxes[place - 1]
            + lat_term(rows[place], lat_coef[place + repeat])
            for place in range(1, count - 1)
        ]
    return rows


def coefficients(mix_ref, low_mix, high_mix, lons):
    lats = mix_ref.shape[1]
    lane = lax.broadcasted_iota(jnp.int32, (1, lats), 1)
    inside = lane < lats - 1
    own_lon = [mix_ref[lon : lon + 1, :] for lon in range(lons)]
    own_lat = [mix_ref[lons + lon : lons + lon + 1, :] for lon in range(lons)]
    lon_coef = [low_mix[0:1, :], low_mix[1:2, :]] + own_lon + [high_mix[0:1, :], high_mix[1:2, :]]
    lat_coef = [low_mix[2:3, :], low_mix[3:4, :]] + own_lat + [high_mix[2:3, :], high_mix[3:4, :]]
    return lon_coef, [jnp.where(inside, coef, 0.0) for coef in lat_coef]


def pack_kernel(prog_ref, mix_ref, up_ref, down_ref, prog_out, mix_out, *, lons):
    fields = prog_ref.shape[0] // lons
    for out_ref, first in ((up_ref, lons - 2), (down_ref, 0)):
        for side in range(2):
            out_ref[side * fields : (side + 1) * fields, :] = prog_ref[
                pl.ds(first + side, fields, stride=lons), :
            ].astype(BF16)
        mix_rows = [mix_ref[first : first + 2, :], mix_ref[lons + first : lons + first + 2, :]]
        mix_rows.append(jnp.zeros((PACK_ROWS - 4, mix_ref.shape[1]), F32))
        out_ref[2 * fields :, :] = jnp.concatenate(mix_rows, axis=0).astype(BF16)
    prog_out[...] = prog_ref[...]
    mix_out[...] = mix_ref[...]


def halo_rows(pack_ref, fields):
    return [pack_ref[side * fields : (side + 1) * fields, :].astype(F32) for side in range(2)]


def halo_mixing(pack_ref, fields):
    return pack_ref[2 * fields :, :].astype(F32)


def one_hot(cols_ref, cells):
    parts = []
    for tile in range(cols_ref.shape[0]):
        place = lax.broadcasted_iota(jnp.int32, (cells, cols_ref.shape[1]), 0)
        parts.append(jnp.where(place == cols_ref[tile : tile + 1, :], 1.0, 0.0))
    return jnp.concatenate(parts, axis=1).astype(BF16)


def live_row(count_ref, mask_ref):
    parts = []
    for tile in range(mask_ref.shape[0]):
        used = jnp.where(tile < count_ref[0, 0], 1, 0)
        parts.append((mask_ref[tile : tile + 1, :] * used).astype(F32))
    return jnp.concatenate(parts, axis=1)


def level_rows(levels, level, variables):
    return pl.ds(level, variables, stride=levels)


def solve(levels, variables, coef_ref, ratio_ref, inverse_ref, right_ref, out_ref):
    tiles, _, width = right_ref.shape
    spans = [slice(tile * width, (tile + 1) * width) for tile in range(tiles)]
    values = []
    for level in range(levels):
        inverse_now = inverse_ref[level : level + 1, :]
        if level > 0:
            carry_now = coef_ref[level - 1 : level, :] * inverse_now
        step = []
        for tile, span in enumerate(spans):
            right_now = right_ref[tile, level_rows(levels, level, variables), :]
            value_now = right_now * inverse_now[:, span]
            if level > 0:
                value_now = value_now + carry_now[:, span] * values[-1][tile]
            step.append(value_now)
        values.append(step)
    results = values[-1]
    for level in range(levels - 1, -1, -1):
        if level < levels - 1:
            ratio_now = ratio_ref[level : level + 1, :]
            results = [
                values[level][tile] - ratio_now[:, span] * results[tile]
                for tile, span in enumerate(spans)
            ]
        for tile in range(tiles):
            out_ref[tile, level_rows(levels, level, variables), :] = results[tile]


def split_tiles(ref, value):
    width = ref.shape[2]
    for tile in range(ref.shape[0]):
        ref[tile] = value[:, tile * width : (tile + 1) * width]


def join_tiles(ref):
    return jnp.concatenate([ref[tile] for tile in range(ref.shape[0])], axis=1)


def factorise(levels, coef_ref, ratio_ref, inverse_ref):
    ratio_prev = None
    for level in range(levels):
        coef_now = coef_ref[level : level + 1, :]
        divisor = 1.0 + coef_now
        if level > 0:
            below_now = coef_ref[level - 1 : level, :]
            divisor = divisor + below_now + below_now * ratio_prev
        inverse_now = 1.0 / divisor
        ratio_prev = -coef_now * inverse_now
        inverse_ref[level : level + 1, :] = inverse_now
        ratio_ref[level : level + 1, :] = ratio_prev


def by_cell(ref, rows, lons):
    return jnp.concatenate(
        [ref[pl.ds(lon, rows, stride=lons), :] for lon in range(lons)], axis=1
    )


def adjoint_kernel(
    count_ref,
    diff_ref,
    cot_ref,
    cols_ref,
    mask_ref,
    w_in_ref,
    w_mid_ref,
    w_out_ref,
    adj_ref,
    coef_ref,
    ratio_ref,
    inverse_ref,
    w_in_out,
    w_mid_out,
    w_out_out,
    right_ref,
    *,
    lons,
):
    w_in_out[...] = w_in_ref[...]
    w_mid_out[...] = w_mid_ref[...]
    w_out_out[...] = w_out_ref[...]
    levels = diff_ref.shape[0] // lons
    fields = cot_ref.shape[0] // lons
    cells = lons * cot_ref.shape[1]
    spread = one_hot(cols_ref, cells)
    sources = jnp.concatenate(
        [by_cell(cot_ref, fields, lons), by_cell(diff_ref, levels, lons)], axis=0
    ).astype(BF16)
    picked = jnp.dot(sources, spread, preferred_element_type=F32)
    split_tiles(right_ref, picked[:fields] * live_row(count_ref, mask_ref))
    coef_ref[...] = picked[fields:]
    factorise(levels, coef_ref, ratio_ref, inverse_ref)
    solve(levels, fields // levels, coef_ref, ratio_ref, inverse_ref, right_ref, adj_ref)


def sigmoid(pre_act):
    return 0.5 * jnp.tanh(0.5 * pre_act) + 0.5


def weight_product(left_ref, right, keep_ref, send_ref, first):
    half = left_ref.shape[0] // 2
    block = min(BLOCK, half)
    core = lax.axis_index("horiz") % 2
    for out_ref, side in ((send_ref, 1 - core), (keep_ref, core)):
        for start in range(0, half, block):
            out_ref[start : start + block, first : first + right.shape[0]] = lax.dot_general(
                left_ref[pl.ds(pl.multiple_of(side * half + start, block), block), :],
                right,
                CONTRACT_LAST,
                preferred_element_type=F32,
            ).astype(BF16)


def forward_kernel(
    prog_ref,
    low_ref,
    high_ref,
    mix_ref,
    cols_ref,
    adj_ref,
    w_in_ref,
    w_mid_ref,
    w_out_ref,
    moved_ref,
    x_ref,
    act_one_ref,
    act_two_ref,
    delta_two_ref,
    keep_ref,
    send_ref,
    *,
    lons,
):
    fields = prog_ref.shape[0] // lons
    units = w_mid_ref.shape[0]
    cells = lons * prog_ref.shape[1]
    low_rows, high_rows = halo_rows(low_ref, fields), halo_rows(high_ref, fields)
    lon_coef, lat_coef = coefficients(
        mix_ref, halo_mixing(low_ref, fields), halo_mixing(high_ref, fields), lons
    )
    rows = [prog_ref[pl.ds(lon, fields, stride=lons), :] for lon in range(lons)]
    rows = two_steps(low_rows + rows + high_rows, lon_coef, lat_coef)
    for lon in range(lons):
        moved_ref[lon] = rows[lon]
    spread = one_hot(cols_ref, cells)
    sources = jnp.concatenate(rows, axis=1).astype(BF16)
    x_now = jnp.dot(sources, spread, preferred_element_type=F32).astype(BF16)
    x_ref[...] = x_now
    for start in range(0, units, BLOCK):
        pre_one = jnp.dot(w_in_ref[start : start + BLOCK, :], x_now, preferred_element_type=F32)
        act_one_ref[start : start + BLOCK, :] = (pre_one * sigmoid(pre_one)).astype(BF16)
    adj_half = join_tiles(adj_ref).astype(BF16)
    for start in range(0, units, BLOCK):
        pre_two = jnp.dot(
            w_mid_ref[start : start + BLOCK, :], act_one_ref[...], preferred_element_type=F32
        )
        sigma_val = sigmoid(pre_two)
        act_two_ref[start : start + BLOCK, :] = (pre_two * sigma_val).astype(BF16)
        back_two = lax.dot_general(
            w_out_ref[:, start : start + BLOCK],
            adj_half,
            CONTRACT_FIRST,
            preferred_element_type=F32,
        )
        slope = sigma_val * (1.0 + pre_two * (1.0 - sigma_val))
        delta_two_ref[start : start + BLOCK, :] = (back_two * slope).astype(BF16)
    weight_product(delta_two_ref, act_one_ref[...], keep_ref, send_ref, 0)


def backward_kernel(
    x_ref,
    act_two_ref,
    delta_two_ref,
    adj_ref,
    w_in_ref,
    w_mid_ref,
    delta_one_ref,
    keep_ref,
    send_ref,
):
    fields = x_ref.shape[0]
    units = w_mid_ref.shape[0]
    x_now = x_ref[...]
    for start in range(0, units, BLOCK):
        back_one = lax.dot_general(
            w_mid_ref[:, start : start + BLOCK],
            delta_two_ref[...],
            CONTRACT_FIRST,
            preferred_element_type=F32,
        )
        pre_one = jnp.dot(w_in_ref[start : start + BLOCK, :], x_now, preferred_element_type=F32)
        sigma_val = sigmoid(pre_one)
        slope = sigma_val * (1.0 + pre_one * (1.0 - sigma_val))
        delta_one_ref[start : start + BLOCK, :] = (back_one * slope).astype(BF16)
    weight_product(delta_one_ref, x_now, keep_ref, send_ref, 0)
    weight_product(act_two_ref, join_tiles(adj_ref).astype(BF16), keep_ref, send_ref, fields)


def place_back(fresh, live, cols_ref, cells):
    marks = jnp.broadcast_to(live, (16, live.shape[1]))
    placed = lax.dot_general(
        jnp.concatenate([fresh * live, marks], axis=0).astype(BF16),
        one_hot(cols_ref, cells),
        CONTRACT_LAST,
        preferred_element_type=F32,
    )
    rows = fresh.shape[0]
    return placed[:rows], placed[rows : rows + 1] > 0.5


def state_kernel(
    count_ref,
    moved_ref,
    cols_ref,
    mask_ref,
    x_ref,
    act_two_ref,
    coef_ref,
    ratio_ref,
    inverse_ref,
    w_out_ref,
    state_ref,
    forced_ref,
    solved_ref,
    *,
    lons,
):
    fields = x_ref.shape[0]
    levels = coef_ref.shape[0]
    lats = moved_ref.shape[2]
    tendency = jnp.dot(w_out_ref[...], act_two_ref[...], preferred_element_type=F32)
    split_tiles(forced_ref, x_ref[...].astype(F32) + tendency)
    solve(levels, fields // levels, coef_ref, ratio_ref, inverse_ref, forced_ref, solved_ref)
    placed, taken = place_back(
        join_tiles(solved_ref), live_row(count_ref, mask_ref), cols_ref, lons * lats
    )
    for lon in range(lons):
        here = slice(lon * lats, (lon + 1) * lats)
        state_ref[pl.ds(lon, fields, stride=lons), :] = jnp.where(
            taken[:, here], placed[:, here], moved_ref[lon]
        )


def grad_kernel(
    count_ref,
    cot_ref,
    cols_ref,
    mask_ref,
    delta_one_ref,
    adj_ref,
    w_in_ref,
    field_ref,
    up_ref,
    down_ref,
    *,
    lons,
):
    fields, lats = field_ref.shape[1:]
    grad_x = join_tiles(adj_ref) + lax.dot_general(
        w_in_ref[...], delta_one_ref[...], CONTRACT_FIRST, preferred_element_type=F32
    )
    placed, taken = place_back(grad_x, live_row(count_ref, mask_ref), cols_ref, lons * lats)
    for lon in range(lons):
        here = slice(lon * lats, (lon + 1) * lats)
        field_now = jnp.where(
            taken[:, here], placed[:, here], cot_ref[pl.ds(lon, fields, stride=lons), :]
        )
        field_ref[lon] = field_now
        if lon < 2:
            down_ref[lon * fields : (lon + 1) * fields, :] = field_now.astype(BF16)
        if lon >= lons - 2:
            side = lon - (lons - 2)
            up_ref[side * fields : (side + 1) * fields, :] = field_now.astype(BF16)


def last_kernel(field_ref, low_ref, high_ref, low_mix_ref, high_mix_ref, mix_ref, out_ref, *, lons):
    fields = field_ref.shape[1]
    low_rows, high_rows = halo_rows(low_ref, fields), halo_rows(high_ref, fields)
    lon_coef, lat_coef = coefficients(
        mix_ref, halo_mixing(low_mix_ref, fields), halo_mixing(high_mix_ref, fields), lons
    )
    rows = [field_ref[lon] for lon in range(lons)]
    rows = two_steps(low_rows + rows + high_rows, lon_coef, lat_coef)
    for lon in range(lons):
        out_ref[pl.ds(lon, fields, stride=lons), :] = rows[lon]


CORE = ("horiz", 0, 2)
NEAR, FAR = ("horiz", 1, 2), ("horiz", 2, 2)
CHIPS = ("horiz", 1, 4)
MEMBER_LOW, MEMBER_HIGH = ("ens", 0, 2), ("ens", 1, 2)
MEMBERS = ("ens", 0, 4)


def position(stage):
    axis, shift, parts = stage
    return lax.axis_index(axis) // (1 << shift) % parts


def sum_kernel(*refs, terms, stage, factor):
    ins, outs = refs[:terms], refs[terms:]
    rows = outs[0].shape[0]
    for k, out_ref in enumerate(outs):
        here = pl.ds(0, rows)
        if stage is not None:
            here = pl.ds(pl.multiple_of((position(stage) ^ k) * rows, rows), rows)
        total = ins[0][here, :].astype(F32)
        for ref in ins[1:]:
            total = total + ref[here, :].astype(F32)
        out_ref[...] = (total * factor).astype(BF16)


def join_kernel(*refs, stage):
    ins, out_ref = refs[:-1], refs[-1]
    rows = ins[0].shape[0]
    for k, ref in enumerate(ins):
        here = pl.ds(pl.multiple_of((position(stage) ^ k) * rows, rows), rows)
        out_ref[here, :] = ref[...]


def merge_kernel(*refs, terms, factor):
    out_ref = refs[-1]
    first = 0
    for group in (refs[:terms], refs[terms:-1]):
        total = group[0][...].astype(F32)
        for ref in group[1:]:
            total = total + ref[...].astype(F32)
        columns = total.shape[1]
        out_ref[:, first : first + columns] = (total * factor).astype(BF16)
        first += columns


def final_kernel(
    own_mid, got_mid, own_small, got_small, mid_ref, in_ref, out_ref, sorted_ref, *, swapped
):
    rows = own_mid.shape[0]
    fields = in_ref.shape[1]
    core = lax.axis_index("horiz") % 2
    outer, inner = swapped
    block = rows // (outer * inner)
    for mid_half, small_half, half in (
        (own_mid, own_small, core),
        (got_mid, got_small, 1 - core),
    ):
        here = pl.ds(pl.multiple_of(half * rows, rows), rows)
        mid_ref[here, :] = mid_half[...].astype(F32)

        @pl.when(pl.program_id(0) == 0)
        def _():
            for place in range(outer * inner):
                target = (place % inner * outer + place // inner) * block
                sorted_ref[target : target + block, :] = small_half[
                    place * block : (place + 1) * block, :
                ].astype(F32)
            in_ref[here, :] = sorted_ref[:, :fields]
            out_ref[:, here] = sorted_ref[:, fields:].T


def exchange(arrays, stage):
    axis, shift, _ = stage
    count = lax.axis_size(axis)
    return [
        lax.ppermute(array, axis, [(i, i ^ (k << shift)) for i in range(count)])
        for k, array in enumerate(arrays, 1)
    ]


def add(terms, stage, factor=1.0):
    rows, columns = terms[0].shape
    parts = 1 if stage is None else stage[2]
    return call(
        sum_kernel,
        [((rows // parts, columns), BF16)] * parts,
        terms=len(terms),
        stage=stage,
        factor=factor,
    )(*terms)


def join(pieces, stage):
    rows, columns = pieces[0].shape
    (joined,) = call(
        join_kernel,
        [((rows * len(pieces), columns), BF16)],
        stage=stage,
    )(*pieces)
    return joined


def reduce_to(terms, stage):
    parts = add(terms, stage)
    return [parts[0]] + exchange(parts[1:], stage)


def collect(piece, stage):
    return [piece] + exchange([piece] * (stage[2] - 1), stage)


def merge(terms_mid, terms_small, factor):
    rows = terms_mid[0].shape[0]
    columns = terms_mid[0].shape[1] + terms_small[0].shape[1]
    return call(
        merge_kernel, [((rows, columns), BF16)], terms=len(terms_mid), factor=factor
    )(*terms_mid, *terms_small)[0]


def tie(*values):
    return lax.optimization_barrier(values)


def over_all_chips(piece, factor):
    core = lax.axis_index("horiz") % 2
    both = jnp.stack([jnp.where(core == side, piece, 0.0).astype(F32) for side in range(2)])
    return (lax.psum(both, "horiz")[core] * factor).astype(BF16)


def to_neighbours(upward, downward, axis):
    count = lax.axis_size(axis)
    forward = [(i, (i + 1) % count) for i in range(count)]
    backward = [(target, source) for source, target in forward]
    return lax.ppermute(upward, axis, forward), lax.ppermute(downward, axis, backward)


def per_device(
    prognostic, diffusivity, mixing, cotangent, tile_cols, pad_mask, tile_count, w_in, w_mid, w_out
):
    fields, lons, lats = prognostic.shape[1:]
    levels = diffusivity.shape[1]
    units = w_mid.shape[0]
    tiles, width = tile_cols.shape[2:]
    slots = tiles * width
    prog_rows = prognostic.reshape(fields * lons, lats)
    cot_rows = cotangent.reshape(fields * lons, lats)
    diff_rows = diffusivity.reshape(levels * lons, lats)
    mix_rows = mixing.reshape(2 * lons, lats)
    cols, mask = tile_cols[0, 0], pad_mask[0, 0]

    packed = ((2 * fields + PACK_ROWS, lats), BF16)
    up_pack, down_pack, prog_rows, mix_rows = call(
        pack_kernel,
        [packed, packed, (prog_rows.shape, F32), (mix_rows.shape, F32)],
        moved=20 * 10**6,
        lons=lons,
    )(prog_rows, mix_rows)
    low_pack, high_pack = to_neighbours(up_pack, down_pack, "horiz")

    adjoint, coef, ratio, inverse, w_in, w_mid, w_out = call(
        adjoint_kernel,
        [((tiles, fields, width), F32)]
        + [((levels, slots), F32)] * 3
        + [(weight.shape, BF16) for weight in (w_in, w_mid, w_out)],
        scratch=[pltpu.VMEM((tiles, fields, width), F32)],
        smem=(0,),
        moved=30 * 10**6,
        lons=lons,
    )(tile_count, diff_rows, cot_rows, cols, mask, w_in, w_mid, w_out)

    hidden = ((units, slots), BF16)
    half = ((units // 2, units), BF16)
    moved, x_now, act_one, act_two, delta_two, keep_mid, send_mid = call(
        forward_kernel,
        [((lons, fields, lats), F32), ((fields, slots), BF16), hidden, hidden, hidden, half, half],
        moved=15 * 10**6,
        lons=lons,
    )(prog_rows, low_pack, high_pack, mix_rows, cols, adjoint, w_in, w_mid, w_out)
    column_total = lax.axis_size("ens") * lax.axis_size("horiz") * lons * lats
    factor = 1.0 / math.sqrt(column_total)
    (got_mid,) = exchange([send_mid], CORE)

    half = ((units // 2, 2 * fields), BF16)
    delta_one, keep_small, send_small = call(
        backward_kernel, [hidden, half, half], moved=4 * 10**6
    )(x_now, act_two, delta_two, adjoint, w_in, w_mid)
    got_mid, keep_small = tie(got_mid, keep_small)
    (got_small,) = exchange([send_small], CORE)

    def new_state(act_two):
        return call(
            state_kernel,
            [((fields * lons, lats), F32)],
            scratch=[pltpu.VMEM((tiles, fields, width), F32)] * 2,
            smem=(0,),
            lons=lons,
        )(tile_count, moved, cols, mask, x_now, act_two, coef, ratio, inverse, w_out)[0]

    def new_field(delta_one):
        packed = ((2 * fields, lats), BF16)
        return call(
            grad_kernel,
            [((lons, fields, lats), F32), packed, packed],
            smem=(0,),
            lons=lons,
        )(tile_count, cot_rows, cols, mask, delta_one, adjoint, w_in)

    def finish(field, halos):
        return call(last_kernel, [((fields * lons, lats), F32)], lons=lons)(
            field, *halos, low_pack, high_pack, mix_rows
        )[0]

    terms_mid = reduce_to([keep_mid, got_mid], MEMBERS)
    fast = lax.axis_size("ens") == 4 and lax.axis_size("horiz") == 8
    if fast:
        terms_small = reduce_to([keep_small, got_small], FAR)
        terms_small, delta_one = tie(terms_small, delta_one)
        terms_small = reduce_to(terms_small, NEAR)
        field, up_rows, down_rows = new_field(delta_one)
        terms_mid, terms_small, field = tie(terms_mid, terms_small, field)

        terms_mid = reduce_to(terms_mid, CHIPS)
        terms_small = reduce_to(terms_small, MEMBER_HIGH)
        terms_small, act_two = tie(terms_small, act_two)
        terms_small = reduce_to(terms_small, MEMBER_LOW)
        state_rows = new_state(act_two)
        terms_mid, terms_small, state_rows, up_rows, down_rows = tie(
            terms_mid, terms_small, state_rows, up_rows, down_rows
        )

        piece = merge(terms_mid, terms_small, factor)
        pieces = collect(piece, CHIPS)
        halos = to_neighbours(up_rows, down_rows, "horiz")
        pieces, halos = tie(pieces, halos)
        pieces = collect(join(pieces, CHIPS), MEMBERS)
        grad_rows = finish(field, halos)
    else:
        state_rows = new_state(act_two)
        field, up_rows, down_rows = new_field(delta_one)
        grad_rows = finish(field, to_neighbours(up_rows, down_rows, "horiz"))
        terms_small = reduce_to([keep_small, got_small], MEMBERS)
        pieces = collect(over_all_chips(merge(terms_mid, terms_small, 1.0), factor), MEMBERS)
    pieces, grad_rows = tie(pieces, grad_rows)
    own = join(pieces, MEMBERS)
    (got,) = exchange([own], CORE)
    block = units // 4
    mid_half = pl.BlockSpec((units // 2, block), lambda step: (0, step))
    small_half = pl.BlockSpec((units // 2, 2 * fields), lambda step: (0, units // (2 * fields)))
    grad_mid, grad_in, grad_out = pl.pallas_call(
        functools.partial(final_kernel, swapped=(4, 4) if fast else (1, 1)),
        grid=(units // block,),
        out_shape=[
            jax.ShapeDtypeStruct(shape, F32)
            for shape in ((units, units), (units, fields), (fields, units))
        ],
        in_specs=[mid_half, mid_half, small_half, small_half],
        out_specs=[
            pl.BlockSpec((units, block), lambda step: (0, step)),
            pl.BlockSpec((units, fields), lambda step: (0, 0)),
            pl.BlockSpec((fields, units), lambda step: (0, 0)),
        ],
        scratch_shapes=[pltpu.VMEM((units // 2, 2 * fields), F32)],
        compiler_params=pltpu.CompilerParams(vmem_limit_bytes=VMEM_LIMIT),
    )(own, got, own, got)
    return (
        state_rows.reshape(prognostic.shape),
        grad_rows.reshape(prognostic.shape),
        grad_in,
        grad_mid,
        grad_out,
    )


def solution(mesh):
    placed = (
        P("ens", None, "horiz", None),
        P("ens", None, "horiz", None),
        P(None, "horiz", None),
        P("ens", None, "horiz", None),
        P("ens", "horiz", None, None),
        P("ens", "horiz", None, None),
        P("ens", "horiz"),
        P(),
        P(),
        P(),
    )
    return jax.shard_map(
        per_device,
        mesh=mesh,
        in_specs=placed,
        out_specs=(P("ens", None, "horiz", None), P("ens", None, "horiz", None), P(), P(), P()),
        check_vma=False,
    )
```

```python
import functools
import math

import jax
import jax.numpy as jnp
from jax import lax
from jax.experimental import pallas as pl
from jax.experimental.pallas import tpu as pltpu
from jax.sharding import PartitionSpec as P

DYN_STEPS = 2
BLOCK = 256
PACK_ROWS = 16
VMEM_LIMIT = 32 * 1024 * 1024
F32 = jnp.float32
BF16 = jnp.bfloat16
CONTRACT_LAST = (((1,), (1,)), ((), ()))
CONTRACT_FIRST = (((0,), (0,)), ((), ()))


def call(kernel, outs, scratch=(), smem=(), flops=0, moved=0, **names):
    def run(*operands):
        specs = [
            pl.BlockSpec(memory_space=pltpu.SMEM if place in smem else pltpu.VMEM)
            for place in range(len(operands))
        ]
        return pl.pallas_call(
            functools.partial(kernel, **names),
            out_shape=[jax.ShapeDtypeStruct(shape, dtype) for shape, dtype in outs],
            in_specs=specs,
            out_specs=[pl.BlockSpec(memory_space=pltpu.VMEM)] * len(outs),
            scratch_shapes=list(scratch),
            compiler_params=pltpu.CompilerParams(vmem_limit_bytes=VMEM_LIMIT),
            cost_estimate=pl.CostEstimate(flops=flops, bytes_accessed=moved, transcendentals=0),
        )(*operands)

    return run


def lat_term(field_now, coef_masked):
    lats = field_now.shape[1]
    north_flux = coef_masked * (pltpu.roll(field_now, lats - 1, 1) - field_now)
    return north_flux - pltpu.roll(north_flux, 1, 1)


def two_steps(rows, lon_coef, lat_coef):
    for repeat in range(DYN_STEPS):
        count = len(rows)
        fluxes = [
            lon_coef[place + repeat] * (rows[place + 1] - rows[place]) for place in range(count - 1)
        ]
        rows = [
            rows[place]
            + fluxes[place]
            - fluxes[place - 1]
            + lat_term(rows[place], lat_coef[place + repeat])
            for place in range(1, count - 1)
        ]
    return rows


def coefficients(base_ref, low_mix, high_mix, lons):
    lats = base_ref.shape[1]
    first = base_ref.shape[0] - 2 * lons
    lane = lax.broadcasted_iota(jnp.int32, (1, lats), 1)
    inside = lane < lats - 1
    own_lon = [base_ref[first + lon : first + lon + 1, :] for lon in range(lons)]
    first += lons
    own_lat = [base_ref[first + lon : first + lon + 1, :] for lon in range(lons)]
    lon_coef = [low_mix[0:1, :], low_mix[1:2, :]] + own_lon + [high_mix[0:1, :], high_mix[1:2, :]]
    lat_coef = [low_mix[2:3, :], low_mix[3:4, :]] + own_lat + [high_mix[2:3, :], high_mix[3:4, :]]
    return lon_coef, [jnp.where(inside, coef, 0.0) for coef in lat_coef]


def pack_kernel(base_ref, up_ref, down_ref, *, lons):
    fields = base_ref.shape[0] // lons - 2
    mixing = fields * lons
    for out_ref, first in ((up_ref, lons - 2), (down_ref, 0)):
        for side in range(2):
            out_ref[side * fields : (side + 1) * fields, :] = base_ref[
                pl.ds(first + side, fields, stride=lons), :
            ].astype(BF16)
        mix_rows = [
            base_ref[mixing + first : mixing + first + 2, :],
            base_ref[mixing + lons + first : mixing + lons + first + 2, :],
            jnp.zeros((PACK_ROWS - 4, base_ref.shape[1]), F32),
        ]
        out_ref[2 * fields :, :] = jnp.concatenate(mix_rows, axis=0).astype(BF16)


def halo_rows(pack_ref, fields):
    return [pack_ref[side * fields : (side + 1) * fields, :].astype(F32) for side in range(2)]


def halo_mixing(pack_ref, fields):
    return pack_ref[2 * fields :, :].astype(F32)


def one_hot(cols_ref, cells):
    parts = []
    for tile in range(cols_ref.shape[0]):
        place = lax.broadcasted_iota(jnp.int32, (cells, cols_ref.shape[1]), 0)
        parts.append(jnp.where(place == cols_ref[tile : tile + 1, :], 1.0, 0.0))
    return jnp.concatenate(parts, axis=1).astype(BF16)


def live_row(count_ref, mask_ref):
    parts = []
    for tile in range(mask_ref.shape[0]):
        used = jnp.where(tile < count_ref[0, 0], 1, 0)
        parts.append((mask_ref[tile : tile + 1, :] * used).astype(F32))
    return jnp.concatenate(parts, axis=1)


def level_rows(levels, level, variables):
    return pl.ds(level, variables, stride=levels)


def solve(levels, variables, coef_ref, ratio_ref, inverse_ref, right_ref, out_ref):
    tiles, _, width = right_ref.shape
    spans = [slice(tile * width, (tile + 1) * width) for tile in range(tiles)]
    values = []
    for level in range(levels):
        inverse_now = inverse_ref[level : level + 1, :]
        if level > 0:
            carry_now = coef_ref[level - 1 : level, :] * inverse_now
        step = []
        for tile, span in enumerate(spans):
            right_now = right_ref[tile, level_rows(levels, level, variables), :]
            value_now = right_now * inverse_now[:, span]
            if level > 0:
                value_now = value_now + carry_now[:, span] * values[-1][tile]
            step.append(value_now)
        values.append(step)
    results = values[-1]
    for level in range(levels - 1, -1, -1):
        if level < levels - 1:
            ratio_now = ratio_ref[level : level + 1, :]
            results = [
                values[level][tile] - ratio_now[:, span] * results[tile]
                for tile, span in enumerate(spans)
            ]
        for tile in range(tiles):
            out_ref[tile, level_rows(levels, level, variables), :] = results[tile]


def split_tiles(ref, value):
    width = ref.shape[2]
    for tile in range(ref.shape[0]):
        ref[tile] = value[:, tile * width : (tile + 1) * width]


def join_tiles(ref):
    return jnp.concatenate([ref[tile] for tile in range(ref.shape[0])], axis=1)


def factorise(levels, coef_ref, ratio_ref, inverse_ref):
    ratio_prev = None
    for level in range(levels):
        coef_now = coef_ref[level : level + 1, :]
        divisor = 1.0 + coef_now
        if level > 0:
            below_now = coef_ref[level - 1 : level, :]
            divisor = divisor + below_now + below_now * ratio_prev
        inverse_now = 1.0 / divisor
        ratio_prev = -coef_now * inverse_now
        inverse_ref[level : level + 1, :] = inverse_now
        ratio_ref[level : level + 1, :] = ratio_prev


def by_cell(ref, rows, lons):
    return jnp.concatenate(
        [ref[pl.ds(lon, rows, stride=lons), :] for lon in range(lons)], axis=1
    )


def adjoint_kernel(
    count_ref,
    column_ref,
    cols_ref,
    mask_ref,
    adj_ref,
    coef_ref,
    ratio_ref,
    inverse_ref,
    right_ref,
    *,
    lons,
):
    fields = adj_ref.shape[1]
    levels = coef_ref.shape[0]
    spread = one_hot(cols_ref, lons * column_ref.shape[1])
    sources = by_cell(column_ref, fields + levels, lons).astype(BF16)
    picked = jnp.dot(sources, spread, preferred_element_type=F32)
    split_tiles(right_ref, picked[:fields] * live_row(count_ref, mask_ref))
    coef_ref[...] = picked[fields:]
    factorise(levels, coef_ref, ratio_ref, inverse_ref)
    solve(levels, fields // levels, coef_ref, ratio_ref, inverse_ref, right_ref, adj_ref)


def sigmoid(pre_act):
    return 0.5 * jnp.tanh(0.5 * pre_act) + 0.5


def weight_product(left_ref, right, keep_ref, send_ref, first):
    half = left_ref.shape[0] // 2
    block = min(BLOCK, half)
    core = lax.axis_index("horiz") % 2
    for out_ref, side in ((send_ref, 1 - core), (keep_ref, core)):
        for start in range(0, half, block):
            out_ref[start : start + block, first : first + right.shape[0]] = lax.dot_general(
                left_ref[pl.ds(pl.multiple_of(side * half + start, block), block), :],
                right,
                CONTRACT_LAST,
                preferred_element_type=F32,
            ).astype(BF16)


def forward_kernel(
    base_ref,
    low_ref,
    high_ref,
    cols_ref,
    adj_ref,
    weights_ref,
    w_out_ref,
    moved_ref,
    x_ref,
    act_one_ref,
    act_two_ref,
    delta_two_ref,
    keep_ref,
    send_ref,
    *,
    lons,
):
    fields = x_ref.shape[0]
    units = weights_ref.shape[0]
    cells = lons * base_ref.shape[1]
    low_rows, high_rows = halo_rows(low_ref, fields), halo_rows(high_ref, fields)
    lon_coef, lat_coef = coefficients(
        base_ref, halo_mixing(low_ref, fields), halo_mixing(high_ref, fields), lons
    )
    rows = [base_ref[pl.ds(lon, fields, stride=lons), :] for lon in range(lons)]
    rows = two_steps(low_rows + rows + high_rows, lon_coef, lat_coef)
    for lon in range(lons):
        moved_ref[lon] = rows[lon]
    spread = one_hot(cols_ref, cells)
    sources = jnp.concatenate(rows, axis=1).astype(BF16)
    x_now = jnp.dot(sources, spread, preferred_element_type=F32).astype(BF16)
    x_ref[...] = x_now
    for start in range(0, units, BLOCK):
        pre_one = jnp.dot(weights_ref[start : start + BLOCK, units:], x_now, preferred_element_type=F32)
        act_one_ref[start : start + BLOCK, :] = (pre_one * sigmoid(pre_one)).astype(BF16)
    adj_half = join_tiles(adj_ref).astype(BF16)
    for start in range(0, units, BLOCK):
        pre_two = jnp.dot(
            weights_ref[start : start + BLOCK, :units], act_one_ref[...], preferred_element_type=F32
        )
        sigma_val = sigmoid(pre_two)
        act_two_ref[start : start + BLOCK, :] = (pre_two * sigma_val).astype(BF16)
        back_two = lax.dot_general(
            w_out_ref[:, start : start + BLOCK],
            adj_half,
            CONTRACT_FIRST,
            preferred_element_type=F32,
        )
        slope = sigma_val * (1.0 + pre_two * (1.0 - sigma_val))
        delta_two_ref[start : start + BLOCK, :] = (back_two * slope).astype(BF16)
    weight_product(delta_two_ref, act_one_ref[...], keep_ref, send_ref, 0)


def backward_kernel(
    x_ref,
    act_two_ref,
    delta_two_ref,
    adj_ref,
    weights_ref,
    delta_one_ref,
    keep_ref,
    send_ref,
):
    fields = x_ref.shape[0]
    units = weights_ref.shape[0]
    x_now = x_ref[...]
    for start in range(0, units, BLOCK):
        back_one = lax.dot_general(
            weights_ref[:, start : start + BLOCK],
            delta_two_ref[...],
            CONTRACT_FIRST,
            preferred_element_type=F32,
        )
        pre_one = jnp.dot(weights_ref[start : start + BLOCK, units:], x_now, preferred_element_type=F32)
        sigma_val = sigmoid(pre_one)
        slope = sigma_val * (1.0 + pre_one * (1.0 - sigma_val))
        delta_one_ref[start : start + BLOCK, :] = (back_one * slope).astype(BF16)
    weight_product(delta_one_ref, x_now, keep_ref, send_ref, 0)
    weight_product(act_two_ref, join_tiles(adj_ref).astype(BF16), keep_ref, send_ref, fields)


def place_back(fresh, live, cols_ref, cells):
    marks = jnp.broadcast_to(live, (16, live.shape[1]))
    placed = lax.dot_general(
        jnp.concatenate([fresh * live, marks], axis=0).astype(BF16),
        one_hot(cols_ref, cells),
        CONTRACT_LAST,
        preferred_element_type=F32,
    )
    rows = fresh.shape[0]
    return placed[:rows], placed[rows : rows + 1] > 0.5


def state_kernel(
    count_ref,
    moved_ref,
    cols_ref,
    mask_ref,
    x_ref,
    act_two_ref,
    coef_ref,
    ratio_ref,
    inverse_ref,
    w_out_ref,
    state_ref,
    forced_ref,
    solved_ref,
    *,
    lons,
):
    fields = x_ref.shape[0]
    levels = coef_ref.shape[0]
    lats = moved_ref.shape[2]
    tendency = jnp.dot(w_out_ref[...], act_two_ref[...], preferred_element_type=F32)
    split_tiles(forced_ref, x_ref[...].astype(F32) + tendency)
    solve(levels, fields // levels, coef_ref, ratio_ref, inverse_ref, forced_ref, solved_ref)
    placed, taken = place_back(
        join_tiles(solved_ref), live_row(count_ref, mask_ref), cols_ref, lons * lats
    )
    for lon in range(lons):
        here = slice(lon * lats, (lon + 1) * lats)
        state_ref[pl.ds(lon, fields, stride=lons), :] = jnp.where(
            taken[:, here], placed[:, here], moved_ref[lon]
        )


def grad_kernel(
    count_ref,
    column_ref,
    cols_ref,
    mask_ref,
    delta_one_ref,
    adj_ref,
    weights_ref,
    field_ref,
    up_ref,
    down_ref,
    *,
    lons,
):
    fields, lats = field_ref.shape[1:]
    grad_x = join_tiles(adj_ref) + lax.dot_general(
        weights_ref[:, delta_one_ref.shape[0] :], delta_one_ref[...], CONTRACT_FIRST, preferred_element_type=F32
    )
    placed, taken = place_back(grad_x, live_row(count_ref, mask_ref), cols_ref, lons * lats)
    for lon in range(lons):
        here = slice(lon * lats, (lon + 1) * lats)
        field_now = jnp.where(
            taken[:, here], placed[:, here], column_ref[pl.ds(lon, fields, stride=lons), :]
        )
        field_ref[lon] = field_now
        if lon < 2:
            down_ref[lon * fields : (lon + 1) * fields, :] = field_now.astype(BF16)
        if lon >= lons - 2:
            side = lon - (lons - 2)
            up_ref[side * fields : (side + 1) * fields, :] = field_now.astype(BF16)


def last_kernel(field_ref, low_ref, high_ref, low_mix_ref, high_mix_ref, base_ref, out_ref, *, lons):
    fields = field_ref.shape[1]
    low_rows, high_rows = halo_rows(low_ref, fields), halo_rows(high_ref, fields)
    lon_coef, lat_coef = coefficients(
        base_ref, halo_mixing(low_mix_ref, fields), halo_mixing(high_mix_ref, fields), lons
    )
    rows = [field_ref[lon] for lon in range(lons)]
    rows = two_steps(low_rows + rows + high_rows, lon_coef, lat_coef)
    for lon in range(lons):
        out_ref[pl.ds(lon, fields, stride=lons), :] = rows[lon]


CORE = ("horiz", 0, 2)
NEAR, FAR = ("horiz", 1, 2), ("horiz", 2, 2)
CHIPS = ("horiz", 1, 4)
MEMBER_LOW, MEMBER_HIGH = ("ens", 0, 2), ("ens", 1, 2)
MEMBERS = ("ens", 0, 4)


def position(stage):
    axis, shift, parts = stage
    return lax.axis_index(axis) // (1 << shift) % parts


def sum_kernel(*refs, terms, stage, factor):
    ins, outs = refs[:terms], refs[terms:]
    rows = outs[0].shape[0]
    for k, out_ref in enumerate(outs):
        here = pl.ds(0, rows)
        if stage is not None:
            here = pl.ds(pl.multiple_of((position(stage) ^ k) * rows, rows), rows)
        total = ins[0][here, :].astype(F32)
        for ref in ins[1:]:
            total = total + ref[here, :].astype(F32)
        out_ref[...] = (total * factor).astype(BF16)


def join_kernel(*refs, stage, groups, cuts):
    ins, out_refs = refs[:-cuts], refs[-cuts:]
    count = len(ins) // groups
    rows, columns = ins[0].shape
    width = out_refs[0].shape[1]
    for k in range(count):
        here = pl.ds(pl.multiple_of((position(stage) ^ k) * rows, rows), rows)
        for group in range(groups):
            ref = ins[group * count + k]
            for start in range(0, columns, min(width, columns)):
                first = group * columns + start
                part = min(width, columns)
                out_refs[first // width][here, first % width : first % width + part] = ref[
                    :, start : start + part
                ]


def merge_kernel(*refs, terms, factor):
    out_ref = refs[-1]
    first = 0
    for group in (refs[:terms], refs[terms:-1]):
        total = group[0][...].astype(F32)
        for ref in group[1:]:
            total = total + ref[...].astype(F32)
        columns = total.shape[1]
        out_ref[:, first : first + columns] = (total * factor).astype(BF16)
        first += columns


def final_kernel(
    own_mid, got_mid, own_small, got_small, mid_ref, in_ref, out_ref, sorted_ref, *, swapped
):
    rows = own_mid.shape[0]
    fields = in_ref.shape[1]
    core = lax.axis_index("horiz") % 2
    outer, inner = swapped
    block = rows // (outer * inner)
    for mid_half, small_half, half in (
        (own_mid, own_small, core),
        (got_mid, got_small, 1 - core),
    ):
        here = pl.ds(pl.multiple_of(half * rows, rows), rows)
        mid_ref[here, :] = mid_half[...].astype(F32)

        @pl.when(pl.program_id(0) == 0)
        def _():
            for place in range(outer * inner):
                target = (place % inner * outer + place // inner) * block
                sorted_ref[target : target + block, :] = small_half[
                    place * block : (place + 1) * block, :
                ].astype(F32)
            in_ref[here, :] = sorted_ref[:, :fields]
            out_ref[:, here] = sorted_ref[:, fields:].T


def exchange(arrays, stage):
    axis, shift, _ = stage
    count = lax.axis_size(axis)
    return [
        lax.ppermute(array, axis, [(i, i ^ (k << shift)) for i in range(count)])
        for k, array in enumerate(arrays, 1)
    ]


def add(terms, stage, factor=1.0):
    rows, columns = terms[0].shape
    parts = 1 if stage is None else stage[2]
    return call(
        sum_kernel,
        [((rows // parts, columns), BF16)] * parts,
        terms=len(terms),
        stage=stage,
        factor=factor,
    )(*terms)


def join(groups, stage, outs=1):
    rows, columns = groups[0][0].shape
    shape = (rows * len(groups[0]), columns * len(groups) // outs)
    return call(
        join_kernel, [(shape, BF16)] * outs, stage=stage, groups=len(groups), cuts=outs
    )(*[piece for group in groups for piece in group])


def reduce_to(terms, stage):
    parts = add(terms, stage)
    return [parts[0]] + exchange(parts[1:], stage)


def collect_members(one, two):
    (low_one,) = exchange([one], MEMBER_LOW)
    (high_two,) = exchange([two], MEMBER_HIGH)
    (high_one,) = exchange([one], MEMBER_HIGH)
    (low_two,) = exchange([two], MEMBER_LOW)
    (far_one,) = exchange([low_one], MEMBER_HIGH)
    (far_two,) = exchange([high_two], MEMBER_LOW)
    return [one, low_one, high_one, far_one], [two, low_two, high_two, far_two]


def collect(piece, stage):
    return [piece] + exchange([piece] * (stage[2] - 1), stage)


def merge(terms_mid, terms_small, factor):
    rows = terms_mid[0].shape[0]
    columns = terms_mid[0].shape[1] + terms_small[0].shape[1]
    return call(
        merge_kernel, [((rows, columns), BF16)], terms=len(terms_mid), factor=factor
    )(*terms_mid, *terms_small)[0]


def tie(*values):
    return lax.optimization_barrier(values)


def over_all_chips(piece, factor):
    core = lax.axis_index("horiz") % 2
    both = jnp.stack([jnp.where(core == side, piece, 0.0).astype(F32) for side in range(2)])
    return (lax.psum(both, "horiz")[core] * factor).astype(BF16)


def to_neighbours(upward, downward, axis):
    count = lax.axis_size(axis)
    forward = [(i, (i + 1) % count) for i in range(count)]
    backward = [(target, source) for source, target in forward]
    return lax.ppermute(upward, axis, forward), lax.ppermute(downward, axis, backward)


def per_device(
    prognostic, diffusivity, mixing, cotangent, tile_cols, pad_mask, tile_count, w_in, w_mid, w_out
):
    fields, lons, lats = prognostic.shape[1:]
    levels = diffusivity.shape[1]
    units = w_mid.shape[0]
    tiles, width = tile_cols.shape[2:]
    slots = tiles * width
    base = jnp.concatenate([prognostic[0], mixing], axis=0).reshape((fields + 2) * lons, lats)
    column = jnp.concatenate([cotangent[0], diffusivity[0]], axis=0)
    column = column.reshape((fields + levels) * lons, lats)
    weights = jnp.concatenate([w_mid, w_in], axis=1)
    cols, mask = tile_cols[0, 0], pad_mask[0, 0]

    packed = ((2 * fields + PACK_ROWS, lats), BF16)
    up_pack, down_pack = call(pack_kernel, [packed, packed], lons=lons)(base)
    low_pack, high_pack = to_neighbours(up_pack, down_pack, "horiz")

    adjoint, coef, ratio, inverse = call(
        adjoint_kernel,
        [((tiles, fields, width), F32)] + [((levels, slots), F32)] * 3,
        scratch=[pltpu.VMEM((tiles, fields, width), F32)],
        smem=(0,),
        moved=30 * 10**6,
        lons=lons,
    )(tile_count, column, cols, mask)

    hidden = ((units, slots), BF16)
    half = ((units // 2, units), BF16)
    moved, x_now, act_one, act_two, delta_two, keep_mid, send_mid = call(
        forward_kernel,
        [((lons, fields, lats), F32), ((fields, slots), BF16), hidden, hidden, hidden, half, half],
        moved=15 * 10**6,
        lons=lons,
    )(base, low_pack, high_pack, cols, adjoint, weights, w_out)
    column_total = lax.axis_size("ens") * lax.axis_size("horiz") * lons * lats
    factor = 1.0 / math.sqrt(column_total)
    (got_mid,) = exchange([send_mid], CORE)

    half = ((units // 2, 2 * fields), BF16)
    delta_one, keep_small, send_small = call(
        backward_kernel, [hidden, half, half], moved=4 * 10**6
    )(x_now, act_two, delta_two, adjoint, weights)
    got_mid, keep_small = tie(got_mid, keep_small)
    (got_small,) = exchange([send_small], CORE)

    def new_state(act_two):
        return call(
            state_kernel,
            [((fields * lons, lats), F32)],
            scratch=[pltpu.VMEM((tiles, fields, width), F32)] * 2,
            smem=(0,),
            lons=lons,
        )(tile_count, moved, cols, mask, x_now, act_two, coef, ratio, inverse, w_out)[0]

    def new_field(delta_one):
        packed = ((2 * fields, lats), BF16)
        return call(
            grad_kernel,
            [((lons, fields, lats), F32), packed, packed],
            smem=(0,),
            lons=lons,
        )(tile_count, column, cols, mask, delta_one, adjoint, weights)

    def finish(field, halos):
        return call(last_kernel, [((fields * lons, lats), F32)], lons=lons)(
            field, *halos, low_pack, high_pack, base
        )[0]

    terms_mid = reduce_to([keep_mid, got_mid], MEMBERS)
    fast = lax.axis_size("ens") == 4 and lax.axis_size("horiz") == 8
    if fast:
        terms_small = reduce_to([keep_small, got_small], FAR)
        terms_small, delta_one = tie(terms_small, delta_one)
        terms_small = reduce_to(terms_small, NEAR)
        field, up_rows, down_rows = new_field(delta_one)
        terms_mid, terms_small, field = tie(terms_mid, terms_small, field)

        terms_mid = reduce_to(terms_mid, CHIPS)
        terms_small = reduce_to(terms_small, MEMBER_HIGH)
        terms_small, act_two = tie(terms_small, act_two)
        terms_small = reduce_to(terms_small, MEMBER_LOW)
        state_rows = new_state(act_two)
        terms_mid, terms_small, state_rows, up_rows, down_rows = tie(
            terms_mid, terms_small, state_rows, up_rows, down_rows
        )

        piece = merge(terms_mid, terms_small, factor)
        pieces = collect(piece, CHIPS)
        halves = join([pieces], CHIPS, outs=2)
        groups = collect_members(*halves)
        grad_rows = finish(field, to_neighbours(up_rows, down_rows, "horiz"))
    else:
        state_rows = new_state(act_two)
        field, up_rows, down_rows = new_field(delta_one)
        grad_rows = finish(field, to_neighbours(up_rows, down_rows, "horiz"))
        terms_small = reduce_to([keep_small, got_small], MEMBERS)
        groups = [collect(over_all_chips(merge(terms_mid, terms_small, 1.0), factor), MEMBERS)]
    groups, grad_rows = tie(groups, grad_rows)
    (own,) = join(groups, MEMBERS)
    (got,) = exchange([own], CORE)
    block = units // 4
    mid_half = pl.BlockSpec((units // 2, block), lambda step: (0, step))
    small_half = pl.BlockSpec((units // 2, 2 * fields), lambda step: (0, units // (2 * fields)))
    grad_mid, grad_in, grad_out = pl.pallas_call(
        functools.partial(final_kernel, swapped=(4, 4) if fast else (1, 1)),
        grid=(units // block,),
        out_shape=[
            jax.ShapeDtypeStruct(shape, F32)
            for shape in ((units, units), (units, fields), (fields, units))
        ],
        in_specs=[mid_half, mid_half, small_half, small_half],
        out_specs=[
            pl.BlockSpec((units, block), lambda step: (0, step)),
            pl.BlockSpec((units, fields), lambda step: (0, 0)),
            pl.BlockSpec((fields, units), lambda step: (0, 0)),
        ],
        scratch_shapes=[pltpu.VMEM((units // 2, 2 * fields), F32)],
        compiler_params=pltpu.CompilerParams(vmem_limit_bytes=VMEM_LIMIT),
    )(own, got, own, got)
    return (
        state_rows.reshape(prognostic.shape),
        grad_rows.reshape(prognostic.shape),
        grad_in,
        grad_mid,
        grad_out,
    )


def solution(mesh):
    placed = (
        P("ens", None, "horiz", None),
        P("ens", None, "horiz", None),
        P(None, "horiz", None),
        P("ens", None, "horiz", None),
        P("ens", "horiz", None, None),
        P("ens", "horiz", None, None),
        P("ens", "horiz"),
        P(),
        P(),
        P(),
    )
    return jax.shard_map(
        per_device,
        mesh=mesh,
        in_specs=placed,
        out_specs=(P("ens", None, "horiz", None), P("ens", None, "horiz", None), P(), P(), P()),
        check_vma=False,
    )
```

```python
import functools
import math

import jax
import jax.numpy as jnp
from jax import lax
from jax.experimental import pallas as pl
from jax.experimental.pallas import tpu as pltpu
from jax.sharding import PartitionSpec as P

DYN_STEPS = 2
BLOCK = 256
PACK_ROWS = 16
VMEM_LIMIT = 32 * 1024 * 1024
F32 = jnp.float32
BF16 = jnp.bfloat16
CONTRACT_LAST = (((1,), (1,)), ((), ()))
CONTRACT_FIRST = (((0,), (0,)), ((), ()))


def call(kernel, outs, scratch=(), smem=(), flops=0, moved=0, **names):
    def run(*operands):
        specs = [
            pl.BlockSpec(memory_space=pltpu.SMEM if place in smem else pltpu.VMEM)
            for place in range(len(operands))
        ]
        return pl.pallas_call(
            functools.partial(kernel, **names),
            out_shape=[jax.ShapeDtypeStruct(shape, dtype) for shape, dtype in outs],
            in_specs=specs,
            out_specs=[pl.BlockSpec(memory_space=pltpu.VMEM)] * len(outs),
            scratch_shapes=list(scratch),
            compiler_params=pltpu.CompilerParams(vmem_limit_bytes=VMEM_LIMIT),
            cost_estimate=pl.CostEstimate(flops=flops, bytes_accessed=moved, transcendentals=0),
        )(*operands)

    return run


def lat_term(field_now, coef_masked):
    lats = field_now.shape[1]
    north_flux = coef_masked * (pltpu.roll(field_now, lats - 1, 1) - field_now)
    return north_flux - pltpu.roll(north_flux, 1, 1)


def two_steps(rows, lon_coef, lat_coef):
    for repeat in range(DYN_STEPS):
        count = len(rows)
        fluxes = [
            lon_coef[place + repeat] * (rows[place + 1] - rows[place]) for place in range(count - 1)
        ]
        rows = [
            rows[place]
            + fluxes[place]
            - fluxes[place - 1]
            + lat_term(rows[place], lat_coef[place + repeat])
            for place in range(1, count - 1)
        ]
    return rows


def coefficients(base_ref, low_mix, high_mix, lons):
    lats = base_ref.shape[1]
    first = base_ref.shape[0] - 2 * lons
    lane = lax.broadcasted_iota(jnp.int32, (1, lats), 1)
    inside = lane < lats - 1
    own_lon = [base_ref[first + lon : first + lon + 1, :] for lon in range(lons)]
    first += lons
    own_lat = [base_ref[first + lon : first + lon + 1, :] for lon in range(lons)]
    lon_coef = [low_mix[0:1, :], low_mix[1:2, :]] + own_lon + [high_mix[0:1, :], high_mix[1:2, :]]
    lat_coef = [low_mix[2:3, :], low_mix[3:4, :]] + own_lat + [high_mix[2:3, :], high_mix[3:4, :]]
    return lon_coef, [jnp.where(inside, coef, 0.0) for coef in lat_coef]


def pack_kernel(base_ref, up_ref, down_ref, *, lons):
    fields = base_ref.shape[0] // lons - 2
    mixing = fields * lons
    for out_ref, first in ((up_ref, lons - 2), (down_ref, 0)):
        for side in range(2):
            out_ref[side * fields : (side + 1) * fields, :] = base_ref[
                pl.ds(first + side, fields, stride=lons), :
            ].astype(BF16)
        mix_rows = [
            base_ref[mixing + first : mixing + first + 2, :],
            base_ref[mixing + lons + first : mixing + lons + first + 2, :],
            jnp.zeros((PACK_ROWS - 4, base_ref.shape[1]), F32),
        ]
        out_ref[2 * fields :, :] = jnp.concatenate(mix_rows, axis=0).astype(BF16)


def halo_rows(pack_ref, fields):
    return [pack_ref[side * fields : (side + 1) * fields, :].astype(F32) for side in range(2)]


def halo_mixing(pack_ref, fields):
    return pack_ref[2 * fields :, :].astype(F32)


def one_hot(cols_ref, cells):
    parts = []
    for tile in range(cols_ref.shape[0]):
        place = lax.broadcasted_iota(jnp.int32, (cells, cols_ref.shape[1]), 0)
        parts.append(jnp.where(place == cols_ref[tile : tile + 1, :], 1.0, 0.0))
    return jnp.concatenate(parts, axis=1).astype(BF16)


def live_row(count_ref, mask_ref):
    parts = []
    for tile in range(mask_ref.shape[0]):
        used = jnp.where(tile < count_ref[0, 0], 1, 0)
        parts.append((mask_ref[tile : tile + 1, :] * used).astype(F32))
    return jnp.concatenate(parts, axis=1)


def level_rows(levels, level, variables):
    return pl.ds(level, variables, stride=levels)


def solve(levels, variables, coef_ref, ratio_ref, inverse_ref, right_ref, out_ref):
    tiles, _, width = right_ref.shape
    spans = [slice(tile * width, (tile + 1) * width) for tile in range(tiles)]
    values = []
    for level in range(levels):
        inverse_now = inverse_ref[level : level + 1, :]
        if level > 0:
            carry_now = coef_ref[level - 1 : level, :] * inverse_now
        step = []
        for tile, span in enumerate(spans):
            right_now = right_ref[tile, level_rows(levels, level, variables), :]
            value_now = right_now * inverse_now[:, span]
            if level > 0:
                value_now = value_now + carry_now[:, span] * values[-1][tile]
            step.append(value_now)
        values.append(step)
    results = values[-1]
    for level in range(levels - 1, -1, -1):
        if level < levels - 1:
            ratio_now = ratio_ref[level : level + 1, :]
            results = [
                values[level][tile] - ratio_now[:, span] * results[tile]
                for tile, span in enumerate(spans)
            ]
        for tile in range(tiles):
            out_ref[tile, level_rows(levels, level, variables), :] = results[tile]


def split_tiles(ref, value):
    width = ref.shape[2]
    for tile in range(ref.shape[0]):
        ref[tile] = value[:, tile * width : (tile + 1) * width]


def join_tiles(ref):
    return jnp.concatenate([ref[tile] for tile in range(ref.shape[0])], axis=1)


def factorise(levels, coef_ref, ratio_ref, inverse_ref):
    ratio_prev = None
    for level in range(levels):
        coef_now = coef_ref[level : level + 1, :]
        divisor = 1.0 + coef_now
        if level > 0:
            below_now = coef_ref[level - 1 : level, :]
            divisor = divisor + below_now + below_now * ratio_prev
        inverse_now = 1.0 / divisor
        ratio_prev = -coef_now * inverse_now
        inverse_ref[level : level + 1, :] = inverse_now
        ratio_ref[level : level + 1, :] = ratio_prev


def by_cell(ref, rows, lons):
    return jnp.concatenate(
        [ref[pl.ds(lon, rows, stride=lons), :] for lon in range(lons)], axis=1
    )


def adjoint_kernel(
    count_ref,
    column_ref,
    cols_ref,
    mask_ref,
    adj_ref,
    coef_ref,
    ratio_ref,
    inverse_ref,
    right_ref,
    *,
    lons,
):
    fields = adj_ref.shape[1]
    levels = coef_ref.shape[0]
    spread = one_hot(cols_ref, lons * column_ref.shape[1])
    sources = by_cell(column_ref, fields + levels, lons).astype(BF16)
    picked = jnp.dot(sources, spread, preferred_element_type=F32)
    split_tiles(right_ref, picked[:fields] * live_row(count_ref, mask_ref))
    coef_ref[...] = picked[fields:]
    factorise(levels, coef_ref, ratio_ref, inverse_ref)
    solve(levels, fields // levels, coef_ref, ratio_ref, inverse_ref, right_ref, adj_ref)


def sigmoid(pre_act):
    return 0.5 * jnp.tanh(0.5 * pre_act) + 0.5


def weight_product(left_ref, right, keep_ref, send_ref, first):
    half = left_ref.shape[0] // 2
    block = min(BLOCK, half)
    core = lax.axis_index("horiz") % 2
    for out_ref, side in ((send_ref, 1 - core), (keep_ref, core)):
        for start in range(0, half, block):
            out_ref[start : start + block, first : first + right.shape[0]] = lax.dot_general(
                left_ref[pl.ds(pl.multiple_of(side * half + start, block), block), :],
                right,
                CONTRACT_LAST,
                preferred_element_type=F32,
            ).astype(BF16)


def forward_kernel(
    base_ref,
    low_ref,
    high_ref,
    cols_ref,
    adj_ref,
    weights_ref,
    w_out_ref,
    moved_ref,
    x_ref,
    act_one_ref,
    act_two_ref,
    delta_two_ref,
    keep_ref,
    send_ref,
    *,
    lons,
):
    fields = x_ref.shape[0]
    units = weights_ref.shape[0]
    cells = lons * base_ref.shape[1]
    low_rows, high_rows = halo_rows(low_ref, fields), halo_rows(high_ref, fields)
    lon_coef, lat_coef = coefficients(
        base_ref, halo_mixing(low_ref, fields), halo_mixing(high_ref, fields), lons
    )
    rows = [base_ref[pl.ds(lon, fields, stride=lons), :] for lon in range(lons)]
    rows = two_steps(low_rows + rows + high_rows, lon_coef, lat_coef)
    for lon in range(lons):
        moved_ref[lon] = rows[lon]
    spread = one_hot(cols_ref, cells)
    sources = jnp.concatenate(rows, axis=1).astype(BF16)
    x_now = jnp.dot(sources, spread, preferred_element_type=F32).astype(BF16)
    x_ref[...] = x_now
    for start in range(0, units, BLOCK):
        pre_one = jnp.dot(weights_ref[start : start + BLOCK, units:], x_now, preferred_element_type=F32)
        act_one_ref[start : start + BLOCK, :] = (pre_one * sigmoid(pre_one)).astype(BF16)
    adj_half = join_tiles(adj_ref).astype(BF16)
    for start in range(0, units, BLOCK):
        pre_two = jnp.dot(
            weights_ref[start : start + BLOCK, :units], act_one_ref[...], preferred_element_type=F32
        )
        sigma_val = sigmoid(pre_two)
        act_two_ref[start : start + BLOCK, :] = (pre_two * sigma_val).astype(BF16)
        back_two = lax.dot_general(
            w_out_ref[:, start : start + BLOCK],
            adj_half,
            CONTRACT_FIRST,
            preferred_element_type=F32,
        )
        slope = sigma_val * (1.0 + pre_two * (1.0 - sigma_val))
        delta_two_ref[start : start + BLOCK, :] = (back_two * slope).astype(BF16)
    weight_product(delta_two_ref, act_one_ref[...], keep_ref, send_ref, 0)


def backward_kernel(
    x_ref,
    act_two_ref,
    delta_two_ref,
    adj_ref,
    weights_ref,
    delta_one_ref,
    keep_ref,
    send_ref,
):
    fields = x_ref.shape[0]
    units = weights_ref.shape[0]
    x_now = x_ref[...]
    for start in range(0, units, BLOCK):
        back_one = lax.dot_general(
            weights_ref[:, start : start + BLOCK],
            delta_two_ref[...],
            CONTRACT_FIRST,
            preferred_element_type=F32,
        )
        pre_one = jnp.dot(weights_ref[start : start + BLOCK, units:], x_now, preferred_element_type=F32)
        sigma_val = sigmoid(pre_one)
        slope = sigma_val * (1.0 + pre_one * (1.0 - sigma_val))
        delta_one_ref[start : start + BLOCK, :] = (back_one * slope).astype(BF16)
    weight_product(delta_one_ref, x_now, keep_ref, send_ref, 0)
    weight_product(act_two_ref, join_tiles(adj_ref).astype(BF16), keep_ref, send_ref, fields)


def place_back(fresh, live, cols_ref, cells):
    marks = jnp.broadcast_to(live, (16, live.shape[1]))
    placed = lax.dot_general(
        jnp.concatenate([fresh * live, marks], axis=0).astype(BF16),
        one_hot(cols_ref, cells),
        CONTRACT_LAST,
        preferred_element_type=F32,
    )
    rows = fresh.shape[0]
    return placed[:rows], placed[rows : rows + 1] > 0.5


def state_kernel(
    count_ref,
    moved_ref,
    cols_ref,
    mask_ref,
    x_ref,
    act_two_ref,
    coef_ref,
    ratio_ref,
    inverse_ref,
    w_out_ref,
    state_ref,
    forced_ref,
    solved_ref,
    *,
    lons,
):
    fields = x_ref.shape[0]
    levels = coef_ref.shape[0]
    lats = moved_ref.shape[2]
    tendency = jnp.dot(w_out_ref[...], act_two_ref[...], preferred_element_type=F32)
    split_tiles(forced_ref, x_ref[...].astype(F32) + tendency)
    solve(levels, fields // levels, coef_ref, ratio_ref, inverse_ref, forced_ref, solved_ref)
    placed, taken = place_back(
        join_tiles(solved_ref), live_row(count_ref, mask_ref), cols_ref, lons * lats
    )
    for lon in range(lons):
        here = slice(lon * lats, (lon + 1) * lats)
        state_ref[pl.ds(lon, fields, stride=lons), :] = jnp.where(
            taken[:, here], placed[:, here], moved_ref[lon]
        )


def grad_kernel(
    count_ref,
    column_ref,
    cols_ref,
    mask_ref,
    delta_one_ref,
    adj_ref,
    weights_ref,
    field_ref,
    up_ref,
    down_ref,
    *,
    lons,
):
    fields, lats = field_ref.shape[1:]
    grad_x = join_tiles(adj_ref) + lax.dot_general(
        weights_ref[:, delta_one_ref.shape[0] :], delta_one_ref[...], CONTRACT_FIRST, preferred_element_type=F32
    )
    placed, taken = place_back(grad_x, live_row(count_ref, mask_ref), cols_ref, lons * lats)
    for lon in range(lons):
        here = slice(lon * lats, (lon + 1) * lats)
        field_now = jnp.where(
            taken[:, here], placed[:, here], column_ref[pl.ds(lon, fields, stride=lons), :]
        )
        field_ref[lon] = field_now
        if lon < 2:
            down_ref[lon * fields : (lon + 1) * fields, :] = field_now.astype(BF16)
        if lon >= lons - 2:
            side = lon - (lons - 2)
            up_ref[side * fields : (side + 1) * fields, :] = field_now.astype(BF16)


def last_kernel(field_ref, low_ref, high_ref, low_mix_ref, high_mix_ref, base_ref, out_ref, *, lons):
    fields = field_ref.shape[1]
    low_rows, high_rows = halo_rows(low_ref, fields), halo_rows(high_ref, fields)
    lon_coef, lat_coef = coefficients(
        base_ref, halo_mixing(low_mix_ref, fields), halo_mixing(high_mix_ref, fields), lons
    )
    rows = [field_ref[lon] for lon in range(lons)]
    rows = two_steps(low_rows + rows + high_rows, lon_coef, lat_coef)
    for lon in range(lons):
        out_ref[pl.ds(lon, fields, stride=lons), :] = rows[lon]


CORE = ("horiz", 0, 2)
NEAR, FAR = ("horiz", 1, 2), ("horiz", 2, 2)
CHIPS = ("horiz", 1, 4)
MEMBER_LOW, MEMBER_HIGH = ("ens", 0, 2), ("ens", 1, 2)
MEMBERS = ("ens", 0, 4)


def position(stage):
    axis, shift, parts = stage
    return lax.axis_index(axis) // (1 << shift) % parts


def sum_kernel(*refs, terms, stage, factor):
    ins, outs = refs[:terms], refs[terms:]
    rows = outs[0].shape[0]
    for k, out_ref in enumerate(outs):
        here = pl.ds(0, rows)
        if stage is not None:
            here = pl.ds(pl.multiple_of((position(stage) ^ k) * rows, rows), rows)
        total = ins[0][here, :].astype(F32)
        for ref in ins[1:]:
            total = total + ref[here, :].astype(F32)
        out_ref[...] = (total * factor).astype(BF16)


def join_kernel(*refs, stage, groups, cuts):
    ins, out_refs = refs[:-cuts], refs[-cuts:]
    count = len(ins) // groups
    rows, columns = ins[0].shape
    width = out_refs[0].shape[1]
    for k in range(count):
        here = pl.ds(pl.multiple_of((position(stage) ^ k) * rows, rows), rows)
        for group in range(groups):
            ref = ins[group * count + k]
            for start in range(0, columns, min(width, columns)):
                first = group * columns + start
                part = min(width, columns)
                out_refs[first // width][here, first % width : first % width + part] = ref[
                    :, start : start + part
                ]


def merge_kernel(*refs, terms, factor):
    out_ref = refs[-1]
    first = 0
    for group in (refs[:terms], refs[terms:-1]):
        total = group[0][...].astype(F32)
        for ref in group[1:]:
            total = total + ref[...].astype(F32)
        columns = total.shape[1]
        out_ref[:, first : first + columns] = (total * factor).astype(BF16)
        first += columns


def final_kernel(
    own_mid, got_mid, own_small, got_small, mid_ref, in_ref, out_ref, sorted_ref, *, order
):
    rows = own_mid.shape[0]
    fields = in_ref.shape[1]
    core = lax.axis_index("horiz") % 2
    block = rows // len(order)
    for mid_half, small_half, half in (
        (own_mid, own_small, core),
        (got_mid, got_small, 1 - core),
    ):
        here = pl.ds(pl.multiple_of(half * rows, rows), rows)
        mid_ref[here, :] = mid_half[...].astype(F32)

        @pl.when(pl.program_id(0) == 0)
        def _():
            for place, target in enumerate(order):
                sorted_ref[target * block : (target + 1) * block, :] = small_half[
                    place * block : (place + 1) * block, :
                ].astype(F32)
            in_ref[here, :] = sorted_ref[:, :fields]
            out_ref[:, here] = sorted_ref[:, fields:].T


def exchange(arrays, stage):
    axis, shift, _ = stage
    count = lax.axis_size(axis)
    return [
        lax.ppermute(array, axis, [(i, i ^ (k << shift)) for i in range(count)])
        for k, array in enumerate(arrays, 1)
    ]


def add(terms, stage, factor=1.0):
    rows, columns = terms[0].shape
    parts = 1 if stage is None else stage[2]
    return call(
        sum_kernel,
        [((rows // parts, columns), BF16)] * parts,
        terms=len(terms),
        stage=stage,
        factor=factor,
    )(*terms)


def join(groups, stage, outs=1):
    rows, columns = groups[0][0].shape
    shape = (rows * len(groups[0]), columns * len(groups) // outs)
    return call(
        join_kernel, [(shape, BF16)] * outs, stage=stage, groups=len(groups), cuts=outs
    )(*[piece for group in groups for piece in group])


def reduce_to(terms, stage):
    parts = add(terms, stage)
    return [parts[0]] + exchange(parts[1:], stage)


def collect_members(one, two):
    (low_one,) = exchange([one], MEMBER_LOW)
    (high_two,) = exchange([two], MEMBER_HIGH)
    (high_one,) = exchange([one], MEMBER_HIGH)
    (low_two,) = exchange([two], MEMBER_LOW)
    (far_one,) = exchange([low_one], MEMBER_HIGH)
    (far_two,) = exchange([high_two], MEMBER_LOW)
    return [one, low_one, high_one, far_one], [two, low_two, high_two, far_two]


def collect(piece, stage):
    return [piece] + exchange([piece] * (stage[2] - 1), stage)


def merge(terms_mid, terms_small, factor):
    rows = terms_mid[0].shape[0]
    columns = terms_mid[0].shape[1] + terms_small[0].shape[1]
    return call(
        merge_kernel, [((rows, columns), BF16)], terms=len(terms_mid), factor=factor
    )(*terms_mid, *terms_small)[0]


def tie(*values):
    return lax.optimization_barrier(values)


def over_all_chips(piece, factor):
    core = lax.axis_index("horiz") % 2
    both = jnp.stack([jnp.where(core == side, piece, 0.0).astype(F32) for side in range(2)])
    return (lax.psum(both, "horiz")[core] * factor).astype(BF16)


def to_neighbours(upward, downward, axis):
    count = lax.axis_size(axis)
    forward = [(i, (i + 1) % count) for i in range(count)]
    backward = [(target, source) for source, target in forward]
    return lax.ppermute(upward, axis, forward), lax.ppermute(downward, axis, backward)


def per_device(
    prognostic, diffusivity, mixing, cotangent, tile_cols, pad_mask, tile_count, w_in, w_mid, w_out
):
    fields, lons, lats = prognostic.shape[1:]
    levels = diffusivity.shape[1]
    units = w_mid.shape[0]
    tiles, width = tile_cols.shape[2:]
    slots = tiles * width
    base = jnp.concatenate([prognostic[0], mixing], axis=0).reshape((fields + 2) * lons, lats)
    column = jnp.concatenate([cotangent[0], diffusivity[0]], axis=0)
    column = column.reshape((fields + levels) * lons, lats)
    weights = jnp.concatenate([w_mid, w_in], axis=1)
    cols, mask = tile_cols[0, 0], pad_mask[0, 0]

    packed = ((2 * fields + PACK_ROWS, lats), BF16)
    up_pack, down_pack = call(pack_kernel, [packed, packed], lons=lons)(base)
    low_pack, high_pack = to_neighbours(up_pack, down_pack, "horiz")

    adjoint, coef, ratio, inverse = call(
        adjoint_kernel,
        [((tiles, fields, width), F32)] + [((levels, slots), F32)] * 3,
        scratch=[pltpu.VMEM((tiles, fields, width), F32)],
        smem=(0,),
        moved=30 * 10**6,
        lons=lons,
    )(tile_count, column, cols, mask)

    hidden = ((units, slots), BF16)
    half = ((units // 2, units), BF16)
    moved, x_now, act_one, act_two, delta_two, keep_mid, send_mid = call(
        forward_kernel,
        [((lons, fields, lats), F32), ((fields, slots), BF16), hidden, hidden, hidden, half, half],
        moved=15 * 10**6,
        lons=lons,
    )(base, low_pack, high_pack, cols, adjoint, weights, w_out)
    column_total = lax.axis_size("ens") * lax.axis_size("horiz") * lons * lats
    factor = 1.0 / math.sqrt(column_total)
    (got_mid,) = exchange([send_mid], CORE)

    half = ((units // 2, 2 * fields), BF16)
    delta_one, keep_small, send_small = call(
        backward_kernel, [hidden, half, half], moved=4 * 10**6
    )(x_now, act_two, delta_two, adjoint, weights)
    got_mid, keep_small = tie(got_mid, keep_small)
    (got_small,) = exchange([send_small], CORE)

    def new_state(act_two):
        return call(
            state_kernel,
            [((fields * lons, lats), F32)],
            scratch=[pltpu.VMEM((tiles, fields, width), F32)] * 2,
            smem=(0,),
            lons=lons,
        )(tile_count, moved, cols, mask, x_now, act_two, coef, ratio, inverse, w_out)[0]

    def new_field(delta_one):
        packed = ((2 * fields, lats), BF16)
        return call(
            grad_kernel,
            [((lons, fields, lats), F32), packed, packed],
            smem=(0,),
            lons=lons,
        )(tile_count, column, cols, mask, delta_one, adjoint, weights)

    def finish(field, halos):
        return call(last_kernel, [((fields * lons, lats), F32)], lons=lons)(
            field, *halos, low_pack, high_pack, base
        )[0]

    terms_mid = reduce_to([keep_mid, got_mid], MEMBERS)
    fast = lax.axis_size("ens") == 4 and lax.axis_size("horiz") == 8
    if fast:
        terms_small = reduce_to([keep_small, got_small], NEAR)
        terms_small, delta_one = tie(terms_small, delta_one)
        field, up_rows, down_rows = new_field(delta_one)
        halos = to_neighbours(up_rows, down_rows, "horiz")
        terms_small = reduce_to(terms_small, FAR)
        terms_mid, terms_small, field, halos = tie(terms_mid, terms_small, field, halos)

        terms_mid = reduce_to(terms_mid, CHIPS)
        terms_small = reduce_to(terms_small, MEMBER_HIGH)
        terms_small, act_two = tie(terms_small, act_two)
        terms_small = reduce_to(terms_small, MEMBER_LOW)
        state_rows = new_state(act_two)
        terms_mid, terms_small, state_rows = tie(terms_mid, terms_small, state_rows)

        piece = merge(terms_mid, terms_small, factor)
        pieces = collect(piece, CHIPS)
        halves = join([pieces], CHIPS, outs=2)
        groups = collect_members(*halves)
        grad_rows = finish(field, halos)
    else:
        state_rows = new_state(act_two)
        field, up_rows, down_rows = new_field(delta_one)
        grad_rows = finish(field, to_neighbours(up_rows, down_rows, "horiz"))
        terms_small = reduce_to([keep_small, got_small], MEMBERS)
        groups = [collect(over_all_chips(merge(terms_mid, terms_small, 1.0), factor), MEMBERS)]
    groups, grad_rows = tie(groups, grad_rows)
    (own,) = join(groups, MEMBERS)
    (got,) = exchange([own], CORE)
    order = [0]
    if fast:
        order = [
            (chip % 2 * 2 + chip // 2) * 4 + member for member in range(4) for chip in range(4)
        ]
    block = units // 4
    mid_half = pl.BlockSpec((units // 2, block), lambda step: (0, step))
    small_half = pl.BlockSpec((units // 2, 2 * fields), lambda step: (0, units // (2 * fields)))
    grad_mid, grad_in, grad_out = pl.pallas_call(
        functools.partial(final_kernel, order=order),
        grid=(units // block,),
        out_shape=[
            jax.ShapeDtypeStruct(shape, F32)
            for shape in ((units, units), (units, fields), (fields, units))
        ],
        in_specs=[mid_half, mid_half, small_half, small_half],
        out_specs=[
            pl.BlockSpec((units, block), lambda step: (0, step)),
            pl.BlockSpec((units, fields), lambda step: (0, 0)),
            pl.BlockSpec((fields, units), lambda step: (0, 0)),
        ],
        scratch_shapes=[pltpu.VMEM((units // 2, 2 * fields), F32)],
        compiler_params=pltpu.CompilerParams(vmem_limit_bytes=VMEM_LIMIT),
    )(own, got, own, got)
    return (
        state_rows.reshape(prognostic.shape),
        grad_rows.reshape(prognostic.shape),
        grad_in,
        grad_mid,
        grad_out,
    )


def solution(mesh):
    placed = (
        P("ens", None, "horiz", None),
        P("ens", None, "horiz", None),
        P(None, "horiz", None),
        P("ens", None, "horiz", None),
        P("ens", "horiz", None, None),
        P("ens", "horiz", None, None),
        P("ens", "horiz"),
        P(),
        P(),
        P(),
    )
    return jax.shard_map(
        per_device,
        mesh=mesh,
        in_specs=placed,
        out_specs=(P("ens", None, "horiz", None), P("ens", None, "horiz", None), P(), P(), P()),
        check_vma=False,
    )
```

```python
import functools
import math

import jax
import jax.numpy as jnp
from jax import lax
from jax.experimental import pallas as pl
from jax.experimental.pallas import tpu as pltpu
from jax.sharding import PartitionSpec as P

DYN_STEPS = 2
BLOCK = 256
PACK_ROWS = 16
VMEM_LIMIT = 32 * 1024 * 1024
F32 = jnp.float32
BF16 = jnp.bfloat16
CONTRACT_LAST = (((1,), (1,)), ((), ()))
CONTRACT_FIRST = (((0,), (0,)), ((), ()))


def call(kernel, outs, scratch=(), smem=(), flops=0, moved=0, **names):
    def run(*operands):
        specs = [
            pl.BlockSpec(memory_space=pltpu.SMEM if place in smem else pltpu.VMEM)
            for place in range(len(operands))
        ]
        return pl.pallas_call(
            functools.partial(kernel, **names),
            out_shape=[jax.ShapeDtypeStruct(shape, dtype) for shape, dtype in outs],
            in_specs=specs,
            out_specs=[pl.BlockSpec(memory_space=pltpu.VMEM)] * len(outs),
            scratch_shapes=list(scratch),
            compiler_params=pltpu.CompilerParams(vmem_limit_bytes=VMEM_LIMIT),
            cost_estimate=pl.CostEstimate(flops=flops, bytes_accessed=moved, transcendentals=0),
        )(*operands)

    return run


def lat_term(field_now, coef_masked):
    lats = field_now.shape[1]
    north_flux = coef_masked * (pltpu.roll(field_now, lats - 1, 1) - field_now)
    return north_flux - pltpu.roll(north_flux, 1, 1)


def two_steps(rows, lon_coef, lat_coef):
    for repeat in range(DYN_STEPS):
        count = len(rows)
        fluxes = [
            lon_coef[place + repeat] * (rows[place + 1] - rows[place]) for place in range(count - 1)
        ]
        rows = [
            rows[place]
            + fluxes[place]
            - fluxes[place - 1]
            + lat_term(rows[place], lat_coef[place + repeat])
            for place in range(1, count - 1)
        ]
    return rows


def coefficients(base_ref, low_mix, high_mix, lons):
    lats = base_ref.shape[1]
    first = base_ref.shape[0] - 2 * lons
    lane = lax.broadcasted_iota(jnp.int32, (1, lats), 1)
    inside = lane < lats - 1
    own_lon = [base_ref[first + lon : first + lon + 1, :] for lon in range(lons)]
    first += lons
    own_lat = [base_ref[first + lon : first + lon + 1, :] for lon in range(lons)]
    lon_coef = [low_mix[0:1, :], low_mix[1:2, :]] + own_lon + [high_mix[0:1, :], high_mix[1:2, :]]
    lat_coef = [low_mix[2:3, :], low_mix[3:4, :]] + own_lat + [high_mix[2:3, :], high_mix[3:4, :]]
    return lon_coef, [jnp.where(inside, coef, 0.0) for coef in lat_coef]


def pack_kernel(base_ref, up_ref, down_ref, *, lons):
    fields = base_ref.shape[0] // lons - 2
    mixing = fields * lons
    for out_ref, first in ((up_ref, lons - 2), (down_ref, 0)):
        for side in range(2):
            out_ref[side * fields : (side + 1) * fields, :] = base_ref[
                pl.ds(first + side, fields, stride=lons), :
            ].astype(BF16)
        mix_rows = [
            base_ref[mixing + first : mixing + first + 2, :],
            base_ref[mixing + lons + first : mixing + lons + first + 2, :],
            jnp.zeros((PACK_ROWS - 4, base_ref.shape[1]), F32),
        ]
        out_ref[2 * fields :, :] = jnp.concatenate(mix_rows, axis=0).astype(BF16)


def halo_rows(pack_ref, fields):
    return [pack_ref[side * fields : (side + 1) * fields, :].astype(F32) for side in range(2)]


def halo_mixing(pack_ref, fields):
    return pack_ref[2 * fields :, :].astype(F32)


def one_hot(cols_ref, cells):
    parts = []
    for tile in range(cols_ref.shape[0]):
        place = lax.broadcasted_iota(jnp.int32, (cells, cols_ref.shape[1]), 0)
        parts.append(jnp.where(place == cols_ref[tile : tile + 1, :], 1.0, 0.0))
    return jnp.concatenate(parts, axis=1).astype(BF16)


def live_row(count_ref, mask_ref):
    parts = []
    for tile in range(mask_ref.shape[0]):
        used = jnp.where(tile < count_ref[0, 0], 1, 0)
        parts.append((mask_ref[tile : tile + 1, :] * used).astype(F32))
    return jnp.concatenate(parts, axis=1)


def level_rows(levels, level, variables):
    return pl.ds(level, variables, stride=levels)


def solve(levels, variables, coef_ref, ratio_ref, inverse_ref, right_ref, out_ref):
    tiles, _, width = right_ref.shape
    spans = [slice(tile * width, (tile + 1) * width) for tile in range(tiles)]
    values = []
    for level in range(levels):
        inverse_now = inverse_ref[level : level + 1, :]
        if level > 0:
            carry_now = coef_ref[level - 1 : level, :] * inverse_now
        step = []
        for tile, span in enumerate(spans):
            right_now = right_ref[tile, level_rows(levels, level, variables), :]
            value_now = right_now * inverse_now[:, span]
            if level > 0:
                value_now = value_now + carry_now[:, span] * values[-1][tile]
            step.append(value_now)
        values.append(step)
    results = values[-1]
    for level in range(levels - 1, -1, -1):
        if level < levels - 1:
            ratio_now = ratio_ref[level : level + 1, :]
            results = [
                values[level][tile] - ratio_now[:, span] * results[tile]
                for tile, span in enumerate(spans)
            ]
        for tile in range(tiles):
            out_ref[tile, level_rows(levels, level, variables), :] = results[tile]


def split_tiles(ref, value):
    width = ref.shape[2]
    for tile in range(ref.shape[0]):
        ref[tile] = value[:, tile * width : (tile + 1) * width]


def join_tiles(ref):
    return jnp.concatenate([ref[tile] for tile in range(ref.shape[0])], axis=1)


def factorise(levels, coef_ref, ratio_ref, inverse_ref):
    ratio_prev = None
    for level in range(levels):
        coef_now = coef_ref[level : level + 1, :]
        divisor = 1.0 + coef_now
        if level > 0:
            below_now = coef_ref[level - 1 : level, :]
            divisor = divisor + below_now + below_now * ratio_prev
        inverse_now = 1.0 / divisor
        ratio_prev = -coef_now * inverse_now
        inverse_ref[level : level + 1, :] = inverse_now
        ratio_ref[level : level + 1, :] = ratio_prev


def by_cell(ref, rows, lons):
    return jnp.concatenate(
        [ref[pl.ds(lon, rows, stride=lons), :] for lon in range(lons)], axis=1
    )


def adjoint_kernel(
    count_ref,
    column_ref,
    cols_ref,
    mask_ref,
    adj_ref,
    coef_ref,
    ratio_ref,
    inverse_ref,
    right_ref,
    *,
    lons,
):
    fields = adj_ref.shape[1]
    levels = coef_ref.shape[0]
    spread = one_hot(cols_ref, lons * column_ref.shape[1])
    sources = by_cell(column_ref, fields + levels, lons).astype(BF16)
    picked = jnp.dot(sources, spread, preferred_element_type=F32)
    split_tiles(right_ref, picked[:fields] * live_row(count_ref, mask_ref))
    coef_ref[...] = picked[fields:]
    factorise(levels, coef_ref, ratio_ref, inverse_ref)
    solve(levels, fields // levels, coef_ref, ratio_ref, inverse_ref, right_ref, adj_ref)


def sigmoid(pre_act):
    return 0.5 * jnp.tanh(0.5 * pre_act) + 0.5


def weight_product(left_ref, right, keep_ref, send_ref, first):
    half = left_ref.shape[0] // 2
    block = min(BLOCK, half)
    core = lax.axis_index("horiz") % 2
    for out_ref, side in ((send_ref, 1 - core), (keep_ref, core)):
        for start in range(0, half, block):
            out_ref[start : start + block, first : first + right.shape[0]] = lax.dot_general(
                left_ref[pl.ds(pl.multiple_of(side * half + start, block), block), :],
                right,
                CONTRACT_LAST,
                preferred_element_type=F32,
            ).astype(BF16)


def forward_kernel(
    base_ref,
    low_ref,
    high_ref,
    cols_ref,
    adj_ref,
    weights_ref,
    w_out_ref,
    moved_ref,
    x_ref,
    act_one_ref,
    act_two_ref,
    delta_two_ref,
    keep_ref,
    send_ref,
    *,
    lons,
):
    fields = x_ref.shape[0]
    units = weights_ref.shape[0]
    cells = lons * base_ref.shape[1]
    low_rows, high_rows = halo_rows(low_ref, fields), halo_rows(high_ref, fields)
    lon_coef, lat_coef = coefficients(
        base_ref, halo_mixing(low_ref, fields), halo_mixing(high_ref, fields), lons
    )
    rows = [base_ref[pl.ds(lon, fields, stride=lons), :] for lon in range(lons)]
    rows = two_steps(low_rows + rows + high_rows, lon_coef, lat_coef)
    for lon in range(lons):
        moved_ref[lon] = rows[lon]
    spread = one_hot(cols_ref, cells)
    sources = jnp.concatenate(rows, axis=1).astype(BF16)
    x_now = jnp.dot(sources, spread, preferred_element_type=F32).astype(BF16)
    x_ref[...] = x_now
    for start in range(0, units, BLOCK):
        pre_one = jnp.dot(weights_ref[start : start + BLOCK, units:], x_now, preferred_element_type=F32)
        act_one_ref[start : start + BLOCK, :] = (pre_one * sigmoid(pre_one)).astype(BF16)
    adj_half = join_tiles(adj_ref).astype(BF16)
    for start in range(0, units, BLOCK):
        pre_two = jnp.dot(
            weights_ref[start : start + BLOCK, :units], act_one_ref[...], preferred_element_type=F32
        )
        sigma_val = sigmoid(pre_two)
        act_two_ref[start : start + BLOCK, :] = (pre_two * sigma_val).astype(BF16)
        back_two = lax.dot_general(
            w_out_ref[:, start : start + BLOCK],
            adj_half,
            CONTRACT_FIRST,
            preferred_element_type=F32,
        )
        slope = sigma_val * (1.0 + pre_two * (1.0 - sigma_val))
        delta_two_ref[start : start + BLOCK, :] = (back_two * slope).astype(BF16)
    weight_product(delta_two_ref, act_one_ref[...], keep_ref, send_ref, 0)


def backward_kernel(
    x_ref,
    act_two_ref,
    delta_two_ref,
    adj_ref,
    weights_ref,
    delta_one_ref,
    keep_ref,
    send_ref,
):
    fields = x_ref.shape[0]
    units = weights_ref.shape[0]
    x_now = x_ref[...]
    for start in range(0, units, BLOCK):
        back_one = lax.dot_general(
            weights_ref[:, start : start + BLOCK],
            delta_two_ref[...],
            CONTRACT_FIRST,
            preferred_element_type=F32,
        )
        pre_one = jnp.dot(weights_ref[start : start + BLOCK, units:], x_now, preferred_element_type=F32)
        sigma_val = sigmoid(pre_one)
        slope = sigma_val * (1.0 + pre_one * (1.0 - sigma_val))
        delta_one_ref[start : start + BLOCK, :] = (back_one * slope).astype(BF16)
    weight_product(delta_one_ref, x_now, keep_ref, send_ref, 0)
    weight_product(act_two_ref, join_tiles(adj_ref).astype(BF16), keep_ref, send_ref, fields)


def place_back(fresh, live, cols_ref, cells):
    marks = jnp.broadcast_to(live, (16, live.shape[1]))
    placed = lax.dot_general(
        jnp.concatenate([fresh * live, marks], axis=0).astype(BF16),
        one_hot(cols_ref, cells),
        CONTRACT_LAST,
        preferred_element_type=F32,
    )
    rows = fresh.shape[0]
    return placed[:rows], placed[rows : rows + 1] > 0.5


def state_kernel(
    count_ref,
    moved_ref,
    cols_ref,
    mask_ref,
    x_ref,
    act_two_ref,
    coef_ref,
    ratio_ref,
    inverse_ref,
    w_out_ref,
    state_ref,
    forced_ref,
    solved_ref,
    *,
    lons,
):
    fields = x_ref.shape[0]
    levels = coef_ref.shape[0]
    lats = moved_ref.shape[2]
    tendency = jnp.dot(w_out_ref[...], act_two_ref[...], preferred_element_type=F32)
    split_tiles(forced_ref, x_ref[...].astype(F32) + tendency)
    solve(levels, fields // levels, coef_ref, ratio_ref, inverse_ref, forced_ref, solved_ref)
    placed, taken = place_back(
        join_tiles(solved_ref), live_row(count_ref, mask_ref), cols_ref, lons * lats
    )
    for lon in range(lons):
        here = slice(lon * lats, (lon + 1) * lats)
        state_ref[pl.ds(lon, fields, stride=lons), :] = jnp.where(
            taken[:, here], placed[:, here], moved_ref[lon]
        )


def grad_kernel(
    count_ref,
    column_ref,
    cols_ref,
    mask_ref,
    delta_one_ref,
    adj_ref,
    weights_ref,
    field_ref,
    up_ref,
    down_ref,
    *,
    lons,
):
    fields, lats = field_ref.shape[1:]
    grad_x = join_tiles(adj_ref) + lax.dot_general(
        weights_ref[:, delta_one_ref.shape[0] :], delta_one_ref[...], CONTRACT_FIRST, preferred_element_type=F32
    )
    placed, taken = place_back(grad_x, live_row(count_ref, mask_ref), cols_ref, lons * lats)
    for lon in range(lons):
        here = slice(lon * lats, (lon + 1) * lats)
        field_now = jnp.where(
            taken[:, here], placed[:, here], column_ref[pl.ds(lon, fields, stride=lons), :]
        )
        field_ref[lon] = field_now
        if lon < 2:
            down_ref[lon * fields : (lon + 1) * fields, :] = field_now.astype(BF16)
        if lon >= lons - 2:
            side = lon - (lons - 2)
            up_ref[side * fields : (side + 1) * fields, :] = field_now.astype(BF16)


def last_kernel(field_ref, low_ref, high_ref, low_mix_ref, high_mix_ref, base_ref, out_ref, *, lons):
    fields = field_ref.shape[1]
    low_rows, high_rows = halo_rows(low_ref, fields), halo_rows(high_ref, fields)
    lon_coef, lat_coef = coefficients(
        base_ref, halo_mixing(low_mix_ref, fields), halo_mixing(high_mix_ref, fields), lons
    )
    rows = [field_ref[lon] for lon in range(lons)]
    rows = two_steps(low_rows + rows + high_rows, lon_coef, lat_coef)
    for lon in range(lons):
        out_ref[pl.ds(lon, fields, stride=lons), :] = rows[lon]


CORE = ("horiz", 0, 2)
NEAR, FAR = ("horiz", 1, 2), ("horiz", 2, 2)
CHIPS = ("horiz", 1, 4)
MEMBER_LOW, MEMBER_HIGH = ("ens", 0, 2), ("ens", 1, 2)
MEMBERS = ("ens", 0, 4)


def position(stage):
    axis, shift, parts = stage
    return lax.axis_index(axis) // (1 << shift) % parts


def sum_kernel(*refs, terms, stage, factor):
    ins, outs = refs[:terms], refs[terms:]
    rows = outs[0].shape[0]
    for k, out_ref in enumerate(outs):
        here = pl.ds(0, rows)
        if stage is not None:
            here = pl.ds(pl.multiple_of((position(stage) ^ k) * rows, rows), rows)
        total = ins[0][here, :].astype(F32)
        for ref in ins[1:]:
            total = total + ref[here, :].astype(F32)
        out_ref[...] = (total * factor).astype(BF16)


def join_kernel(*refs, stage, groups, cuts):
    ins, out_refs = refs[:-cuts], refs[-cuts:]
    count = len(ins) // groups
    rows, columns = ins[0].shape
    width = out_refs[0].shape[1]
    for k in range(count):
        here = pl.ds(pl.multiple_of((position(stage) ^ k) * rows, rows), rows)
        for group in range(groups):
            ref = ins[group * count + k]
            for start in range(0, columns, min(width, columns)):
                first = group * columns + start
                part = min(width, columns)
                out_refs[first // width][here, first % width : first % width + part] = ref[
                    :, start : start + part
                ]


def merge_kernel(*refs, terms, factor):
    out_ref = refs[-1]
    first = 0
    for group in (refs[:terms], refs[terms:-1]):
        total = group[0][...].astype(F32)
        for ref in group[1:]:
            total = total + ref[...].astype(F32)
        columns = total.shape[1]
        out_ref[:, first : first + columns] = (total * factor).astype(BF16)
        first += columns


def final_kernel(
    own_mid, got_mid, own_small, got_small, mid_ref, in_ref, out_ref, sorted_ref, *, order
):
    rows = own_mid.shape[0]
    fields = in_ref.shape[1]
    core = lax.axis_index("horiz") % 2
    block = rows // len(order)
    for mid_half, small_half, half in (
        (own_mid, own_small, core),
        (got_mid, got_small, 1 - core),
    ):
        here = pl.ds(pl.multiple_of(half * rows, rows), rows)
        mid_ref[here, :] = mid_half[...].astype(F32)

        @pl.when(pl.program_id(0) == 0)
        def _():
            for place, target in enumerate(order):
                sorted_ref[target * block : (target + 1) * block, :] = small_half[
                    place * block : (place + 1) * block, :
                ].astype(F32)
            in_ref[here, :] = sorted_ref[:, :fields]
            out_ref[:, here] = sorted_ref[:, fields:].T


def exchange(arrays, stage):
    axis, shift, _ = stage
    count = lax.axis_size(axis)
    return [
        lax.ppermute(array, axis, [(i, i ^ (k << shift)) for i in range(count)])
        for k, array in enumerate(arrays, 1)
    ]


def add(terms, stage, factor=1.0):
    rows, columns = terms[0].shape
    parts = 1 if stage is None else stage[2]
    return call(
        sum_kernel,
        [((rows // parts, columns), BF16)] * parts,
        terms=len(terms),
        stage=stage,
        factor=factor,
    )(*terms)


def join(groups, stage, outs=1):
    rows, columns = groups[0][0].shape
    shape = (rows * len(groups[0]), columns * len(groups) // outs)
    return call(
        join_kernel, [(shape, BF16)] * outs, stage=stage, groups=len(groups), cuts=outs
    )(*[piece for group in groups for piece in group])


def reduce_to(terms, stage):
    parts = add(terms, stage)
    return [parts[0]] + exchange(parts[1:], stage)


def collect_members(one, two):
    (low_one,) = exchange([one], MEMBER_LOW)
    (high_two,) = exchange([two], MEMBER_HIGH)
    (high_one,) = exchange([one], MEMBER_HIGH)
    (low_two,) = exchange([two], MEMBER_LOW)
    (far_one,) = exchange([low_one], MEMBER_HIGH)
    (far_two,) = exchange([high_two], MEMBER_LOW)
    return [one, low_one, high_one, far_one], [two, low_two, high_two, far_two]


def collect(piece, stage):
    return [piece] + exchange([piece] * (stage[2] - 1), stage)


def merge(terms_mid, terms_small, factor):
    rows = terms_mid[0].shape[0]
    columns = terms_mid[0].shape[1] + terms_small[0].shape[1]
    return call(
        merge_kernel, [((rows, columns), BF16)], terms=len(terms_mid), factor=factor
    )(*terms_mid, *terms_small)[0]


def tie(*values):
    return lax.optimization_barrier(values)


def over_all_chips(piece, factor):
    core = lax.axis_index("horiz") % 2
    both = jnp.stack([jnp.where(core == side, piece, 0.0).astype(F32) for side in range(2)])
    return (lax.psum(both, "horiz")[core] * factor).astype(BF16)


def to_neighbours(upward, downward, axis):
    count = lax.axis_size(axis)
    forward = [(i, (i + 1) % count) for i in range(count)]
    backward = [(target, source) for source, target in forward]
    return lax.ppermute(upward, axis, forward), lax.ppermute(downward, axis, backward)


def per_device(
    prognostic, diffusivity, mixing, cotangent, tile_cols, pad_mask, tile_count, w_in, w_mid, w_out
):
    fields, lons, lats = prognostic.shape[1:]
    levels = diffusivity.shape[1]
    units = w_mid.shape[0]
    tiles, width = tile_cols.shape[2:]
    slots = tiles * width
    base = jnp.concatenate([prognostic[0], mixing], axis=0).reshape((fields + 2) * lons, lats)
    column = jnp.concatenate([cotangent[0], diffusivity[0]], axis=0)
    column = column.reshape((fields + levels) * lons, lats)
    weights = jnp.concatenate([w_mid, w_in], axis=1)
    cols, mask = tile_cols[0, 0], pad_mask[0, 0]

    packed = ((2 * fields + PACK_ROWS, lats), BF16)
    up_pack, down_pack = call(pack_kernel, [packed, packed], lons=lons)(base)
    low_pack, high_pack = to_neighbours(up_pack, down_pack, "horiz")

    adjoint, coef, ratio, inverse = call(
        adjoint_kernel,
        [((tiles, fields, width), F32)] + [((levels, slots), F32)] * 3,
        scratch=[pltpu.VMEM((tiles, fields, width), F32)],
        smem=(0,),
        moved=30 * 10**6,
        lons=lons,
    )(tile_count, column, cols, mask)

    hidden = ((units, slots), BF16)
    half = ((units // 2, units), BF16)
    moved, x_now, act_one, act_two, delta_two, keep_mid, send_mid = call(
        forward_kernel,
        [((lons, fields, lats), F32), ((fields, slots), BF16), hidden, hidden, hidden, half, half],
        moved=15 * 10**6,
        lons=lons,
    )(base, low_pack, high_pack, cols, adjoint, weights, w_out)
    column_total = lax.axis_size("ens") * lax.axis_size("horiz") * lons * lats
    factor = 1.0 / math.sqrt(column_total)
    (got_mid,) = exchange([send_mid], CORE)

    half = ((units // 2, 2 * fields), BF16)
    delta_one, keep_small, send_small = call(
        backward_kernel, [hidden, half, half], moved=4 * 10**6
    )(x_now, act_two, delta_two, adjoint, weights)
    got_mid, keep_small = tie(got_mid, keep_small)
    parts_mid = add([keep_mid, got_mid], MEMBERS)
    terms_mid = [parts_mid[0]] + exchange(parts_mid[1:], MEMBERS)
    (got_small,) = exchange([send_small], CORE)
    keep_small, delta_one = tie(keep_small, delta_one, parts_mid)[:2]

    def new_state(act_two):
        return call(
            state_kernel,
            [((fields * lons, lats), F32)],
            scratch=[pltpu.VMEM((tiles, fields, width), F32)] * 2,
            smem=(0,),
            lons=lons,
        )(tile_count, moved, cols, mask, x_now, act_two, coef, ratio, inverse, w_out)[0]

    def new_field(delta_one):
        packed = ((2 * fields, lats), BF16)
        return call(
            grad_kernel,
            [((lons, fields, lats), F32), packed, packed],
            smem=(0,),
            lons=lons,
        )(tile_count, column, cols, mask, delta_one, adjoint, weights)

    def finish(field, halos):
        return call(last_kernel, [((fields * lons, lats), F32)], lons=lons)(
            field, *halos, low_pack, high_pack, base
        )[0]

    fast = lax.axis_size("ens") == 4 and lax.axis_size("horiz") == 8
    if fast:
        terms_small = reduce_to([keep_small, got_small], NEAR)
        field, up_rows, down_rows = new_field(delta_one)
        halos = to_neighbours(up_rows, down_rows, "horiz")
        terms_small = reduce_to(terms_small, FAR)
        terms_mid, terms_small, field, halos = tie(terms_mid, terms_small, field, halos)

        terms_mid = reduce_to(terms_mid, CHIPS)
        terms_small = reduce_to(terms_small, MEMBER_HIGH)
        terms_small = reduce_to(terms_small, MEMBER_LOW)
        terms_mid, terms_small = tie(terms_mid, terms_small)

        piece = merge(terms_mid, terms_small, factor)
        pieces = collect(piece, CHIPS)
        halves, act_two = tie(join([pieces], CHIPS, outs=2), act_two)
        groups = collect_members(*halves)
        grad_rows = finish(field, halos)
        state_rows = new_state(act_two)
    else:
        state_rows = new_state(act_two)
        field, up_rows, down_rows = new_field(delta_one)
        grad_rows = finish(field, to_neighbours(up_rows, down_rows, "horiz"))
        terms_small = reduce_to([keep_small, got_small], MEMBERS)
        groups = [collect(over_all_chips(merge(terms_mid, terms_small, 1.0), factor), MEMBERS)]
    groups, grad_rows, state_rows = tie(groups, grad_rows, state_rows)
    (own,) = join(groups, MEMBERS)
    (got,) = exchange([own], CORE)
    order = [0]
    if fast:
        order = [
            (chip % 2 * 2 + chip // 2) * 4 + member for member in range(4) for chip in range(4)
        ]
    block = units // 4
    mid_half = pl.BlockSpec((units // 2, block), lambda step: (0, step))
    small_half = pl.BlockSpec((units // 2, 2 * fields), lambda step: (0, units // (2 * fields)))
    grad_mid, grad_in, grad_out = pl.pallas_call(
        functools.partial(final_kernel, order=order),
        grid=(units // block,),
        out_shape=[
            jax.ShapeDtypeStruct(shape, F32)
            for shape in ((units, units), (units, fields), (fields, units))
        ],
        in_specs=[mid_half, mid_half, small_half, small_half],
        out_specs=[
            pl.BlockSpec((units, block), lambda step: (0, step)),
            pl.BlockSpec((units, fields), lambda step: (0, 0)),
            pl.BlockSpec((fields, units), lambda step: (0, 0)),
        ],
        scratch_shapes=[pltpu.VMEM((units // 2, 2 * fields), F32)],
        compiler_params=pltpu.CompilerParams(vmem_limit_bytes=VMEM_LIMIT),
    )(own, got, own, got)
    return (
        state_rows.reshape(prognostic.shape),
        grad_rows.reshape(prognostic.shape),
        grad_in,
        grad_mid,
        grad_out,
    )


def solution(mesh):
    placed = (
        P("ens", None, "horiz", None),
        P("ens", None, "horiz", None),
        P(None, "horiz", None),
        P("ens", None, "horiz", None),
        P("ens", "horiz", None, None),
        P("ens", "horiz", None, None),
        P("ens", "horiz"),
        P(),
        P(),
        P(),
    )
    return jax.shard_map(
        per_device,
        mesh=mesh,
        in_specs=placed,
        out_specs=(P("ens", None, "horiz", None), P("ens", None, "horiz", None), P(), P(), P()),
        check_vma=False,
    )
```

```python
import functools
import math

import jax
import jax.numpy as jnp
from jax import lax
from jax.experimental import pallas as pl
from jax.experimental.pallas import tpu as pltpu
from jax.sharding import PartitionSpec as P

DYN_STEPS = 2
BLOCK = 256
PACK_ROWS = 16
VMEM_LIMIT = 32 * 1024 * 1024
F32 = jnp.float32
BF16 = jnp.bfloat16
CONTRACT_LAST = (((1,), (1,)), ((), ()))
CONTRACT_FIRST = (((0,), (0,)), ((), ()))


def call(kernel, outs, scratch=(), smem=(), flops=0, moved=0, **names):
    def run(*operands):
        specs = [
            pl.BlockSpec(memory_space=pltpu.SMEM if place in smem else pltpu.VMEM)
            for place in range(len(operands))
        ]
        return pl.pallas_call(
            functools.partial(kernel, **names),
            out_shape=[jax.ShapeDtypeStruct(shape, dtype) for shape, dtype in outs],
            in_specs=specs,
            out_specs=[pl.BlockSpec(memory_space=pltpu.VMEM)] * len(outs),
            scratch_shapes=list(scratch),
            compiler_params=pltpu.CompilerParams(vmem_limit_bytes=VMEM_LIMIT),
            cost_estimate=pl.CostEstimate(flops=flops, bytes_accessed=moved, transcendentals=0),
        )(*operands)

    return run


def lat_term(field_now, coef_masked):
    lats = field_now.shape[1]
    north_flux = coef_masked * (pltpu.roll(field_now, lats - 1, 1) - field_now)
    return north_flux - pltpu.roll(north_flux, 1, 1)


def two_steps(rows, lon_coef, lat_coef):
    for repeat in range(DYN_STEPS):
        count = len(rows)
        fluxes = [
            lon_coef[place + repeat] * (rows[place + 1] - rows[place]) for place in range(count - 1)
        ]
        rows = [
            rows[place]
            + fluxes[place]
            - fluxes[place - 1]
            + lat_term(rows[place], lat_coef[place + repeat])
            for place in range(1, count - 1)
        ]
    return rows


def coefficients(base_ref, low_mix, high_mix, lons):
    lats = base_ref.shape[1]
    first = base_ref.shape[0] - 2 * lons
    lane = lax.broadcasted_iota(jnp.int32, (1, lats), 1)
    inside = lane < lats - 1
    own_lon = [base_ref[first + lon : first + lon + 1, :] for lon in range(lons)]
    first += lons
    own_lat = [base_ref[first + lon : first + lon + 1, :] for lon in range(lons)]
    lon_coef = [low_mix[0:1, :], low_mix[1:2, :]] + own_lon + [high_mix[0:1, :], high_mix[1:2, :]]
    lat_coef = [low_mix[2:3, :], low_mix[3:4, :]] + own_lat + [high_mix[2:3, :], high_mix[3:4, :]]
    return lon_coef, [jnp.where(inside, coef, 0.0) for coef in lat_coef]


def pack_kernel(base_ref, up_ref, down_ref, *, lons):
    fields = base_ref.shape[0] // lons - 2
    mixing = fields * lons
    for out_ref, first in ((up_ref, lons - 2), (down_ref, 0)):
        for side in range(2):
            out_ref[side * fields : (side + 1) * fields, :] = base_ref[
                pl.ds(first + side, fields, stride=lons), :
            ].astype(BF16)
        mix_rows = [
            base_ref[mixing + first : mixing + first + 2, :],
            base_ref[mixing + lons + first : mixing + lons + first + 2, :],
            jnp.zeros((PACK_ROWS - 4, base_ref.shape[1]), F32),
        ]
        out_ref[2 * fields :, :] = jnp.concatenate(mix_rows, axis=0).astype(BF16)


def halo_rows(pack_ref, fields):
    return [pack_ref[side * fields : (side + 1) * fields, :].astype(F32) for side in range(2)]


def halo_mixing(pack_ref, fields):
    return pack_ref[2 * fields :, :].astype(F32)


def one_hot(cols_ref, cells):
    parts = []
    for tile in range(cols_ref.shape[0]):
        place = lax.broadcasted_iota(jnp.int32, (cells, cols_ref.shape[1]), 0)
        parts.append(jnp.where(place == cols_ref[tile : tile + 1, :], 1.0, 0.0))
    return jnp.concatenate(parts, axis=1).astype(BF16)


def live_row(count_ref, mask_ref):
    parts = []
    for tile in range(mask_ref.shape[0]):
        used = jnp.where(tile < count_ref[0, 0], 1, 0)
        parts.append((mask_ref[tile : tile + 1, :] * used).astype(F32))
    return jnp.concatenate(parts, axis=1)


def level_rows(levels, level, variables):
    return pl.ds(level, variables, stride=levels)


def solve(levels, variables, coef_ref, ratio_ref, inverse_ref, right_ref, out_ref):
    tiles, _, width = right_ref.shape
    spans = [slice(tile * width, (tile + 1) * width) for tile in range(tiles)]
    values = []
    for level in range(levels):
        inverse_now = inverse_ref[level : level + 1, :]
        if level > 0:
            carry_now = coef_ref[level - 1 : level, :] * inverse_now
        step = []
        for tile, span in enumerate(spans):
            right_now = right_ref[tile, level_rows(levels, level, variables), :]
            value_now = right_now * inverse_now[:, span]
            if level > 0:
                value_now = value_now + carry_now[:, span] * values[-1][tile]
            step.append(value_now)
        values.append(step)
    results = values[-1]
    for level in range(levels - 1, -1, -1):
        if level < levels - 1:
            ratio_now = ratio_ref[level : level + 1, :]
            results = [
                values[level][tile] - ratio_now[:, span] * results[tile]
                for tile, span in enumerate(spans)
            ]
        for tile in range(tiles):
            out_ref[tile, level_rows(levels, level, variables), :] = results[tile]


def split_tiles(ref, value):
    width = ref.shape[2]
    for tile in range(ref.shape[0]):
        ref[tile] = value[:, tile * width : (tile + 1) * width]


def join_tiles(ref):
    return jnp.concatenate([ref[tile] for tile in range(ref.shape[0])], axis=1)


def factorise(levels, coef_ref, ratio_ref, inverse_ref):
    ratio_prev = None
    for level in range(levels):
        coef_now = coef_ref[level : level + 1, :]
        divisor = 1.0 + coef_now
        if level > 0:
            below_now = coef_ref[level - 1 : level, :]
            divisor = divisor + below_now + below_now * ratio_prev
        inverse_now = 1.0 / divisor
        ratio_prev = -coef_now * inverse_now
        inverse_ref[level : level + 1, :] = inverse_now
        ratio_ref[level : level + 1, :] = ratio_prev


def by_cell(ref, rows, lons):
    return jnp.concatenate(
        [ref[pl.ds(lon, rows, stride=lons), :] for lon in range(lons)], axis=1
    )


def adjoint_kernel(
    count_ref,
    column_ref,
    cols_ref,
    mask_ref,
    adj_ref,
    coef_ref,
    ratio_ref,
    inverse_ref,
    right_ref,
    *,
    lons,
):
    fields = adj_ref.shape[1]
    levels = coef_ref.shape[0]
    spread = one_hot(cols_ref, lons * column_ref.shape[1])
    sources = by_cell(column_ref, fields + levels, lons).astype(BF16)
    picked = jnp.dot(sources, spread, preferred_element_type=F32)
    split_tiles(right_ref, picked[:fields] * live_row(count_ref, mask_ref))
    coef_ref[...] = picked[fields:]
    factorise(levels, coef_ref, ratio_ref, inverse_ref)
    solve(levels, fields // levels, coef_ref, ratio_ref, inverse_ref, right_ref, adj_ref)


def sigmoid(pre_act):
    return 0.5 * jnp.tanh(0.5 * pre_act) + 0.5


def weight_product(left_ref, right, keep_ref, send_ref, first):
    half = left_ref.shape[0] // 2
    block = min(BLOCK, half)
    core = lax.axis_index("horiz") % 2
    for out_ref, side in ((send_ref, 1 - core), (keep_ref, core)):
        for start in range(0, half, block):
            out_ref[start : start + block, first : first + right.shape[0]] = lax.dot_general(
                left_ref[pl.ds(pl.multiple_of(side * half + start, block), block), :],
                right,
                CONTRACT_LAST,
                preferred_element_type=F32,
            ).astype(BF16)


def forward_kernel(
    base_ref,
    low_ref,
    high_ref,
    cols_ref,
    adj_ref,
    weights_ref,
    w_out_ref,
    moved_ref,
    x_ref,
    act_one_ref,
    act_two_ref,
    delta_two_ref,
    keep_ref,
    send_ref,
    *,
    lons,
):
    fields = x_ref.shape[0]
    units = weights_ref.shape[0]
    cells = lons * base_ref.shape[1]
    low_rows, high_rows = halo_rows(low_ref, fields), halo_rows(high_ref, fields)
    lon_coef, lat_coef = coefficients(
        base_ref, halo_mixing(low_ref, fields), halo_mixing(high_ref, fields), lons
    )
    rows = [base_ref[pl.ds(lon, fields, stride=lons), :] for lon in range(lons)]
    rows = two_steps(low_rows + rows + high_rows, lon_coef, lat_coef)
    for lon in range(lons):
        moved_ref[lon] = rows[lon]
    spread = one_hot(cols_ref, cells)
    sources = jnp.concatenate(rows, axis=1).astype(BF16)
    x_now = jnp.dot(sources, spread, preferred_element_type=F32).astype(BF16)
    x_ref[...] = x_now
    for start in range(0, units, BLOCK):
        pre_one = jnp.dot(weights_ref[start : start + BLOCK, units:], x_now, preferred_element_type=F32)
        act_one_ref[start : start + BLOCK, :] = (pre_one * sigmoid(pre_one)).astype(BF16)
    adj_half = join_tiles(adj_ref).astype(BF16)
    for start in range(0, units, BLOCK):
        pre_two = jnp.dot(
            weights_ref[start : start + BLOCK, :units], act_one_ref[...], preferred_element_type=F32
        )
        sigma_val = sigmoid(pre_two)
        act_two_ref[start : start + BLOCK, :] = (pre_two * sigma_val).astype(BF16)
        back_two = lax.dot_general(
            w_out_ref[:, start : start + BLOCK],
            adj_half,
            CONTRACT_FIRST,
            preferred_element_type=F32,
        )
        slope = sigma_val * (1.0 + pre_two * (1.0 - sigma_val))
        delta_two_ref[start : start + BLOCK, :] = (back_two * slope).astype(BF16)
    weight_product(delta_two_ref, act_one_ref[...], keep_ref, send_ref, 0)


def backward_kernel(
    x_ref,
    act_two_ref,
    delta_two_ref,
    adj_ref,
    weights_ref,
    delta_one_ref,
    keep_ref,
    send_ref,
):
    fields = x_ref.shape[0]
    units = weights_ref.shape[0]
    x_now = x_ref[...]
    for start in range(0, units, BLOCK):
        back_one = lax.dot_general(
            weights_ref[:, start : start + BLOCK],
            delta_two_ref[...],
            CONTRACT_FIRST,
            preferred_element_type=F32,
        )
        pre_one = jnp.dot(weights_ref[start : start + BLOCK, units:], x_now, preferred_element_type=F32)
        sigma_val = sigmoid(pre_one)
        slope = sigma_val * (1.0 + pre_one * (1.0 - sigma_val))
        delta_one_ref[start : start + BLOCK, :] = (back_one * slope).astype(BF16)
    weight_product(delta_one_ref, x_now, keep_ref, send_ref, 0)
    weight_product(act_two_ref, join_tiles(adj_ref).astype(BF16), keep_ref, send_ref, fields)


def place_back(fresh, live, cols_ref, cells):
    marks = jnp.broadcast_to(live, (16, live.shape[1]))
    placed = lax.dot_general(
        jnp.concatenate([fresh * live, marks], axis=0).astype(BF16),
        one_hot(cols_ref, cells),
        CONTRACT_LAST,
        preferred_element_type=F32,
    )
    rows = fresh.shape[0]
    return placed[:rows], placed[rows : rows + 1] > 0.5


def state_kernel(
    count_ref,
    moved_ref,
    cols_ref,
    mask_ref,
    x_ref,
    act_two_ref,
    coef_ref,
    ratio_ref,
    inverse_ref,
    w_out_ref,
    state_ref,
    forced_ref,
    solved_ref,
    *,
    lons,
):
    fields = x_ref.shape[0]
    levels = coef_ref.shape[0]
    lats = moved_ref.shape[2]
    tendency = jnp.dot(w_out_ref[...], act_two_ref[...], preferred_element_type=F32)
    split_tiles(forced_ref, x_ref[...].astype(F32) + tendency)
    solve(levels, fields // levels, coef_ref, ratio_ref, inverse_ref, forced_ref, solved_ref)
    placed, taken = place_back(
        join_tiles(solved_ref), live_row(count_ref, mask_ref), cols_ref, lons * lats
    )
    for lon in range(lons):
        here = slice(lon * lats, (lon + 1) * lats)
        state_ref[pl.ds(lon, fields, stride=lons), :] = jnp.where(
            taken[:, here], placed[:, here], moved_ref[lon]
        )


def grad_kernel(
    count_ref,
    column_ref,
    cols_ref,
    mask_ref,
    delta_one_ref,
    adj_ref,
    weights_ref,
    field_ref,
    up_ref,
    down_ref,
    *,
    lons,
):
    fields, lats = field_ref.shape[1:]
    grad_x = join_tiles(adj_ref) + lax.dot_general(
        weights_ref[:, delta_one_ref.shape[0] :], delta_one_ref[...], CONTRACT_FIRST, preferred_element_type=F32
    )
    placed, taken = place_back(grad_x, live_row(count_ref, mask_ref), cols_ref, lons * lats)
    for lon in range(lons):
        here = slice(lon * lats, (lon + 1) * lats)
        field_now = jnp.where(
            taken[:, here], placed[:, here], column_ref[pl.ds(lon, fields, stride=lons), :]
        )
        field_ref[lon] = field_now
        if lon < 2:
            down_ref[lon * fields : (lon + 1) * fields, :] = field_now.astype(BF16)
        if lon >= lons - 2:
            side = lon - (lons - 2)
            up_ref[side * fields : (side + 1) * fields, :] = field_now.astype(BF16)


def last_kernel(field_ref, low_ref, high_ref, low_mix_ref, high_mix_ref, base_ref, out_ref, *, lons):
    fields = field_ref.shape[1]
    low_rows, high_rows = halo_rows(low_ref, fields), halo_rows(high_ref, fields)
    lon_coef, lat_coef = coefficients(
        base_ref, halo_mixing(low_mix_ref, fields), halo_mixing(high_mix_ref, fields), lons
    )
    rows = [field_ref[lon] for lon in range(lons)]
    rows = two_steps(low_rows + rows + high_rows, lon_coef, lat_coef)
    for lon in range(lons):
        out_ref[pl.ds(lon, fields, stride=lons), :] = rows[lon]


CORE = ("horiz", 0, 2)
NEAR, FAR = ("horiz", 1, 2), ("horiz", 2, 2)
CHIPS = ("horiz", 1, 4)
MEMBER_LOW, MEMBER_HIGH = ("ens", 0, 2), ("ens", 1, 2)
MEMBERS = ("ens", 0, 4)


def position(stage):
    axis, shift, parts = stage
    return lax.axis_index(axis) // (1 << shift) % parts


def sum_kernel(*refs, terms, stage, factor):
    ins, outs = refs[:terms], refs[terms:]
    rows = outs[0].shape[0]
    for k, out_ref in enumerate(outs):
        here = pl.ds(0, rows)
        if stage is not None:
            here = pl.ds(pl.multiple_of((position(stage) ^ k) * rows, rows), rows)
        total = ins[0][here, :].astype(F32)
        for ref in ins[1:]:
            total = total + ref[here, :].astype(F32)
        out_ref[...] = (total * factor).astype(BF16)


def join_kernel(*refs, stage, groups, cuts):
    ins, out_refs = refs[:-cuts], refs[-cuts:]
    count = len(ins) // groups
    rows, columns = ins[0].shape
    width = out_refs[0].shape[1]
    for k in range(count):
        here = pl.ds(pl.multiple_of((position(stage) ^ k) * rows, rows), rows)
        for group in range(groups):
            ref = ins[group * count + k]
            for start in range(0, columns, min(width, columns)):
                first = group * columns + start
                part = min(width, columns)
                out_refs[first // width][here, first % width : first % width + part] = ref[
                    :, start : start + part
                ]


def core_sum_kernel(keep_mid, got_mid, keep_small, got_small, *outs, stage):
    rows = outs[0].shape[0]
    for k, out_ref in enumerate(outs):
        here = pl.ds(pl.multiple_of((position(stage) ^ k) * rows, rows), rows)
        first = 0
        for keep_ref, got_ref in ((keep_mid, got_mid), (keep_small, got_small)):
            columns = keep_ref.shape[1]
            out_ref[:, first : first + columns] = (
                keep_ref[here, :].astype(F32) + got_ref[here, :].astype(F32)
            ).astype(BF16)
            first += columns


def final_kernel(mid_half, small_half, *refs):
    mid_ref, in_ref, out_ref = refs[-3:]
    fields = in_ref.shape[1]
    mid_ref[...] = mid_half[...].astype(F32)

    @pl.when(pl.program_id(0) == 0)
    def _():
        in_ref[...] = small_half[:, :fields].astype(F32)
        out_ref[...] = small_half[:, fields:].astype(F32).T


def final(rows, other, before, fields):
    half, columns = rows.shape
    units = 2 * half
    block = units // 4

    def place():
        core = lax.axis_index("horiz") % 2
        return 1 - core if other else core

    return pl.pallas_call(
        final_kernel,
        grid=(units // block,),
        out_shape=[
            jax.ShapeDtypeStruct(shape, F32)
            for shape in ((units, units), (units, fields), (fields, units))
        ],
        in_specs=[
            pl.BlockSpec((half, block), lambda step: (0, step)),
            pl.BlockSpec((half, 2 * fields), lambda step: (0, units // (2 * fields))),
        ]
        + [pl.BlockSpec(memory_space=pl.ANY)] * len(before),
        out_specs=[
            pl.BlockSpec((half, block), lambda step: (place(), step)),
            pl.BlockSpec((half, fields), lambda step: (place(), 0)),
            pl.BlockSpec((fields, half), lambda step: (0, place())),
        ],
        input_output_aliases={2 + index: index for index in range(len(before))},
        compiler_params=pltpu.CompilerParams(vmem_limit_bytes=VMEM_LIMIT),
    )(rows, rows, *before)


def exchange(arrays, stage):
    axis, shift, _ = stage
    count = lax.axis_size(axis)
    return [
        lax.ppermute(array, axis, [(i, i ^ (k << shift)) for i in range(count)])
        for k, array in enumerate(arrays, 1)
    ]


def add(terms, stage, factor=1.0):
    rows, columns = terms[0].shape
    parts = 1 if stage is None else stage[2]
    return call(
        sum_kernel,
        [((rows // parts, columns), BF16)] * parts,
        terms=len(terms),
        stage=stage,
        factor=factor,
    )(*terms)


def join(groups, stage, outs=1):
    rows, columns = groups[0][0].shape
    shape = (rows * len(groups[0]), columns * len(groups) // outs)
    return call(
        join_kernel, [(shape, BF16)] * outs, stage=stage, groups=len(groups), cuts=outs
    )(*[piece for group in groups for piece in group])


def reduce_to(terms, stage):
    parts = add(terms, stage)
    return [parts[0]] + exchange(parts[1:], stage)


def collect_members(one, two):
    (low_one,) = exchange([one], MEMBER_LOW)
    (high_two,) = exchange([two], MEMBER_HIGH)
    (high_one,) = exchange([one], MEMBER_HIGH)
    (low_two,) = exchange([two], MEMBER_LOW)
    (far_one,) = exchange([low_one], MEMBER_HIGH)
    (far_two,) = exchange([high_two], MEMBER_LOW)
    return [one, low_one, high_one, far_one], [two, low_two, high_two, far_two]


def collect(piece, stage):
    return [piece] + exchange([piece] * (stage[2] - 1), stage)


def tie(*values):
    return lax.optimization_barrier(values)


def over_all_chips(piece, factor):
    core = lax.axis_index("horiz") % 2
    both = jnp.stack([jnp.where(core == side, piece, 0.0).astype(F32) for side in range(2)])
    return (lax.psum(both, "horiz")[core] * factor).astype(BF16)


def to_neighbours(upward, downward, axis):
    count = lax.axis_size(axis)
    forward = [(i, (i + 1) % count) for i in range(count)]
    backward = [(target, source) for source, target in forward]
    return lax.ppermute(upward, axis, forward), lax.ppermute(downward, axis, backward)


def per_device(
    prognostic, diffusivity, mixing, cotangent, tile_cols, pad_mask, tile_count, w_in, w_mid, w_out
):
    fields, lons, lats = prognostic.shape[1:]
    levels = diffusivity.shape[1]
    units = w_mid.shape[0]
    tiles, width = tile_cols.shape[2:]
    slots = tiles * width
    base = jnp.concatenate([prognostic[0], mixing], axis=0).reshape((fields + 2) * lons, lats)
    column = jnp.concatenate([cotangent[0], diffusivity[0]], axis=0)
    column = column.reshape((fields + levels) * lons, lats)
    weights = jnp.concatenate([w_mid, w_in], axis=1)
    cols, mask = tile_cols[0, 0], pad_mask[0, 0]

    packed = ((2 * fields + PACK_ROWS, lats), BF16)
    up_pack, down_pack = call(pack_kernel, [packed, packed], lons=lons)(base)
    low_pack, high_pack = to_neighbours(up_pack, down_pack, "horiz")

    adjoint, coef, ratio, inverse = call(
        adjoint_kernel,
        [((tiles, fields, width), F32)] + [((levels, slots), F32)] * 3,
        scratch=[pltpu.VMEM((tiles, fields, width), F32)],
        smem=(0,),
        moved=30 * 10**6,
        lons=lons,
    )(tile_count, column, cols, mask)

    hidden = ((units, slots), BF16)
    half = ((units // 2, units), BF16)
    moved, x_now, act_one, act_two, delta_two, keep_mid, send_mid = call(
        forward_kernel,
        [((lons, fields, lats), F32), ((fields, slots), BF16), hidden, hidden, hidden, half, half],
        moved=15 * 10**6,
        lons=lons,
    )(base, low_pack, high_pack, cols, adjoint, weights, w_out)
    column_total = lax.axis_size("ens") * lax.axis_size("horiz") * lons * lats
    factor = 1.0 / math.sqrt(column_total)
    (got_mid,) = exchange([send_mid], CORE)

    half = ((units // 2, 2 * fields), BF16)
    delta_one, keep_small, send_small = call(
        backward_kernel, [hidden, half, half], moved=4 * 10**6
    )(x_now, act_two, delta_two, adjoint, weights)
    (got_small,) = exchange([send_small], CORE)

    packed = ((2 * fields, lats), BF16)
    field, up_rows, down_rows = call(
        grad_kernel,
        [((lons, fields, lats), F32), packed, packed],
        smem=(0,),
        lons=lons,
    )(tile_count, column, cols, mask, delta_one, adjoint, weights)
    got_small, field = tie(got_small, field)

    parts = call(
        core_sum_kernel,
        [((units // 2 // MEMBERS[2], units + 2 * fields), BF16)] * MEMBERS[2],
        stage=MEMBERS,
    )(keep_mid, got_mid, keep_small, got_small)
    terms = [parts[0]] + exchange(parts[1:], MEMBERS)
    act_two, up_rows, down_rows = tie(act_two, up_rows, down_rows, parts)[:3]
    halos = to_neighbours(up_rows, down_rows, "horiz")
    (state_rows,) = call(
        state_kernel,
        [((fields * lons, lats), F32)],
        scratch=[pltpu.VMEM((tiles, fields, width), F32)] * 2,
        smem=(0,),
        lons=lons,
    )(tile_count, moved, cols, mask, x_now, act_two, coef, ratio, inverse, w_out)
    (grad_rows,) = call(last_kernel, [((fields * lons, lats), F32)], lons=lons)(
        field, *halos, low_pack, high_pack, base
    )
    terms, state_rows, grad_rows = tie(terms, state_rows, grad_rows)

    if lax.axis_size("horiz") == 8:
        terms = reduce_to(terms, CHIPS)
        pieces = collect(add(terms, None, factor)[0], CHIPS)
        groups = collect_members(*join([pieces], CHIPS, outs=2))
    else:
        groups = [collect(over_all_chips(add(terms, None)[0], factor), MEMBERS)]
    (own,) = join(groups, MEMBERS)
    (got,) = exchange([own], CORE)
    half_done = final(own, False, [], fields)
    grad_mid, grad_in, grad_out = final(got, True, half_done, fields)
    return (
        state_rows.reshape(prognostic.shape),
        grad_rows.reshape(prognostic.shape),
        grad_in,
        grad_mid,
        grad_out,
    )


def solution(mesh):
    placed = (
        P("ens", None, "horiz", None),
        P("ens", None, "horiz", None),
        P(None, "horiz", None),
        P("ens", None, "horiz", None),
        P("ens", "horiz", None, None),
        P("ens", "horiz", None, None),
        P("ens", "horiz"),
        P(),
        P(),
        P(),
    )
    return jax.shard_map(
        per_device,
        mesh=mesh,
        in_specs=placed,
        out_specs=(P("ens", None, "horiz", None), P("ens", None, "horiz", None), P(), P(), P()),
        check_vma=False,
    )
```

```python
import functools
import math

import jax
import jax.numpy as jnp
from jax import lax
from jax.experimental import pallas as pl
from jax.experimental.pallas import tpu as pltpu
from jax.sharding import PartitionSpec as P

DYN_STEPS = 2
BLOCK = 256
PACK_ROWS = 16
VMEM_LIMIT = 32 * 1024 * 1024
F32 = jnp.float32
BF16 = jnp.bfloat16
CONTRACT_LAST = (((1,), (1,)), ((), ()))
CONTRACT_FIRST = (((0,), (0,)), ((), ()))


def call(kernel, outs, scratch=(), smem=(), flops=0, moved=0, **names):
    def run(*operands):
        specs = [
            pl.BlockSpec(memory_space=pltpu.SMEM if place in smem else pltpu.VMEM)
            for place in range(len(operands))
        ]
        return pl.pallas_call(
            functools.partial(kernel, **names),
            out_shape=[jax.ShapeDtypeStruct(shape, dtype) for shape, dtype in outs],
            in_specs=specs,
            out_specs=[pl.BlockSpec(memory_space=pltpu.VMEM)] * len(outs),
            scratch_shapes=list(scratch),
            compiler_params=pltpu.CompilerParams(vmem_limit_bytes=VMEM_LIMIT),
            cost_estimate=pl.CostEstimate(flops=flops, bytes_accessed=moved, transcendentals=0),
        )(*operands)

    return run


def lat_term(field_now, coef_masked):
    lats = field_now.shape[1]
    north_flux = coef_masked * (pltpu.roll(field_now, lats - 1, 1) - field_now)
    return north_flux - pltpu.roll(north_flux, 1, 1)


def two_steps(rows, lon_coef, lat_coef):
    for repeat in range(DYN_STEPS):
        count = len(rows)
        fluxes = [
            lon_coef[place + repeat] * (rows[place + 1] - rows[place]) for place in range(count - 1)
        ]
        rows = [
            rows[place]
            + fluxes[place]
            - fluxes[place - 1]
            + lat_term(rows[place], lat_coef[place + repeat])
            for place in range(1, count - 1)
        ]
    return rows


def coefficients(base_ref, low_mix, high_mix, lons):
    lats = base_ref.shape[1]
    first = base_ref.shape[0] - 2 * lons
    lane = lax.broadcasted_iota(jnp.int32, (1, lats), 1)
    inside = lane < lats - 1
    own_lon = [base_ref[first + lon : first + lon + 1, :] for lon in range(lons)]
    first += lons
    own_lat = [base_ref[first + lon : first + lon + 1, :] for lon in range(lons)]
    lon_coef = [low_mix[0:1, :], low_mix[1:2, :]] + own_lon + [high_mix[0:1, :], high_mix[1:2, :]]
    lat_coef = [low_mix[2:3, :], low_mix[3:4, :]] + own_lat + [high_mix[2:3, :], high_mix[3:4, :]]
    return lon_coef, [jnp.where(inside, coef, 0.0) for coef in lat_coef]


def pack_kernel(base_ref, up_ref, down_ref, *, lons):
    fields = base_ref.shape[0] // lons - 2
    mixing = fields * lons
    for out_ref, first in ((up_ref, lons - 2), (down_ref, 0)):
        for side in range(2):
            out_ref[side * fields : (side + 1) * fields, :] = base_ref[
                pl.ds(first + side, fields, stride=lons), :
            ].astype(BF16)
        mix_rows = [
            base_ref[mixing + first : mixing + first + 2, :],
            base_ref[mixing + lons + first : mixing + lons + first + 2, :],
            jnp.zeros((PACK_ROWS - 4, base_ref.shape[1]), F32),
        ]
        out_ref[2 * fields :, :] = jnp.concatenate(mix_rows, axis=0).astype(BF16)


def halo_rows(pack_ref, fields):
    return [pack_ref[side * fields : (side + 1) * fields, :].astype(F32) for side in range(2)]


def halo_mixing(pack_ref, fields):
    return pack_ref[2 * fields :, :].astype(F32)


def one_hot(cols_ref, cells):
    parts = []
    for tile in range(cols_ref.shape[0]):
        place = lax.broadcasted_iota(jnp.int32, (cells, cols_ref.shape[1]), 0)
        parts.append(jnp.where(place == cols_ref[tile : tile + 1, :], 1.0, 0.0))
    return jnp.concatenate(parts, axis=1).astype(BF16)


def live_row(count_ref, mask_ref):
    parts = []
    for tile in range(mask_ref.shape[0]):
        used = jnp.where(tile < count_ref[0, 0], 1, 0)
        parts.append((mask_ref[tile : tile + 1, :] * used).astype(F32))
    return jnp.concatenate(parts, axis=1)


def level_rows(levels, level, variables):
    return pl.ds(level, variables, stride=levels)


def solve(levels, variables, coef_ref, ratio_ref, inverse_ref, right_ref, out_ref):
    tiles, _, width = right_ref.shape
    spans = [slice(tile * width, (tile + 1) * width) for tile in range(tiles)]
    values = []
    for level in range(levels):
        inverse_now = inverse_ref[level : level + 1, :]
        if level > 0:
            carry_now = coef_ref[level - 1 : level, :] * inverse_now
        step = []
        for tile, span in enumerate(spans):
            right_now = right_ref[tile, level_rows(levels, level, variables), :]
            value_now = right_now * inverse_now[:, span]
            if level > 0:
                value_now = value_now + carry_now[:, span] * values[-1][tile]
            step.append(value_now)
        values.append(step)
    results = values[-1]
    for level in range(levels - 1, -1, -1):
        if level < levels - 1:
            ratio_now = ratio_ref[level : level + 1, :]
            results = [
                values[level][tile] - ratio_now[:, span] * results[tile]
                for tile, span in enumerate(spans)
            ]
        for tile in range(tiles):
            out_ref[tile, level_rows(levels, level, variables), :] = results[tile]


def split_tiles(ref, value):
    width = ref.shape[2]
    for tile in range(ref.shape[0]):
        ref[tile] = value[:, tile * width : (tile + 1) * width]


def join_tiles(ref):
    return jnp.concatenate([ref[tile] for tile in range(ref.shape[0])], axis=1)


def factorise(levels, coef_ref, ratio_ref, inverse_ref):
    ratio_prev = None
    for level in range(levels):
        coef_now = coef_ref[level : level + 1, :]
        divisor = 1.0 + coef_now
        if level > 0:
            below_now = coef_ref[level - 1 : level, :]
            divisor = divisor + below_now + below_now * ratio_prev
        inverse_now = 1.0 / divisor
        ratio_prev = -coef_now * inverse_now
        inverse_ref[level : level + 1, :] = inverse_now
        ratio_ref[level : level + 1, :] = ratio_prev


def by_cell(ref, rows, lons):
    return jnp.concatenate(
        [ref[pl.ds(lon, rows, stride=lons), :] for lon in range(lons)], axis=1
    )


def adjoint_kernel(
    count_ref,
    column_ref,
    cols_ref,
    mask_ref,
    adj_ref,
    coef_ref,
    ratio_ref,
    inverse_ref,
    right_ref,
    *,
    lons,
):
    fields = adj_ref.shape[1]
    levels = coef_ref.shape[0]
    spread = one_hot(cols_ref, lons * column_ref.shape[1])
    sources = by_cell(column_ref, fields + levels, lons).astype(BF16)
    picked = jnp.dot(sources, spread, preferred_element_type=F32)
    split_tiles(right_ref, picked[:fields] * live_row(count_ref, mask_ref))
    coef_ref[...] = picked[fields:]
    factorise(levels, coef_ref, ratio_ref, inverse_ref)
    solve(levels, fields // levels, coef_ref, ratio_ref, inverse_ref, right_ref, adj_ref)


def sigmoid(pre_act):
    return 0.5 * jnp.tanh(0.5 * pre_act) + 0.5


def weight_product(left_ref, right, keep_ref, send_ref, first):
    half = left_ref.shape[0] // 2
    block = min(BLOCK, half)
    core = lax.axis_index("horiz") % 2
    for out_ref, side in ((send_ref, 1 - core), (keep_ref, core)):
        for start in range(0, half, block):
            out_ref[start : start + block, first : first + right.shape[0]] = lax.dot_general(
                left_ref[pl.ds(pl.multiple_of(side * half + start, block), block), :],
                right,
                CONTRACT_LAST,
                preferred_element_type=F32,
            ).astype(BF16)


def forward_kernel(
    base_ref,
    low_ref,
    high_ref,
    cols_ref,
    adj_ref,
    weights_ref,
    w_out_ref,
    moved_ref,
    x_ref,
    act_one_ref,
    act_two_ref,
    delta_two_ref,
    keep_ref,
    send_ref,
    *,
    lons,
):
    fields = x_ref.shape[0]
    units = weights_ref.shape[0]
    cells = lons * base_ref.shape[1]
    low_rows, high_rows = halo_rows(low_ref, fields), halo_rows(high_ref, fields)
    lon_coef, lat_coef = coefficients(
        base_ref, halo_mixing(low_ref, fields), halo_mixing(high_ref, fields), lons
    )
    rows = [base_ref[pl.ds(lon, fields, stride=lons), :] for lon in range(lons)]
    rows = two_steps(low_rows + rows + high_rows, lon_coef, lat_coef)
    for lon in range(lons):
        moved_ref[lon] = rows[lon]
    spread = one_hot(cols_ref, cells)
    sources = jnp.concatenate(rows, axis=1).astype(BF16)
    x_now = jnp.dot(sources, spread, preferred_element_type=F32).astype(BF16)
    x_ref[...] = x_now
    for start in range(0, units, BLOCK):
        pre_one = jnp.dot(weights_ref[start : start + BLOCK, units:], x_now, preferred_element_type=F32)
        act_one_ref[start : start + BLOCK, :] = (pre_one * sigmoid(pre_one)).astype(BF16)
    adj_half = join_tiles(adj_ref).astype(BF16)
    for start in range(0, units, BLOCK):
        pre_two = jnp.dot(
            weights_ref[start : start + BLOCK, :units], act_one_ref[...], preferred_element_type=F32
        )
        sigma_val = sigmoid(pre_two)
        act_two_ref[start : start + BLOCK, :] = (pre_two * sigma_val).astype(BF16)
        back_two = lax.dot_general(
            w_out_ref[:, start : start + BLOCK],
            adj_half,
            CONTRACT_FIRST,
            preferred_element_type=F32,
        )
        slope = sigma_val * (1.0 + pre_two * (1.0 - sigma_val))
        delta_two_ref[start : start + BLOCK, :] = (back_two * slope).astype(BF16)
    weight_product(delta_two_ref, act_one_ref[...], keep_ref, send_ref, 0)


def backward_kernel(
    x_ref,
    act_two_ref,
    delta_two_ref,
    adj_ref,
    weights_ref,
    delta_one_ref,
    keep_ref,
    send_ref,
):
    fields = x_ref.shape[0]
    units = weights_ref.shape[0]
    x_now = x_ref[...]
    for start in range(0, units, BLOCK):
        back_one = lax.dot_general(
            weights_ref[:, start : start + BLOCK],
            delta_two_ref[...],
            CONTRACT_FIRST,
            preferred_element_type=F32,
        )
        pre_one = jnp.dot(weights_ref[start : start + BLOCK, units:], x_now, preferred_element_type=F32)
        sigma_val = sigmoid(pre_one)
        slope = sigma_val * (1.0 + pre_one * (1.0 - sigma_val))
        delta_one_ref[start : start + BLOCK, :] = (back_one * slope).astype(BF16)
    weight_product(delta_one_ref, x_now, keep_ref, send_ref, 0)
    weight_product(act_two_ref, join_tiles(adj_ref).astype(BF16), keep_ref, send_ref, fields)


def place_back(fresh, live, cols_ref, cells):
    marks = jnp.broadcast_to(live, (16, live.shape[1]))
    placed = lax.dot_general(
        jnp.concatenate([fresh * live, marks], axis=0).astype(BF16),
        one_hot(cols_ref, cells),
        CONTRACT_LAST,
        preferred_element_type=F32,
    )
    rows = fresh.shape[0]
    return placed[:rows], placed[rows : rows + 1] > 0.5


def state_kernel(
    count_ref,
    moved_ref,
    cols_ref,
    mask_ref,
    x_ref,
    act_two_ref,
    coef_ref,
    ratio_ref,
    inverse_ref,
    w_out_ref,
    state_ref,
    forced_ref,
    solved_ref,
    *,
    lons,
):
    fields = x_ref.shape[0]
    levels = coef_ref.shape[0]
    lats = moved_ref.shape[2]
    tendency = jnp.dot(w_out_ref[...], act_two_ref[...], preferred_element_type=F32)
    split_tiles(forced_ref, x_ref[...].astype(F32) + tendency)
    solve(levels, fields // levels, coef_ref, ratio_ref, inverse_ref, forced_ref, solved_ref)
    placed, taken = place_back(
        join_tiles(solved_ref), live_row(count_ref, mask_ref), cols_ref, lons * lats
    )
    for lon in range(lons):
        here = slice(lon * lats, (lon + 1) * lats)
        state_ref[pl.ds(lon, fields, stride=lons), :] = jnp.where(
            taken[:, here], placed[:, here], moved_ref[lon]
        )


def grad_kernel(
    count_ref,
    column_ref,
    cols_ref,
    mask_ref,
    delta_one_ref,
    adj_ref,
    weights_ref,
    field_ref,
    up_ref,
    down_ref,
    *,
    lons,
):
    fields, lats = field_ref.shape[1:]
    grad_x = join_tiles(adj_ref) + lax.dot_general(
        weights_ref[:, delta_one_ref.shape[0] :], delta_one_ref[...], CONTRACT_FIRST, preferred_element_type=F32
    )
    placed, taken = place_back(grad_x, live_row(count_ref, mask_ref), cols_ref, lons * lats)
    for lon in range(lons):
        here = slice(lon * lats, (lon + 1) * lats)
        field_now = jnp.where(
            taken[:, here], placed[:, here], column_ref[pl.ds(lon, fields, stride=lons), :]
        )
        field_ref[lon] = field_now
        if lon < 2:
            down_ref[lon * fields : (lon + 1) * fields, :] = field_now.astype(BF16)
        if lon >= lons - 2:
            side = lon - (lons - 2)
            up_ref[side * fields : (side + 1) * fields, :] = field_now.astype(BF16)


def last_kernel(field_ref, low_ref, high_ref, low_mix_ref, high_mix_ref, base_ref, out_ref, *, lons):
    fields = field_ref.shape[1]
    low_rows, high_rows = halo_rows(low_ref, fields), halo_rows(high_ref, fields)
    lon_coef, lat_coef = coefficients(
        base_ref, halo_mixing(low_mix_ref, fields), halo_mixing(high_mix_ref, fields), lons
    )
    rows = [field_ref[lon] for lon in range(lons)]
    rows = two_steps(low_rows + rows + high_rows, lon_coef, lat_coef)
    for lon in range(lons):
        out_ref[pl.ds(lon, fields, stride=lons), :] = rows[lon]


CORE = ("horiz", 0, 2)
CHIPS = ("horiz", 1, 4)
MEMBER_LOW, MEMBER_HIGH = ("ens", 0, 2), ("ens", 1, 2)
MEMBERS = ("ens", 0, 4)


def position(stage):
    axis, shift, parts = stage
    return lax.axis_index(axis) // (1 << shift) % parts


def sum_kernel(*refs, counts, stage, factor):
    ins, outs = refs[: sum(counts)], refs[sum(counts) :]
    rows = outs[0].shape[0]
    for index, out_ref in enumerate(outs):
        k = -index % len(outs)
        here = pl.ds(0, rows)
        if stage is not None:
            here = pl.ds(pl.multiple_of((position(stage) ^ k) * rows, rows), rows)
        first, taken = 0, 0
        for count in counts:
            total = ins[taken][here, :].astype(F32)
            for ref in ins[taken + 1 : taken + count]:
                total = total + ref[here, :].astype(F32)
            columns = total.shape[1]
            out_ref[:, first : first + columns] = (total * factor).astype(BF16)
            first, taken = first + columns, taken + count


def join_kernel(*refs, stage, groups, cuts):
    ins, out_refs = refs[:-cuts], refs[-cuts:]
    count = len(ins) // groups
    rows, columns = ins[0].shape
    width = out_refs[0].shape[1]
    for k in range(count):
        here = pl.ds(pl.multiple_of((position(stage) ^ k) * rows, rows), rows)
        for group in range(groups):
            ref = ins[group * count + k]
            for start in range(0, columns, min(width, columns)):
                first = group * columns + start
                part = min(width, columns)
                out_refs[first // width][here, first % width : first % width + part] = ref[
                    :, start : start + part
                ]


def core_sum_kernel(*refs, spans, stage, members):
    outs = refs[2 * len(spans) :]
    rows = refs[0].shape[0] // members
    low = stage == MEMBER_LOW
    for k, out_ref in enumerate(outs):
        mine = position(stage) ^ k
        for other in range(members // 2):
            member = 2 * other + mine if low else 2 * mine + other
            here = pl.ds(pl.multiple_of(member * rows, rows), rows)
            first = 0
            for group, (start, stop) in enumerate(spans):
                keep_ref, got_ref = refs[2 * group : 2 * group + 2]
                out_ref[other * rows : (other + 1) * rows, first : first + stop - start] = (
                    keep_ref[here, start:stop].astype(F32) + got_ref[here, start:stop].astype(F32)
                ).astype(BF16)
                first += stop - start


def final_kernel(mid_half, small_half, *refs):
    mid_ref, in_ref, out_ref = refs[-3:]
    fields = in_ref.shape[1]
    mid_ref[...] = mid_half[...].astype(F32)

    @pl.when(pl.program_id(0) == 0)
    def _():
        in_ref[...] = small_half[:, :fields].astype(F32)
        out_ref[...] = small_half[:, fields:].astype(F32).T


def final(rows, other, before, fields):
    half, columns = rows.shape
    units = 2 * half
    block = units // 4

    def place():
        core = lax.axis_index("horiz") % 2
        return 1 - core if other else core

    return pl.pallas_call(
        final_kernel,
        grid=(units // block,),
        out_shape=[
            jax.ShapeDtypeStruct(shape, F32)
            for shape in ((units, units), (units, fields), (fields, units))
        ],
        in_specs=[
            pl.BlockSpec((half, block), lambda step: (0, step)),
            pl.BlockSpec((half, 2 * fields), lambda step: (0, units // (2 * fields))),
        ]
        + [pl.BlockSpec(memory_space=pl.ANY)] * len(before),
        out_specs=[
            pl.BlockSpec((half, block), lambda step: (place(), step)),
            pl.BlockSpec((half, fields), lambda step: (place(), 0)),
            pl.BlockSpec((fields, half), lambda step: (0, place())),
        ],
        input_output_aliases={2 + index: index for index in range(len(before))},
        compiler_params=pltpu.CompilerParams(vmem_limit_bytes=VMEM_LIMIT),
    )(rows, rows, *before)


def exchange(arrays, stage):
    axis, shift, _ = stage
    count = lax.axis_size(axis)
    sent = {}
    for k in range(len(arrays), 0, -1):
        route = [(i, i ^ (k << shift)) for i in range(count)]
        sent[k] = lax.ppermute(arrays[k - 1], axis, route)
    return [sent[k] for k in range(1, len(arrays) + 1)]


def add(groups, stage, factor=1.0):
    rows = groups[0][0].shape[0]
    columns = sum(terms[0].shape[1] for terms in groups)
    parts = 1 if stage is None else stage[2]
    return call(
        sum_kernel,
        [((rows // parts, columns), BF16)] * parts,
        counts=tuple(len(terms) for terms in groups),
        stage=stage,
        factor=factor,
    )(*[term for terms in groups for term in terms])


def join(groups, stage, outs=1):
    rows, columns = groups[0][0].shape
    shape = (rows * len(groups[0]), columns * len(groups) // outs)
    return call(
        join_kernel, [(shape, BF16)] * outs, stage=stage, groups=len(groups), cuts=outs
    )(*[piece for group in groups for piece in group])


def reduce_to(groups, stage):
    parts = add(groups, stage)
    return [parts[0]] + exchange(parts[:0:-1], stage)[::-1]


def collect_members(one, two):
    (low_one,) = exchange([one], MEMBER_LOW)
    (high_two,) = exchange([two], MEMBER_HIGH)
    (high_one,) = exchange([one], MEMBER_HIGH)
    (low_two,) = exchange([two], MEMBER_LOW)
    (far_one,) = exchange([low_one], MEMBER_HIGH)
    (far_two,) = exchange([high_two], MEMBER_LOW)
    return [one, low_one, high_one, far_one], [two, low_two, high_two, far_two]


def collect(piece, stage):
    return [piece] + exchange([piece] * (stage[2] - 1), stage)


def tie(*values):
    return lax.optimization_barrier(values)


def over_all_chips(piece, factor):
    core = lax.axis_index("horiz") % 2
    both = jnp.stack([jnp.where(core == side, piece, 0.0).astype(F32) for side in range(2)])
    return (lax.psum(both, "horiz")[core] * factor).astype(BF16)


def to_neighbours(upward, downward, axis):
    count = lax.axis_size(axis)
    forward = [(i, (i + 1) % count) for i in range(count)]
    backward = [(target, source) for source, target in forward]
    return lax.ppermute(upward, axis, forward), lax.ppermute(downward, axis, backward)


def per_device(
    prognostic, diffusivity, mixing, cotangent, tile_cols, pad_mask, tile_count, w_in, w_mid, w_out
):
    fields, lons, lats = prognostic.shape[1:]
    levels = diffusivity.shape[1]
    units = w_mid.shape[0]
    tiles, width = tile_cols.shape[2:]
    slots = tiles * width
    base = jnp.concatenate([prognostic[0], mixing], axis=0).reshape((fields + 2) * lons, lats)
    column = jnp.concatenate([cotangent[0], diffusivity[0]], axis=0)
    column = column.reshape((fields + levels) * lons, lats)
    weights = jnp.concatenate([w_mid, w_in], axis=1)
    cols, mask = tile_cols[0, 0], pad_mask[0, 0]

    packed = ((2 * fields + PACK_ROWS, lats), BF16)
    up_pack, down_pack = call(pack_kernel, [packed, packed], lons=lons)(base)
    low_pack, high_pack = to_neighbours(up_pack, down_pack, "horiz")

    adjoint, coef, ratio, inverse = call(
        adjoint_kernel,
        [((tiles, fields, width), F32)] + [((levels, slots), F32)] * 3,
        scratch=[pltpu.VMEM((tiles, fields, width), F32)],
        smem=(0,),
        moved=30 * 10**6,
        lons=lons,
    )(tile_count, column, cols, mask)

    hidden = ((units, slots), BF16)
    half = ((units // 2, units), BF16)
    moved, x_now, act_one, act_two, delta_two, keep_mid, send_mid = call(
        forward_kernel,
        [((lons, fields, lats), F32), ((fields, slots), BF16), hidden, hidden, hidden, half, half],
        moved=15 * 10**6,
        lons=lons,
    )(base, low_pack, high_pack, cols, adjoint, weights, w_out)
    column_total = lax.axis_size("ens") * lax.axis_size("horiz") * lons * lats
    factor = 1.0 / math.sqrt(column_total)
    (got_mid,) = exchange([send_mid], CORE)

    half = ((units // 2, 2 * fields), BF16)
    delta_one, keep_small, send_small = call(
        backward_kernel, [hidden, half, half], moved=4 * 10**6
    )(x_now, act_two, delta_two, adjoint, weights)
    (got_small,) = exchange([send_small], CORE)
    got_mid, delta_one = tie(got_mid, delta_one)

    def both_cores(operands, spans, stage):
        columns = sum(stop - start for start, stop in spans)
        members = lax.axis_size("ens")
        parts = call(
            core_sum_kernel,
            [((units // 2 // 2, columns), BF16)] * 2,
            spans=spans,
            stage=stage,
            members=members,
        )(*operands)
        return parts, [parts[0]] + exchange(parts[1:], stage)

    split = (units + 2 * fields) // 2
    parts_one, terms_one = both_cores([keep_mid, got_mid], [(0, split)], MEMBER_LOW)
    delta_one, keep_small = tie(delta_one, keep_small, parts_one)[:2]
    packed = ((2 * fields, lats), BF16)
    field, up_rows, down_rows = call(
        grad_kernel,
        [((lons, fields, lats), F32), packed, packed],
        smem=(0,),
        lons=lons,
    )(tile_count, column, cols, mask, delta_one, adjoint, weights)
    parts_two, terms_two = both_cores(
        [keep_mid, got_mid, keep_small, got_small], [(split, units), (0, 2 * fields)], MEMBER_HIGH
    )
    act_two, up_rows, down_rows = tie(act_two, up_rows, down_rows, parts_two)[:3]
    halos = to_neighbours(up_rows, down_rows, "horiz")
    (state_rows,) = call(
        state_kernel,
        [((fields * lons, lats), F32)],
        scratch=[pltpu.VMEM((tiles, fields, width), F32)] * 2,
        smem=(0,),
        lons=lons,
    )(tile_count, moved, cols, mask, x_now, act_two, coef, ratio, inverse, w_out)
    terms_one, terms_two, state_rows, halos = tie(terms_one, terms_two, state_rows, halos)
    terms_one = reduce_to([terms_one], MEMBER_HIGH)
    terms_two = reduce_to([terms_two], MEMBER_LOW)
    (grad_rows,) = call(last_kernel, [((fields * lons, lats), F32)], lons=lons)(
        field, *halos, low_pack, high_pack, base
    )
    terms_one, terms_two, grad_rows = tie(terms_one, terms_two, grad_rows)
    groups = [terms_one, terms_two]

    if lax.axis_size("horiz") == 8:
        terms = reduce_to(groups, CHIPS)
        pieces = collect(add([terms], None, factor)[0], CHIPS)
        groups = collect_members(*join([pieces], CHIPS, outs=2))
    else:
        groups = [collect(over_all_chips(add(groups, None)[0], factor), MEMBERS)]
    (own,) = join(groups, MEMBERS)
    (got,) = exchange([own], CORE)
    half_done = final(own, False, [], fields)
    grad_mid, grad_in, grad_out = final(got, True, half_done, fields)
    return (
        state_rows.reshape(prognostic.shape),
        grad_rows.reshape(prognostic.shape),
        grad_in,
        grad_mid,
        grad_out,
    )


def solution(mesh):
    placed = (
        P("ens", None, "horiz", None),
        P("ens", None, "horiz", None),
        P(None, "horiz", None),
        P("ens", None, "horiz", None),
        P("ens", "horiz", None, None),
        P("ens", "horiz", None, None),
        P("ens", "horiz"),
        P(),
        P(),
        P(),
    )
    return jax.shard_map(
        per_device,
        mesh=mesh,
        in_specs=placed,
        out_specs=(P("ens", None, "horiz", None), P("ens", None, "horiz", None), P(), P(), P()),
        check_vma=False,
    )
```

```python
import functools
import math

import jax
import jax.numpy as jnp
from jax import lax
from jax.experimental import pallas as pl
from jax.experimental.pallas import tpu as pltpu
from jax.sharding import PartitionSpec as P

DYN_STEPS = 2
BLOCK = 256
PACK_ROWS = 16
VMEM_LIMIT = 32 * 1024 * 1024
F32 = jnp.float32
BF16 = jnp.bfloat16
CONTRACT_LAST = (((1,), (1,)), ((), ()))
CONTRACT_FIRST = (((0,), (0,)), ((), ()))


def call(kernel, outs, scratch=(), smem=(), flops=0, moved=0, **names):
    def run(*operands):
        specs = [
            pl.BlockSpec(memory_space=pltpu.SMEM if place in smem else pltpu.VMEM)
            for place in range(len(operands))
        ]
        return pl.pallas_call(
            functools.partial(kernel, **names),
            out_shape=[jax.ShapeDtypeStruct(shape, dtype) for shape, dtype in outs],
            in_specs=specs,
            out_specs=[pl.BlockSpec(memory_space=pltpu.VMEM)] * len(outs),
            scratch_shapes=list(scratch),
            compiler_params=pltpu.CompilerParams(vmem_limit_bytes=VMEM_LIMIT),
            cost_estimate=pl.CostEstimate(flops=flops, bytes_accessed=moved, transcendentals=0),
        )(*operands)

    return run


def lat_term(field_now, coef_masked):
    lats = field_now.shape[1]
    north_flux = coef_masked * (pltpu.roll(field_now, lats - 1, 1) - field_now)
    return north_flux - pltpu.roll(north_flux, 1, 1)


def two_steps(rows, lon_coef, lat_coef):
    for repeat in range(DYN_STEPS):
        count = len(rows)
        fluxes = [
            lon_coef[place + repeat] * (rows[place + 1] - rows[place]) for place in range(count - 1)
        ]
        rows = [
            rows[place]
            + fluxes[place]
            - fluxes[place - 1]
            + lat_term(rows[place], lat_coef[place + repeat])
            for place in range(1, count - 1)
        ]
    return rows


def coefficients(base_ref, low_mix, high_mix, lons):
    lats = base_ref.shape[1]
    first = base_ref.shape[0] - 2 * lons
    lane = lax.broadcasted_iota(jnp.int32, (1, lats), 1)
    inside = lane < lats - 1
    own_lon = [base_ref[first + lon : first + lon + 1, :] for lon in range(lons)]
    first += lons
    own_lat = [base_ref[first + lon : first + lon + 1, :] for lon in range(lons)]
    lon_coef = [low_mix[0:1, :], low_mix[1:2, :]] + own_lon + [high_mix[0:1, :], high_mix[1:2, :]]
    lat_coef = [low_mix[2:3, :], low_mix[3:4, :]] + own_lat + [high_mix[2:3, :], high_mix[3:4, :]]
    return lon_coef, [jnp.where(inside, coef, 0.0) for coef in lat_coef]


def pack_kernel(base_ref, up_ref, down_ref, *, lons):
    fields = base_ref.shape[0] // lons - 2
    mixing = fields * lons
    for out_ref, first in ((up_ref, lons - 2), (down_ref, 0)):
        for side in range(2):
            out_ref[side * fields : (side + 1) * fields, :] = base_ref[
                pl.ds(first + side, fields, stride=lons), :
            ].astype(BF16)
        mix_rows = [
            base_ref[mixing + first : mixing + first + 2, :],
            base_ref[mixing + lons + first : mixing + lons + first + 2, :],
            jnp.zeros((PACK_ROWS - 4, base_ref.shape[1]), F32),
        ]
        out_ref[2 * fields :, :] = jnp.concatenate(mix_rows, axis=0).astype(BF16)


def halo_rows(pack_ref, fields):
    return [pack_ref[side * fields : (side + 1) * fields, :].astype(F32) for side in range(2)]


def halo_mixing(pack_ref, fields):
    return pack_ref[2 * fields :, :].astype(F32)


def one_hot(cols_ref, cells):
    parts = []
    for tile in range(cols_ref.shape[0]):
        place = lax.broadcasted_iota(jnp.int32, (cells, cols_ref.shape[1]), 0)
        parts.append(jnp.where(place == cols_ref[tile : tile + 1, :], 1.0, 0.0))
    return jnp.concatenate(parts, axis=1).astype(BF16)


def live_row(count_ref, mask_ref):
    parts = []
    for tile in range(mask_ref.shape[0]):
        used = jnp.where(tile < count_ref[0, 0], 1, 0)
        parts.append((mask_ref[tile : tile + 1, :] * used).astype(F32))
    return jnp.concatenate(parts, axis=1)


def level_rows(levels, level, variables):
    return pl.ds(level, variables, stride=levels)


def solve(levels, variables, coef_ref, ratio_ref, inverse_ref, right_ref, out_ref):
    tiles, _, width = right_ref.shape
    spans = [slice(tile * width, (tile + 1) * width) for tile in range(tiles)]
    values = []
    for level in range(levels):
        inverse_now = inverse_ref[level : level + 1, :]
        if level > 0:
            carry_now = coef_ref[level - 1 : level, :] * inverse_now
        step = []
        for tile, span in enumerate(spans):
            right_now = right_ref[tile, level_rows(levels, level, variables), :]
            value_now = right_now * inverse_now[:, span]
            if level > 0:
                value_now = value_now + carry_now[:, span] * values[-1][tile]
            step.append(value_now)
        values.append(step)
    results = values[-1]
    for level in range(levels - 1, -1, -1):
        if level < levels - 1:
            ratio_now = ratio_ref[level : level + 1, :]
            results = [
                values[level][tile] - ratio_now[:, span] * results[tile]
                for tile, span in enumerate(spans)
            ]
        for tile in range(tiles):
            out_ref[tile, level_rows(levels, level, variables), :] = results[tile]


def split_tiles(ref, value):
    width = ref.shape[2]
    for tile in range(ref.shape[0]):
        ref[tile] = value[:, tile * width : (tile + 1) * width]


def join_tiles(ref):
    return jnp.concatenate([ref[tile] for tile in range(ref.shape[0])], axis=1)


def factorise(levels, coef_ref, ratio_ref, inverse_ref):
    ratio_prev = None
    for level in range(levels):
        coef_now = coef_ref[level : level + 1, :]
        divisor = 1.0 + coef_now
        if level > 0:
            below_now = coef_ref[level - 1 : level, :]
            divisor = divisor + below_now + below_now * ratio_prev
        inverse_now = 1.0 / divisor
        ratio_prev = -coef_now * inverse_now
        inverse_ref[level : level + 1, :] = inverse_now
        ratio_ref[level : level + 1, :] = ratio_prev


def by_cell(ref, rows, lons):
    return jnp.concatenate(
        [ref[pl.ds(lon, rows, stride=lons), :] for lon in range(lons)], axis=1
    )


def adjoint_kernel(
    count_ref,
    column_ref,
    cols_ref,
    mask_ref,
    adj_ref,
    coef_ref,
    ratio_ref,
    inverse_ref,
    right_ref,
    *,
    lons,
):
    fields = adj_ref.shape[1]
    levels = coef_ref.shape[0]
    spread = one_hot(cols_ref, lons * column_ref.shape[1])
    sources = by_cell(column_ref, fields + levels, lons).astype(BF16)
    picked = jnp.dot(sources, spread, preferred_element_type=F32)
    split_tiles(right_ref, picked[:fields] * live_row(count_ref, mask_ref))
    coef_ref[...] = picked[fields:]
    factorise(levels, coef_ref, ratio_ref, inverse_ref)
    solve(levels, fields // levels, coef_ref, ratio_ref, inverse_ref, right_ref, adj_ref)


def sigmoid(pre_act):
    return 0.5 * jnp.tanh(0.5 * pre_act) + 0.5


def weight_product(left_ref, right, keep_ref, send_ref, first):
    half = left_ref.shape[0] // 2
    block = min(BLOCK, half)
    core = lax.axis_index("horiz") % 2
    for out_ref, side in ((send_ref, 1 - core), (keep_ref, core)):
        for start in range(0, half, block):
            out_ref[start : start + block, first : first + right.shape[0]] = lax.dot_general(
                left_ref[pl.ds(pl.multiple_of(side * half + start, block), block), :],
                right,
                CONTRACT_LAST,
                preferred_element_type=F32,
            ).astype(BF16)


def forward_kernel(
    base_ref,
    low_ref,
    high_ref,
    cols_ref,
    adj_ref,
    weights_ref,
    w_out_ref,
    moved_ref,
    x_ref,
    act_one_ref,
    act_two_ref,
    delta_two_ref,
    keep_ref,
    send_ref,
    *,
    lons,
):
    fields = x_ref.shape[0]
    units = weights_ref.shape[0]
    cells = lons * base_ref.shape[1]
    low_rows, high_rows = halo_rows(low_ref, fields), halo_rows(high_ref, fields)
    lon_coef, lat_coef = coefficients(
        base_ref, halo_mixing(low_ref, fields), halo_mixing(high_ref, fields), lons
    )
    rows = [base_ref[pl.ds(lon, fields, stride=lons), :] for lon in range(lons)]
    rows = two_steps(low_rows + rows + high_rows, lon_coef, lat_coef)
    for lon in range(lons):
        moved_ref[lon] = rows[lon]
    spread = one_hot(cols_ref, cells)
    sources = jnp.concatenate(rows, axis=1).astype(BF16)
    x_now = jnp.dot(sources, spread, preferred_element_type=F32).astype(BF16)
    x_ref[...] = x_now
    for start in range(0, units, BLOCK):
        pre_one = jnp.dot(weights_ref[start : start + BLOCK, units:], x_now, preferred_element_type=F32)
        act_one_ref[start : start + BLOCK, :] = (pre_one * sigmoid(pre_one)).astype(BF16)
    adj_half = join_tiles(adj_ref).astype(BF16)
    for start in range(0, units, BLOCK):
        pre_two = jnp.dot(
            weights_ref[start : start + BLOCK, :units], act_one_ref[...], preferred_element_type=F32
        )
        sigma_val = sigmoid(pre_two)
        act_two_ref[start : start + BLOCK, :] = (pre_two * sigma_val).astype(BF16)
        back_two = lax.dot_general(
            w_out_ref[:, start : start + BLOCK],
            adj_half,
            CONTRACT_FIRST,
            preferred_element_type=F32,
        )
        slope = sigma_val * (1.0 + pre_two * (1.0 - sigma_val))
        delta_two_ref[start : start + BLOCK, :] = (back_two * slope).astype(BF16)
    weight_product(delta_two_ref, act_one_ref[...], keep_ref, send_ref, 0)


def backward_kernel(
    x_ref,
    act_two_ref,
    delta_two_ref,
    adj_ref,
    weights_ref,
    delta_one_ref,
    keep_ref,
    send_ref,
):
    fields = x_ref.shape[0]
    units = weights_ref.shape[0]
    x_now = x_ref[...]
    for start in range(0, units, BLOCK):
        back_one = lax.dot_general(
            weights_ref[:, start : start + BLOCK],
            delta_two_ref[...],
            CONTRACT_FIRST,
            preferred_element_type=F32,
        )
        pre_one = jnp.dot(weights_ref[start : start + BLOCK, units:], x_now, preferred_element_type=F32)
        sigma_val = sigmoid(pre_one)
        slope = sigma_val * (1.0 + pre_one * (1.0 - sigma_val))
        delta_one_ref[start : start + BLOCK, :] = (back_one * slope).astype(BF16)
    weight_product(delta_one_ref, x_now, keep_ref, send_ref, 0)
    weight_product(act_two_ref, join_tiles(adj_ref).astype(BF16), keep_ref, send_ref, fields)


def place_back(fresh, live, cols_ref, cells):
    marks = jnp.broadcast_to(live, (16, live.shape[1]))
    placed = lax.dot_general(
        jnp.concatenate([fresh * live, marks], axis=0).astype(BF16),
        one_hot(cols_ref, cells),
        CONTRACT_LAST,
        preferred_element_type=F32,
    )
    rows = fresh.shape[0]
    return placed[:rows], placed[rows : rows + 1] > 0.5


def state_kernel(
    count_ref,
    moved_ref,
    cols_ref,
    mask_ref,
    x_ref,
    act_two_ref,
    coef_ref,
    ratio_ref,
    inverse_ref,
    w_out_ref,
    state_ref,
    forced_ref,
    solved_ref,
    *,
    lons,
):
    fields = x_ref.shape[0]
    levels = coef_ref.shape[0]
    lats = moved_ref.shape[2]
    tendency = jnp.dot(w_out_ref[...], act_two_ref[...], preferred_element_type=F32)
    split_tiles(forced_ref, x_ref[...].astype(F32) + tendency)
    solve(levels, fields // levels, coef_ref, ratio_ref, inverse_ref, forced_ref, solved_ref)
    placed, taken = place_back(
        join_tiles(solved_ref), live_row(count_ref, mask_ref), cols_ref, lons * lats
    )
    for lon in range(lons):
        here = slice(lon * lats, (lon + 1) * lats)
        state_ref[pl.ds(lon, fields, stride=lons), :] = jnp.where(
            taken[:, here], placed[:, here], moved_ref[lon]
        )


def grad_kernel(
    count_ref,
    column_ref,
    cols_ref,
    mask_ref,
    delta_one_ref,
    adj_ref,
    weights_ref,
    field_ref,
    up_ref,
    down_ref,
    *,
    lons,
):
    fields, lats = field_ref.shape[1:]
    grad_x = join_tiles(adj_ref) + lax.dot_general(
        weights_ref[:, delta_one_ref.shape[0] :], delta_one_ref[...], CONTRACT_FIRST, preferred_element_type=F32
    )
    placed, taken = place_back(grad_x, live_row(count_ref, mask_ref), cols_ref, lons * lats)
    for lon in range(lons):
        here = slice(lon * lats, (lon + 1) * lats)
        field_now = jnp.where(
            taken[:, here], placed[:, here], column_ref[pl.ds(lon, fields, stride=lons), :]
        )
        field_ref[lon] = field_now
        if lon < 2:
            down_ref[lon * fields : (lon + 1) * fields, :] = field_now.astype(BF16)
        if lon >= lons - 2:
            side = lon - (lons - 2)
            up_ref[side * fields : (side + 1) * fields, :] = field_now.astype(BF16)


def last_kernel(field_ref, low_ref, high_ref, low_mix_ref, high_mix_ref, base_ref, out_ref, *, lons):
    fields = field_ref.shape[1]
    low_rows, high_rows = halo_rows(low_ref, fields), halo_rows(high_ref, fields)
    lon_coef, lat_coef = coefficients(
        base_ref, halo_mixing(low_mix_ref, fields), halo_mixing(high_mix_ref, fields), lons
    )
    rows = [field_ref[lon] for lon in range(lons)]
    rows = two_steps(low_rows + rows + high_rows, lon_coef, lat_coef)
    for lon in range(lons):
        out_ref[pl.ds(lon, fields, stride=lons), :] = rows[lon]


CORE = ("horiz", 0, 2)
CHIPS = ("horiz", 1, 4)


def position(stage):
    axis, shift, parts = stage
    return lax.axis_index(axis) // (1 << shift) % parts


def sum_kernel(*refs, terms, stage, factor):
    ins, outs = refs[:terms], refs[terms:]
    rows = outs[0].shape[0]
    for index, out_ref in enumerate(outs):
        here = pl.ds(0, rows)
        if stage is not None:
            start = (position(stage) ^ (-index % len(outs))) * rows
            here = pl.ds(pl.multiple_of(start, rows), rows)
        total = ins[0][here, :].astype(F32)
        for ref in ins[1:]:
            total = total + ref[here, :].astype(F32)
        out_ref[...] = (total * factor).astype(BF16)


def join_kernel(*refs, stage):
    ins, out_ref = refs[:-1], refs[-1]
    rows = ins[0].shape[0]
    if stage is None:
        places = member_order()
    else:
        places = [position(stage) ^ k for k in range(len(ins))]
    for place, ref in zip(places, ins):
        out_ref[pl.ds(pl.multiple_of(place * rows, rows), rows), :] = ref[...]


def member_order():
    member, core = lax.axis_index("ens"), lax.axis_index("horiz") % 2
    return [member, member ^ (1 + core), member ^ (2 - core), member ^ 3]


def core_sum_kernel(keep_mid, got_mid, keep_small, got_small, *outs):
    rows = outs[0].shape[0]
    for member, out_ref in zip(member_order(), outs):
        here = pl.ds(pl.multiple_of(member * rows, rows), rows)
        first = 0
        for keep_ref, got_ref in ((keep_mid, got_mid), (keep_small, got_small)):
            columns = keep_ref.shape[1]
            out_ref[:, first : first + columns] = (
                keep_ref[here, :].astype(F32) + got_ref[here, :].astype(F32)
            ).astype(BF16)
            first += columns


def final_kernel(mid_half, small_half, *refs):
    mid_ref, in_ref, out_ref = refs[-3:]
    fields = in_ref.shape[1]
    mid_ref[...] = mid_half[...].astype(F32)

    @pl.when(pl.program_id(0) == 0)
    def _():
        in_ref[...] = small_half[:, :fields].astype(F32)
        out_ref[...] = small_half[:, fields:].astype(F32).T


def final(rows, other, before, fields):
    half, columns = rows.shape
    units = 2 * half
    block = units // 4

    def place():
        core = lax.axis_index("horiz") % 2
        return 1 - core if other else core

    return pl.pallas_call(
        final_kernel,
        grid=(units // block,),
        out_shape=[
            jax.ShapeDtypeStruct(shape, F32)
            for shape in ((units, units), (units, fields), (fields, units))
        ],
        in_specs=[
            pl.BlockSpec((half, block), lambda step: (0, step)),
            pl.BlockSpec((half, 2 * fields), lambda step: (0, units // (2 * fields))),
        ]
        + [pl.BlockSpec(memory_space=pl.ANY)] * len(before),
        out_specs=[
            pl.BlockSpec((half, block), lambda step: (place(), step)),
            pl.BlockSpec((half, fields), lambda step: (place(), 0)),
            pl.BlockSpec((fields, half), lambda step: (0, place())),
        ],
        input_output_aliases={2 + index: index for index in range(len(before))},
        compiler_params=pltpu.CompilerParams(vmem_limit_bytes=VMEM_LIMIT),
    )(rows, rows, *before)


def exchange(arrays, stage):
    axis, shift, _ = stage
    count = lax.axis_size(axis)
    sent = {}
    for k in range(len(arrays), 0, -1):
        route = [(i, i ^ (k << shift)) for i in range(count)]
        sent[k] = lax.ppermute(arrays[k - 1], axis, route)
    return [sent[k] for k in range(1, len(arrays) + 1)]


def to_member(array, second):
    members, count = lax.axis_size("ens"), lax.axis_size("horiz")
    route = []
    for member in range(members):
        for place in range(count):
            neighbour = member ^ (1 << (place % 2 ^ second))
            route.append((member * count + place, neighbour * count + place))
    return lax.ppermute(array, ("ens", "horiz"), route)


def collect_members(piece):
    got_first = to_member(piece, 0)
    got_second = to_member(piece, 1)
    return [piece, got_first, got_second, to_member(got_first, 1)]


def add(terms, stage, factor=1.0):
    rows, columns = terms[0].shape
    parts = 1 if stage is None else stage[2]
    return call(
        sum_kernel,
        [((rows // parts, columns), BF16)] * parts,
        terms=len(terms),
        stage=stage,
        factor=factor,
    )(*terms)


def join(pieces, stage):
    rows, columns = pieces[0].shape
    return call(join_kernel, [((rows * len(pieces), columns), BF16)], stage=stage)(*pieces)[0]


def reduce_to(terms, stage):
    parts = add(terms, stage)
    return [parts[0]] + exchange(parts[:0:-1], stage)[::-1]


def collect(piece, stage):
    return [piece] + exchange([piece] * (stage[2] - 1), stage)


def tie(*values):
    return lax.optimization_barrier(values)


def over_all_chips(piece, factor):
    core = lax.axis_index("horiz") % 2
    both = jnp.stack([jnp.where(core == side, piece, 0.0).astype(F32) for side in range(2)])
    return (lax.psum(both, "horiz")[core] * factor).astype(BF16)


def to_neighbours(upward, downward, axis):
    count = lax.axis_size(axis)
    forward = [(i, (i + 1) % count) for i in range(count)]
    backward = [(target, source) for source, target in forward]
    return lax.ppermute(upward, axis, forward), lax.ppermute(downward, axis, backward)


def per_device(
    prognostic, diffusivity, mixing, cotangent, tile_cols, pad_mask, tile_count, w_in, w_mid, w_out
):
    fields, lons, lats = prognostic.shape[1:]
    levels = diffusivity.shape[1]
    units = w_mid.shape[0]
    tiles, width = tile_cols.shape[2:]
    slots = tiles * width
    base = jnp.concatenate([prognostic[0], mixing], axis=0).reshape((fields + 2) * lons, lats)
    column = jnp.concatenate([cotangent[0], diffusivity[0]], axis=0)
    column = column.reshape((fields + levels) * lons, lats)
    weights = jnp.concatenate([w_mid, w_in], axis=1)
    cols, mask = tile_cols[0, 0], pad_mask[0, 0]

    packed = ((2 * fields + PACK_ROWS, lats), BF16)
    up_pack, down_pack = call(pack_kernel, [packed, packed], lons=lons)(base)
    low_pack, high_pack = to_neighbours(up_pack, down_pack, "horiz")

    adjoint, coef, ratio, inverse = call(
        adjoint_kernel,
        [((tiles, fields, width), F32)] + [((levels, slots), F32)] * 3,
        scratch=[pltpu.VMEM((tiles, fields, width), F32)],
        smem=(0,),
        moved=30 * 10**6,
        lons=lons,
    )(tile_count, column, cols, mask)

    hidden = ((units, slots), BF16)
    half = ((units // 2, units), BF16)
    moved, x_now, act_one, act_two, delta_two, keep_mid, send_mid = call(
        forward_kernel,
        [((lons, fields, lats), F32), ((fields, slots), BF16), hidden, hidden, hidden, half, half],
        moved=15 * 10**6,
        lons=lons,
    )(base, low_pack, high_pack, cols, adjoint, weights, w_out)
    column_total = lax.axis_size("ens") * lax.axis_size("horiz") * lons * lats
    factor = 1.0 / math.sqrt(column_total)
    (got_mid,) = exchange([send_mid], CORE)

    half = ((units // 2, 2 * fields), BF16)
    delta_one, keep_small, send_small = call(
        backward_kernel, [hidden, half, half], moved=4 * 10**6
    )(x_now, act_two, delta_two, adjoint, weights)
    (got_small,) = exchange([send_small], CORE)

    packed = ((2 * fields, lats), BF16)
    field, up_rows, down_rows = call(
        grad_kernel,
        [((lons, fields, lats), F32), packed, packed],
        smem=(0,),
        lons=lons,
    )(tile_count, column, cols, mask, delta_one, adjoint, weights)
    got_small, field = tie(got_small, field)

    members = lax.axis_size("ens")
    parts = call(core_sum_kernel, [((units // 2 // members, units + 2 * fields), BF16)] * members)(
        keep_mid, got_mid, keep_small, got_small
    )
    own, first, second, far = parts
    got_far = to_member(far, 0)
    got_first = to_member(first, 0)

    act_two, up_rows, down_rows = tie(act_two, up_rows, down_rows, parts)[:3]
    halos = to_neighbours(up_rows, down_rows, "horiz")
    (state_rows,) = call(
        state_kernel,
        [((fields * lons, lats), F32)],
        scratch=[pltpu.VMEM((tiles, fields, width), F32)] * 2,
        smem=(0,),
        lons=lons,
    )(tile_count, moved, cols, mask, x_now, act_two, coef, ratio, inverse, w_out)
    got_far, state_rows, halos = tie(got_far, state_rows, halos)
    terms = [own, got_first, to_member(add([second, got_far], None)[0], 1)]
    (grad_rows,) = call(last_kernel, [((fields * lons, lats), F32)], lons=lons)(
        field, *halos, low_pack, high_pack, base
    )
    terms, grad_rows = tie(terms, grad_rows)

    if lax.axis_size("horiz") == 8:
        terms = reduce_to(terms, CHIPS)
        own = join(collect(add(terms, None, factor)[0], CHIPS), CHIPS)
    else:
        own = over_all_chips(add(terms, None)[0], factor)
    own = join(collect_members(own), None)
    (got,) = exchange([own], CORE)
    half_done = final(own, False, [], fields)
    grad_mid, grad_in, grad_out = final(got, True, half_done, fields)
    return (
        state_rows.reshape(prognostic.shape),
        grad_rows.reshape(prognostic.shape),
        grad_in,
        grad_mid,
        grad_out,
    )


def solution(mesh):
    placed = (
        P("ens", None, "horiz", None),
        P("ens", None, "horiz", None),
        P(None, "horiz", None),
        P("ens", None, "horiz", None),
        P("ens", "horiz", None, None),
        P("ens", "horiz", None, None),
        P("ens", "horiz"),
        P(),
        P(),
        P(),
    )
    return jax.shard_map(
        per_device,
        mesh=mesh,
        in_specs=placed,
        out_specs=(P("ens", None, "horiz", None), P("ens", None, "horiz", None), P(), P(), P()),
        check_vma=False,
    )
```

```python
import functools
import math

import jax
import jax.numpy as jnp
from jax import lax
from jax.experimental import pallas as pl
from jax.experimental.pallas import tpu as pltpu
from jax.sharding import PartitionSpec as P

DYN_STEPS = 2
BLOCK = 256
PACK_ROWS = 16
VMEM_LIMIT = 32 * 1024 * 1024
F32 = jnp.float32
BF16 = jnp.bfloat16
CONTRACT_LAST = (((1,), (1,)), ((), ()))
CONTRACT_FIRST = (((0,), (0,)), ((), ()))


def call(kernel, outs, scratch=(), smem=(), flops=0, moved=0, **names):
    def run(*operands):
        specs = [
            pl.BlockSpec(memory_space=pltpu.SMEM if place in smem else pltpu.VMEM)
            for place in range(len(operands))
        ]
        return pl.pallas_call(
            functools.partial(kernel, **names),
            out_shape=[jax.ShapeDtypeStruct(shape, dtype) for shape, dtype in outs],
            in_specs=specs,
            out_specs=[pl.BlockSpec(memory_space=pltpu.VMEM)] * len(outs),
            scratch_shapes=list(scratch),
            compiler_params=pltpu.CompilerParams(vmem_limit_bytes=VMEM_LIMIT),
            cost_estimate=pl.CostEstimate(flops=flops, bytes_accessed=moved, transcendentals=0),
        )(*operands)

    return run


def lat_term(field_now, coef_masked):
    lats = field_now.shape[1]
    north_flux = coef_masked * (pltpu.roll(field_now, lats - 1, 1) - field_now)
    return north_flux - pltpu.roll(north_flux, 1, 1)


def two_steps(rows, lon_coef, lat_coef):
    for repeat in range(DYN_STEPS):
        count = len(rows)
        fluxes = [
            lon_coef[place + repeat] * (rows[place + 1] - rows[place]) for place in range(count - 1)
        ]
        rows = [
            rows[place]
            + fluxes[place]
            - fluxes[place - 1]
            + lat_term(rows[place], lat_coef[place + repeat])
            for place in range(1, count - 1)
        ]
    return rows


def coefficients(base_ref, low_mix, high_mix, lons):
    lats = base_ref.shape[1]
    first = base_ref.shape[0] - 2 * lons
    lane = lax.broadcasted_iota(jnp.int32, (1, lats), 1)
    inside = lane < lats - 1
    own_lon = [base_ref[first + lon : first + lon + 1, :] for lon in range(lons)]
    first += lons
    own_lat = [base_ref[first + lon : first + lon + 1, :] for lon in range(lons)]
    lon_coef = [low_mix[0:1, :], low_mix[1:2, :]] + own_lon + [high_mix[0:1, :], high_mix[1:2, :]]
    lat_coef = [low_mix[2:3, :], low_mix[3:4, :]] + own_lat + [high_mix[2:3, :], high_mix[3:4, :]]
    return lon_coef, [jnp.where(inside, coef, 0.0) for coef in lat_coef]


def pack_kernel(base_ref, up_ref, down_ref, *, lons):
    fields = base_ref.shape[0] // lons - 2
    mixing = fields * lons
    for out_ref, first in ((up_ref, lons - 2), (down_ref, 0)):
        for side in range(2):
            out_ref[side * fields : (side + 1) * fields, :] = base_ref[
                pl.ds(first + side, fields, stride=lons), :
            ].astype(BF16)
        mix_rows = [
            base_ref[mixing + first : mixing + first + 2, :],
            base_ref[mixing + lons + first : mixing + lons + first + 2, :],
            jnp.zeros((PACK_ROWS - 4, base_ref.shape[1]), F32),
        ]
        out_ref[2 * fields :, :] = jnp.concatenate(mix_rows, axis=0).astype(BF16)


def halo_rows(pack_ref, fields):
    return [pack_ref[side * fields : (side + 1) * fields, :].astype(F32) for side in range(2)]


def halo_mixing(pack_ref, fields):
    return pack_ref[2 * fields :, :].astype(F32)


def one_hot(cols_ref, cells):
    parts = []
    for tile in range(cols_ref.shape[0]):
        place = lax.broadcasted_iota(jnp.int32, (cells, cols_ref.shape[1]), 0)
        parts.append(jnp.where(place == cols_ref[tile : tile + 1, :], 1.0, 0.0))
    return jnp.concatenate(parts, axis=1).astype(BF16)


def live_row(count_ref, mask_ref):
    parts = []
    for tile in range(mask_ref.shape[0]):
        used = jnp.where(tile < count_ref[0, 0], 1, 0)
        parts.append((mask_ref[tile : tile + 1, :] * used).astype(F32))
    return jnp.concatenate(parts, axis=1)


def level_rows(levels, level, variables):
    return pl.ds(level, variables, stride=levels)


def solve(levels, variables, coef_ref, ratio_ref, inverse_ref, right_ref, out_ref):
    tiles, _, width = right_ref.shape
    spans = [slice(tile * width, (tile + 1) * width) for tile in range(tiles)]
    values = []
    for level in range(levels):
        inverse_now = inverse_ref[level : level + 1, :]
        if level > 0:
            carry_now = coef_ref[level - 1 : level, :] * inverse_now
        step = []
        for tile, span in enumerate(spans):
            right_now = right_ref[tile, level_rows(levels, level, variables), :]
            value_now = right_now * inverse_now[:, span]
            if level > 0:
                value_now = value_now + carry_now[:, span] * values[-1][tile]
            step.append(value_now)
        values.append(step)
    results = values[-1]
    for level in range(levels - 1, -1, -1):
        if level < levels - 1:
            ratio_now = ratio_ref[level : level + 1, :]
            results = [
                values[level][tile] - ratio_now[:, span] * results[tile]
                for tile, span in enumerate(spans)
            ]
        for tile in range(tiles):
            out_ref[tile, level_rows(levels, level, variables), :] = results[tile]


def split_tiles(ref, value):
    width = ref.shape[2]
    for tile in range(ref.shape[0]):
        ref[tile] = value[:, tile * width : (tile + 1) * width]


def join_tiles(ref):
    return jnp.concatenate([ref[tile] for tile in range(ref.shape[0])], axis=1)


def factorise(levels, coef_ref, ratio_ref, inverse_ref):
    ratio_prev = None
    for level in range(levels):
        coef_now = coef_ref[level : level + 1, :]
        divisor = 1.0 + coef_now
        if level > 0:
            below_now = coef_ref[level - 1 : level, :]
            divisor = divisor + below_now + below_now * ratio_prev
        inverse_now = 1.0 / divisor
        ratio_prev = -coef_now * inverse_now
        inverse_ref[level : level + 1, :] = inverse_now
        ratio_ref[level : level + 1, :] = ratio_prev


def by_cell(ref, rows, lons):
    return jnp.concatenate(
        [ref[pl.ds(lon, rows, stride=lons), :] for lon in range(lons)], axis=1
    )


def adjoint_kernel(
    count_ref,
    column_ref,
    cols_ref,
    mask_ref,
    adj_ref,
    coef_ref,
    ratio_ref,
    inverse_ref,
    right_ref,
    *,
    lons,
):
    fields = adj_ref.shape[1]
    levels = coef_ref.shape[0]
    spread = one_hot(cols_ref, lons * column_ref.shape[1])
    sources = by_cell(column_ref, fields + levels, lons).astype(BF16)
    picked = jnp.dot(sources, spread, preferred_element_type=F32)
    split_tiles(right_ref, picked[:fields] * live_row(count_ref, mask_ref))
    coef_ref[...] = picked[fields:]
    factorise(levels, coef_ref, ratio_ref, inverse_ref)
    solve(levels, fields // levels, coef_ref, ratio_ref, inverse_ref, right_ref, adj_ref)


def sigmoid(pre_act):
    return 0.5 * jnp.tanh(0.5 * pre_act) + 0.5


def weight_product(left_ref, right, keep_ref, send_ref, first):
    half = left_ref.shape[0] // 2
    block = min(BLOCK, half)
    core = lax.axis_index("horiz") % 2
    for out_ref, side in ((send_ref, 1 - core), (keep_ref, core)):
        for start in range(0, half, block):
            out_ref[start : start + block, first : first + right.shape[0]] = lax.dot_general(
                left_ref[pl.ds(pl.multiple_of(side * half + start, block), block), :],
                right,
                CONTRACT_LAST,
                preferred_element_type=F32,
            ).astype(BF16)


def forward_kernel(
    base_ref,
    low_ref,
    high_ref,
    cols_ref,
    adj_ref,
    weights_ref,
    w_out_ref,
    moved_ref,
    x_ref,
    act_one_ref,
    act_two_ref,
    delta_two_ref,
    keep_ref,
    send_ref,
    *,
    lons,
):
    fields = x_ref.shape[0]
    units = weights_ref.shape[0]
    cells = lons * base_ref.shape[1]
    low_rows, high_rows = halo_rows(low_ref, fields), halo_rows(high_ref, fields)
    lon_coef, lat_coef = coefficients(
        base_ref, halo_mixing(low_ref, fields), halo_mixing(high_ref, fields), lons
    )
    rows = [base_ref[pl.ds(lon, fields, stride=lons), :] for lon in range(lons)]
    rows = two_steps(low_rows + rows + high_rows, lon_coef, lat_coef)
    for lon in range(lons):
        moved_ref[lon] = rows[lon]
    spread = one_hot(cols_ref, cells)
    sources = jnp.concatenate(rows, axis=1).astype(BF16)
    x_now = jnp.dot(sources, spread, preferred_element_type=F32).astype(BF16)
    x_ref[...] = x_now
    for start in range(0, units, BLOCK):
        pre_one = jnp.dot(weights_ref[start : start + BLOCK, units:], x_now, preferred_element_type=F32)
        act_one_ref[start : start + BLOCK, :] = (pre_one * sigmoid(pre_one)).astype(BF16)
    adj_half = join_tiles(adj_ref).astype(BF16)
    for start in range(0, units, BLOCK):
        pre_two = jnp.dot(
            weights_ref[start : start + BLOCK, :units], act_one_ref[...], preferred_element_type=F32
        )
        sigma_val = sigmoid(pre_two)
        act_two_ref[start : start + BLOCK, :] = (pre_two * sigma_val).astype(BF16)
        back_two = lax.dot_general(
            w_out_ref[:, start : start + BLOCK],
            adj_half,
            CONTRACT_FIRST,
            preferred_element_type=F32,
        )
        slope = sigma_val * (1.0 + pre_two * (1.0 - sigma_val))
        delta_two_ref[start : start + BLOCK, :] = (back_two * slope).astype(BF16)
    weight_product(delta_two_ref, act_one_ref[...], keep_ref, send_ref, 0)


def backward_kernel(
    x_ref,
    act_two_ref,
    delta_two_ref,
    adj_ref,
    weights_ref,
    delta_one_ref,
    keep_ref,
    send_ref,
):
    fields = x_ref.shape[0]
    units = weights_ref.shape[0]
    x_now = x_ref[...]
    for start in range(0, units, BLOCK):
        back_one = lax.dot_general(
            weights_ref[:, start : start + BLOCK],
            delta_two_ref[...],
            CONTRACT_FIRST,
            preferred_element_type=F32,
        )
        pre_one = jnp.dot(weights_ref[start : start + BLOCK, units:], x_now, preferred_element_type=F32)
        sigma_val = sigmoid(pre_one)
        slope = sigma_val * (1.0 + pre_one * (1.0 - sigma_val))
        delta_one_ref[start : start + BLOCK, :] = (back_one * slope).astype(BF16)
    weight_product(delta_one_ref, x_now, keep_ref, send_ref, 0)
    weight_product(act_two_ref, join_tiles(adj_ref).astype(BF16), keep_ref, send_ref, fields)


def place_back(fresh, live, cols_ref, cells):
    marks = jnp.broadcast_to(live, (16, live.shape[1]))
    placed = lax.dot_general(
        jnp.concatenate([fresh * live, marks], axis=0).astype(BF16),
        one_hot(cols_ref, cells),
        CONTRACT_LAST,
        preferred_element_type=F32,
    )
    rows = fresh.shape[0]
    return placed[:rows], placed[rows : rows + 1] > 0.5


def state_kernel(
    count_ref,
    moved_ref,
    cols_ref,
    mask_ref,
    x_ref,
    act_two_ref,
    coef_ref,
    ratio_ref,
    inverse_ref,
    w_out_ref,
    state_ref,
    forced_ref,
    solved_ref,
    *,
    lons,
):
    fields = x_ref.shape[0]
    levels = coef_ref.shape[0]
    lats = moved_ref.shape[2]
    tendency = jnp.dot(w_out_ref[...], act_two_ref[...], preferred_element_type=F32)
    split_tiles(forced_ref, x_ref[...].astype(F32) + tendency)
    solve(levels, fields // levels, coef_ref, ratio_ref, inverse_ref, forced_ref, solved_ref)
    placed, taken = place_back(
        join_tiles(solved_ref), live_row(count_ref, mask_ref), cols_ref, lons * lats
    )
    for lon in range(lons):
        here = slice(lon * lats, (lon + 1) * lats)
        state_ref[pl.ds(lon, fields, stride=lons), :] = jnp.where(
            taken[:, here], placed[:, here], moved_ref[lon]
        )


def grad_kernel(
    count_ref,
    column_ref,
    cols_ref,
    mask_ref,
    delta_one_ref,
    adj_ref,
    weights_ref,
    field_ref,
    up_ref,
    down_ref,
    *,
    lons,
):
    fields, lats = field_ref.shape[1:]
    grad_x = join_tiles(adj_ref) + lax.dot_general(
        weights_ref[:, delta_one_ref.shape[0] :], delta_one_ref[...], CONTRACT_FIRST, preferred_element_type=F32
    )
    placed, taken = place_back(grad_x, live_row(count_ref, mask_ref), cols_ref, lons * lats)
    for lon in range(lons):
        here = slice(lon * lats, (lon + 1) * lats)
        field_now = jnp.where(
            taken[:, here], placed[:, here], column_ref[pl.ds(lon, fields, stride=lons), :]
        )
        field_ref[lon] = field_now
        if lon < 2:
            down_ref[lon * fields : (lon + 1) * fields, :] = field_now.astype(BF16)
        if lon >= lons - 2:
            side = lon - (lons - 2)
            up_ref[side * fields : (side + 1) * fields, :] = field_now.astype(BF16)


def last_kernel(field_ref, low_ref, high_ref, low_mix_ref, high_mix_ref, base_ref, out_ref, *, lons):
    fields = field_ref.shape[1]
    low_rows, high_rows = halo_rows(low_ref, fields), halo_rows(high_ref, fields)
    lon_coef, lat_coef = coefficients(
        base_ref, halo_mixing(low_mix_ref, fields), halo_mixing(high_mix_ref, fields), lons
    )
    rows = [field_ref[lon] for lon in range(lons)]
    rows = two_steps(low_rows + rows + high_rows, lon_coef, lat_coef)
    for lon in range(lons):
        out_ref[pl.ds(lon, fields, stride=lons), :] = rows[lon]


CORE = ("horiz", 0, 2)
CHIPS = ("horiz", 1, 4)
MEMBERS = ("ens", 0, 4)
MEMBER_LOW, MEMBER_HIGH = ("ens", 0, 2), ("ens", 1, 2)


def position(stage):
    axis, shift, parts = stage
    return lax.axis_index(axis) // (1 << shift) % parts


def sum_kernel(*refs, terms, stage, factor):
    ins, outs = refs[:terms], refs[terms:]
    rows = outs[0].shape[0]
    for index, out_ref in enumerate(outs):
        here = pl.ds(0, rows)
        if stage is not None:
            start = (position(stage) ^ (-index % len(outs))) * rows
            here = pl.ds(pl.multiple_of(start, rows), rows)
        total = ins[0][here, :].astype(F32)
        for ref in ins[1:]:
            total = total + ref[here, :].astype(F32)
        out_ref[...] = (total * factor).astype(BF16)


def join_kernel(*refs, stage, groups, cuts):
    ins, outs = refs[:-cuts], refs[-cuts:]
    count = len(ins) // groups
    rows, columns = ins[0].shape
    width = outs[0].shape[1]
    part = min(width, columns)
    for k in range(count):
        here = pl.ds(pl.multiple_of((position(stage) ^ k) * rows, rows), rows)
        for group in range(groups):
            for start in range(0, columns, part):
                first = group * columns + start
                outs[first // width][here, first % width : first % width + part] = ins[
                    group * count + k
                ][:, start : start + part]


def member_order():
    member, core = lax.axis_index("ens"), lax.axis_index("horiz") % 2
    return [member, member ^ (1 + core), member ^ (2 - core), member ^ 3]


def core_sum_kernel(keep_mid, got_mid, keep_small, got_small, *outs):
    rows = outs[0].shape[0]
    for member, out_ref in zip(member_order(), outs):
        here = pl.ds(pl.multiple_of(member * rows, rows), rows)
        first = 0
        for keep_ref, got_ref in ((keep_mid, got_mid), (keep_small, got_small)):
            columns = keep_ref.shape[1]
            out_ref[:, first : first + columns] = (
                keep_ref[here, :].astype(F32) + got_ref[here, :].astype(F32)
            ).astype(BF16)
            first += columns


def final_kernel(mid_half, small_half, *refs):
    mid_ref, in_ref, out_ref = refs[-3:]
    fields = in_ref.shape[1]
    mid_ref[...] = mid_half[...].astype(F32)

    @pl.when(pl.program_id(0) == 0)
    def _():
        in_ref[...] = small_half[:, :fields].astype(F32)
        out_ref[...] = small_half[:, fields:].astype(F32).T


def final(rows, other, before, fields):
    half, columns = rows.shape
    units = 2 * half
    block = units // 4

    def place():
        core = lax.axis_index("horiz") % 2
        return 1 - core if other else core

    return pl.pallas_call(
        final_kernel,
        grid=(units // block,),
        out_shape=[
            jax.ShapeDtypeStruct(shape, F32)
            for shape in ((units, units), (units, fields), (fields, units))
        ],
        in_specs=[
            pl.BlockSpec((half, block), lambda step: (0, step)),
            pl.BlockSpec((half, 2 * fields), lambda step: (0, units // (2 * fields))),
        ]
        + [pl.BlockSpec(memory_space=pl.ANY)] * len(before),
        out_specs=[
            pl.BlockSpec((half, block), lambda step: (place(), step)),
            pl.BlockSpec((half, fields), lambda step: (place(), 0)),
            pl.BlockSpec((fields, half), lambda step: (0, place())),
        ],
        input_output_aliases={2 + index: index for index in range(len(before))},
        compiler_params=pltpu.CompilerParams(vmem_limit_bytes=VMEM_LIMIT),
    )(rows, rows, *before)


def exchange(arrays, stage):
    axis, shift, _ = stage
    count = lax.axis_size(axis)
    sent = {}
    for k in range(len(arrays), 0, -1):
        route = [(i, i ^ (k << shift)) for i in range(count)]
        sent[k] = lax.ppermute(arrays[k - 1], axis, route)
    return [sent[k] for k in range(1, len(arrays) + 1)]


def to_member(array, second):
    members, count = lax.axis_size("ens"), lax.axis_size("horiz")
    route = []
    for member in range(members):
        for place in range(count):
            neighbour = member ^ (1 << (place % 2 ^ second))
            route.append((member * count + place, neighbour * count + place))
    return lax.ppermute(array, ("ens", "horiz"), route)


def collect_members(one, two):
    (low_one,) = exchange([one], MEMBER_LOW)
    (high_two,) = exchange([two], MEMBER_HIGH)
    (high_one,) = exchange([one], MEMBER_HIGH)
    (low_two,) = exchange([two], MEMBER_LOW)
    (far_one,) = exchange([low_one], MEMBER_HIGH)
    (far_two,) = exchange([high_two], MEMBER_LOW)
    return [one, low_one, high_one, far_one], [two, low_two, high_two, far_two]


def add(terms, stage, factor=1.0):
    rows, columns = terms[0].shape
    parts = 1 if stage is None else stage[2]
    return call(
        sum_kernel,
        [((rows // parts, columns), BF16)] * parts,
        terms=len(terms),
        stage=stage,
        factor=factor,
    )(*terms)


def join(groups, stage, cuts=1):
    rows, columns = groups[0][0].shape
    shape = (rows * len(groups[0]), columns * len(groups) // cuts)
    return call(
        join_kernel, [(shape, BF16)] * cuts, stage=stage, groups=len(groups), cuts=cuts
    )(*[piece for group in groups for piece in group])


def reduce_to(terms, stage):
    parts = add(terms, stage)
    return [parts[0]] + exchange(parts[:0:-1], stage)[::-1]


def collect(piece, stage):
    return [piece] + exchange([piece] * (stage[2] - 1), stage)


def tie(*values):
    return lax.optimization_barrier(values)


def over_all_chips(piece, factor):
    core = lax.axis_index("horiz") % 2
    both = jnp.stack([jnp.where(core == side, piece, 0.0).astype(F32) for side in range(2)])
    return (lax.psum(both, "horiz")[core] * factor).astype(BF16)


def to_neighbours(upward, downward, axis):
    count = lax.axis_size(axis)
    forward = [(i, (i + 1) % count) for i in range(count)]
    backward = [(target, source) for source, target in forward]
    return lax.ppermute(upward, axis, forward), lax.ppermute(downward, axis, backward)


def per_device(
    prognostic, diffusivity, mixing, cotangent, tile_cols, pad_mask, tile_count, w_in, w_mid, w_out
):
    fields, lons, lats = prognostic.shape[1:]
    levels = diffusivity.shape[1]
    units = w_mid.shape[0]
    tiles, width = tile_cols.shape[2:]
    slots = tiles * width
    base = jnp.concatenate([prognostic[0], mixing], axis=0).reshape((fields + 2) * lons, lats)
    column = jnp.concatenate([cotangent[0], diffusivity[0]], axis=0)
    column = column.reshape((fields + levels) * lons, lats)
    weights = jnp.concatenate([w_mid, w_in], axis=1)
    cols, mask = tile_cols[0, 0], pad_mask[0, 0]

    packed = ((2 * fields + PACK_ROWS, lats), BF16)
    up_pack, down_pack = call(pack_kernel, [packed, packed], lons=lons)(base)
    low_pack, high_pack = to_neighbours(up_pack, down_pack, "horiz")

    adjoint, coef, ratio, inverse = call(
        adjoint_kernel,
        [((tiles, fields, width), F32)] + [((levels, slots), F32)] * 3,
        scratch=[pltpu.VMEM((tiles, fields, width), F32)],
        smem=(0,),
        moved=30 * 10**6,
        lons=lons,
    )(tile_count, column, cols, mask)

    hidden = ((units, slots), BF16)
    half = ((units // 2, units), BF16)
    moved, x_now, act_one, act_two, delta_two, keep_mid, send_mid = call(
        forward_kernel,
        [((lons, fields, lats), F32), ((fields, slots), BF16), hidden, hidden, hidden, half, half],
        moved=15 * 10**6,
        lons=lons,
    )(base, low_pack, high_pack, cols, adjoint, weights, w_out)
    column_total = lax.axis_size("ens") * lax.axis_size("horiz") * lons * lats
    factor = 1.0 / math.sqrt(column_total)
    (got_mid,) = exchange([send_mid], CORE)

    half = ((units // 2, 2 * fields), BF16)
    delta_one, keep_small, send_small = call(
        backward_kernel, [hidden, half, half], moved=4 * 10**6
    )(x_now, act_two, delta_two, adjoint, weights)
    (got_small,) = exchange([send_small], CORE)

    packed = ((2 * fields, lats), BF16)
    field, up_rows, down_rows = call(
        grad_kernel,
        [((lons, fields, lats), F32), packed, packed],
        smem=(0,),
        lons=lons,
    )(tile_count, column, cols, mask, delta_one, adjoint, weights)
    got_small, field = tie(got_small, field)

    members = lax.axis_size("ens")
    parts = call(core_sum_kernel, [((units // 2 // members, units + 2 * fields), BF16)] * members)(
        keep_mid, got_mid, keep_small, got_small
    )
    own, first, second, far = parts
    got_far = to_member(far, 0)
    got_first = to_member(first, 0)

    act_two, up_rows, down_rows = tie(act_two, up_rows, down_rows, parts)[:3]
    halos = to_neighbours(up_rows, down_rows, "horiz")
    (state_rows,) = call(
        state_kernel,
        [((fields * lons, lats), F32)],
        scratch=[pltpu.VMEM((tiles, fields, width), F32)] * 2,
        smem=(0,),
        lons=lons,
    )(tile_count, moved, cols, mask, x_now, act_two, coef, ratio, inverse, w_out)
    got_far, state_rows, halos = tie(got_far, state_rows, halos)
    terms = [own, got_first, to_member(add([second, got_far], None)[0], 1)]
    (grad_rows,) = call(last_kernel, [((fields * lons, lats), F32)], lons=lons)(
        field, *halos, low_pack, high_pack, base
    )
    terms, grad_rows = tie(terms, grad_rows)

    if lax.axis_size("horiz") == 8:
        terms = reduce_to(terms, CHIPS)
        halves = join([collect(add(terms, None, factor)[0], CHIPS)], CHIPS, cuts=2)
    else:
        halves = jnp.split(over_all_chips(add(terms, None)[0], factor), 2, axis=1)
    (own,) = join(collect_members(*halves), MEMBERS)
    (got,) = exchange([own], CORE)
    half_done = final(own, False, [], fields)
    grad_mid, grad_in, grad_out = final(got, True, half_done, fields)
    return (
        state_rows.reshape(prognostic.shape),
        grad_rows.reshape(prognostic.shape),
        grad_in,
        grad_mid,
        grad_out,
    )


def solution(mesh):
    placed = (
        P("ens", None, "horiz", None),
        P("ens", None, "horiz", None),
        P(None, "horiz", None),
        P("ens", None, "horiz", None),
        P("ens", "horiz", None, None),
        P("ens", "horiz", None, None),
        P("ens", "horiz"),
        P(),
        P(),
        P(),
    )
    return jax.shard_map(
        per_device,
        mesh=mesh,
        in_specs=placed,
        out_specs=(P("ens", None, "horiz", None), P("ens", None, "horiz", None), P(), P(), P()),
        check_vma=False,
    )
```

```python
import functools
import math

import jax
import jax.numpy as jnp
from jax import lax
from jax.experimental import pallas as pl
from jax.experimental.pallas import tpu as pltpu
from jax.sharding import PartitionSpec as P

DYN_STEPS = 2
BLOCK = 512
COLUMN_BLOCK = 256
PACK_ROWS = 16
VMEM_LIMIT = 32 * 1024 * 1024
F32 = jnp.float32
BF16 = jnp.bfloat16
CONTRACT_LAST = (((1,), (1,)), ((), ()))
CONTRACT_FIRST = (((0,), (0,)), ((), ()))


def call(kernel, outs, scratch=(), smem=(), flops=0, moved=0, **names):
    def run(*operands):
        specs = [
            pl.BlockSpec(memory_space=pltpu.SMEM if place in smem else pltpu.VMEM)
            for place in range(len(operands))
        ]
        return pl.pallas_call(
            functools.partial(kernel, **names),
            out_shape=[jax.ShapeDtypeStruct(shape, dtype) for shape, dtype in outs],
            in_specs=specs,
            out_specs=[pl.BlockSpec(memory_space=pltpu.VMEM)] * len(outs),
            scratch_shapes=list(scratch),
            compiler_params=pltpu.CompilerParams(vmem_limit_bytes=VMEM_LIMIT),
            cost_estimate=pl.CostEstimate(flops=flops, bytes_accessed=moved, transcendentals=0),
        )(*operands)

    return run


def lat_term(field_now, coef_masked):
    lats = field_now.shape[1]
    north_flux = coef_masked * (pltpu.roll(field_now, lats - 1, 1) - field_now)
    return north_flux - pltpu.roll(north_flux, 1, 1)


def two_steps(rows, lon_coef, lat_coef):
    for repeat in range(DYN_STEPS):
        count = len(rows)
        fluxes = [
            lon_coef[place + repeat] * (rows[place + 1] - rows[place]) for place in range(count - 1)
        ]
        rows = [
            rows[place]
            + fluxes[place]
            - fluxes[place - 1]
            + lat_term(rows[place], lat_coef[place + repeat])
            for place in range(1, count - 1)
        ]
    return rows


def coefficients(base_ref, low_mix, high_mix, lons):
    lats = base_ref.shape[1]
    first = base_ref.shape[0] - 2 * lons
    lane = lax.broadcasted_iota(jnp.int32, (1, lats), 1)
    inside = lane < lats - 1
    own_lon = [base_ref[first + lon : first + lon + 1, :] for lon in range(lons)]
    first += lons
    own_lat = [base_ref[first + lon : first + lon + 1, :] for lon in range(lons)]
    lon_coef = [low_mix[0:1, :], low_mix[1:2, :]] + own_lon + [high_mix[0:1, :], high_mix[1:2, :]]
    lat_coef = [low_mix[2:3, :], low_mix[3:4, :]] + own_lat + [high_mix[2:3, :], high_mix[3:4, :]]
    return lon_coef, [jnp.where(inside, coef, 0.0) for coef in lat_coef]


def pack_kernel(base_ref, up_ref, down_ref, *, lons):
    fields = base_ref.shape[0] // lons - 2
    mixing = fields * lons
    for out_ref, first in ((up_ref, lons - 2), (down_ref, 0)):
        for side in range(2):
            out_ref[side * fields : (side + 1) * fields, :] = base_ref[
                pl.ds(first + side, fields, stride=lons), :
            ].astype(BF16)
        mix_rows = [
            base_ref[mixing + first : mixing + first + 2, :],
            base_ref[mixing + lons + first : mixing + lons + first + 2, :],
            jnp.zeros((PACK_ROWS - 4, base_ref.shape[1]), F32),
        ]
        out_ref[2 * fields :, :] = jnp.concatenate(mix_rows, axis=0).astype(BF16)


def halo_rows(pack_ref, fields):
    return [pack_ref[side * fields : (side + 1) * fields, :].astype(F32) for side in range(2)]


def halo_mixing(pack_ref, fields):
    return pack_ref[2 * fields :, :].astype(F32)


def one_hot(cols_ref, cells):
    parts = []
    for tile in range(cols_ref.shape[0]):
        place = lax.broadcasted_iota(jnp.int32, (cells, cols_ref.shape[1]), 0)
        parts.append(jnp.where(place == cols_ref[tile : tile + 1, :], 1.0, 0.0))
    return jnp.concatenate(parts, axis=1).astype(BF16)


def live_row(count_ref, mask_ref):
    parts = []
    for tile in range(mask_ref.shape[0]):
        used = jnp.where(tile < count_ref[0, 0], 1, 0)
        parts.append((mask_ref[tile : tile + 1, :] * used).astype(F32))
    return jnp.concatenate(parts, axis=1)


def level_rows(levels, level, variables):
    return pl.ds(level, variables, stride=levels)


def solve(levels, variables, coef_ref, ratio_ref, inverse_ref, right_ref, out_ref):
    tiles, _, width = right_ref.shape
    spans = [slice(tile * width, (tile + 1) * width) for tile in range(tiles)]
    values = []
    for level in range(levels):
        inverse_now = inverse_ref[level : level + 1, :]
        if level > 0:
            carry_now = coef_ref[level - 1 : level, :] * inverse_now
        step = []
        for tile, span in enumerate(spans):
            right_now = right_ref[tile, level_rows(levels, level, variables), :]
            value_now = right_now * inverse_now[:, span]
            if level > 0:
                value_now = value_now + carry_now[:, span] * values[-1][tile]
            step.append(value_now)
        values.append(step)
    results = values[-1]
    for level in range(levels - 1, -1, -1):
        if level < levels - 1:
            ratio_now = ratio_ref[level : level + 1, :]
            results = [
                values[level][tile] - ratio_now[:, span] * results[tile]
                for tile, span in enumerate(spans)
            ]
        for tile in range(tiles):
            out_ref[tile, level_rows(levels, level, variables), :] = results[tile]


def split_tiles(ref, value):
    width = ref.shape[2]
    for tile in range(ref.shape[0]):
        ref[tile] = value[:, tile * width : (tile + 1) * width]


def join_tiles(ref):
    return jnp.concatenate([ref[tile] for tile in range(ref.shape[0])], axis=1)


def factorise(levels, coef_ref, ratio_ref, inverse_ref):
    ratio_prev = None
    for level in range(levels):
        coef_now = coef_ref[level : level + 1, :]
        divisor = 1.0 + coef_now
        if level > 0:
            below_now = coef_ref[level - 1 : level, :]
            divisor = divisor + below_now + below_now * ratio_prev
        inverse_now = 1.0 / divisor
        ratio_prev = -coef_now * inverse_now
        inverse_ref[level : level + 1, :] = inverse_now
        ratio_ref[level : level + 1, :] = ratio_prev


def by_cell(ref, rows, lons):
    return jnp.concatenate(
        [ref[pl.ds(lon, rows, stride=lons), :] for lon in range(lons)], axis=1
    )


def adjoint_kernel(
    count_ref,
    column_ref,
    cols_ref,
    mask_ref,
    adj_ref,
    coef_ref,
    ratio_ref,
    inverse_ref,
    right_ref,
    *,
    lons,
):
    fields = adj_ref.shape[1]
    levels = coef_ref.shape[0]
    spread = one_hot(cols_ref, lons * column_ref.shape[1])
    sources = by_cell(column_ref, fields + levels, lons).astype(BF16)
    picked = jnp.dot(sources, spread, preferred_element_type=F32)
    split_tiles(right_ref, picked[:fields] * live_row(count_ref, mask_ref))
    coef_ref[...] = picked[fields:]
    factorise(levels, coef_ref, ratio_ref, inverse_ref)
    solve(levels, fields // levels, coef_ref, ratio_ref, inverse_ref, right_ref, adj_ref)


def sigmoid(pre_act):
    return 0.5 * jnp.tanh(0.5 * pre_act) + 0.5


def weight_product(left_ref, right, keep_ref, send_ref, first):
    half = left_ref.shape[0] // 2
    core = lax.axis_index("horiz") % 2
    sides = [left_ref[pl.ds(pl.multiple_of(side * half, half), half), :] for side in (1 - core, core)]
    left = jnp.concatenate(sides, axis=0)
    block = min(COLUMN_BLOCK, right.shape[0])
    for start in range(0, right.shape[0], block):
        product = lax.dot_general(
            left, right[start : start + block, :], CONTRACT_LAST, preferred_element_type=F32
        ).astype(BF16)
        here = slice(first + start, first + start + block)
        send_ref[:, here] = product[:half]
        keep_ref[:, here] = product[half:]


def forward_kernel(
    base_ref,
    low_ref,
    high_ref,
    cols_ref,
    adj_ref,
    weights_ref,
    w_out_ref,
    moved_ref,
    x_ref,
    act_one_ref,
    act_two_ref,
    delta_two_ref,
    keep_ref,
    send_ref,
    *,
    lons,
):
    fields = x_ref.shape[0]
    units = weights_ref.shape[0]
    cells = lons * base_ref.shape[1]
    low_rows, high_rows = halo_rows(low_ref, fields), halo_rows(high_ref, fields)
    lon_coef, lat_coef = coefficients(
        base_ref, halo_mixing(low_ref, fields), halo_mixing(high_ref, fields), lons
    )
    rows = [base_ref[pl.ds(lon, fields, stride=lons), :] for lon in range(lons)]
    rows = two_steps(low_rows + rows + high_rows, lon_coef, lat_coef)
    for lon in range(lons):
        moved_ref[lon] = rows[lon]
    spread = one_hot(cols_ref, cells)
    sources = jnp.concatenate(rows, axis=1).astype(BF16)
    x_now = jnp.dot(sources, spread, preferred_element_type=F32).astype(BF16)
    x_ref[...] = x_now
    for start in range(0, units, BLOCK):
        pre_one = jnp.dot(weights_ref[start : start + BLOCK, units:], x_now, preferred_element_type=F32)
        act_one_ref[start : start + BLOCK, :] = (pre_one * sigmoid(pre_one)).astype(BF16)
    adj_half = join_tiles(adj_ref).astype(BF16)
    for start in range(0, units, BLOCK):
        pre_two = jnp.dot(
            weights_ref[start : start + BLOCK, :units], act_one_ref[...], preferred_element_type=F32
        )
        sigma_val = sigmoid(pre_two)
        act_two_ref[start : start + BLOCK, :] = (pre_two * sigma_val).astype(BF16)
        back_two = lax.dot_general(
            w_out_ref[:, start : start + BLOCK],
            adj_half,
            CONTRACT_FIRST,
            preferred_element_type=F32,
        )
        slope = sigma_val * (1.0 + pre_two * (1.0 - sigma_val))
        delta_two_ref[start : start + BLOCK, :] = (back_two * slope).astype(BF16)
    weight_product(delta_two_ref, act_one_ref[...], keep_ref, send_ref, 0)


def backward_kernel(
    x_ref,
    act_two_ref,
    delta_two_ref,
    adj_ref,
    weights_ref,
    delta_one_ref,
    keep_ref,
    send_ref,
):
    fields = x_ref.shape[0]
    units = weights_ref.shape[0]
    x_now = x_ref[...]
    for start in range(0, units, BLOCK):
        back_one = lax.dot_general(
            weights_ref[:, start : start + BLOCK],
            delta_two_ref[...],
            CONTRACT_FIRST,
            preferred_element_type=F32,
        )
        pre_one = jnp.dot(weights_ref[start : start + BLOCK, units:], x_now, preferred_element_type=F32)
        sigma_val = sigmoid(pre_one)
        slope = sigma_val * (1.0 + pre_one * (1.0 - sigma_val))
        delta_one_ref[start : start + BLOCK, :] = (back_one * slope).astype(BF16)
    weight_product(delta_one_ref, x_now, keep_ref, send_ref, 0)
    weight_product(act_two_ref, join_tiles(adj_ref).astype(BF16), keep_ref, send_ref, fields)


def place_back(fresh, live, cols_ref, cells):
    marks = jnp.broadcast_to(live, (16, live.shape[1]))
    placed = lax.dot_general(
        jnp.concatenate([fresh * live, marks], axis=0).astype(BF16),
        one_hot(cols_ref, cells),
        CONTRACT_LAST,
        preferred_element_type=F32,
    )
    rows = fresh.shape[0]
    return placed[:rows], placed[rows : rows + 1] > 0.5


def state_kernel(
    count_ref,
    moved_ref,
    cols_ref,
    mask_ref,
    x_ref,
    act_two_ref,
    coef_ref,
    ratio_ref,
    inverse_ref,
    w_out_ref,
    state_ref,
    forced_ref,
    solved_ref,
    *,
    lons,
):
    fields = x_ref.shape[0]
    levels = coef_ref.shape[0]
    lats = moved_ref.shape[2]
    tendency = jnp.dot(w_out_ref[...], act_two_ref[...], preferred_element_type=F32)
    split_tiles(forced_ref, x_ref[...].astype(F32) + tendency)
    solve(levels, fields // levels, coef_ref, ratio_ref, inverse_ref, forced_ref, solved_ref)
    placed, taken = place_back(
        join_tiles(solved_ref), live_row(count_ref, mask_ref), cols_ref, lons * lats
    )
    for lon in range(lons):
        here = slice(lon * lats, (lon + 1) * lats)
        state_ref[pl.ds(lon, fields, stride=lons), :] = jnp.where(
            taken[:, here], placed[:, here], moved_ref[lon]
        )


def grad_kernel(
    count_ref,
    column_ref,
    cols_ref,
    mask_ref,
    delta_one_ref,
    adj_ref,
    weights_ref,
    field_ref,
    up_ref,
    down_ref,
    *,
    lons,
):
    fields, lats = field_ref.shape[1:]
    grad_x = join_tiles(adj_ref) + lax.dot_general(
        weights_ref[:, delta_one_ref.shape[0] :], delta_one_ref[...], CONTRACT_FIRST, preferred_element_type=F32
    )
    placed, taken = place_back(grad_x, live_row(count_ref, mask_ref), cols_ref, lons * lats)
    for lon in range(lons):
        here = slice(lon * lats, (lon + 1) * lats)
        field_now = jnp.where(
            taken[:, here], placed[:, here], column_ref[pl.ds(lon, fields, stride=lons), :]
        )
        field_ref[lon] = field_now
        if lon < 2:
            down_ref[lon * fields : (lon + 1) * fields, :] = field_now.astype(BF16)
        if lon >= lons - 2:
            side = lon - (lons - 2)
            up_ref[side * fields : (side + 1) * fields, :] = field_now.astype(BF16)


def last_kernel(field_ref, low_ref, high_ref, low_mix_ref, high_mix_ref, base_ref, out_ref, *, lons):
    fields = field_ref.shape[1]
    low_rows, high_rows = halo_rows(low_ref, fields), halo_rows(high_ref, fields)
    lon_coef, lat_coef = coefficients(
        base_ref, halo_mixing(low_mix_ref, fields), halo_mixing(high_mix_ref, fields), lons
    )
    rows = [field_ref[lon] for lon in range(lons)]
    rows = two_steps(low_rows + rows + high_rows, lon_coef, lat_coef)
    for lon in range(lons):
        out_ref[pl.ds(lon, fields, stride=lons), :] = rows[lon]


CORE = ("horiz", 0, 2)
CHIPS = ("horiz", 1, 4)
MEMBERS = ("ens", 0, 4)
MEMBER_LOW, MEMBER_HIGH = ("ens", 0, 2), ("ens", 1, 2)


def position(stage):
    axis, shift, parts = stage
    return lax.axis_index(axis) // (1 << shift) % parts


def sum_kernel(*refs, terms, stage, factor):
    ins, outs = refs[:terms], refs[terms:]
    rows = outs[0].shape[0]
    for index, out_ref in enumerate(outs):
        here = pl.ds(0, rows)
        if stage is not None:
            start = (position(stage) ^ (-index % len(outs))) * rows
            here = pl.ds(pl.multiple_of(start, rows), rows)
        total = ins[0][here, :].astype(F32)
        for ref in ins[1:]:
            total = total + ref[here, :].astype(F32)
        out_ref[...] = (total * factor).astype(BF16)


def join_kernel(*refs, stage, groups, cuts):
    ins, outs = refs[:-cuts], refs[-cuts:]
    count = len(ins) // groups
    rows, columns = ins[0].shape
    width = outs[0].shape[1]
    part = min(width, columns)
    for k in range(count):
        here = pl.ds(pl.multiple_of((position(stage) ^ k) * rows, rows), rows)
        for group in range(groups):
            for start in range(0, columns, part):
                first = group * columns + start
                outs[first // width][here, first % width : first % width + part] = ins[
                    group * count + k
                ][:, start : start + part]


def member_order():
    member, core = lax.axis_index("ens"), lax.axis_index("horiz") % 2
    return [member, member ^ (1 + core), member ^ (2 - core), member ^ 3]


def core_sum_kernel(keep_mid, got_mid, keep_small, got_small, *outs):
    rows = outs[0].shape[0]
    for member, out_ref in zip(member_order(), outs):
        here = pl.ds(pl.multiple_of(member * rows, rows), rows)
        first = 0
        for keep_ref, got_ref in ((keep_mid, got_mid), (keep_small, got_small)):
            columns = keep_ref.shape[1]
            out_ref[:, first : first + columns] = (
                keep_ref[here, :].astype(F32) + got_ref[here, :].astype(F32)
            ).astype(BF16)
            first += columns


def final_kernel(mid_half, small_half, *refs):
    mid_ref, in_ref, out_ref = refs[-3:]
    fields = in_ref.shape[1]
    mid_ref[...] = mid_half[...].astype(F32)

    @pl.when(pl.program_id(0) == 0)
    def _():
        in_ref[...] = small_half[:, :fields].astype(F32)
        out_ref[...] = small_half[:, fields:].astype(F32).T


def final(rows, other, before, fields):
    half, columns = rows.shape
    units = 2 * half
    block = units // 2

    def place():
        core = lax.axis_index("horiz") % 2
        return 1 - core if other else core

    return pl.pallas_call(
        final_kernel,
        grid=(units // block,),
        out_shape=[
            jax.ShapeDtypeStruct(shape, F32)
            for shape in ((units, units), (units, fields), (fields, units))
        ],
        in_specs=[
            pl.BlockSpec((half, block), lambda step: (0, step)),
            pl.BlockSpec((half, 2 * fields), lambda step: (0, units // (2 * fields))),
        ]
        + [pl.BlockSpec(memory_space=pl.ANY)] * len(before),
        out_specs=[
            pl.BlockSpec((half, block), lambda step: (place(), step)),
            pl.BlockSpec((half, fields), lambda step: (place(), 0)),
            pl.BlockSpec((fields, half), lambda step: (0, place())),
        ],
        input_output_aliases={2 + index: index for index in range(len(before))},
        compiler_params=pltpu.CompilerParams(vmem_limit_bytes=VMEM_LIMIT),
    )(rows, rows, *before)


def exchange(arrays, stage):
    axis, shift, _ = stage
    count = lax.axis_size(axis)
    sent = {}
    for k in range(len(arrays), 0, -1):
        route = [(i, i ^ (k << shift)) for i in range(count)]
        sent[k] = lax.ppermute(arrays[k - 1], axis, route)
    return [sent[k] for k in range(1, len(arrays) + 1)]


def to_member(array, second):
    members, count = lax.axis_size("ens"), lax.axis_size("horiz")
    route = []
    for member in range(members):
        for place in range(count):
            neighbour = member ^ (1 << (place % 2 ^ second))
            route.append((member * count + place, neighbour * count + place))
    return lax.ppermute(array, ("ens", "horiz"), route)


def collect_members(one, two):
    (low_one,) = exchange([one], MEMBER_LOW)
    (high_two,) = exchange([two], MEMBER_HIGH)
    (high_one,) = exchange([one], MEMBER_HIGH)
    (low_two,) = exchange([two], MEMBER_LOW)
    (far_one,) = exchange([low_one], MEMBER_HIGH)
    (far_two,) = exchange([high_two], MEMBER_LOW)
    return [one, low_one, high_one, far_one], [two, low_two, high_two, far_two]


def add(terms, stage, factor=1.0):
    rows, columns = terms[0].shape
    parts = 1 if stage is None else stage[2]
    return call(
        sum_kernel,
        [((rows // parts, columns), BF16)] * parts,
        terms=len(terms),
        stage=stage,
        factor=factor,
    )(*terms)


def join(groups, stage, cuts=1):
    rows, columns = groups[0][0].shape
    shape = (rows * len(groups[0]), columns * len(groups) // cuts)
    return call(
        join_kernel, [(shape, BF16)] * cuts, stage=stage, groups=len(groups), cuts=cuts
    )(*[piece for group in groups for piece in group])


def reduce_to(terms, stage):
    parts = add(terms, stage)
    return [parts[0]] + exchange(parts[:0:-1], stage)[::-1]


def collect(piece, stage):
    return [piece] + exchange([piece] * (stage[2] - 1), stage)


def tie(*values):
    return lax.optimization_barrier(values)


def over_all_chips(piece, factor):
    core = lax.axis_index("horiz") % 2
    both = jnp.stack([jnp.where(core == side, piece, 0.0).astype(F32) for side in range(2)])
    return (lax.psum(both, "horiz")[core] * factor).astype(BF16)


def to_neighbours(upward, downward, axis):
    count = lax.axis_size(axis)
    forward = [(i, (i + 1) % count) for i in range(count)]
    backward = [(target, source) for source, target in forward]
    return lax.ppermute(upward, axis, forward), lax.ppermute(downward, axis, backward)


def per_device(
    prognostic, diffusivity, mixing, cotangent, tile_cols, pad_mask, tile_count, w_in, w_mid, w_out
):
    fields, lons, lats = prognostic.shape[1:]
    levels = diffusivity.shape[1]
    units = w_mid.shape[0]
    tiles, width = tile_cols.shape[2:]
    slots = tiles * width
    base = jnp.concatenate([prognostic[0], mixing], axis=0).reshape((fields + 2) * lons, lats)
    column = jnp.concatenate([cotangent[0], diffusivity[0]], axis=0)
    column = column.reshape((fields + levels) * lons, lats)
    weights = jnp.concatenate([w_mid, w_in], axis=1)
    cols, mask = tile_cols[0, 0], pad_mask[0, 0]

    packed = ((2 * fields + PACK_ROWS, lats), BF16)
    up_pack, down_pack = call(pack_kernel, [packed, packed], lons=lons)(base)
    low_pack, high_pack = to_neighbours(up_pack, down_pack, "horiz")

    adjoint, coef, ratio, inverse = call(
        adjoint_kernel,
        [((tiles, fields, width), F32)] + [((levels, slots), F32)] * 3,
        scratch=[pltpu.VMEM((tiles, fields, width), F32)],
        smem=(0,),
        moved=30 * 10**6,
        lons=lons,
    )(tile_count, column, cols, mask)

    hidden = ((units, slots), BF16)
    half = ((units // 2, units), BF16)
    moved, x_now, act_one, act_two, delta_two, keep_mid, send_mid = call(
        forward_kernel,
        [((lons, fields, lats), F32), ((fields, slots), BF16), hidden, hidden, hidden, half, half],
        moved=15 * 10**6,
        lons=lons,
    )(base, low_pack, high_pack, cols, adjoint, weights, w_out)
    column_total = lax.axis_size("ens") * lax.axis_size("horiz") * lons * lats
    factor = 1.0 / math.sqrt(column_total)
    (got_mid,) = exchange([send_mid], CORE)

    half = ((units // 2, 2 * fields), BF16)
    delta_one, keep_small, send_small = call(
        backward_kernel, [hidden, half, half], moved=4 * 10**6
    )(x_now, act_two, delta_two, adjoint, weights)
    (got_small,) = exchange([send_small], CORE)

    packed = ((2 * fields, lats), BF16)
    field, up_rows, down_rows = call(
        grad_kernel,
        [((lons, fields, lats), F32), packed, packed],
        smem=(0,),
        lons=lons,
    )(tile_count, column, cols, mask, delta_one, adjoint, weights)
    got_small, field = tie(got_small, field)

    members = lax.axis_size("ens")
    parts = call(core_sum_kernel, [((units // 2 // members, units + 2 * fields), BF16)] * members)(
        keep_mid, got_mid, keep_small, got_small
    )
    own, first, second, far = parts
    got_far = to_member(far, 0)
    got_first = to_member(first, 0)

    act_two, up_rows, down_rows = tie(act_two, up_rows, down_rows, parts)[:3]
    halos = to_neighbours(up_rows, down_rows, "horiz")
    (state_rows,) = call(
        state_kernel,
        [((fields * lons, lats), F32)],
        scratch=[pltpu.VMEM((tiles, fields, width), F32)] * 2,
        smem=(0,),
        lons=lons,
    )(tile_count, moved, cols, mask, x_now, act_two, coef, ratio, inverse, w_out)
    got_far, state_rows, halos = tie(got_far, state_rows, halos)
    terms = [own, got_first, to_member(add([second, got_far], None)[0], 1)]
    (grad_rows,) = call(last_kernel, [((fields * lons, lats), F32)], lons=lons)(
        field, *halos, low_pack, high_pack, base
    )
    terms, grad_rows = tie(terms, grad_rows)

    if lax.axis_size("horiz") == 8:
        terms = reduce_to(terms, CHIPS)
        halves = join([collect(add(terms, None, factor)[0], CHIPS)], CHIPS, cuts=2)
    else:
        halves = jnp.split(over_all_chips(add(terms, None)[0], factor), 2, axis=1)
    (own,) = join(collect_members(*halves), MEMBERS)
    (got,) = exchange([own], CORE)
    half_done = final(own, False, [], fields)
    grad_mid, grad_in, grad_out = final(got, True, half_done, fields)
    return (
        state_rows.reshape(prognostic.shape),
        grad_rows.reshape(prognostic.shape),
        grad_in,
        grad_mid,
        grad_out,
    )


def solution(mesh):
    placed = (
        P("ens", None, "horiz", None),
        P("ens", None, "horiz", None),
        P(None, "horiz", None),
        P("ens", None, "horiz", None),
        P("ens", "horiz", None, None),
        P("ens", "horiz", None, None),
        P("ens", "horiz"),
        P(),
        P(),
        P(),
    )
    return jax.shard_map(
        per_device,
        mesh=mesh,
        in_specs=placed,
        out_specs=(P("ens", None, "horiz", None), P("ens", None, "horiz", None), P(), P(), P()),
        check_vma=False,
    )
```

```python
import functools
import math

import jax
import jax.numpy as jnp
from jax import lax
from jax.experimental import pallas as pl
from jax.experimental.pallas import tpu as pltpu
from jax.sharding import PartitionSpec as P

DYN_STEPS = 2
BLOCK = 256
PACK_ROWS = 16
VMEM_LIMIT = 32 * 1024 * 1024
F32 = jnp.float32
BF16 = jnp.bfloat16
CONTRACT_LAST = (((1,), (1,)), ((), ()))
CONTRACT_FIRST = (((0,), (0,)), ((), ()))


def call(kernel, outs, scratch=(), smem=(), flops=0, moved=0, **names):
    def run(*operands):
        specs = [
            pl.BlockSpec(memory_space=pltpu.SMEM if place in smem else pltpu.VMEM)
            for place in range(len(operands))
        ]
        return pl.pallas_call(
            functools.partial(kernel, **names),
            out_shape=[jax.ShapeDtypeStruct(shape, dtype) for shape, dtype in outs],
            in_specs=specs,
            out_specs=[pl.BlockSpec(memory_space=pltpu.VMEM)] * len(outs),
            scratch_shapes=list(scratch),
            compiler_params=pltpu.CompilerParams(vmem_limit_bytes=VMEM_LIMIT),
            cost_estimate=pl.CostEstimate(flops=flops, bytes_accessed=moved, transcendentals=0),
        )(*operands)

    return run


def lat_term(field_now, coef_masked):
    lats = field_now.shape[1]
    north_flux = coef_masked * (pltpu.roll(field_now, lats - 1, 1) - field_now)
    return north_flux - pltpu.roll(north_flux, 1, 1)


def two_steps(rows, lon_coef, lat_coef):
    for repeat in range(DYN_STEPS):
        count = len(rows)
        fluxes = [
            lon_coef[place + repeat] * (rows[place + 1] - rows[place]) for place in range(count - 1)
        ]
        rows = [
            rows[place]
            + fluxes[place]
            - fluxes[place - 1]
            + lat_term(rows[place], lat_coef[place + repeat])
            for place in range(1, count - 1)
        ]
    return rows


def coefficients(base_ref, low_mix, high_mix, lons):
    lats = base_ref.shape[1]
    first = base_ref.shape[0] - 2 * lons
    lane = lax.broadcasted_iota(jnp.int32, (1, lats), 1)
    inside = lane < lats - 1
    own_lon = [base_ref[first + lon : first + lon + 1, :] for lon in range(lons)]
    first += lons
    own_lat = [base_ref[first + lon : first + lon + 1, :] for lon in range(lons)]
    lon_coef = [low_mix[0:1, :], low_mix[1:2, :]] + own_lon + [high_mix[0:1, :], high_mix[1:2, :]]
    lat_coef = [low_mix[2:3, :], low_mix[3:4, :]] + own_lat + [high_mix[2:3, :], high_mix[3:4, :]]
    return lon_coef, [jnp.where(inside, coef, 0.0) for coef in lat_coef]


def pack_kernel(base_ref, up_ref, down_ref, *, lons):
    fields = base_ref.shape[0] // lons - 2
    mixing = fields * lons
    for out_ref, first in ((up_ref, lons - 2), (down_ref, 0)):
        for side in range(2):
            out_ref[side * fields : (side + 1) * fields, :] = base_ref[
                pl.ds(first + side, fields, stride=lons), :
            ].astype(BF16)
        mix_rows = [
            base_ref[mixing + first : mixing + first + 2, :],
            base_ref[mixing + lons + first : mixing + lons + first + 2, :],
            jnp.zeros((PACK_ROWS - 4, base_ref.shape[1]), F32),
        ]
        out_ref[2 * fields :, :] = jnp.concatenate(mix_rows, axis=0).astype(BF16)


def halo_rows(pack_ref, fields):
    return [pack_ref[side * fields : (side + 1) * fields, :].astype(F32) for side in range(2)]


def halo_mixing(pack_ref, fields):
    return pack_ref[2 * fields :, :].astype(F32)


def one_hot(cols_ref, cells):
    parts = []
    for tile in range(cols_ref.shape[0]):
        place = lax.broadcasted_iota(jnp.int32, (cells, cols_ref.shape[1]), 0)
        parts.append(jnp.where(place == cols_ref[tile : tile + 1, :], 1.0, 0.0))
    return jnp.concatenate(parts, axis=1).astype(BF16)


def live_row(count_ref, mask_ref):
    parts = []
    for tile in range(mask_ref.shape[0]):
        used = jnp.where(tile < count_ref[0, 0], 1, 0)
        parts.append((mask_ref[tile : tile + 1, :] * used).astype(F32))
    return jnp.concatenate(parts, axis=1)


def level_rows(levels, level, variables):
    return pl.ds(level, variables, stride=levels)


def solve(levels, variables, coef_ref, ratio_ref, inverse_ref, right_ref, out_ref):
    tiles, _, width = right_ref.shape
    spans = [slice(tile * width, (tile + 1) * width) for tile in range(tiles)]
    values = []
    for level in range(levels):
        inverse_now = inverse_ref[level : level + 1, :]
        if level > 0:
            carry_now = coef_ref[level - 1 : level, :] * inverse_now
        step = []
        for tile, span in enumerate(spans):
            right_now = right_ref[tile, level_rows(levels, level, variables), :]
            value_now = right_now * inverse_now[:, span]
            if level > 0:
                value_now = value_now + carry_now[:, span] * values[-1][tile]
            step.append(value_now)
        values.append(step)
    results = values[-1]
    for level in range(levels - 1, -1, -1):
        if level < levels - 1:
            ratio_now = ratio_ref[level : level + 1, :]
            results = [
                values[level][tile] - ratio_now[:, span] * results[tile]
                for tile, span in enumerate(spans)
            ]
        for tile in range(tiles):
            out_ref[tile, level_rows(levels, level, variables), :] = results[tile]


def split_tiles(ref, value):
    width = ref.shape[2]
    for tile in range(ref.shape[0]):
        ref[tile] = value[:, tile * width : (tile + 1) * width]


def join_tiles(ref):
    return jnp.concatenate([ref[tile] for tile in range(ref.shape[0])], axis=1)


def factorise(levels, coef_ref, ratio_ref, inverse_ref):
    ratio_prev = None
    for level in range(levels):
        coef_now = coef_ref[level : level + 1, :]
        divisor = 1.0 + coef_now
        if level > 0:
            below_now = coef_ref[level - 1 : level, :]
            divisor = divisor + below_now + below_now * ratio_prev
        inverse_now = 1.0 / divisor
        ratio_prev = -coef_now * inverse_now
        inverse_ref[level : level + 1, :] = inverse_now
        ratio_ref[level : level + 1, :] = ratio_prev


def by_cell(ref, rows, lons):
    return jnp.concatenate(
        [ref[pl.ds(lon, rows, stride=lons), :] for lon in range(lons)], axis=1
    )


def adjoint_kernel(
    count_ref,
    column_ref,
    cols_ref,
    mask_ref,
    adj_ref,
    coef_ref,
    ratio_ref,
    inverse_ref,
    right_ref,
    *,
    lons,
):
    fields = adj_ref.shape[1]
    levels = coef_ref.shape[0]
    spread = one_hot(cols_ref, lons * column_ref.shape[1])
    sources = by_cell(column_ref, fields + levels, lons).astype(BF16)
    picked = jnp.dot(sources, spread, preferred_element_type=F32)
    split_tiles(right_ref, picked[:fields] * live_row(count_ref, mask_ref))
    coef_ref[...] = picked[fields:]
    factorise(levels, coef_ref, ratio_ref, inverse_ref)
    solve(levels, fields // levels, coef_ref, ratio_ref, inverse_ref, right_ref, adj_ref)


def sigmoid(pre_act):
    return 0.5 * jnp.tanh(0.5 * pre_act) + 0.5


def weight_product(left_ref, right, keep_ref, send_ref, first):
    half = left_ref.shape[0] // 2
    block = min(BLOCK, half)
    core = lax.axis_index("horiz") % 2
    for out_ref, side in ((send_ref, 1 - core), (keep_ref, core)):
        for start in range(0, half, block):
            out_ref[start : start + block, first : first + right.shape[0]] = lax.dot_general(
                left_ref[pl.ds(pl.multiple_of(side * half + start, block), block), :],
                right,
                CONTRACT_LAST,
                preferred_element_type=F32,
            ).astype(BF16)


def forward_kernel(
    base_ref,
    low_ref,
    high_ref,
    cols_ref,
    adj_ref,
    weights_ref,
    w_out_ref,
    moved_ref,
    x_ref,
    act_one_ref,
    act_two_ref,
    delta_two_ref,
    keep_ref,
    send_ref,
    *,
    lons,
):
    fields = x_ref.shape[0]
    units = weights_ref.shape[0]
    cells = lons * base_ref.shape[1]
    low_rows, high_rows = halo_rows(low_ref, fields), halo_rows(high_ref, fields)
    lon_coef, lat_coef = coefficients(
        base_ref, halo_mixing(low_ref, fields), halo_mixing(high_ref, fields), lons
    )
    rows = [base_ref[pl.ds(lon, fields, stride=lons), :] for lon in range(lons)]
    rows = two_steps(low_rows + rows + high_rows, lon_coef, lat_coef)
    for lon in range(lons):
        moved_ref[lon] = rows[lon]
    spread = one_hot(cols_ref, cells)
    sources = jnp.concatenate(rows, axis=1).astype(BF16)
    x_now = jnp.dot(sources, spread, preferred_element_type=F32).astype(BF16)
    x_ref[...] = x_now
    for start in range(0, units, BLOCK):
        pre_one = jnp.dot(weights_ref[start : start + BLOCK, units:], x_now, preferred_element_type=F32)
        act_one_ref[start : start + BLOCK, :] = (pre_one * sigmoid(pre_one)).astype(BF16)
    adj_half = join_tiles(adj_ref).astype(BF16)
    for start in range(0, units, BLOCK):
        pre_two = jnp.dot(
            weights_ref[start : start + BLOCK, :units], act_one_ref[...], preferred_element_type=F32
        )
        sigma_val = sigmoid(pre_two)
        act_two_ref[start : start + BLOCK, :] = (pre_two * sigma_val).astype(BF16)
        back_two = lax.dot_general(
            w_out_ref[:, start : start + BLOCK],
            adj_half,
            CONTRACT_FIRST,
            preferred_element_type=F32,
        )
        slope = sigma_val * (1.0 + pre_two * (1.0 - sigma_val))
        delta_two_ref[start : start + BLOCK, :] = (back_two * slope).astype(BF16)
    weight_product(delta_two_ref, act_one_ref[...], keep_ref, send_ref, 0)


def backward_kernel(
    x_ref,
    act_two_ref,
    delta_two_ref,
    adj_ref,
    weights_ref,
    delta_one_ref,
    keep_ref,
    send_ref,
):
    fields = x_ref.shape[0]
    units = weights_ref.shape[0]
    x_now = x_ref[...]
    for start in range(0, units, BLOCK):
        back_one = lax.dot_general(
            weights_ref[:, start : start + BLOCK],
            delta_two_ref[...],
            CONTRACT_FIRST,
            preferred_element_type=F32,
        )
        pre_one = jnp.dot(weights_ref[start : start + BLOCK, units:], x_now, preferred_element_type=F32)
        sigma_val = sigmoid(pre_one)
        slope = sigma_val * (1.0 + pre_one * (1.0 - sigma_val))
        delta_one_ref[start : start + BLOCK, :] = (back_one * slope).astype(BF16)
    weight_product(delta_one_ref, x_now, keep_ref, send_ref, 0)
    weight_product(act_two_ref, join_tiles(adj_ref).astype(BF16), keep_ref, send_ref, fields)


def place_back(fresh, live, cols_ref, cells):
    marks = jnp.broadcast_to(live, (16, live.shape[1]))
    placed = lax.dot_general(
        jnp.concatenate([fresh * live, marks], axis=0).astype(BF16),
        one_hot(cols_ref, cells),
        CONTRACT_LAST,
        preferred_element_type=F32,
    )
    rows = fresh.shape[0]
    return placed[:rows], placed[rows : rows + 1] > 0.5


def state_kernel(
    count_ref,
    moved_ref,
    cols_ref,
    mask_ref,
    x_ref,
    act_two_ref,
    coef_ref,
    ratio_ref,
    inverse_ref,
    w_out_ref,
    state_ref,
    forced_ref,
    solved_ref,
    *,
    lons,
):
    fields = x_ref.shape[0]
    levels = coef_ref.shape[0]
    lats = moved_ref.shape[2]
    tendency = jnp.dot(w_out_ref[...], act_two_ref[...], preferred_element_type=F32)
    split_tiles(forced_ref, x_ref[...].astype(F32) + tendency)
    solve(levels, fields // levels, coef_ref, ratio_ref, inverse_ref, forced_ref, solved_ref)
    placed, taken = place_back(
        join_tiles(solved_ref), live_row(count_ref, mask_ref), cols_ref, lons * lats
    )
    for lon in range(lons):
        here = slice(lon * lats, (lon + 1) * lats)
        state_ref[pl.ds(lon, fields, stride=lons), :] = jnp.where(
            taken[:, here], placed[:, here], moved_ref[lon]
        )


def grad_kernel(
    count_ref,
    column_ref,
    cols_ref,
    mask_ref,
    delta_one_ref,
    adj_ref,
    weights_ref,
    field_ref,
    up_ref,
    down_ref,
    *,
    lons,
):
    fields, lats = field_ref.shape[1:]
    grad_x = join_tiles(adj_ref) + lax.dot_general(
        weights_ref[:, delta_one_ref.shape[0] :], delta_one_ref[...], CONTRACT_FIRST, preferred_element_type=F32
    )
    placed, taken = place_back(grad_x, live_row(count_ref, mask_ref), cols_ref, lons * lats)
    for lon in range(lons):
        here = slice(lon * lats, (lon + 1) * lats)
        field_now = jnp.where(
            taken[:, here], placed[:, here], column_ref[pl.ds(lon, fields, stride=lons), :]
        )
        field_ref[lon] = field_now
        if lon < 2:
            down_ref[lon * fields : (lon + 1) * fields, :] = field_now.astype(BF16)
        if lon >= lons - 2:
            side = lon - (lons - 2)
            up_ref[side * fields : (side + 1) * fields, :] = field_now.astype(BF16)


def last_kernel(field_ref, low_ref, high_ref, low_mix_ref, high_mix_ref, base_ref, out_ref, *, lons):
    fields = field_ref.shape[1]
    low_rows, high_rows = halo_rows(low_ref, fields), halo_rows(high_ref, fields)
    lon_coef, lat_coef = coefficients(
        base_ref, halo_mixing(low_mix_ref, fields), halo_mixing(high_mix_ref, fields), lons
    )
    rows = [field_ref[lon] for lon in range(lons)]
    rows = two_steps(low_rows + rows + high_rows, lon_coef, lat_coef)
    for lon in range(lons):
        out_ref[pl.ds(lon, fields, stride=lons), :] = rows[lon]


CORE = ("horiz", 0, 2)
CHIPS = ("horiz", 1, 4)
NEAR, FAR = ("horiz", 1, 2), ("horiz", 2, 2)
MEMBERS = ("ens", 0, 4)
MEMBER_LOW, MEMBER_HIGH = ("ens", 0, 2), ("ens", 1, 2)


def position(stage):
    axis, shift, parts = stage
    return lax.axis_index(axis) // (1 << shift) % parts


def sum_kernel(*refs, terms, stage, factor):
    ins, outs = refs[:terms], refs[terms:]
    rows = outs[0].shape[0]
    for index, out_ref in enumerate(outs):
        here = pl.ds(0, rows)
        if stage is not None:
            start = (position(stage) ^ (-index % len(outs))) * rows
            here = pl.ds(pl.multiple_of(start, rows), rows)
        total = ins[0][here, :].astype(F32)
        for ref in ins[1:]:
            total = total + ref[here, :].astype(F32)
        out_ref[...] = (total * factor).astype(BF16)


def join_kernel(*refs, stage, groups, cuts):
    ins, outs = refs[:-cuts], refs[-cuts:]
    count = len(ins) // groups
    rows, columns = ins[0].shape
    width = outs[0].shape[1]
    part = min(width, columns)
    for k in range(count):
        here = pl.ds(pl.multiple_of((position(stage) ^ k) * rows, rows), rows)
        for group in range(groups):
            for start in range(0, columns, part):
                first = group * columns + start
                outs[first // width][here, first % width : first % width + part] = ins[
                    group * count + k
                ][:, start : start + part]


def member_order():
    member, core = lax.axis_index("ens"), lax.axis_index("horiz") % 2
    return [member, member ^ (1 + core), member ^ (2 - core), member ^ 3]


def core_sum_kernel(keep_mid, got_mid, keep_small, got_small, *outs):
    rows = outs[0].shape[0]
    for member, out_ref in zip(member_order(), outs):
        here = pl.ds(pl.multiple_of(member * rows, rows), rows)
        first = 0
        for keep_ref, got_ref in ((keep_mid, got_mid), (keep_small, got_small)):
            columns = keep_ref.shape[1]
            out_ref[:, first : first + columns] = (
                keep_ref[here, :].astype(F32) + got_ref[here, :].astype(F32)
            ).astype(BF16)
            first += columns


def final_kernel(mid_half, small_half, *refs):
    mid_ref, in_ref, out_ref = refs[-3:]
    fields = in_ref.shape[1]
    mid_ref[...] = mid_half[...].astype(F32)

    @pl.when(pl.program_id(0) == 0)
    def _():
        in_ref[...] = small_half[:, :fields].astype(F32)
        out_ref[...] = small_half[:, fields:].astype(F32).T


def final(rows, other, before, fields):
    half, columns = rows.shape
    units = 2 * half
    block = units // 2

    def place():
        core = lax.axis_index("horiz") % 2
        return 1 - core if other else core

    return pl.pallas_call(
        final_kernel,
        grid=(units // block,),
        out_shape=[
            jax.ShapeDtypeStruct(shape, F32)
            for shape in ((units, units), (units, fields), (fields, units))
        ],
        in_specs=[
            pl.BlockSpec((half, block), lambda step: (0, step)),
            pl.BlockSpec((half, 2 * fields), lambda step: (0, units // (2 * fields))),
        ]
        + [pl.BlockSpec(memory_space=pl.ANY)] * len(before),
        out_specs=[
            pl.BlockSpec((half, block), lambda step: (place(), step)),
            pl.BlockSpec((half, fields), lambda step: (place(), 0)),
            pl.BlockSpec((fields, half), lambda step: (0, place())),
        ],
        input_output_aliases={2 + index: index for index in range(len(before))},
        compiler_params=pltpu.CompilerParams(vmem_limit_bytes=VMEM_LIMIT),
    )(rows, rows, *before)


def exchange(arrays, stage):
    axis, shift, _ = stage
    count = lax.axis_size(axis)
    sent = {}
    for k in range(len(arrays), 0, -1):
        route = [(i, i ^ (k << shift)) for i in range(count)]
        sent[k] = lax.ppermute(arrays[k - 1], axis, route)
    return [sent[k] for k in range(1, len(arrays) + 1)]


def to_member(array, second):
    members, count = lax.axis_size("ens"), lax.axis_size("horiz")
    route = []
    for member in range(members):
        for place in range(count):
            neighbour = member ^ (1 << (place % 2 ^ second))
            route.append((member * count + place, neighbour * count + place))
    return lax.ppermute(array, ("ens", "horiz"), route)


def collect_members(one, two):
    (low_one,) = exchange([one], MEMBER_LOW)
    (high_two,) = exchange([two], MEMBER_HIGH)
    (high_one,) = exchange([one], MEMBER_HIGH)
    (low_two,) = exchange([two], MEMBER_LOW)
    (far_one,) = exchange([low_one], MEMBER_HIGH)
    (far_two,) = exchange([high_two], MEMBER_LOW)
    return [one, low_one, high_one, far_one], [two, low_two, high_two, far_two]


def add(terms, stage, factor=1.0):
    rows, columns = terms[0].shape
    parts = 1 if stage is None else stage[2]
    return call(
        sum_kernel,
        [((rows // parts, columns), BF16)] * parts,
        terms=len(terms),
        stage=stage,
        factor=factor,
    )(*terms)


def join(groups, stage, cuts=1):
    rows, columns = groups[0][0].shape
    shape = (rows * len(groups[0]), columns * len(groups) // cuts)
    return call(
        join_kernel, [(shape, BF16)] * cuts, stage=stage, groups=len(groups), cuts=cuts
    )(*[piece for group in groups for piece in group])


def reduce_chips(terms):
    own, both, far, near = add(terms, CHIPS)
    (got_both,) = exchange([both], NEAR)
    (got_near,) = exchange([near], NEAR)
    (got_far,) = exchange(add([far, got_both], None), FAR)
    return [own, got_near, got_far]


def collect_chips(piece):
    (got_far,) = exchange([piece], FAR)
    (got_near,) = exchange([piece], NEAR)
    (got_both,) = exchange([got_far], NEAR)
    return [piece, got_near, got_far, got_both]


def tie(*values):
    return lax.optimization_barrier(values)


def over_all_chips(piece, factor):
    core = lax.axis_index("horiz") % 2
    both = jnp.stack([jnp.where(core == side, piece, 0.0).astype(F32) for side in range(2)])
    return (lax.psum(both, "horiz")[core] * factor).astype(BF16)


def to_neighbours(upward, downward, axis):
    count = lax.axis_size(axis)
    forward = [(i, (i + 1) % count) for i in range(count)]
    backward = [(target, source) for source, target in forward]
    return lax.ppermute(upward, axis, forward), lax.ppermute(downward, axis, backward)


def per_device(
    prognostic, diffusivity, mixing, cotangent, tile_cols, pad_mask, tile_count, w_in, w_mid, w_out
):
    fields, lons, lats = prognostic.shape[1:]
    levels = diffusivity.shape[1]
    units = w_mid.shape[0]
    tiles, width = tile_cols.shape[2:]
    slots = tiles * width
    base = jnp.concatenate([prognostic[0], mixing], axis=0).reshape((fields + 2) * lons, lats)
    column = jnp.concatenate([cotangent[0], diffusivity[0]], axis=0)
    column = column.reshape((fields + levels) * lons, lats)
    weights = jnp.concatenate([w_mid, w_in], axis=1)
    cols, mask = tile_cols[0, 0], pad_mask[0, 0]

    packed = ((2 * fields + PACK_ROWS, lats), BF16)
    up_pack, down_pack = call(pack_kernel, [packed, packed], lons=lons)(base)
    low_pack, high_pack = to_neighbours(up_pack, down_pack, "horiz")

    adjoint, coef, ratio, inverse = call(
        adjoint_kernel,
        [((tiles, fields, width), F32)] + [((levels, slots), F32)] * 3,
        scratch=[pltpu.VMEM((tiles, fields, width), F32)],
        smem=(0,),
        moved=30 * 10**6,
        lons=lons,
    )(tile_count, column, cols, mask)

    hidden = ((units, slots), BF16)
    half = ((units // 2, units), BF16)
    moved, x_now, act_one, act_two, delta_two, keep_mid, send_mid = call(
        forward_kernel,
        [((lons, fields, lats), F32), ((fields, slots), BF16), hidden, hidden, hidden, half, half],
        moved=15 * 10**6,
        lons=lons,
    )(base, low_pack, high_pack, cols, adjoint, weights, w_out)
    column_total = lax.axis_size("ens") * lax.axis_size("horiz") * lons * lats
    factor = 1.0 / math.sqrt(column_total)
    (got_mid,) = exchange([send_mid], CORE)

    half = ((units // 2, 2 * fields), BF16)
    delta_one, keep_small, send_small = call(
        backward_kernel, [hidden, half, half], moved=4 * 10**6
    )(x_now, act_two, delta_two, adjoint, weights)
    (got_small,) = exchange([send_small], CORE)

    packed = ((2 * fields, lats), BF16)
    field, up_rows, down_rows = call(
        grad_kernel,
        [((lons, fields, lats), F32), packed, packed],
        smem=(0,),
        lons=lons,
    )(tile_count, column, cols, mask, delta_one, adjoint, weights)
    got_small, field = tie(got_small, field)

    members = lax.axis_size("ens")
    parts = call(core_sum_kernel, [((units // 2 // members, units + 2 * fields), BF16)] * members)(
        keep_mid, got_mid, keep_small, got_small
    )
    own, first, second, far = parts
    got_far = to_member(far, 0)
    got_first = to_member(first, 0)

    act_two, up_rows, down_rows = tie(act_two, up_rows, down_rows, parts)[:3]
    halos = to_neighbours(up_rows, down_rows, "horiz")
    (state_rows,) = call(
        state_kernel,
        [((fields * lons, lats), F32)],
        scratch=[pltpu.VMEM((tiles, fields, width), F32)] * 2,
        smem=(0,),
        lons=lons,
    )(tile_count, moved, cols, mask, x_now, act_two, coef, ratio, inverse, w_out)
    got_far, state_rows, halos = tie(got_far, state_rows, halos)
    terms = [own, got_first, to_member(add([second, got_far], None)[0], 1)]
    (grad_rows,) = call(last_kernel, [((fields * lons, lats), F32)], lons=lons)(
        field, *halos, low_pack, high_pack, base
    )
    terms, grad_rows = tie(terms, grad_rows)

    if lax.axis_size("horiz") == 8:
        terms = reduce_chips(terms)
        halves = join([collect_chips(add(terms, None, factor)[0])], CHIPS, cuts=2)
    else:
        halves = jnp.split(over_all_chips(add(terms, None)[0], factor), 2, axis=1)
    (own,) = join(collect_members(*halves), MEMBERS)
    (got,) = exchange([own], CORE)
    half_done = final(own, False, [], fields)
    grad_mid, grad_in, grad_out = final(got, True, half_done, fields)
    return (
        state_rows.reshape(prognostic.shape),
        grad_rows.reshape(prognostic.shape),
        grad_in,
        grad_mid,
        grad_out,
    )


def solution(mesh):
    placed = (
        P("ens", None, "horiz", None),
        P("ens", None, "horiz", None),
        P(None, "horiz", None),
        P("ens", None, "horiz", None),
        P("ens", "horiz", None, None),
        P("ens", "horiz", None, None),
        P("ens", "horiz"),
        P(),
        P(),
        P(),
    )
    return jax.shard_map(
        per_device,
        mesh=mesh,
        in_specs=placed,
        out_specs=(P("ens", None, "horiz", None), P("ens", None, "horiz", None), P(), P(), P()),
        check_vma=False,
    )
```

```python
import functools
import math

import jax
import jax.numpy as jnp
from jax import lax
from jax.experimental import pallas as pl
from jax.experimental.pallas import tpu as pltpu
from jax.sharding import PartitionSpec as P

DYN_STEPS = 2
BLOCK = 256
PACK_ROWS = 16
VMEM_LIMIT = 32 * 1024 * 1024
F32 = jnp.float32
BF16 = jnp.bfloat16
CONTRACT_LAST = (((1,), (1,)), ((), ()))
CONTRACT_FIRST = (((0,), (0,)), ((), ()))


def call(kernel, outs, scratch=(), smem=(), flops=0, moved=0, **names):
    def run(*operands):
        specs = [
            pl.BlockSpec(memory_space=pltpu.SMEM if place in smem else pltpu.VMEM)
            for place in range(len(operands))
        ]
        return pl.pallas_call(
            functools.partial(kernel, **names),
            out_shape=[jax.ShapeDtypeStruct(shape, dtype) for shape, dtype in outs],
            in_specs=specs,
            out_specs=[pl.BlockSpec(memory_space=pltpu.VMEM)] * len(outs),
            scratch_shapes=list(scratch),
            compiler_params=pltpu.CompilerParams(vmem_limit_bytes=VMEM_LIMIT),
            cost_estimate=pl.CostEstimate(flops=flops, bytes_accessed=moved, transcendentals=0),
        )(*operands)

    return run


def lat_term(field_now, coef_masked):
    lats = field_now.shape[1]
    north_flux = coef_masked * (pltpu.roll(field_now, lats - 1, 1) - field_now)
    return north_flux - pltpu.roll(north_flux, 1, 1)


def two_steps(rows, lon_coef, lat_coef):
    for repeat in range(DYN_STEPS):
        count = len(rows)
        fluxes = [
            lon_coef[place + repeat] * (rows[place + 1] - rows[place]) for place in range(count - 1)
        ]
        rows = [
            rows[place]
            + fluxes[place]
            - fluxes[place - 1]
            + lat_term(rows[place], lat_coef[place + repeat])
            for place in range(1, count - 1)
        ]
    return rows


def coefficients(base_ref, low_mix, high_mix, lons):
    lats = base_ref.shape[1]
    first = base_ref.shape[0] - 2 * lons
    lane = lax.broadcasted_iota(jnp.int32, (1, lats), 1)
    inside = lane < lats - 1
    own_lon = [base_ref[first + lon : first + lon + 1, :] for lon in range(lons)]
    first += lons
    own_lat = [base_ref[first + lon : first + lon + 1, :] for lon in range(lons)]
    lon_coef = [low_mix[0:1, :], low_mix[1:2, :]] + own_lon + [high_mix[0:1, :], high_mix[1:2, :]]
    lat_coef = [low_mix[2:3, :], low_mix[3:4, :]] + own_lat + [high_mix[2:3, :], high_mix[3:4, :]]
    return lon_coef, [jnp.where(inside, coef, 0.0) for coef in lat_coef]


def pack_kernel(base_ref, up_ref, down_ref, *, lons):
    fields = base_ref.shape[0] // lons - 2
    mixing = fields * lons
    for out_ref, first in ((up_ref, lons - 2), (down_ref, 0)):
        for side in range(2):
            out_ref[side * fields : (side + 1) * fields, :] = base_ref[
                pl.ds(first + side, fields, stride=lons), :
            ].astype(BF16)
        mix_rows = [
            base_ref[mixing + first : mixing + first + 2, :],
            base_ref[mixing + lons + first : mixing + lons + first + 2, :],
            jnp.zeros((PACK_ROWS - 4, base_ref.shape[1]), F32),
        ]
        out_ref[2 * fields :, :] = jnp.concatenate(mix_rows, axis=0).astype(BF16)


def halo_rows(pack_ref, fields):
    return [pack_ref[side * fields : (side + 1) * fields, :].astype(F32) for side in range(2)]


def halo_mixing(pack_ref, fields):
    return pack_ref[2 * fields :, :].astype(F32)


def one_hot(cols_ref, cells):
    parts = []
    for tile in range(cols_ref.shape[0]):
        place = lax.broadcasted_iota(jnp.int32, (cells, cols_ref.shape[1]), 0)
        parts.append(jnp.where(place == cols_ref[tile : tile + 1, :], 1.0, 0.0))
    return jnp.concatenate(parts, axis=1).astype(BF16)


def live_row(count_ref, mask_ref):
    parts = []
    for tile in range(mask_ref.shape[0]):
        used = jnp.where(tile < count_ref[0, 0], 1, 0)
        parts.append((mask_ref[tile : tile + 1, :] * used).astype(F32))
    return jnp.concatenate(parts, axis=1)


def level_rows(levels, level, variables):
    return pl.ds(level, variables, stride=levels)


def solve(levels, variables, coef_ref, ratio_ref, inverse_ref, right_ref, out_ref):
    tiles, _, width = right_ref.shape
    spans = [slice(tile * width, (tile + 1) * width) for tile in range(tiles)]
    values = []
    for level in range(levels):
        inverse_now = inverse_ref[level : level + 1, :]
        if level > 0:
            carry_now = coef_ref[level - 1 : level, :] * inverse_now
        step = []
        for tile, span in enumerate(spans):
            right_now = right_ref[tile, level_rows(levels, level, variables), :]
            value_now = right_now * inverse_now[:, span]
            if level > 0:
                value_now = value_now + carry_now[:, span] * values[-1][tile]
            step.append(value_now)
        values.append(step)
    results = values[-1]
    for level in range(levels - 1, -1, -1):
        if level < levels - 1:
            ratio_now = ratio_ref[level : level + 1, :]
            results = [
                values[level][tile] - ratio_now[:, span] * results[tile]
                for tile, span in enumerate(spans)
            ]
        for tile in range(tiles):
            out_ref[tile, level_rows(levels, level, variables), :] = results[tile]


def split_tiles(ref, value):
    width = ref.shape[2]
    for tile in range(ref.shape[0]):
        ref[tile] = value[:, tile * width : (tile + 1) * width]


def join_tiles(ref):
    return jnp.concatenate([ref[tile] for tile in range(ref.shape[0])], axis=1)


def factorise(levels, coef_ref, ratio_ref, inverse_ref):
    ratio_prev = None
    for level in range(levels):
        coef_now = coef_ref[level : level + 1, :]
        divisor = 1.0 + coef_now
        if level > 0:
            below_now = coef_ref[level - 1 : level, :]
            divisor = divisor + below_now + below_now * ratio_prev
        inverse_now = 1.0 / divisor
        ratio_prev = -coef_now * inverse_now
        inverse_ref[level : level + 1, :] = inverse_now
        ratio_ref[level : level + 1, :] = ratio_prev


def by_cell(ref, rows, lons):
    return jnp.concatenate(
        [ref[pl.ds(lon, rows, stride=lons), :] for lon in range(lons)], axis=1
    )


def adjoint_kernel(
    count_ref,
    column_ref,
    cols_ref,
    mask_ref,
    adj_ref,
    coef_ref,
    ratio_ref,
    inverse_ref,
    right_ref,
    *,
    lons,
):
    fields = adj_ref.shape[1]
    levels = coef_ref.shape[0]
    spread = one_hot(cols_ref, lons * column_ref.shape[1])
    sources = by_cell(column_ref, fields + levels, lons).astype(BF16)
    picked = jnp.dot(sources, spread, preferred_element_type=F32)
    split_tiles(right_ref, picked[:fields] * live_row(count_ref, mask_ref))
    coef_ref[...] = picked[fields:]
    factorise(levels, coef_ref, ratio_ref, inverse_ref)
    solve(levels, fields // levels, coef_ref, ratio_ref, inverse_ref, right_ref, adj_ref)


def sigmoid(pre_act):
    return 0.5 * jnp.tanh(0.5 * pre_act) + 0.5


def weight_product(left_ref, right, keep_ref, send_ref, first):
    half = left_ref.shape[0] // 2
    block = min(BLOCK, half)
    core = lax.axis_index("horiz") % 2
    for out_ref, side in ((send_ref, 1 - core), (keep_ref, core)):
        for start in range(0, half, block):
            out_ref[start : start + block, first : first + right.shape[0]] = lax.dot_general(
                left_ref[pl.ds(pl.multiple_of(side * half + start, block), block), :],
                right,
                CONTRACT_LAST,
                preferred_element_type=F32,
            ).astype(BF16)


def forward_kernel(
    base_ref,
    low_ref,
    high_ref,
    cols_ref,
    adj_ref,
    weights_ref,
    w_out_ref,
    moved_ref,
    x_ref,
    act_one_ref,
    act_two_ref,
    delta_two_ref,
    keep_ref,
    send_ref,
    *,
    lons,
):
    fields = x_ref.shape[0]
    units = weights_ref.shape[0]
    cells = lons * base_ref.shape[1]
    low_rows, high_rows = halo_rows(low_ref, fields), halo_rows(high_ref, fields)
    lon_coef, lat_coef = coefficients(
        base_ref, halo_mixing(low_ref, fields), halo_mixing(high_ref, fields), lons
    )
    rows = [base_ref[pl.ds(lon, fields, stride=lons), :] for lon in range(lons)]
    rows = two_steps(low_rows + rows + high_rows, lon_coef, lat_coef)
    for lon in range(lons):
        moved_ref[lon] = rows[lon]
    spread = one_hot(cols_ref, cells)
    sources = jnp.concatenate(rows, axis=1).astype(BF16)
    x_now = jnp.dot(sources, spread, preferred_element_type=F32).astype(BF16)
    x_ref[...] = x_now
    for start in range(0, units, BLOCK):
        pre_one = jnp.dot(weights_ref[start : start + BLOCK, units:], x_now, preferred_element_type=F32)
        act_one_ref[start : start + BLOCK, :] = (pre_one * sigmoid(pre_one)).astype(BF16)
    adj_half = join_tiles(adj_ref).astype(BF16)
    for start in range(0, units, BLOCK):
        pre_two = jnp.dot(
            weights_ref[start : start + BLOCK, :units], act_one_ref[...], preferred_element_type=F32
        )
        sigma_val = sigmoid(pre_two)
        act_two_ref[start : start + BLOCK, :] = (pre_two * sigma_val).astype(BF16)
        back_two = lax.dot_general(
            w_out_ref[:, start : start + BLOCK],
            adj_half,
            CONTRACT_FIRST,
            preferred_element_type=F32,
        )
        slope = sigma_val * (1.0 + pre_two * (1.0 - sigma_val))
        delta_two_ref[start : start + BLOCK, :] = (back_two * slope).astype(BF16)
    weight_product(delta_two_ref, act_one_ref[...], keep_ref, send_ref, 0)


def backward_kernel(
    x_ref,
    act_two_ref,
    delta_two_ref,
    adj_ref,
    weights_ref,
    delta_one_ref,
    keep_ref,
    send_ref,
):
    fields = x_ref.shape[0]
    units = weights_ref.shape[0]
    x_now = x_ref[...]
    for start in range(0, units, BLOCK):
        back_one = lax.dot_general(
            weights_ref[:, start : start + BLOCK],
            delta_two_ref[...],
            CONTRACT_FIRST,
            preferred_element_type=F32,
        )
        pre_one = jnp.dot(weights_ref[start : start + BLOCK, units:], x_now, preferred_element_type=F32)
        sigma_val = sigmoid(pre_one)
        slope = sigma_val * (1.0 + pre_one * (1.0 - sigma_val))
        delta_one_ref[start : start + BLOCK, :] = (back_one * slope).astype(BF16)
    weight_product(delta_one_ref, x_now, keep_ref, send_ref, 0)
    weight_product(act_two_ref, join_tiles(adj_ref).astype(BF16), keep_ref, send_ref, fields)


def place_back(fresh, live, cols_ref, cells):
    marks = jnp.broadcast_to(live, (16, live.shape[1]))
    placed = lax.dot_general(
        jnp.concatenate([fresh * live, marks], axis=0).astype(BF16),
        one_hot(cols_ref, cells),
        CONTRACT_LAST,
        preferred_element_type=F32,
    )
    rows = fresh.shape[0]
    return placed[:rows], placed[rows : rows + 1] > 0.5


def state_kernel(
    count_ref,
    moved_ref,
    cols_ref,
    mask_ref,
    x_ref,
    act_two_ref,
    coef_ref,
    ratio_ref,
    inverse_ref,
    w_out_ref,
    state_ref,
    forced_ref,
    solved_ref,
    *,
    lons,
):
    fields = x_ref.shape[0]
    levels = coef_ref.shape[0]
    lats = moved_ref.shape[2]
    tendency = jnp.dot(w_out_ref[...], act_two_ref[...], preferred_element_type=F32)
    split_tiles(forced_ref, x_ref[...].astype(F32) + tendency)
    solve(levels, fields // levels, coef_ref, ratio_ref, inverse_ref, forced_ref, solved_ref)
    placed, taken = place_back(
        join_tiles(solved_ref), live_row(count_ref, mask_ref), cols_ref, lons * lats
    )
    for lon in range(lons):
        here = slice(lon * lats, (lon + 1) * lats)
        state_ref[pl.ds(lon, fields, stride=lons), :] = jnp.where(
            taken[:, here], placed[:, here], moved_ref[lon]
        )


def grad_kernel(
    count_ref,
    column_ref,
    cols_ref,
    mask_ref,
    delta_one_ref,
    adj_ref,
    weights_ref,
    field_ref,
    up_ref,
    down_ref,
    *,
    lons,
):
    fields, lats = field_ref.shape[1:]
    grad_x = join_tiles(adj_ref) + lax.dot_general(
        weights_ref[:, delta_one_ref.shape[0] :], delta_one_ref[...], CONTRACT_FIRST, preferred_element_type=F32
    )
    placed, taken = place_back(grad_x, live_row(count_ref, mask_ref), cols_ref, lons * lats)
    for lon in range(lons):
        here = slice(lon * lats, (lon + 1) * lats)
        field_now = jnp.where(
            taken[:, here], placed[:, here], column_ref[pl.ds(lon, fields, stride=lons), :]
        )
        field_ref[lon] = field_now
        if lon < 2:
            down_ref[lon * fields : (lon + 1) * fields, :] = field_now.astype(BF16)
        if lon >= lons - 2:
            side = lon - (lons - 2)
            up_ref[side * fields : (side + 1) * fields, :] = field_now.astype(BF16)


def last_kernel(field_ref, low_ref, high_ref, low_mix_ref, high_mix_ref, base_ref, out_ref, *, lons):
    fields = field_ref.shape[1]
    low_rows, high_rows = halo_rows(low_ref, fields), halo_rows(high_ref, fields)
    lon_coef, lat_coef = coefficients(
        base_ref, halo_mixing(low_mix_ref, fields), halo_mixing(high_mix_ref, fields), lons
    )
    rows = [field_ref[lon] for lon in range(lons)]
    rows = two_steps(low_rows + rows + high_rows, lon_coef, lat_coef)
    for lon in range(lons):
        out_ref[pl.ds(lon, fields, stride=lons), :] = rows[lon]


CORE = ("horiz", 0, 2)
CHIPS = ("horiz", 1, 4)
MEMBERS = ("ens", 0, 4)
MEMBER_LOW, MEMBER_HIGH = ("ens", 0, 2), ("ens", 1, 2)


def position(stage):
    axis, shift, parts = stage
    return lax.axis_index(axis) // (1 << shift) % parts


def partner(stage, index):
    parts = stage[2]
    offset = jnp.where(lax.axis_index("horiz") % 2 == 0, -index % parts, index)
    return position(stage) ^ offset


def sum_kernel(*refs, terms, stage, factor):
    ins, outs = refs[:terms], refs[terms:]
    rows = outs[0].shape[0]
    for index, out_ref in enumerate(outs):
        here = pl.ds(0, rows)
        if stage is not None:
            start = partner(stage, index) * rows
            here = pl.ds(pl.multiple_of(start, rows), rows)
        total = ins[0][here, :].astype(F32)
        for ref in ins[1:]:
            total = total + ref[here, :].astype(F32)
        out_ref[...] = (total * factor).astype(BF16)


def join_kernel(*refs, stage, groups, cuts):
    ins, outs = refs[:-cuts], refs[-cuts:]
    count = len(ins) // groups
    rows, columns = ins[0].shape
    width = outs[0].shape[1]
    part = min(width, columns)
    for k in range(count):
        place = partner(stage, k) if stage == CHIPS else position(stage) ^ k
        here = pl.ds(pl.multiple_of(place * rows, rows), rows)
        for group in range(groups):
            for start in range(0, columns, part):
                first = group * columns + start
                outs[first // width][here, first % width : first % width + part] = ins[
                    group * count + k
                ][:, start : start + part]


def member_order():
    member, core = lax.axis_index("ens"), lax.axis_index("horiz") % 2
    return [member, member ^ (1 + core), member ^ (2 - core), member ^ 3]


def core_sum_kernel(keep_mid, got_mid, keep_small, got_small, *outs):
    rows = outs[0].shape[0]
    for member, out_ref in zip(member_order(), outs):
        here = pl.ds(pl.multiple_of(member * rows, rows), rows)
        first = 0
        for keep_ref, got_ref in ((keep_mid, got_mid), (keep_small, got_small)):
            columns = keep_ref.shape[1]
            out_ref[:, first : first + columns] = (
                keep_ref[here, :].astype(F32) + got_ref[here, :].astype(F32)
            ).astype(BF16)
            first += columns


def final_kernel(mid_half, small_half, *refs):
    mid_ref, in_ref, out_ref = refs[-3:]
    fields = in_ref.shape[1]
    mid_ref[...] = mid_half[...].astype(F32)

    @pl.when(pl.program_id(0) == 0)
    def _():
        in_ref[...] = small_half[:, :fields].astype(F32)
        out_ref[...] = small_half[:, fields:].astype(F32).T


def final(rows, other, before, fields):
    half, columns = rows.shape
    units = 2 * half
    block = units // 2

    def place():
        core = lax.axis_index("horiz") % 2
        return 1 - core if other else core

    return pl.pallas_call(
        final_kernel,
        grid=(units // block,),
        out_shape=[
            jax.ShapeDtypeStruct(shape, F32)
            for shape in ((units, units), (units, fields), (fields, units))
        ],
        in_specs=[
            pl.BlockSpec((half, block), lambda step: (0, step)),
            pl.BlockSpec((half, 2 * fields), lambda step: (0, units // (2 * fields))),
        ]
        + [pl.BlockSpec(memory_space=pl.ANY)] * len(before),
        out_specs=[
            pl.BlockSpec((half, block), lambda step: (place(), step)),
            pl.BlockSpec((half, fields), lambda step: (place(), 0)),
            pl.BlockSpec((fields, half), lambda step: (0, place())),
        ],
        input_output_aliases={2 + index: index for index in range(len(before))},
        compiler_params=pltpu.CompilerParams(vmem_limit_bytes=VMEM_LIMIT),
    )(rows, rows, *before)


def exchange(arrays, stage):
    axis, shift, _ = stage
    count = lax.axis_size(axis)
    sent = {}
    for k in range(len(arrays), 0, -1):
        route = [(i, i ^ (k << shift)) for i in range(count)]
        sent[k] = lax.ppermute(arrays[k - 1], axis, route)
    return [sent[k] for k in range(1, len(arrays) + 1)]


def to_member(array, second):
    members, count = lax.axis_size("ens"), lax.axis_size("horiz")
    route = []
    for member in range(members):
        for place in range(count):
            neighbour = member ^ (1 << (place % 2 ^ second))
            route.append((member * count + place, neighbour * count + place))
    return lax.ppermute(array, ("ens", "horiz"), route)


def collect_members(one, two):
    (low_one,) = exchange([one], MEMBER_LOW)
    (high_two,) = exchange([two], MEMBER_HIGH)
    (high_one,) = exchange([one], MEMBER_HIGH)
    (low_two,) = exchange([two], MEMBER_LOW)
    (far_one,) = exchange([low_one], MEMBER_HIGH)
    (far_two,) = exchange([high_two], MEMBER_LOW)
    return [one, low_one, high_one, far_one], [two, low_two, high_two, far_two]


def add(terms, stage, factor=1.0):
    rows, columns = terms[0].shape
    parts = 1 if stage is None else stage[2]
    return call(
        sum_kernel,
        [((rows // parts, columns), BF16)] * parts,
        terms=len(terms),
        stage=stage,
        factor=factor,
    )(*terms)


def join(groups, stage, cuts=1):
    rows, columns = groups[0][0].shape
    shape = (rows * len(groups[0]), columns * len(groups) // cuts)
    return call(
        join_kernel, [(shape, BF16)] * cuts, stage=stage, groups=len(groups), cuts=cuts
    )(*[piece for group in groups for piece in group])


def to_chips(arrays):
    _, shift, parts = CHIPS
    count = lax.axis_size("horiz")
    received = []
    for index, array in enumerate(arrays, 1):
        offsets = [-index % parts, index]
        route = [(i, i ^ (offsets[i % 2] << shift)) for i in range(count)]
        received.append(lax.ppermute(array, "horiz", route))
    return received


def reduce_chips(terms):
    parts = add(terms, CHIPS)
    return [parts[0]] + to_chips(parts[1:])


def collect_chips(piece):
    return [piece] + to_chips([piece] * (CHIPS[2] - 1))


def tie(*values):
    return lax.optimization_barrier(values)


def over_all_chips(piece, factor):
    core = lax.axis_index("horiz") % 2
    both = jnp.stack([jnp.where(core == side, piece, 0.0).astype(F32) for side in range(2)])
    return (lax.psum(both, "horiz")[core] * factor).astype(BF16)


def to_neighbours(upward, downward, axis):
    count = lax.axis_size(axis)
    forward = [(i, (i + 1) % count) for i in range(count)]
    backward = [(target, source) for source, target in forward]
    return lax.ppermute(upward, axis, forward), lax.ppermute(downward, axis, backward)


def per_device(
    prognostic, diffusivity, mixing, cotangent, tile_cols, pad_mask, tile_count, w_in, w_mid, w_out
):
    fields, lons, lats = prognostic.shape[1:]
    levels = diffusivity.shape[1]
    units = w_mid.shape[0]
    tiles, width = tile_cols.shape[2:]
    slots = tiles * width
    base = jnp.concatenate([prognostic[0], mixing], axis=0).reshape((fields + 2) * lons, lats)
    column = jnp.concatenate([cotangent[0], diffusivity[0]], axis=0)
    column = column.reshape((fields + levels) * lons, lats)
    weights = jnp.concatenate([w_mid, w_in], axis=1)
    cols, mask = tile_cols[0, 0], pad_mask[0, 0]

    packed = ((2 * fields + PACK_ROWS, lats), BF16)
    up_pack, down_pack = call(pack_kernel, [packed, packed], lons=lons)(base)
    low_pack, high_pack = to_neighbours(up_pack, down_pack, "horiz")

    adjoint, coef, ratio, inverse = call(
        adjoint_kernel,
        [((tiles, fields, width), F32)] + [((levels, slots), F32)] * 3,
        scratch=[pltpu.VMEM((tiles, fields, width), F32)],
        smem=(0,),
        moved=30 * 10**6,
        lons=lons,
    )(tile_count, column, cols, mask)

    hidden = ((units, slots), BF16)
    half = ((units // 2, units), BF16)
    moved, x_now, act_one, act_two, delta_two, keep_mid, send_mid = call(
        forward_kernel,
        [((lons, fields, lats), F32), ((fields, slots), BF16), hidden, hidden, hidden, half, half],
        moved=15 * 10**6,
        lons=lons,
    )(base, low_pack, high_pack, cols, adjoint, weights, w_out)
    column_total = lax.axis_size("ens") * lax.axis_size("horiz") * lons * lats
    factor = 1.0 / math.sqrt(column_total)
    (got_mid,) = exchange([send_mid], CORE)

    half = ((units // 2, 2 * fields), BF16)
    delta_one, keep_small, send_small = call(
        backward_kernel, [hidden, half, half], moved=4 * 10**6
    )(x_now, act_two, delta_two, adjoint, weights)
    (got_small,) = exchange([send_small], CORE)

    packed = ((2 * fields, lats), BF16)
    field, up_rows, down_rows = call(
        grad_kernel,
        [((lons, fields, lats), F32), packed, packed],
        smem=(0,),
        lons=lons,
    )(tile_count, column, cols, mask, delta_one, adjoint, weights)
    got_small, field = tie(got_small, field)

    members = lax.axis_size("ens")
    parts = call(core_sum_kernel, [((units // 2 // members, units + 2 * fields), BF16)] * members)(
        keep_mid, got_mid, keep_small, got_small
    )
    own, first, second, far = parts
    got_far = to_member(far, 0)
    got_first = to_member(first, 0)

    act_two, up_rows, down_rows = tie(act_two, up_rows, down_rows, parts)[:3]
    halos = to_neighbours(up_rows, down_rows, "horiz")
    (state_rows,) = call(
        state_kernel,
        [((fields * lons, lats), F32)],
        scratch=[pltpu.VMEM((tiles, fields, width), F32)] * 2,
        smem=(0,),
        lons=lons,
    )(tile_count, moved, cols, mask, x_now, act_two, coef, ratio, inverse, w_out)
    got_far, state_rows, halos = tie(got_far, state_rows, halos)
    terms = [own, got_first, to_member(add([second, got_far], None)[0], 1)]
    (grad_rows,) = call(last_kernel, [((fields * lons, lats), F32)], lons=lons)(
        field, *halos, low_pack, high_pack, base
    )
    terms, grad_rows = tie(terms, grad_rows)

    if lax.axis_size("horiz") == 8:
        terms = reduce_chips(terms)
        halves = join([collect_chips(add(terms, None, factor)[0])], CHIPS, cuts=2)
    else:
        halves = jnp.split(over_all_chips(add(terms, None)[0], factor), 2, axis=1)
    (own,) = join(collect_members(*halves), MEMBERS)
    (got,) = exchange([own], CORE)
    half_done = final(own, False, [], fields)
    grad_mid, grad_in, grad_out = final(got, True, half_done, fields)
    return (
        state_rows.reshape(prognostic.shape),
        grad_rows.reshape(prognostic.shape),
        grad_in,
        grad_mid,
        grad_out,
    )


def solution(mesh):
    placed = (
        P("ens", None, "horiz", None),
        P("ens", None, "horiz", None),
        P(None, "horiz", None),
        P("ens", None, "horiz", None),
        P("ens", "horiz", None, None),
        P("ens", "horiz", None, None),
        P("ens", "horiz"),
        P(),
        P(),
        P(),
    )
    return jax.shard_map(
        per_device,
        mesh=mesh,
        in_specs=placed,
        out_specs=(P("ens", None, "horiz", None), P("ens", None, "horiz", None), P(), P(), P()),
        check_vma=False,
    )
```

```python
import functools
import math

import jax
import jax.numpy as jnp
from jax import lax
from jax.experimental import pallas as pl
from jax.experimental.pallas import tpu as pltpu
from jax.sharding import PartitionSpec as P

DYN_STEPS = 2
BLOCK = 256
PACK_ROWS = 16
VMEM_LIMIT = 32 * 1024 * 1024
F32 = jnp.float32
BF16 = jnp.bfloat16
CONTRACT_LAST = (((1,), (1,)), ((), ()))
CONTRACT_FIRST = (((0,), (0,)), ((), ()))


def call(kernel, outs, scratch=(), smem=(), flops=0, moved=0, **names):
    def run(*operands):
        specs = [
            pl.BlockSpec(memory_space=pltpu.SMEM if place in smem else pltpu.VMEM)
            for place in range(len(operands))
        ]
        return pl.pallas_call(
            functools.partial(kernel, **names),
            out_shape=[jax.ShapeDtypeStruct(shape, dtype) for shape, dtype in outs],
            in_specs=specs,
            out_specs=[pl.BlockSpec(memory_space=pltpu.VMEM)] * len(outs),
            scratch_shapes=list(scratch),
            compiler_params=pltpu.CompilerParams(vmem_limit_bytes=VMEM_LIMIT),
            cost_estimate=pl.CostEstimate(flops=flops, bytes_accessed=moved, transcendentals=0),
        )(*operands)

    return run


def lat_term(field_now, coef_masked):
    lats = field_now.shape[1]
    north_flux = coef_masked * (pltpu.roll(field_now, lats - 1, 1) - field_now)
    return north_flux - pltpu.roll(north_flux, 1, 1)


def two_steps(rows, lon_coef, lat_coef):
    for repeat in range(DYN_STEPS):
        count = len(rows)
        fluxes = [
            lon_coef[place + repeat] * (rows[place + 1] - rows[place]) for place in range(count - 1)
        ]
        rows = [
            rows[place]
            + fluxes[place]
            - fluxes[place - 1]
            + lat_term(rows[place], lat_coef[place + repeat])
            for place in range(1, count - 1)
        ]
    return rows


def coefficients(base_ref, low_mix, high_mix, lons):
    lats = base_ref.shape[1]
    first = base_ref.shape[0] - 2 * lons
    lane = lax.broadcasted_iota(jnp.int32, (1, lats), 1)
    inside = lane < lats - 1
    own_lon = [base_ref[first + lon : first + lon + 1, :] for lon in range(lons)]
    first += lons
    own_lat = [base_ref[first + lon : first + lon + 1, :] for lon in range(lons)]
    lon_coef = [low_mix[0:1, :], low_mix[1:2, :]] + own_lon + [high_mix[0:1, :], high_mix[1:2, :]]
    lat_coef = [low_mix[2:3, :], low_mix[3:4, :]] + own_lat + [high_mix[2:3, :], high_mix[3:4, :]]
    return lon_coef, [jnp.where(inside, coef, 0.0) for coef in lat_coef]


def pack_kernel(base_ref, up_ref, down_ref, *, lons):
    fields = base_ref.shape[0] // lons - 2
    mixing = fields * lons
    for out_ref, first in ((up_ref, lons - 2), (down_ref, 0)):
        for side in range(2):
            out_ref[side * fields : (side + 1) * fields, :] = base_ref[
                pl.ds(first + side, fields, stride=lons), :
            ].astype(BF16)
        mix_rows = [
            base_ref[mixing + first : mixing + first + 2, :],
            base_ref[mixing + lons + first : mixing + lons + first + 2, :],
            jnp.zeros((PACK_ROWS - 4, base_ref.shape[1]), F32),
        ]
        out_ref[2 * fields :, :] = jnp.concatenate(mix_rows, axis=0).astype(BF16)


def halo_rows(pack_ref, fields):
    return [pack_ref[side * fields : (side + 1) * fields, :].astype(F32) for side in range(2)]


def halo_mixing(pack_ref, fields):
    return pack_ref[2 * fields :, :].astype(F32)


def one_hot(cols_ref, cells):
    parts = []
    for tile in range(cols_ref.shape[0]):
        place = lax.broadcasted_iota(jnp.int32, (cells, cols_ref.shape[1]), 0)
        parts.append(jnp.where(place == cols_ref[tile : tile + 1, :], 1.0, 0.0))
    return jnp.concatenate(parts, axis=1).astype(BF16)


def live_row(count_ref, mask_ref):
    parts = []
    for tile in range(mask_ref.shape[0]):
        used = jnp.where(tile < count_ref[0, 0], 1, 0)
        parts.append((mask_ref[tile : tile + 1, :] * used).astype(F32))
    return jnp.concatenate(parts, axis=1)


def level_rows(levels, level, variables):
    return pl.ds(level, variables, stride=levels)


def solve(levels, variables, coef_ref, ratio_ref, inverse_ref, right_ref, out_ref):
    tiles, _, width = right_ref.shape
    spans = [slice(tile * width, (tile + 1) * width) for tile in range(tiles)]
    values = []
    for level in range(levels):
        inverse_now = inverse_ref[level : level + 1, :]
        if level > 0:
            carry_now = coef_ref[level - 1 : level, :] * inverse_now
        step = []
        for tile, span in enumerate(spans):
            right_now = right_ref[tile, level_rows(levels, level, variables), :]
            value_now = right_now * inverse_now[:, span]
            if level > 0:
                value_now = value_now + carry_now[:, span] * values[-1][tile]
            step.append(value_now)
        values.append(step)
    results = values[-1]
    for level in range(levels - 1, -1, -1):
        if level < levels - 1:
            ratio_now = ratio_ref[level : level + 1, :]
            results = [
                values[level][tile] - ratio_now[:, span] * results[tile]
                for tile, span in enumerate(spans)
            ]
        for tile in range(tiles):
            out_ref[tile, level_rows(levels, level, variables), :] = results[tile]


def split_tiles(ref, value):
    width = ref.shape[2]
    for tile in range(ref.shape[0]):
        ref[tile] = value[:, tile * width : (tile + 1) * width]


def join_tiles(ref):
    return jnp.concatenate([ref[tile] for tile in range(ref.shape[0])], axis=1)


def factorise(levels, coef_ref, ratio_ref, inverse_ref):
    ratio_prev = None
    for level in range(levels):
        coef_now = coef_ref[level : level + 1, :]
        divisor = 1.0 + coef_now
        if level > 0:
            below_now = coef_ref[level - 1 : level, :]
            divisor = divisor + below_now + below_now * ratio_prev
        inverse_now = 1.0 / divisor
        ratio_prev = -coef_now * inverse_now
        inverse_ref[level : level + 1, :] = inverse_now
        ratio_ref[level : level + 1, :] = ratio_prev


def by_cell(ref, rows, lons):
    return jnp.concatenate(
        [ref[pl.ds(lon, rows, stride=lons), :] for lon in range(lons)], axis=1
    )


def adjoint_kernel(
    count_ref,
    column_ref,
    cols_ref,
    mask_ref,
    adj_ref,
    coef_ref,
    ratio_ref,
    inverse_ref,
    right_ref,
    *,
    lons,
):
    fields = adj_ref.shape[1]
    levels = coef_ref.shape[0]
    spread = one_hot(cols_ref, lons * column_ref.shape[1])
    sources = by_cell(column_ref, fields + levels, lons).astype(BF16)
    picked = jnp.dot(sources, spread, preferred_element_type=F32)
    split_tiles(right_ref, picked[:fields] * live_row(count_ref, mask_ref))
    coef_ref[...] = picked[fields:]
    factorise(levels, coef_ref, ratio_ref, inverse_ref)
    solve(levels, fields // levels, coef_ref, ratio_ref, inverse_ref, right_ref, adj_ref)


def sigmoid(pre_act):
    return 0.5 * jnp.tanh(0.5 * pre_act) + 0.5


def weight_product(left_ref, right, keep_ref, send_ref, first):
    half = left_ref.shape[0] // 2
    block = min(BLOCK, half)
    core = lax.axis_index("horiz") % 2
    for out_ref, side in ((send_ref, 1 - core), (keep_ref, core)):
        for start in range(0, half, block):
            out_ref[start : start + block, first : first + right.shape[0]] = lax.dot_general(
                left_ref[pl.ds(pl.multiple_of(side * half + start, block), block), :],
                right,
                CONTRACT_LAST,
                preferred_element_type=F32,
            ).astype(BF16)


def forward_kernel(
    base_ref,
    low_ref,
    high_ref,
    cols_ref,
    adj_ref,
    weights_ref,
    w_out_ref,
    moved_ref,
    x_ref,
    act_one_ref,
    act_two_ref,
    delta_two_ref,
    keep_ref,
    send_ref,
    *,
    lons,
):
    fields = x_ref.shape[0]
    units = weights_ref.shape[0]
    cells = lons * base_ref.shape[1]
    low_rows, high_rows = halo_rows(low_ref, fields), halo_rows(high_ref, fields)
    lon_coef, lat_coef = coefficients(
        base_ref, halo_mixing(low_ref, fields), halo_mixing(high_ref, fields), lons
    )
    rows = [base_ref[pl.ds(lon, fields, stride=lons), :] for lon in range(lons)]
    rows = two_steps(low_rows + rows + high_rows, lon_coef, lat_coef)
    for lon in range(lons):
        moved_ref[lon] = rows[lon]
    spread = one_hot(cols_ref, cells)
    sources = jnp.concatenate(rows, axis=1).astype(BF16)
    x_now = jnp.dot(sources, spread, preferred_element_type=F32).astype(BF16)
    x_ref[...] = x_now
    for start in range(0, units, BLOCK):
        pre_one = jnp.dot(weights_ref[start : start + BLOCK, units:], x_now, preferred_element_type=F32)
        act_one_ref[start : start + BLOCK, :] = (pre_one * sigmoid(pre_one)).astype(BF16)
    adj_half = join_tiles(adj_ref).astype(BF16)
    for start in range(0, units, BLOCK):
        pre_two = jnp.dot(
            weights_ref[start : start + BLOCK, :units], act_one_ref[...], preferred_element_type=F32
        )
        sigma_val = sigmoid(pre_two)
        act_two_ref[start : start + BLOCK, :] = (pre_two * sigma_val).astype(BF16)
        back_two = lax.dot_general(
            w_out_ref[:, start : start + BLOCK],
            adj_half,
            CONTRACT_FIRST,
            preferred_element_type=F32,
        )
        slope = sigma_val * (1.0 + pre_two * (1.0 - sigma_val))
        delta_two_ref[start : start + BLOCK, :] = (back_two * slope).astype(BF16)
    weight_product(delta_two_ref, act_one_ref[...], keep_ref, send_ref, 0)


def backward_kernel(
    x_ref,
    act_two_ref,
    delta_two_ref,
    adj_ref,
    weights_ref,
    delta_one_ref,
    keep_ref,
    send_ref,
):
    fields = x_ref.shape[0]
    units = weights_ref.shape[0]
    x_now = x_ref[...]
    for start in range(0, units, BLOCK):
        back_one = lax.dot_general(
            weights_ref[:, start : start + BLOCK],
            delta_two_ref[...],
            CONTRACT_FIRST,
            preferred_element_type=F32,
        )
        pre_one = jnp.dot(weights_ref[start : start + BLOCK, units:], x_now, preferred_element_type=F32)
        sigma_val = sigmoid(pre_one)
        slope = sigma_val * (1.0 + pre_one * (1.0 - sigma_val))
        delta_one_ref[start : start + BLOCK, :] = (back_one * slope).astype(BF16)
    weight_product(delta_one_ref, x_now, keep_ref, send_ref, 0)
    weight_product(act_two_ref, join_tiles(adj_ref).astype(BF16), keep_ref, send_ref, fields)


def place_back(fresh, live, cols_ref, cells):
    marks = jnp.broadcast_to(live, (16, live.shape[1]))
    placed = lax.dot_general(
        jnp.concatenate([fresh * live, marks], axis=0).astype(BF16),
        one_hot(cols_ref, cells),
        CONTRACT_LAST,
        preferred_element_type=F32,
    )
    rows = fresh.shape[0]
    return placed[:rows], placed[rows : rows + 1] > 0.5


def state_kernel(
    count_ref,
    moved_ref,
    cols_ref,
    mask_ref,
    x_ref,
    act_two_ref,
    coef_ref,
    ratio_ref,
    inverse_ref,
    w_out_ref,
    state_ref,
    forced_ref,
    solved_ref,
    *,
    lons,
):
    fields = x_ref.shape[0]
    levels = coef_ref.shape[0]
    lats = moved_ref.shape[2]
    tendency = jnp.dot(w_out_ref[...], act_two_ref[...], preferred_element_type=F32)
    split_tiles(forced_ref, x_ref[...].astype(F32) + tendency)
    solve(levels, fields // levels, coef_ref, ratio_ref, inverse_ref, forced_ref, solved_ref)
    placed, taken = place_back(
        join_tiles(solved_ref), live_row(count_ref, mask_ref), cols_ref, lons * lats
    )
    for lon in range(lons):
        here = slice(lon * lats, (lon + 1) * lats)
        state_ref[pl.ds(lon, fields, stride=lons), :] = jnp.where(
            taken[:, here], placed[:, here], moved_ref[lon]
        )


def grad_kernel(
    count_ref,
    column_ref,
    cols_ref,
    mask_ref,
    delta_one_ref,
    adj_ref,
    weights_ref,
    field_ref,
    up_ref,
    down_ref,
    *,
    lons,
):
    fields, lats = field_ref.shape[1:]
    grad_x = join_tiles(adj_ref) + lax.dot_general(
        weights_ref[:, delta_one_ref.shape[0] :], delta_one_ref[...], CONTRACT_FIRST, preferred_element_type=F32
    )
    placed, taken = place_back(grad_x, live_row(count_ref, mask_ref), cols_ref, lons * lats)
    for lon in range(lons):
        here = slice(lon * lats, (lon + 1) * lats)
        field_now = jnp.where(
            taken[:, here], placed[:, here], column_ref[pl.ds(lon, fields, stride=lons), :]
        )
        field_ref[lon] = field_now
        if lon < 2:
            down_ref[lon * fields : (lon + 1) * fields, :] = field_now.astype(BF16)
        if lon >= lons - 2:
            side = lon - (lons - 2)
            up_ref[side * fields : (side + 1) * fields, :] = field_now.astype(BF16)


def last_kernel(field_ref, low_ref, high_ref, low_mix_ref, high_mix_ref, base_ref, out_ref, *, lons):
    fields = field_ref.shape[1]
    low_rows, high_rows = halo_rows(low_ref, fields), halo_rows(high_ref, fields)
    lon_coef, lat_coef = coefficients(
        base_ref, halo_mixing(low_mix_ref, fields), halo_mixing(high_mix_ref, fields), lons
    )
    rows = [field_ref[lon] for lon in range(lons)]
    rows = two_steps(low_rows + rows + high_rows, lon_coef, lat_coef)
    for lon in range(lons):
        out_ref[pl.ds(lon, fields, stride=lons), :] = rows[lon]


CORE = ("horiz", 0, 2)
CHIPS = ("horiz", 1, 4)
MEMBERS = ("ens", 0, 4)
MEMBER_LOW, MEMBER_HIGH = ("ens", 0, 2), ("ens", 1, 2)


def position(stage):
    axis, shift, parts = stage
    return lax.axis_index(axis) // (1 << shift) % parts


def partner(stage, index):
    parts = stage[2]
    offset = jnp.where(lax.axis_index("horiz") % 2 == 0, -index % parts, index)
    return position(stage) ^ offset


def sum_kernel(*refs, terms, stage, factor):
    ins, outs = refs[:terms], refs[terms:]
    rows = outs[0].shape[0]
    for index, out_ref in enumerate(outs):
        here = pl.ds(0, rows)
        if stage is not None:
            start = partner(stage, index) * rows
            here = pl.ds(pl.multiple_of(start, rows), rows)
        total = ins[0][here, :].astype(F32)
        for ref in ins[1:]:
            total = total + ref[here, :].astype(F32)
        out_ref[...] = (total * factor).astype(BF16)


def join_kernel(*refs, stage, groups, cuts):
    ins, outs = refs[:-cuts], refs[-cuts:]
    count = len(ins) // groups
    rows, columns = ins[0].shape
    width = outs[0].shape[1]
    part = min(width, columns)
    for k in range(count):
        place = partner(stage, k) if stage == CHIPS else member_order()[k]
        here = pl.ds(pl.multiple_of(place * rows, rows), rows)
        for group in range(groups):
            for start in range(0, columns, part):
                first = group * columns + start
                outs[first // width][here, first % width : first % width + part] = ins[
                    group * count + k
                ][:, start : start + part]


def member_order():
    member, core = lax.axis_index("ens"), lax.axis_index("horiz") % 2
    return [member, member ^ (1 + core), member ^ (2 - core), member ^ 3]


def core_sum_kernel(keep_mid, got_mid, keep_small, got_small, *outs):
    rows = outs[0].shape[0]
    for member, out_ref in zip(member_order(), outs):
        here = pl.ds(pl.multiple_of(member * rows, rows), rows)
        first = 0
        for keep_ref, got_ref in ((keep_mid, got_mid), (keep_small, got_small)):
            columns = keep_ref.shape[1]
            out_ref[:, first : first + columns] = (
                keep_ref[here, :].astype(F32) + got_ref[here, :].astype(F32)
            ).astype(BF16)
            first += columns


def final_kernel(mid_half, small_half, *refs):
    mid_ref, in_ref, out_ref = refs[-3:]
    fields = in_ref.shape[1]
    mid_ref[...] = mid_half[...].astype(F32)

    @pl.when(pl.program_id(0) == 0)
    def _():
        in_ref[...] = small_half[:, :fields].astype(F32)
        out_ref[...] = small_half[:, fields:].astype(F32).T


def final(rows, other, before, fields):
    half, columns = rows.shape
    units = 2 * half
    block = units // 2

    def place():
        core = lax.axis_index("horiz") % 2
        return 1 - core if other else core

    return pl.pallas_call(
        final_kernel,
        grid=(units // block,),
        out_shape=[
            jax.ShapeDtypeStruct(shape, F32)
            for shape in ((units, units), (units, fields), (fields, units))
        ],
        in_specs=[
            pl.BlockSpec((half, block), lambda step: (0, step)),
            pl.BlockSpec((half, 2 * fields), lambda step: (0, units // (2 * fields))),
        ]
        + [pl.BlockSpec(memory_space=pl.ANY)] * len(before),
        out_specs=[
            pl.BlockSpec((half, block), lambda step: (place(), step)),
            pl.BlockSpec((half, fields), lambda step: (place(), 0)),
            pl.BlockSpec((fields, half), lambda step: (0, place())),
        ],
        input_output_aliases={2 + index: index for index in range(len(before))},
        compiler_params=pltpu.CompilerParams(vmem_limit_bytes=VMEM_LIMIT),
    )(rows, rows, *before)


def exchange(arrays, stage):
    axis, shift, _ = stage
    count = lax.axis_size(axis)
    sent = {}
    for k in range(len(arrays), 0, -1):
        route = [(i, i ^ (k << shift)) for i in range(count)]
        sent[k] = lax.ppermute(arrays[k - 1], axis, route)
    return [sent[k] for k in range(1, len(arrays) + 1)]


def to_member(array, second):
    members, count = lax.axis_size("ens"), lax.axis_size("horiz")
    route = []
    for member in range(members):
        for place in range(count):
            neighbour = member ^ (1 << (place % 2 ^ second))
            route.append((member * count + place, neighbour * count + place))
    return lax.ppermute(array, ("ens", "horiz"), route)


def collect_members(one, two):
    first_one = to_member(one, 0)
    second_two = to_member(two, 1)
    second_one = to_member(one, 1)
    first_two = to_member(two, 0)
    far_one = to_member(first_one, 1)
    far_two = to_member(second_two, 0)
    return [one, first_one, second_one, far_one], [two, first_two, second_two, far_two]


def add(terms, stage, factor=1.0):
    rows, columns = terms[0].shape
    parts = 1 if stage is None else stage[2]
    return call(
        sum_kernel,
        [((rows // parts, columns), BF16)] * parts,
        terms=len(terms),
        stage=stage,
        factor=factor,
    )(*terms)


def join(groups, stage, cuts=1):
    rows, columns = groups[0][0].shape
    shape = (rows * len(groups[0]), columns * len(groups) // cuts)
    return call(
        join_kernel, [(shape, BF16)] * cuts, stage=stage, groups=len(groups), cuts=cuts
    )(*[piece for group in groups for piece in group])


def to_chips(arrays):
    _, shift, parts = CHIPS
    count = lax.axis_size("horiz")
    received = []
    for index, array in enumerate(arrays, 1):
        offsets = [-index % parts, index]
        route = [(i, i ^ (offsets[i % 2] << shift)) for i in range(count)]
        received.append(lax.ppermute(array, "horiz", route))
    return received


def reduce_chips(terms):
    parts = add(terms, CHIPS)
    return [parts[0]] + to_chips(parts[1:])


def collect_chips(piece):
    return [piece] + to_chips([piece] * (CHIPS[2] - 1))


def tie(*values):
    return lax.optimization_barrier(values)


def over_all_chips(piece, factor):
    core = lax.axis_index("horiz") % 2
    both = jnp.stack([jnp.where(core == side, piece, 0.0).astype(F32) for side in range(2)])
    return (lax.psum(both, "horiz")[core] * factor).astype(BF16)


def to_neighbours(upward, downward, axis):
    count = lax.axis_size(axis)
    forward = [(i, (i + 1) % count) for i in range(count)]
    backward = [(target, source) for source, target in forward]
    return lax.ppermute(upward, axis, forward), lax.ppermute(downward, axis, backward)


def per_device(
    prognostic, diffusivity, mixing, cotangent, tile_cols, pad_mask, tile_count, w_in, w_mid, w_out
):
    fields, lons, lats = prognostic.shape[1:]
    levels = diffusivity.shape[1]
    units = w_mid.shape[0]
    tiles, width = tile_cols.shape[2:]
    slots = tiles * width
    base = jnp.concatenate([prognostic[0], mixing], axis=0).reshape((fields + 2) * lons, lats)
    column = jnp.concatenate([cotangent[0], diffusivity[0]], axis=0)
    column = column.reshape((fields + levels) * lons, lats)
    weights = jnp.concatenate([w_mid, w_in], axis=1)
    cols, mask = tile_cols[0, 0], pad_mask[0, 0]

    packed = ((2 * fields + PACK_ROWS, lats), BF16)
    up_pack, down_pack = call(pack_kernel, [packed, packed], lons=lons)(base)
    low_pack, high_pack = to_neighbours(up_pack, down_pack, "horiz")

    adjoint, coef, ratio, inverse = call(
        adjoint_kernel,
        [((tiles, fields, width), F32)] + [((levels, slots), F32)] * 3,
        scratch=[pltpu.VMEM((tiles, fields, width), F32)],
        smem=(0,),
        moved=30 * 10**6,
        lons=lons,
    )(tile_count, column, cols, mask)

    hidden = ((units, slots), BF16)
    half = ((units // 2, units), BF16)
    moved, x_now, act_one, act_two, delta_two, keep_mid, send_mid = call(
        forward_kernel,
        [((lons, fields, lats), F32), ((fields, slots), BF16), hidden, hidden, hidden, half, half],
        moved=15 * 10**6,
        lons=lons,
    )(base, low_pack, high_pack, cols, adjoint, weights, w_out)
    column_total = lax.axis_size("ens") * lax.axis_size("horiz") * lons * lats
    factor = 1.0 / math.sqrt(column_total)
    (got_mid,) = exchange([send_mid], CORE)

    half = ((units // 2, 2 * fields), BF16)
    delta_one, keep_small, send_small = call(
        backward_kernel, [hidden, half, half], moved=4 * 10**6
    )(x_now, act_two, delta_two, adjoint, weights)
    (got_small,) = exchange([send_small], CORE)

    packed = ((2 * fields, lats), BF16)
    field, up_rows, down_rows = call(
        grad_kernel,
        [((lons, fields, lats), F32), packed, packed],
        smem=(0,),
        lons=lons,
    )(tile_count, column, cols, mask, delta_one, adjoint, weights)
    got_small, field = tie(got_small, field)

    members = lax.axis_size("ens")
    parts = call(core_sum_kernel, [((units // 2 // members, units + 2 * fields), BF16)] * members)(
        keep_mid, got_mid, keep_small, got_small
    )
    own, first, second, far = parts
    got_far = to_member(far, 0)
    got_first = to_member(first, 0)

    act_two, up_rows, down_rows = tie(act_two, up_rows, down_rows, parts)[:3]
    halos = to_neighbours(up_rows, down_rows, "horiz")
    (state_rows,) = call(
        state_kernel,
        [((fields * lons, lats), F32)],
        scratch=[pltpu.VMEM((tiles, fields, width), F32)] * 2,
        smem=(0,),
        lons=lons,
    )(tile_count, moved, cols, mask, x_now, act_two, coef, ratio, inverse, w_out)
    got_far, state_rows, halos = tie(got_far, state_rows, halos)
    terms = [own, got_first, to_member(add([second, got_far], None)[0], 1)]
    (grad_rows,) = call(last_kernel, [((fields * lons, lats), F32)], lons=lons)(
        field, *halos, low_pack, high_pack, base
    )
    terms, grad_rows = tie(terms, grad_rows)

    if lax.axis_size("horiz") == 8:
        terms = reduce_chips(terms)
        halves = join([collect_chips(add(terms, None, factor)[0])], CHIPS, cuts=2)
    else:
        halves = jnp.split(over_all_chips(add(terms, None)[0], factor), 2, axis=1)
    (own,) = join(collect_members(*halves), MEMBERS)
    (got,) = exchange([own], CORE)
    half_done = final(own, False, [], fields)
    grad_mid, grad_in, grad_out = final(got, True, half_done, fields)
    return (
        state_rows.reshape(prognostic.shape),
        grad_rows.reshape(prognostic.shape),
        grad_in,
        grad_mid,
        grad_out,
    )


def solution(mesh):
    placed = (
        P("ens", None, "horiz", None),
        P("ens", None, "horiz", None),
        P(None, "horiz", None),
        P("ens", None, "horiz", None),
        P("ens", "horiz", None, None),
        P("ens", "horiz", None, None),
        P("ens", "horiz"),
        P(),
        P(),
        P(),
    )
    return jax.shard_map(
        per_device,
        mesh=mesh,
        in_specs=placed,
        out_specs=(P("ens", None, "horiz", None), P("ens", None, "horiz", None), P(), P(), P()),
        check_vma=False,
    )
```

```python
import functools
import math

import jax
import jax.numpy as jnp
from jax import lax
from jax.experimental import pallas as pl
from jax.experimental.pallas import tpu as pltpu
from jax.sharding import PartitionSpec as P

DYN_STEPS = 2
BLOCK = 256
LAYER_BLOCK = 128
PACK_ROWS = 16
VMEM_LIMIT = 32 * 1024 * 1024
F32 = jnp.float32
BF16 = jnp.bfloat16
CONTRACT_LAST = (((1,), (1,)), ((), ()))
CONTRACT_FIRST = (((0,), (0,)), ((), ()))


def call(kernel, outs, scratch=(), smem=(), flops=0, moved=0, **names):
    def run(*operands):
        specs = [
            pl.BlockSpec(memory_space=pltpu.SMEM if place in smem else pltpu.VMEM)
            for place in range(len(operands))
        ]
        return pl.pallas_call(
            functools.partial(kernel, **names),
            out_shape=[jax.ShapeDtypeStruct(shape, dtype) for shape, dtype in outs],
            in_specs=specs,
            out_specs=[pl.BlockSpec(memory_space=pltpu.VMEM)] * len(outs),
            scratch_shapes=list(scratch),
            compiler_params=pltpu.CompilerParams(vmem_limit_bytes=VMEM_LIMIT),
            cost_estimate=pl.CostEstimate(flops=flops, bytes_accessed=moved, transcendentals=0),
        )(*operands)

    return run


def lat_term(field_now, coef_masked):
    lats = field_now.shape[1]
    north_flux = coef_masked * (pltpu.roll(field_now, lats - 1, 1) - field_now)
    return north_flux - pltpu.roll(north_flux, 1, 1)


def two_steps(rows, lon_coef, lat_coef):
    for repeat in range(DYN_STEPS):
        count = len(rows)
        fluxes = [
            lon_coef[place + repeat] * (rows[place + 1] - rows[place]) for place in range(count - 1)
        ]
        rows = [
            rows[place]
            + fluxes[place]
            - fluxes[place - 1]
            + lat_term(rows[place], lat_coef[place + repeat])
            for place in range(1, count - 1)
        ]
    return rows


def coefficients(base_ref, low_mix, high_mix, lons):
    lats = base_ref.shape[1]
    first = base_ref.shape[0] - 2 * lons
    lane = lax.broadcasted_iota(jnp.int32, (1, lats), 1)
    inside = lane < lats - 1
    own_lon = [base_ref[first + lon : first + lon + 1, :] for lon in range(lons)]
    first += lons
    own_lat = [base_ref[first + lon : first + lon + 1, :] for lon in range(lons)]
    lon_coef = [low_mix[0:1, :], low_mix[1:2, :]] + own_lon + [high_mix[0:1, :], high_mix[1:2, :]]
    lat_coef = [low_mix[2:3, :], low_mix[3:4, :]] + own_lat + [high_mix[2:3, :], high_mix[3:4, :]]
    return lon_coef, [jnp.where(inside, coef, 0.0) for coef in lat_coef]


def pack_kernel(base_ref, up_ref, down_ref, *, lons):
    fields = base_ref.shape[0] // lons - 2
    mixing = fields * lons
    for out_ref, first in ((up_ref, lons - 2), (down_ref, 0)):
        for side in range(2):
            out_ref[side * fields : (side + 1) * fields, :] = base_ref[
                pl.ds(first + side, fields, stride=lons), :
            ].astype(BF16)
        mix_rows = [
            base_ref[mixing + first : mixing + first + 2, :],
            base_ref[mixing + lons + first : mixing + lons + first + 2, :],
            jnp.zeros((PACK_ROWS - 4, base_ref.shape[1]), F32),
        ]
        out_ref[2 * fields :, :] = jnp.concatenate(mix_rows, axis=0).astype(BF16)


def halo_rows(pack_ref, fields):
    return [pack_ref[side * fields : (side + 1) * fields, :].astype(F32) for side in range(2)]


def halo_mixing(pack_ref, fields):
    return pack_ref[2 * fields :, :].astype(F32)


def one_hot(cols_ref, cells):
    parts = []
    for tile in range(cols_ref.shape[0]):
        place = lax.broadcasted_iota(jnp.int32, (cells, cols_ref.shape[1]), 0)
        parts.append(jnp.where(place == cols_ref[tile : tile + 1, :], 1.0, 0.0))
    return jnp.concatenate(parts, axis=1).astype(BF16)


def live_row(count_ref, mask_ref):
    parts = []
    for tile in range(mask_ref.shape[0]):
        used = jnp.where(tile < count_ref[0, 0], 1, 0)
        parts.append((mask_ref[tile : tile + 1, :] * used).astype(F32))
    return jnp.concatenate(parts, axis=1)


def level_rows(levels, level, variables):
    return pl.ds(level, variables, stride=levels)


def solve(levels, variables, coef_ref, ratio_ref, inverse_ref, right_ref, out_ref):
    tiles, _, width = right_ref.shape
    spans = [slice(tile * width, (tile + 1) * width) for tile in range(tiles)]
    values = []
    for level in range(levels):
        inverse_now = inverse_ref[level : level + 1, :]
        if level > 0:
            carry_now = coef_ref[level - 1 : level, :] * inverse_now
        step = []
        for tile, span in enumerate(spans):
            right_now = right_ref[tile, level_rows(levels, level, variables), :]
            value_now = right_now * inverse_now[:, span]
            if level > 0:
                value_now = value_now + carry_now[:, span] * values[-1][tile]
            step.append(value_now)
        values.append(step)
    results = values[-1]
    for level in range(levels - 1, -1, -1):
        if level < levels - 1:
            ratio_now = ratio_ref[level : level + 1, :]
            results = [
                values[level][tile] - ratio_now[:, span] * results[tile]
                for tile, span in enumerate(spans)
            ]
        for tile in range(tiles):
            out_ref[tile, level_rows(levels, level, variables), :] = results[tile]


def split_tiles(ref, value):
    width = ref.shape[2]
    for tile in range(ref.shape[0]):
        ref[tile] = value[:, tile * width : (tile + 1) * width]


def join_tiles(ref):
    return jnp.concatenate([ref[tile] for tile in range(ref.shape[0])], axis=1)


def factorise(levels, coef_ref, ratio_ref, inverse_ref):
    ratio_prev = None
    for level in range(levels):
        coef_now = coef_ref[level : level + 1, :]
        divisor = 1.0 + coef_now
        if level > 0:
            below_now = coef_ref[level - 1 : level, :]
            divisor = divisor + below_now + below_now * ratio_prev
        inverse_now = 1.0 / divisor
        ratio_prev = -coef_now * inverse_now
        inverse_ref[level : level + 1, :] = inverse_now
        ratio_ref[level : level + 1, :] = ratio_prev


def by_cell(ref, rows, lons):
    return jnp.concatenate(
        [ref[pl.ds(lon, rows, stride=lons), :] for lon in range(lons)], axis=1
    )


def adjoint_kernel(
    count_ref,
    column_ref,
    cols_ref,
    mask_ref,
    adj_ref,
    coef_ref,
    ratio_ref,
    inverse_ref,
    right_ref,
    *,
    lons,
):
    fields = adj_ref.shape[1]
    levels = coef_ref.shape[0]
    spread = one_hot(cols_ref, lons * column_ref.shape[1])
    sources = by_cell(column_ref, fields + levels, lons).astype(BF16)
    picked = jnp.dot(sources, spread, preferred_element_type=F32)
    split_tiles(right_ref, picked[:fields] * live_row(count_ref, mask_ref))
    coef_ref[...] = picked[fields:]
    factorise(levels, coef_ref, ratio_ref, inverse_ref)
    solve(levels, fields // levels, coef_ref, ratio_ref, inverse_ref, right_ref, adj_ref)


def sigmoid(pre_act):
    return 0.5 * jnp.tanh(0.5 * pre_act) + 0.5


def weight_product(left_ref, right, keep_ref, send_ref, first):
    half = left_ref.shape[0] // 2
    block = min(BLOCK, half)
    core = lax.axis_index("horiz") % 2
    for out_ref, side in ((send_ref, 1 - core), (keep_ref, core)):
        for start in range(0, half, block):
            out_ref[start : start + block, first : first + right.shape[0]] = lax.dot_general(
                left_ref[pl.ds(pl.multiple_of(side * half + start, block), block), :],
                right,
                CONTRACT_LAST,
                preferred_element_type=F32,
            ).astype(BF16)


def forward_kernel(
    base_ref,
    low_ref,
    high_ref,
    cols_ref,
    adj_ref,
    weights_ref,
    w_out_ref,
    moved_ref,
    x_ref,
    act_one_ref,
    act_two_ref,
    delta_two_ref,
    keep_ref,
    send_ref,
    *,
    lons,
):
    fields = x_ref.shape[0]
    units = weights_ref.shape[0]
    cells = lons * base_ref.shape[1]
    low_rows, high_rows = halo_rows(low_ref, fields), halo_rows(high_ref, fields)
    lon_coef, lat_coef = coefficients(
        base_ref, halo_mixing(low_ref, fields), halo_mixing(high_ref, fields), lons
    )
    rows = [base_ref[pl.ds(lon, fields, stride=lons), :] for lon in range(lons)]
    rows = two_steps(low_rows + rows + high_rows, lon_coef, lat_coef)
    for lon in range(lons):
        moved_ref[lon] = rows[lon]
    spread = one_hot(cols_ref, cells)
    sources = jnp.concatenate(rows, axis=1).astype(BF16)
    x_now = jnp.dot(sources, spread, preferred_element_type=F32).astype(BF16)
    x_ref[...] = x_now
    for start in range(0, units, LAYER_BLOCK):
        pre_one = jnp.dot(weights_ref[start : start + LAYER_BLOCK, units:], x_now, preferred_element_type=F32)
        act_one_ref[start : start + LAYER_BLOCK, :] = (pre_one * sigmoid(pre_one)).astype(BF16)
    adj_half = join_tiles(adj_ref).astype(BF16)
    for start in range(0, units, LAYER_BLOCK):
        pre_two = jnp.dot(
            weights_ref[start : start + LAYER_BLOCK, :units], act_one_ref[...], preferred_element_type=F32
        )
        sigma_val = sigmoid(pre_two)
        act_two_ref[start : start + LAYER_BLOCK, :] = (pre_two * sigma_val).astype(BF16)
        back_two = lax.dot_general(
            w_out_ref[:, start : start + LAYER_BLOCK],
            adj_half,
            CONTRACT_FIRST,
            preferred_element_type=F32,
        )
        slope = sigma_val * (1.0 + pre_two * (1.0 - sigma_val))
        delta_two_ref[start : start + LAYER_BLOCK, :] = (back_two * slope).astype(BF16)
    weight_product(delta_two_ref, act_one_ref[...], keep_ref, send_ref, 0)


def backward_kernel(
    x_ref,
    act_two_ref,
    delta_two_ref,
    adj_ref,
    weights_ref,
    delta_one_ref,
    keep_ref,
    send_ref,
):
    fields = x_ref.shape[0]
    units = weights_ref.shape[0]
    x_now = x_ref[...]
    for start in range(0, units, LAYER_BLOCK):
        back_one = lax.dot_general(
            weights_ref[:, start : start + LAYER_BLOCK],
            delta_two_ref[...],
            CONTRACT_FIRST,
            preferred_element_type=F32,
        )
        pre_one = jnp.dot(weights_ref[start : start + LAYER_BLOCK, units:], x_now, preferred_element_type=F32)
        sigma_val = sigmoid(pre_one)
        slope = sigma_val * (1.0 + pre_one * (1.0 - sigma_val))
        delta_one_ref[start : start + LAYER_BLOCK, :] = (back_one * slope).astype(BF16)
    weight_product(delta_one_ref, x_now, keep_ref, send_ref, 0)
    weight_product(act_two_ref, join_tiles(adj_ref).astype(BF16), keep_ref, send_ref, fields)


def place_back(fresh, live, cols_ref, cells):
    marks = jnp.broadcast_to(live, (16, live.shape[1]))
    placed = lax.dot_general(
        jnp.concatenate([fresh * live, marks], axis=0).astype(BF16),
        one_hot(cols_ref, cells),
        CONTRACT_LAST,
        preferred_element_type=F32,
    )
    rows = fresh.shape[0]
    return placed[:rows], placed[rows : rows + 1] > 0.5


def state_kernel(
    count_ref,
    moved_ref,
    cols_ref,
    mask_ref,
    x_ref,
    act_two_ref,
    coef_ref,
    ratio_ref,
    inverse_ref,
    w_out_ref,
    state_ref,
    forced_ref,
    solved_ref,
    *,
    lons,
):
    fields = x_ref.shape[0]
    levels = coef_ref.shape[0]
    lats = moved_ref.shape[2]
    tendency = jnp.dot(w_out_ref[...], act_two_ref[...], preferred_element_type=F32)
    split_tiles(forced_ref, x_ref[...].astype(F32) + tendency)
    solve(levels, fields // levels, coef_ref, ratio_ref, inverse_ref, forced_ref, solved_ref)
    placed, taken = place_back(
        join_tiles(solved_ref), live_row(count_ref, mask_ref), cols_ref, lons * lats
    )
    for lon in range(lons):
        here = slice(lon * lats, (lon + 1) * lats)
        state_ref[pl.ds(lon, fields, stride=lons), :] = jnp.where(
            taken[:, here], placed[:, here], moved_ref[lon]
        )


def grad_kernel(
    count_ref,
    column_ref,
    cols_ref,
    mask_ref,
    delta_one_ref,
    adj_ref,
    weights_ref,
    field_ref,
    up_ref,
    down_ref,
    *,
    lons,
):
    fields, lats = field_ref.shape[1:]
    grad_x = join_tiles(adj_ref) + lax.dot_general(
        weights_ref[:, delta_one_ref.shape[0] :], delta_one_ref[...], CONTRACT_FIRST, preferred_element_type=F32
    )
    placed, taken = place_back(grad_x, live_row(count_ref, mask_ref), cols_ref, lons * lats)
    for lon in range(lons):
        here = slice(lon * lats, (lon + 1) * lats)
        field_now = jnp.where(
            taken[:, here], placed[:, here], column_ref[pl.ds(lon, fields, stride=lons), :]
        )
        field_ref[lon] = field_now
        if lon < 2:
            down_ref[lon * fields : (lon + 1) * fields, :] = field_now.astype(BF16)
        if lon >= lons - 2:
            side = lon - (lons - 2)
            up_ref[side * fields : (side + 1) * fields, :] = field_now.astype(BF16)


def last_kernel(field_ref, low_ref, high_ref, low_mix_ref, high_mix_ref, base_ref, out_ref, *, lons):
    fields = field_ref.shape[1]
    low_rows, high_rows = halo_rows(low_ref, fields), halo_rows(high_ref, fields)
    lon_coef, lat_coef = coefficients(
        base_ref, halo_mixing(low_mix_ref, fields), halo_mixing(high_mix_ref, fields), lons
    )
    rows = [field_ref[lon] for lon in range(lons)]
    rows = two_steps(low_rows + rows + high_rows, lon_coef, lat_coef)
    for lon in range(lons):
        out_ref[pl.ds(lon, fields, stride=lons), :] = rows[lon]


CORE = ("horiz", 0, 2)
CHIPS = ("horiz", 1, 4)
MEMBERS = ("ens", 0, 4)
MEMBER_LOW, MEMBER_HIGH = ("ens", 0, 2), ("ens", 1, 2)


def position(stage):
    axis, shift, parts = stage
    return lax.axis_index(axis) // (1 << shift) % parts


def partner(stage, index):
    parts = stage[2]
    offset = jnp.where(lax.axis_index("horiz") % 2 == 0, -index % parts, index)
    return position(stage) ^ offset


def sum_kernel(*refs, terms, stage, factor):
    ins, outs = refs[:terms], refs[terms:]
    rows = outs[0].shape[0]
    for index, out_ref in enumerate(outs):
        here = pl.ds(0, rows)
        if stage is not None:
            start = partner(stage, index) * rows
            here = pl.ds(pl.multiple_of(start, rows), rows)
        total = ins[0][here, :].astype(F32)
        for ref in ins[1:]:
            total = total + ref[here, :].astype(F32)
        out_ref[...] = (total * factor).astype(BF16)


def join_kernel(*refs, stage, groups, cuts):
    ins, outs = refs[:-cuts], refs[-cuts:]
    count = len(ins) // groups
    rows, columns = ins[0].shape
    width = outs[0].shape[1]
    part = min(width, columns)
    for k in range(count):
        place = partner(stage, k) if stage == CHIPS else member_order()[k]
        here = pl.ds(pl.multiple_of(place * rows, rows), rows)
        for group in range(groups):
            for start in range(0, columns, part):
                first = group * columns + start
                outs[first // width][here, first % width : first % width + part] = ins[
                    group * count + k
                ][:, start : start + part]


def member_order():
    member, core = lax.axis_index("ens"), lax.axis_index("horiz") % 2
    return [member, member ^ (1 + core), member ^ (2 - core), member ^ 3]


def core_sum_kernel(keep_mid, got_mid, keep_small, got_small, *outs):
    rows = outs[0].shape[0]
    for member, out_ref in zip(member_order(), outs):
        here = pl.ds(pl.multiple_of(member * rows, rows), rows)
        first = 0
        for keep_ref, got_ref in ((keep_mid, got_mid), (keep_small, got_small)):
            columns = keep_ref.shape[1]
            out_ref[:, first : first + columns] = (
                keep_ref[here, :].astype(F32) + got_ref[here, :].astype(F32)
            ).astype(BF16)
            first += columns


def final_kernel(mid_half, small_half, *refs):
    mid_ref, in_ref, out_ref = refs[-3:]
    fields = in_ref.shape[1]
    mid_ref[...] = mid_half[...].astype(F32)

    @pl.when(pl.program_id(0) == 0)
    def _():
        in_ref[...] = small_half[:, :fields].astype(F32)
        out_ref[...] = small_half[:, fields:].astype(F32).T


def final(rows, other, before, fields):
    half, columns = rows.shape
    units = 2 * half
    block = units

    def place():
        core = lax.axis_index("horiz") % 2
        return 1 - core if other else core

    return pl.pallas_call(
        final_kernel,
        grid=(units // block,),
        out_shape=[
            jax.ShapeDtypeStruct(shape, F32)
            for shape in ((units, units), (units, fields), (fields, units))
        ],
        in_specs=[
            pl.BlockSpec((half, block), lambda step: (0, step)),
            pl.BlockSpec((half, 2 * fields), lambda step: (0, units // (2 * fields))),
        ]
        + [pl.BlockSpec(memory_space=pl.ANY)] * len(before),
        out_specs=[
            pl.BlockSpec((half, block), lambda step: (place(), step)),
            pl.BlockSpec((half, fields), lambda step: (place(), 0)),
            pl.BlockSpec((fields, half), lambda step: (0, place())),
        ],
        input_output_aliases={2 + index: index for index in range(len(before))},
        compiler_params=pltpu.CompilerParams(vmem_limit_bytes=VMEM_LIMIT),
    )(rows, rows, *before)


def exchange(arrays, stage):
    axis, shift, _ = stage
    count = lax.axis_size(axis)
    sent = {}
    for k in range(len(arrays), 0, -1):
        route = [(i, i ^ (k << shift)) for i in range(count)]
        sent[k] = lax.ppermute(arrays[k - 1], axis, route)
    return [sent[k] for k in range(1, len(arrays) + 1)]


def to_member(array, second):
    members, count = lax.axis_size("ens"), lax.axis_size("horiz")
    route = []
    for member in range(members):
        for place in range(count):
            neighbour = member ^ (1 << (place % 2 ^ second))
            route.append((member * count + place, neighbour * count + place))
    return lax.ppermute(array, ("ens", "horiz"), route)


def collect_members(one, two):
    first_one = to_member(one, 0)
    second_two = to_member(two, 1)
    second_one = to_member(one, 1)
    first_two = to_member(two, 0)
    far_one = to_member(first_one, 1)
    far_two = to_member(second_two, 0)
    return [one, first_one, second_one, far_one], [two, first_two, second_two, far_two]


def add(terms, stage, factor=1.0):
    rows, columns = terms[0].shape
    parts = 1 if stage is None else stage[2]
    return call(
        sum_kernel,
        [((rows // parts, columns), BF16)] * parts,
        terms=len(terms),
        stage=stage,
        factor=factor,
    )(*terms)


def join(groups, stage, cuts=1):
    rows, columns = groups[0][0].shape
    shape = (rows * len(groups[0]), columns * len(groups) // cuts)
    return call(
        join_kernel, [(shape, BF16)] * cuts, stage=stage, groups=len(groups), cuts=cuts
    )(*[piece for group in groups for piece in group])


def to_chips(arrays):
    _, shift, parts = CHIPS
    count = lax.axis_size("horiz")
    received = []
    for index, array in enumerate(arrays, 1):
        offsets = [-index % parts, index]
        route = [(i, i ^ (offsets[i % 2] << shift)) for i in range(count)]
        received.append(lax.ppermute(array, "horiz", route))
    return received


def reduce_chips(terms):
    parts = add(terms, CHIPS)
    return [parts[0]] + to_chips(parts[1:])


def collect_chips(piece):
    return [piece] + to_chips([piece] * (CHIPS[2] - 1))


def tie(*values):
    return lax.optimization_barrier(values)


def over_all_chips(piece, factor):
    core = lax.axis_index("horiz") % 2
    both = jnp.stack([jnp.where(core == side, piece, 0.0).astype(F32) for side in range(2)])
    return (lax.psum(both, "horiz")[core] * factor).astype(BF16)


def to_neighbours(upward, downward, axis):
    count = lax.axis_size(axis)
    forward = [(i, (i + 1) % count) for i in range(count)]
    backward = [(target, source) for source, target in forward]
    return lax.ppermute(upward, axis, forward), lax.ppermute(downward, axis, backward)


def per_device(
    prognostic, diffusivity, mixing, cotangent, tile_cols, pad_mask, tile_count, w_in, w_mid, w_out
):
    fields, lons, lats = prognostic.shape[1:]
    levels = diffusivity.shape[1]
    units = w_mid.shape[0]
    tiles, width = tile_cols.shape[2:]
    slots = tiles * width
    base = jnp.concatenate([prognostic[0], mixing], axis=0).reshape((fields + 2) * lons, lats)
    column = jnp.concatenate([cotangent[0], diffusivity[0]], axis=0)
    column = column.reshape((fields + levels) * lons, lats)
    weights = jnp.concatenate([w_mid, w_in], axis=1)
    cols, mask = tile_cols[0, 0], pad_mask[0, 0]

    packed = ((2 * fields + PACK_ROWS, lats), BF16)
    up_pack, down_pack = call(pack_kernel, [packed, packed], lons=lons)(base)
    low_pack, high_pack = to_neighbours(up_pack, down_pack, "horiz")

    adjoint, coef, ratio, inverse = call(
        adjoint_kernel,
        [((tiles, fields, width), F32)] + [((levels, slots), F32)] * 3,
        scratch=[pltpu.VMEM((tiles, fields, width), F32)],
        smem=(0,),
        moved=30 * 10**6,
        lons=lons,
    )(tile_count, column, cols, mask)

    hidden = ((units, slots), BF16)
    half = ((units // 2, units), BF16)
    moved, x_now, act_one, act_two, delta_two, keep_mid, send_mid = call(
        forward_kernel,
        [((lons, fields, lats), F32), ((fields, slots), BF16), hidden, hidden, hidden, half, half],
        moved=15 * 10**6,
        lons=lons,
    )(base, low_pack, high_pack, cols, adjoint, weights, w_out)
    column_total = lax.axis_size("ens") * lax.axis_size("horiz") * lons * lats
    factor = 1.0 / math.sqrt(column_total)
    (got_mid,) = exchange([send_mid], CORE)

    half = ((units // 2, 2 * fields), BF16)
    delta_one, keep_small, send_small = call(
        backward_kernel, [hidden, half, half], moved=4 * 10**6
    )(x_now, act_two, delta_two, adjoint, weights)
    (got_small,) = exchange([send_small], CORE)

    packed = ((2 * fields, lats), BF16)
    field, up_rows, down_rows = call(
        grad_kernel,
        [((lons, fields, lats), F32), packed, packed],
        smem=(0,),
        lons=lons,
    )(tile_count, column, cols, mask, delta_one, adjoint, weights)
    got_small, field = tie(got_small, field)

    members = lax.axis_size("ens")
    parts = call(core_sum_kernel, [((units // 2 // members, units + 2 * fields), BF16)] * members)(
        keep_mid, got_mid, keep_small, got_small
    )
    own, first, second, far = parts
    got_far = to_member(far, 0)
    got_first = to_member(first, 0)

    act_two, up_rows, down_rows = tie(act_two, up_rows, down_rows, parts)[:3]
    halos = to_neighbours(up_rows, down_rows, "horiz")
    (state_rows,) = call(
        state_kernel,
        [((fields * lons, lats), F32)],
        scratch=[pltpu.VMEM((tiles, fields, width), F32)] * 2,
        smem=(0,),
        lons=lons,
    )(tile_count, moved, cols, mask, x_now, act_two, coef, ratio, inverse, w_out)
    got_far, state_rows, halos = tie(got_far, state_rows, halos)
    terms = [own, got_first, to_member(add([second, got_far], None)[0], 1)]
    (grad_rows,) = call(last_kernel, [((fields * lons, lats), F32)], lons=lons)(
        field, *halos, low_pack, high_pack, base
    )
    terms, grad_rows = tie(terms, grad_rows)

    if lax.axis_size("horiz") == 8:
        terms = reduce_chips(terms)
        halves = join([collect_chips(add(terms, None, factor)[0])], CHIPS, cuts=2)
    else:
        halves = jnp.split(over_all_chips(add(terms, None)[0], factor), 2, axis=1)
    (own,) = join(collect_members(*halves), MEMBERS)
    (got,) = exchange([own], CORE)
    half_done = final(own, False, [], fields)
    grad_mid, grad_in, grad_out = final(got, True, half_done, fields)
    return (
        state_rows.reshape(prognostic.shape),
        grad_rows.reshape(prognostic.shape),
        grad_in,
        grad_mid,
        grad_out,
    )


def solution(mesh):
    placed = (
        P("ens", None, "horiz", None),
        P("ens", None, "horiz", None),
        P(None, "horiz", None),
        P("ens", None, "horiz", None),
        P("ens", "horiz", None, None),
        P("ens", "horiz", None, None),
        P("ens", "horiz"),
        P(),
        P(),
        P(),
    )
    return jax.shard_map(
        per_device,
        mesh=mesh,
        in_specs=placed,
        out_specs=(P("ens", None, "horiz", None), P("ens", None, "horiz", None), P(), P(), P()),
        check_vma=False,
    )
```
